32 devices in a mesh: fsdp: 8 (over z, y), mem: 4 (over x, core).
Axes of the slice: x: 2, y: 2, z: 4, core: 2. Of those that a mesh axis runs over, the one named last changes fastest.
Arguments:
- suffix: bfloat16 [256, 32, 768], P('fsdp'), may hold values from -6 to 6
- memory: bfloat16 [256, 256, 768], P('fsdp', 'mem'), may hold values from -6 to 6
- counts: int32 [256], P('fsdp'), may hold values from 0 to 256, as said below
- cotangent: bfloat16 [256, 32, 768], P('fsdp'), may hold values from -6 to 6
- self_norm_gain: bfloat16 [768], P('fsdp'), may hold values from 0.5 to 1.5
- self_norm_bias: bfloat16 [768], P('fsdp'), may hold values from -1.5 to 1.5
- self_query: bfloat16 [768, 768], P('fsdp'), may hold values from -0.21875 to 0.21875
- self_key: bfloat16 [768, 768], P('fsdp'), may hold values from -0.21875 to 0.21875
- self_value: bfloat16 [768, 768], P('fsdp'), may hold values from -0.21875 to 0.21875
- self_output: bfloat16 [768, 768], P('fsdp'), may hold values from -0.4375 to 0.4375
- cross_norm_gain: bfloat16 [768], P('fsdp'), may hold values from 0.5 to 1.5
- cross_norm_bias: bfloat16 [768], P('fsdp'), may hold values from -1.5 to 1.5
- cross_query: bfloat16 [768, 768], P('fsdp'), may hold values from -0.21875 to 0.21875
- cross_key: bfloat16 [768, 768], P('fsdp'), may hold values from -0.21875 to 0.21875
- cross_value: bfloat16 [768, 768], P('fsdp'), may hold values from -0.21875 to 0.21875
- cross_output: bfloat16 [768, 768], P('fsdp'), may hold values from -1.25 to 1.25
- dense_norm_gain: bfloat16 [768], P('fsdp'), may hold values from 0.5 to 1.5
- dense_norm_bias: bfloat16 [768], P('fsdp'), may hold values from -1.5 to 1.5
- dense_in: bfloat16 [768, 3072], P('fsdp'), may hold values from -0.21875 to 0.21875
- dense_in_bias: bfloat16 [3072], P('fsdp'), may hold values from -2.5 to 2.5
- dense_out: bfloat16 [3072, 768], P('fsdp'), may hold values from -0.109375 to 0.109375
- dense_out_bias: bfloat16 [768], P('fsdp'), may hold values from -2.5 to 2.5
Outputs:
- block_output: bfloat16 [256, 32, 768], P('fsdp')
- suffix_grad: bfloat16 [256, 32, 768], P('fsdp')
- memory_grad: bfloat16 [256, 256, 768], P('fsdp', 'mem')
- self_norm_gain_grad: float32 [768], P('fsdp')
- self_norm_bias_grad: float32 [768], P('fsdp')
- self_query_grad: float32 [768, 768], P('fsdp')
- self_key_grad: float32 [768, 768], P('fsdp')
- self_value_grad: float32 [768, 768], P('fsdp')
- self_output_grad: float32 [768, 768], P('fsdp')
- cross_norm_gain_grad: float32 [768], P('fsdp')
- cross_norm_bias_grad: float32 [768], P('fsdp')
- cross_query_grad: float32 [768, 768], P('fsdp')
- cross_key_grad: float32 [768, 768], P('fsdp')
- cross_value_grad: float32 [768, 768], P('fsdp')
- cross_output_grad: float32 [768, 768], P('fsdp')
- dense_norm_gain_grad: float32 [768], P('fsdp')
- dense_norm_bias_grad: float32 [768], P('fsdp')
- dense_in_grad: float32 [768, 3072], P('fsdp')
- dense_in_bias_grad: float32 [3072], P('fsdp')
- dense_out_grad: float32 [3072, 768], P('fsdp')
- dense_out_bias_grad: float32 [768], P('fsdp')
The draws below stay inside these ranges and needn't reach their ends.
Inputs may be any that keep to these rules, and one draw needn't show every extreme that they name: memory slots that an example may read are its first counts ones; in every aligned group of 32 examples one example has 256 and another has none.
All inputs are finite; a program needn't handle non-finite values.
Results may differ from the reference program's by a relative error of at most 0.019.
Values may be sent and summed in bfloat16 or wider, within the bound.
No kernel may reach another device: no remote copies, remote signals or barrier semaphores. Data moves between devices by JAX's collectives and lax.ppermute only.
A program may use at most 256 MiB of HBM per device.

```python
import jax
import jax.numpy as jnp
from jax import lax

D = 768
HEADS = 12
HEAD = 64
FF = 3072
SUF = 32
EX_DEV = 32
MICRO = 2
MEM = 256
EXAMPLES = 256


def draw_counts(key, part):
    key = jax.random.fold_in(key, 11)
    first_key, second_key = jax.random.split(key)
    values = jax.random.randint(first_key, (EXAMPLES,), 0, MEM + 1)
    groups = EXAMPLES // EX_DEV
    picked = jax.random.randint(second_key, (groups,), 0, EX_DEV)
    starts = jnp.arange(groups) * EX_DEV
    values = values.at[starts + picked].set(MEM)
    values = values.at[starts + (picked + 1) % EX_DEV].set(0)
    return values.astype(jnp.int32)


def levels(key, shape, cuts, least, high):
    def one(dim, blocks):
        heights = jax.random.uniform(jax.random.fold_in(jax.random.fold_in(key, 6), dim), (blocks,), jnp.float32, least / len(cuts), high / len(cuts))
        return jnp.repeat(jnp.exp(heights), shape[dim] // blocks).reshape((-1,) + (1,) * (len(shape) - dim - 1))

    factor_of = one(*cuts[0])
    for cut in cuts[1:]:
        factor_of = factor_of * one(*cut)
    return factor_of


def scatter_about(stream_key, dims, scale, most, shards=(), dtype=jnp.bfloat16):
    factor_of = levels(stream_key, dims, shards, -0.22, 0.18) if shards else 1.0
    drawn = jax.random.normal(stream_key, dims, jnp.float32) * scale * factor_of
    return jnp.minimum(jnp.maximum(drawn, -most), most).astype(dtype)


def setup_inputs(seed: int = 0) -> dict:
    key_of = jax.random.split(jax.random.key(seed), 23)
    suffix = scatter_about(key_of[0], (EXAMPLES, SUF, D), 1.0, 6.0, ((0, 8),))
    memory = scatter_about(key_of[1], (EXAMPLES, MEM, D), 1.0, 6.0, ((0, 8), (1, 4)))
    counts = draw_counts(jax.random.fold_in(key_of[22], 71), 0)
    cotangent = scatter_about(key_of[3], (EXAMPLES, SUF, D), 1.0, 6.0, ((0, 8),))
    self_norm_gain = jnp.clip(1.0 + 0.1 * jax.random.normal(key_of[4], (D,), jnp.float32), 0.5, 1.5).astype(jnp.bfloat16)
    self_norm_bias = scatter_about(key_of[5], (D,), 0.3, 1.5, ((0, 8),))
    self_query = scatter_about(key_of[6], (D, D), D ** -0.5, 0.21875, ((0, 8),))
    self_key = scatter_about(key_of[7], (D, D), D ** -0.5, 0.21875, ((0, 8),))
    self_value = scatter_about(key_of[8], (D, D), D ** -0.5, 0.21875, ((0, 8),))
    self_output = scatter_about(key_of[9], (D, D), (D // 4) ** -0.5, 0.4375, ((0, 8),))
    cross_norm_gain = jnp.clip(1.0 + 0.1 * jax.random.normal(key_of[10], (D,), jnp.float32), 0.5, 1.5).astype(jnp.bfloat16)
    cross_norm_bias = scatter_about(key_of[11], (D,), 0.3, 1.5, ((0, 8),))
    cross_query = scatter_about(key_of[12], (D, D), D ** -0.5, 0.21875, ((0, 8),))
    cross_key = scatter_about(key_of[13], (D, D), D ** -0.5, 0.21875, ((0, 8),))
    cross_value = scatter_about(key_of[14], (D, D), D ** -0.5, 0.21875, ((0, 8),))
    cross_output = scatter_about(key_of[15], (D, D), (D // 32) ** -0.5, 1.25, ((0, 8),))
    dense_norm_gain = jnp.clip(1.0 + 0.1 * jax.random.normal(key_of[16], (D,), jnp.float32), 0.5, 1.5).astype(jnp.bfloat16)
    dense_norm_bias = scatter_about(key_of[17], (D,), 0.3, 1.5, ((0, 8),))
    dense_in = scatter_about(key_of[18], (D, FF), D ** -0.5, 0.21875, ((0, 8),))
    dense_in_bias = scatter_about(key_of[19], (FF,), 0.5, 2.5, ((0, 8),))
    dense_out = scatter_about(key_of[20], (FF, D), FF ** -0.5, 0.109375, ((0, 8),))
    dense_out_bias = scatter_about(key_of[21], (D,), 0.5, 2.5, ((0, 8),))
    return {"suffix": suffix, "memory": memory, "counts": counts, "cotangent": cotangent, "self_norm_gain": self_norm_gain, "self_norm_bias": self_norm_bias, "self_query": self_query, "self_key": self_key, "self_value": self_value, "self_output": self_output, "cross_norm_gain": cross_norm_gain, "cross_norm_bias": cross_norm_bias, "cross_query": cross_query, "cross_key": cross_key, "cross_value": cross_value, "cross_output": cross_output, "dense_norm_gain": dense_norm_gain, "dense_norm_bias": dense_norm_bias, "dense_in": dense_in, "dense_in_bias": dense_in_bias, "dense_out": dense_out, "dense_out_bias": dense_out_bias}


HIGHEST_PRECISION = lax.Precision.HIGHEST

@jax.custom_vjp
def low(v):
    return lax.optimization_barrier(v.astype(jnp.bfloat16)).astype(jnp.float32)

@jax.custom_vjp
def low_back(v):
    return v

def low_keep(v):
    return (low(v), None)

def low_pass(kept, grad):
    return (grad,)

def back_keep(v):
    return (v, None)

def back_low(kept, grad):
    return (low(grad),)
low.defvjp(low_keep, low_pass)
low_back.defvjp(back_keep, back_low)

def round_both(values):
    return low(low_back(values))

def product(left, right):
    return jnp.matmul(left, right, precision=HIGHEST_PRECISION)

def layer_norm(values, gain, shift):
    mean_row = lax.optimization_barrier(jnp.mean(values, axis=-1, keepdims=True))
    centred = values - mean_row
    spread = lax.optimization_barrier(jnp.mean(centred * centred, axis=-1, keepdims=True))
    return centred * lax.rsqrt(spread + 1e-06) * gain + shift

def block_forward(params, suffix, memory, counts):
    gain_self, shift_self, query_self, keys_self, values_self, output_self, gain_cross, shift_cross, query_cross, keys_cross, values_cross, output_cross, gain_dense, shift_dense, weight_in, bias_in, weight_out, bias_out = params
    batch_size, length, width = suffix.shape
    mem_length = memory.shape[1]
    score_scale = HEAD ** (-0.5)
    normed = low(layer_norm(suffix, gain_self, shift_self))
    queries = round_both(product(normed, query_self)).reshape(batch_size, length, HEADS, HEAD)
    keys_all = round_both(product(normed, keys_self)).reshape(batch_size, length, HEADS, HEAD)
    values_all = round_both(product(normed, values_self)).reshape(batch_size, length, HEADS, HEAD)
    raw_scores = low_back(jnp.einsum('bqhd,bkhd->bhqk', queries, keys_all, precision=HIGHEST_PRECISION) * score_scale)
    causal = jnp.arange(length)[:, None] >= jnp.arange(length)[None, :]
    masked = jnp.where(causal, raw_scores, -1e+30)
    row_top = lax.optimization_barrier(jnp.max(masked, axis=-1, keepdims=True))
    log_total = row_top + jnp.log(lax.optimization_barrier(jnp.sum(jnp.exp(masked - row_top), axis=-1, keepdims=True)))
    weights = low(jnp.exp(masked - log_total))
    attended = round_both(jnp.einsum('bhqk,bkhd->bqhd', weights, values_all, precision=HIGHEST_PRECISION))
    first = suffix + low_back(product(attended.reshape(batch_size, length, width), output_self))
    normed = low(layer_norm(first, gain_cross, shift_cross))
    queries = round_both(product(normed, query_cross)).reshape(batch_size, length, HEADS, HEAD)
    keys_all = round_both(product(memory, keys_cross)).reshape(batch_size, mem_length, HEADS, HEAD)
    values_all = round_both(product(memory, values_cross)).reshape(batch_size, mem_length, HEADS, HEAD)
    raw_scores = low_back(jnp.einsum('bqhd,bkhd->bhqk', queries, keys_all, precision=HIGHEST_PRECISION) * score_scale)
    valid = (jnp.arange(mem_length)[None, :] < counts[:, None])[:, None, None, :]
    masked = jnp.where(valid, raw_scores, -1e+30)
    row_top = jnp.maximum(lax.optimization_barrier(jnp.max(masked, axis=-1, keepdims=True)), 0.0)
    row_total = lax.optimization_barrier(jnp.sum(jnp.exp(masked - row_top), axis=-1, keepdims=True)) + jnp.exp(-row_top)
    log_total = row_top + jnp.log(row_total)
    weights = low(jnp.where(valid, jnp.exp(masked - log_total), 0.0))
    attended = round_both(jnp.einsum('bhqk,bkhd->bqhd', weights, values_all, precision=HIGHEST_PRECISION))
    second = first + low_back(product(attended.reshape(batch_size, length, width), output_cross))
    normed = low(layer_norm(second, gain_dense, shift_dense))
    inner = low_back(product(normed, weight_in) + bias_in)
    hidden = low(jax.nn.gelu(inner, approximate=True))
    return second + low_back(product(hidden, weight_out) + bias_out)

def reference(suffix, memory, counts, cotangent, self_norm_gain, self_norm_bias, self_query, self_key, self_value, self_output, cross_norm_gain, cross_norm_bias, cross_query, cross_key, cross_value, cross_output, dense_norm_gain, dense_norm_bias, dense_in, dense_in_bias, dense_out, dense_out_bias):
    params = tuple((value.astype(jnp.float32) for value in (self_norm_gain, self_norm_bias, self_query, self_key, self_value, self_output, cross_norm_gain, cross_norm_bias, cross_query, cross_key, cross_value, cross_output, dense_norm_gain, dense_norm_bias, dense_in, dense_in_bias, dense_out, dense_out_bias)))
    per_block = EX_DEV // MICRO
    blocks = EXAMPLES // per_block
    stacked = (suffix.reshape(blocks, per_block, SUF, D), memory.reshape(blocks, per_block, MEM, D), counts.reshape(blocks, per_block), cotangent.reshape(blocks, per_block, SUF, D))

    def step(totals, item):
        suffix_part, memory_part, count_part, cot_part = item

        def forward(param_list, suffix_in, memory_in):
            return block_forward(param_list, suffix_in, memory_in, count_part)
        output, pullback = jax.vjp(forward, params, suffix_part.astype(jnp.float32), memory_part.astype(jnp.float32))
        param_grads, suffix_grads, memory_grads = pullback(cot_part.astype(jnp.float32))
        totals = tuple((total + piece for total, piece in zip(totals, param_grads)))
        return (totals, (output.astype(jnp.bfloat16), suffix_grads.astype(jnp.bfloat16), memory_grads.astype(jnp.bfloat16)))
    initial = tuple((jnp.zeros_like(value) for value in params))
    grads, (outputs, suffix_grads, memory_grads) = lax.scan(step, initial, stacked)
    return (outputs.reshape(EXAMPLES, SUF, D), suffix_grads.reshape(EXAMPLES, SUF, D), memory_grads.reshape(EXAMPLES, MEM, D), grads[0], grads[1], grads[2], grads[3], grads[4], grads[5], grads[6], grads[7], grads[8], grads[9], grads[10], grads[11], grads[12], grads[13], grads[14], grads[15], grads[16], grads[17])
```

```python
import jax
import jax.numpy as jnp
from jax import lax
from jax.experimental import pallas as pl
from jax.experimental.pallas import tpu as pltpu
from jax.sharding import PartitionSpec as P

HEADS = 12
HEAD = 64
BF = jnp.bfloat16
F32 = jnp.float32


def swap(value, axis, distance):
    size = lax.axis_size(axis)
    return lax.ppermute(value, axis, [(i, i ^ distance) for i in range(size)])


def fsdp_split(size):
    slow = 4 if size % 4 == 0 else 1
    return slow, size // slow


def pick(value, index, dim):
    return lax.dynamic_index_in_dim(value, index, dim, keepdims=False)


def half_of(value, which, dim):
    half = value.shape[dim] // 2
    return lax.dynamic_slice_in_dim(value, which * half, half, dim)


def gather_pieces(own, slow, fast):
    pieces = {0: own}
    for k in range(1, slow):
        pieces[k * fast] = swap(own, "fsdp", k * fast)
    for b in range(1, fast):
        for k in range(slow):
            pieces[k * fast + b] = swap(pieces[k * fast], "fsdp", b)
    return pieces


def place_kernel(count, dim, where, own, *refs):
    mine = refs[: count - 1]
    theirs = refs[count - 1 : 2 * count - 2]
    out = refs[2 * count - 2]
    sems = refs[2 * count - 1]
    f = where[0]
    c = where[1]
    rows, cols = own.shape
    copies = [
        pltpu.make_async_copy(
            own, out.at[pl.ds(pl.multiple_of(f * rows, 16), rows), :], sems.at[0]
        )
    ]
    for which, group in ((c, mine), (1 - c, theirs)):
        for d in range(1, count):
            shard = f ^ d
            piece = group[d - 1]
            if dim == 1:
                target = out.at[
                    pl.ds(pl.multiple_of(shard * rows, 16), rows),
                    pl.ds(pl.multiple_of(which * (cols // 2), 128), cols // 2),
                ]
            else:
                target = out.at[
                    pl.ds(pl.multiple_of(shard * rows + which * (rows // 2), 16), rows // 2), :
                ]
            copies.append(pltpu.make_async_copy(piece, target, sems.at[len(copies)]))
    for copy in copies:
        copy.start()
    for copy in copies:
        copy.wait()


def assemble(own, mine, theirs, dim, where):
    count = len(mine) + 1
    rows, cols = own.shape
    return pl.pallas_call(
        lambda *refs: place_kernel(count, dim, *refs),
        out_shape=jax.ShapeDtypeStruct((count * rows, cols), own.dtype),
        in_specs=[pl.BlockSpec(memory_space=pltpu.SMEM)]
        + [pl.BlockSpec(memory_space=pl.ANY)] * (2 * count - 1),
        out_specs=pl.BlockSpec(memory_space=pl.ANY),
        scratch_shapes=[pltpu.SemaphoreType.DMA((2 * count - 1,))],
        cost_estimate=pl.CostEstimate(
            flops=0, bytes_accessed=4 * count * rows * cols, transcendentals=0
        ),
    )(where, own, *mine, *theirs)


def gather_weight(own, dim, c, slow, fast, where):
    pieces = gather_pieces(half_of(own, c, dim), slow, fast)
    count = slow * fast
    mine = [pieces[d] for d in range(1, count)]
    theirs = [swap(piece, "mem", 1) for piece in mine]
    return assemble(own, mine, theirs, dim, where)


def scatter_grad(grad, dim, f, c, slow, fast, across):
    count = slow * fast
    rows = grad.shape[0] // count
    grad = grad.reshape(count, rows, grad.shape[1])
    dim = dim + 1
    sent = swap(half_of(grad, 1 - c, dim), "mem", 1)
    part = half_of(grad, c, dim).astype(F32) + sent.astype(F32)
    part = part.astype(BF).reshape((slow, fast) + part.shape[1:])
    z, y = f // fast, f % fast
    total = pick(part, y, 1).astype(F32)
    for b in range(1, fast):
        total = total + swap(pick(part, y ^ b, 1), "fsdp", b).astype(F32)
    part = total.astype(BF)
    total = pick(part, z, 0).astype(F32)
    for k in range(1, slow):
        total = total + swap(pick(part, z ^ k, 0), "fsdp", k * fast).astype(F32)
    k = 1
    while k < across:
        low = total.astype(BF)
        total = low.astype(F32) + swap(low, "mem", 2 * k).astype(F32)
        k *= 2
    other = swap(total, "mem", 1)
    first = jnp.where(c == 0, total, other)
    second = jnp.where(c == 0, other, total)
    return jnp.concatenate([first, second], axis=dim - 1)


def add_everywhere(value):
    for axis in ("mem", "fsdp"):
        k = 1
        while k < lax.axis_size(axis):
            value = value + swap(value, axis, k)
            k *= 2
    return value


def spread_rows(value, m, across):
    examples = value.shape[0]
    out = jnp.zeros((2 * across * examples,) + value.shape[1:], value.dtype)
    blocks = {0: value}
    for k in range(1, across):
        blocks[2 * k] = swap(value, "mem", 2 * k)
    for k in range(across):
        blocks[2 * k + 1] = swap(blocks[2 * k], "mem", 1)
    for d, block in blocks.items():
        out = lax.dynamic_update_slice_in_dim(out, block, (m ^ d) * examples, 0)
    return out


def layer_norm(values, gain, shift):
    mean_row = jnp.mean(values, axis=-1, keepdims=True)
    centred = values - mean_row
    spread = jnp.mean(centred * centred, axis=-1, keepdims=True)
    return centred * lax.rsqrt(spread + 1e-06) * gain + shift


def smooth_gate(values):
    return jax.nn.gelu(values, approximate=True)


def times(left, right):
    return jnp.dot(left, right, preferred_element_type=F32)


def outer_sum(left, right):
    return lax.dot_general(
        left, right, (((0,), (0,)), ((), ())), preferred_element_type=F32
    ).astype(BF)


def times_transposed(left, right):
    return lax.dot_general(left, right, (((1,), (1,)), ((), ())), preferred_element_type=F32)


def per_device(
    suffix,
    memory,
    counts,
    cotangent,
    self_norm_gain,
    self_norm_bias,
    self_query,
    self_key,
    self_value,
    self_output,
    cross_norm_gain,
    cross_norm_bias,
    cross_query,
    cross_key,
    cross_value,
    cross_output,
    dense_norm_gain,
    dense_norm_bias,
    dense_in,
    dense_in_bias,
    dense_out,
    dense_out_bias,
):
    f = lax.axis_index("fsdp")
    m = lax.axis_index("mem")
    c = m % 2
    fsdp = lax.axis_size("fsdp")
    mem = lax.axis_size("mem")
    across = mem // 2
    slow, fast = fsdp_split(fsdp)
    where = jnp.stack([f, c]).astype(jnp.int32)
    examples = suffix.shape[0] // mem
    length = suffix.shape[1]
    width = suffix.shape[2]
    slots = memory.shape[1]
    rows = examples * length
    score_scale = HEAD ** (-0.5)

    def my_examples(value, index):
        return lax.dynamic_slice_in_dim(value, index * examples, examples, 0)

    small = jnp.concatenate(
        [
            self_norm_gain,
            self_norm_bias,
            cross_norm_gain,
            cross_norm_bias,
            dense_norm_gain,
            dense_norm_bias,
            dense_out_bias,
            dense_in_bias,
        ]
    )
    small_pieces = gather_pieces(small, slow, fast)
    vectors = jnp.zeros((fsdp, small.shape[0]), BF)
    for d, piece in small_pieces.items():
        vectors = lax.dynamic_update_slice(vectors, piece[None], (f ^ d, 0))
    part = width // fsdp
    gain_self, shift_self, gain_cross, shift_cross, gain_dense, shift_dense, bias_out = [
        vectors[:, i * part : (i + 1) * part].reshape(width).astype(F32) for i in range(7)
    ]
    bias_in = vectors[:, 7 * part :].reshape(-1).astype(F32)

    self_pack = jnp.concatenate([self_query, self_key, self_value, self_output], axis=1)
    cross_pack = jnp.concatenate([cross_query, cross_key, cross_value, cross_output], axis=1)
    self_full = gather_weight(self_pack, 1, c, slow, fast, where)
    mem_pieces = [my_examples(memory, m)]
    for d in range(1, mem):
        mem_pieces.append(swap(my_examples(memory, m ^ d), "mem", d))
    mem_rows = jnp.concatenate(mem_pieces, axis=1)
    mem_length = mem * slots
    mem_rows = mem_rows.reshape(examples * mem_length, width)
    cross_full = gather_weight(cross_pack, 1, c, slow, fast, where)
    weight_in = gather_weight(dense_in, 1, c, slow, fast, where)
    weight_out = gather_weight(dense_out, 0, c, slow, fast, where)
    qkv_self = self_full[:, : 3 * width]
    output_self = self_full[:, 3 * width :]
    query_cross = cross_full[:, :width]
    kv_cross = cross_full[:, width : 3 * width]
    output_cross = cross_full[:, 3 * width :]

    positions = jnp.concatenate(
        [(m ^ d) * slots + jnp.arange(slots, dtype=jnp.int32) for d in range(mem)]
    )
    causal = jnp.arange(length)[:, None] >= jnp.arange(length)[None, :]
    inputs = my_examples(suffix, m).astype(F32).reshape(rows, width)
    count_part = my_examples(counts, m)
    grad_low = my_examples(cotangent, m).reshape(rows, width)
    cot_rows = grad_low.astype(F32)

    def heads(value):
        return value.reshape(examples, -1, HEADS, HEAD)

    normed_a, norm_back_a = jax.vjp(layer_norm, inputs, gain_self, shift_self)
    act_a = normed_a.astype(BF)
    qkv = times(act_a, qkv_self).astype(BF)
    queries = heads(qkv[:, :width])
    keys_all = heads(qkv[:, width : 2 * width])
    values_all = heads(qkv[:, 2 * width :])
    raw_scores = (
        jnp.einsum("bqhd,bkhd->bhqk", queries, keys_all, preferred_element_type=F32) * score_scale
    )
    masked = jnp.where(causal, raw_scores, -1e30)
    row_top = jnp.max(masked, axis=-1, keepdims=True)
    log_total = row_top + jnp.log(jnp.sum(jnp.exp(masked - row_top), axis=-1, keepdims=True))
    probs_self = jnp.exp(masked - log_total)
    weights_self = probs_self.astype(BF)
    attended = (
        jnp.einsum("bhqk,bkhd->bqhd", weights_self, values_all, preferred_element_type=F32)
        .astype(BF)
        .reshape(rows, width)
    )
    first = inputs + times(attended, output_self)
    normed_b, norm_back_b = jax.vjp(layer_norm, first, gain_cross, shift_cross)
    act_b = normed_b.astype(BF)
    query_mem = heads(times(act_b, query_cross).astype(BF))
    kv_mem = times(mem_rows, kv_cross).astype(BF)
    keys_mem = heads(kv_mem[:, :width])
    values_mem = heads(kv_mem[:, width:])
    raw_mem = (
        jnp.einsum("bqhd,bkhd->bhqk", query_mem, keys_mem, preferred_element_type=F32)
        * score_scale
    )
    valid = (positions[None, :] < count_part[:, None])[:, None, None, :]
    masked_mem = jnp.where(valid, raw_mem, -1e30)
    top_mem = jnp.maximum(jnp.max(masked_mem, axis=-1), 0.0)
    total_mem = jnp.sum(jnp.exp(masked_mem - top_mem[..., None]), axis=-1)
    log_mem = top_mem + jnp.log(total_mem + jnp.exp(-top_mem))
    probs_mem = jnp.where(valid, jnp.exp(masked_mem - log_mem[..., None]), 0.0)
    weights_mem = probs_mem.astype(BF)
    attended_mem = (
        jnp.einsum("bhqk,bkhd->bqhd", weights_mem, values_mem, preferred_element_type=F32)
        .astype(BF)
        .reshape(rows, width)
    )
    second = first + times(attended_mem, output_cross)
    normed_d, norm_back_d = jax.vjp(layer_norm, second, gain_dense, shift_dense)
    act_d = normed_d.astype(BF)
    inner = times(act_d, weight_in) + bias_in
    hidden_full, gate_back = jax.vjp(smooth_gate, inner)
    hidden = hidden_full.astype(BF)
    result = second + times(hidden, weight_out) + bias_out
    block_output = spread_rows(result.astype(BF).reshape(examples, length, width), m, across)

    def reduce(grad, dim):
        return scatter_grad(grad, dim, f, c, slow, fast, across)

    grad_weight_out = reduce(outer_sum(hidden, grad_low), 0)
    grad_bias_out = jnp.sum(cot_rows, axis=0)
    (grad_inner,) = gate_back(times_transposed(grad_low, weight_out))
    inner_low = grad_inner.astype(BF)
    grad_weight_in = reduce(outer_sum(act_d, inner_low), 1)
    grad_bias_in = jnp.sum(inner_low.astype(F32), axis=0)
    grad_second, grad_gain_dense, grad_shift_dense = norm_back_d(
        times_transposed(inner_low, weight_in)
    )
    grad_second = grad_second + cot_rows
    second_low = grad_second.astype(BF)
    grad_output_cross = outer_sum(attended_mem, second_low)
    grad_att_mem = heads(times_transposed(second_low, output_cross).astype(BF))
    grad_probs_mem = jnp.einsum(
        "bqhd,bkhd->bhqk", grad_att_mem, values_mem, preferred_element_type=F32
    )
    row_sums = jnp.sum(probs_mem * grad_probs_mem, axis=-1, keepdims=True)
    grad_raw_mem = (probs_mem * (grad_probs_mem - row_sums)).astype(BF)
    grad_query_mem = (
        (
            jnp.einsum("bhqk,bkhd->bqhd", grad_raw_mem, keys_mem, preferred_element_type=F32)
            * score_scale
        )
        .astype(BF)
        .reshape(rows, width)
    )
    grad_keys_mem = (
        jnp.einsum("bhqk,bqhd->bkhd", grad_raw_mem, query_mem, preferred_element_type=F32)
        * score_scale
    ).astype(BF)
    grad_values_mem = jnp.einsum(
        "bhqk,bqhd->bkhd", weights_mem, grad_att_mem, preferred_element_type=F32
    ).astype(BF)
    grad_kv = jnp.concatenate(
        [
            grad_keys_mem.reshape(examples * mem_length, width),
            grad_values_mem.reshape(examples * mem_length, width),
        ],
        axis=1,
    )
    grad_memory = (
        times_transposed(grad_kv, kv_cross).astype(BF).reshape(examples, mem_length, width)
    )
    memory_grad = jnp.zeros_like(memory)
    for d in range(mem):
        block = grad_memory[:, d * slots : (d + 1) * slots]
        if d:
            block = swap(block, "mem", d)
        memory_grad = lax.dynamic_update_slice_in_dim(memory_grad, block, (m ^ d) * examples, 0)
    grad_cross = reduce(
        jnp.concatenate(
            [outer_sum(act_b, grad_query_mem), outer_sum(mem_rows, grad_kv), grad_output_cross],
            axis=1,
        ),
        1,
    )
    grad_first, grad_gain_cross, grad_shift_cross = norm_back_b(
        times_transposed(grad_query_mem, query_cross)
    )
    grad_first = grad_first + grad_second
    first_low = grad_first.astype(BF)
    grad_output_self = outer_sum(attended, first_low)
    grad_att_self = heads(times_transposed(first_low, output_self).astype(BF))
    grad_probs_self = jnp.einsum(
        "bqhd,bkhd->bhqk", grad_att_self, values_all, preferred_element_type=F32
    )
    rows_self = jnp.sum(probs_self * grad_probs_self, axis=-1, keepdims=True)
    grad_raw_self = (probs_self * (grad_probs_self - rows_self)).astype(BF)
    grad_queries = (
        jnp.einsum("bhqk,bkhd->bqhd", grad_raw_self, keys_all, preferred_element_type=F32)
        * score_scale
    ).astype(BF)
    grad_keys = (
        jnp.einsum("bhqk,bqhd->bkhd", grad_raw_self, queries, preferred_element_type=F32)
        * score_scale
    ).astype(BF)
    grad_values = jnp.einsum(
        "bhqk,bqhd->bkhd", weights_self, grad_att_self, preferred_element_type=F32
    ).astype(BF)
    grad_qkv = jnp.concatenate(
        [
            grad_queries.reshape(rows, width),
            grad_keys.reshape(rows, width),
            grad_values.reshape(rows, width),
        ],
        axis=1,
    )
    grad_self = reduce(
        jnp.concatenate([outer_sum(act_a, grad_qkv), grad_output_self], axis=1), 1
    )
    grad_input, grad_gain_self, grad_shift_self = norm_back_a(
        times_transposed(grad_qkv, qkv_self)
    )
    grad_input = grad_input + grad_first
    suffix_grad = spread_rows(grad_input.astype(BF).reshape(examples, length, width), m, across)

    vector_grads = add_everywhere(
        jnp.concatenate(
            [
                piece.reshape(fsdp, -1)
                for piece in (
                    grad_gain_self,
                    grad_shift_self,
                    grad_gain_cross,
                    grad_shift_cross,
                    grad_gain_dense,
                    grad_shift_dense,
                    grad_bias_out,
                    grad_bias_in,
                )
            ],
            axis=1,
        )
    )
    mine = pick(vector_grads, f, 0)
    vec = [mine[i * part : (i + 1) * part] for i in range(7)]
    g_in = mine[7 * part :]

    def columns(value, i):
        return value[:, i * width : (i + 1) * width]

    return (
        block_output,
        suffix_grad,
        memory_grad,
        vec[0],
        vec[1],
        columns(grad_self, 0),
        columns(grad_self, 1),
        columns(grad_self, 2),
        columns(grad_self, 3),
        vec[2],
        vec[3],
        columns(grad_cross, 0),
        columns(grad_cross, 1),
        columns(grad_cross, 2),
        columns(grad_cross, 3),
        vec[4],
        vec[5],
        grad_weight_in,
        g_in,
        grad_weight_out,
        vec[6],
    )


def solution(mesh):
    rows = P("fsdp", None, None)
    matrix = P("fsdp", None)
    vector = P("fsdp")
    attention = (vector, vector, matrix, matrix, matrix, matrix)
    params = attention + attention + (vector, vector, matrix, vector, matrix, vector)
    return jax.shard_map(
        per_device,
        mesh=mesh,
        in_specs=(rows, P("fsdp", "mem", None), vector, rows) + params,
        out_specs=(rows, rows, P("fsdp", "mem", None)) + params,
        check_vma=False,
    )
```

```python
import functools

import jax
import jax.numpy as jnp
from jax import lax
from jax.experimental import pallas as pl
from jax.experimental.pallas import tpu as pltpu
from jax.sharding import PartitionSpec as P

HEADS = 12
HEAD = 64
TOGETHER = 4
GROUPS = HEADS // TOGETHER
LANES = TOGETHER * HEAD
SCALE = HEAD ** (-0.5)
CHUNK = 768
BF = jnp.bfloat16
F32 = jnp.float32
ANY = pl.BlockSpec(memory_space=pl.ANY)
SMEM = pl.BlockSpec(memory_space=pltpu.SMEM)
VMEM = pl.BlockSpec(memory_space=pltpu.VMEM)


def swap(value, axis, distance):
    size = lax.axis_size(axis)
    return lax.ppermute(value, axis, [(i, i ^ distance) for i in range(size)])


def fsdp_split(size):
    slow = 4 if size % 4 == 0 else 1
    return slow, size // slow


def dot(left, right):
    return jnp.dot(left, right, preferred_element_type=F32)


def dot_nt(left, right):
    return lax.dot_general(left, right, (((1,), (1,)), ((), ())), preferred_element_type=F32)


def dot_tn(left, right):
    return lax.dot_general(left, right, (((0,), (0,)), ((), ())), preferred_element_type=F32)


def rows_of(start, size):
    return pl.ds(pl.multiple_of(start, 16), size)


def weight_block(ref, dim, shard, which, rows):
    if dim == 1:
        half = ref.shape[1] // 2
        return ref.at[rows_of(shard * rows, rows), pl.ds(pl.multiple_of(which * half, 128), half)]
    return ref.at[rows_of(shard * 2 * rows + which * rows, rows), :]


def block_copies(where, whole, dim, mine, theirs, sems, first, out):
    z, y, c = where[0], where[1], where[2]
    fast = len(mine)
    slow, rows = mine[0].shape[0], mine[0].shape[1]
    copies = []
    for which, pieces in ((c, mine), (1 - c, theirs)):
        for b in range(fast):
            for k in range(slow):
                shard = (z ^ k) * fast + (y ^ b)
                place = weight_block(whole, dim, shard, which, rows)
                piece = pieces[b].at[k]
                ends = (place, piece) if out else (piece, place)
                copies.append(pltpu.make_async_copy(*ends, sems.at[first + len(copies)]))
    for copy in copies:
        copy.start()
    return copies


def wait_all(copies):
    for copy in copies:
        copy.wait()


def example_copy(where, source, target, sem):
    count = target.shape[0]
    copy = pltpu.make_async_copy(source.at[pl.ds(where[3] * count, count)], target, sem)
    copy.start()
    return copy


def normalise(values):
    centred = values - jnp.mean(values, axis=-1, keepdims=True)
    scale = lax.rsqrt(jnp.mean(centred * centred, axis=-1, keepdims=True) + 1e-06)
    return centred * scale, scale


def norm_back(grad, gain, hat, scale):
    inner = grad * gain
    mean = jnp.mean(inner, axis=-1, keepdims=True)
    along = jnp.mean(inner * hat, axis=-1, keepdims=True)
    return (
        scale * (inner - mean - hat * along),
        jnp.sum(grad * hat, axis=0, keepdims=True),
        jnp.sum(grad, axis=0, keepdims=True),
    )


def head_mask(rows):
    shape = (TOGETHER * rows, LANES)
    row = lax.broadcasted_iota(jnp.int32, shape, 0) // rows
    lane = lax.broadcasted_iota(jnp.int32, shape, 1) // HEAD
    return (row == lane).astype(F32)


def stack_heads(value, mask):
    return (jnp.concatenate([value] * TOGETHER, axis=0).astype(F32) * mask).astype(BF)


def merge_heads(value, mask):
    rows = value.shape[0] // TOGETHER
    value = value * mask
    total = value[:rows]
    for h in range(1, TOGETHER):
        total = total + value[h * rows : (h + 1) * rows]
    return total


def chunks(size, step=CHUNK):
    return [slice(i, min(i + step, size)) for i in range(0, size, step)]


def self_forward(fast, group, where, suffix, vec, *refs):
    mine, refs = refs[:fast], refs[fast:]
    theirs, refs = refs[:fast], refs[fast:]
    x1, a1, qkv, p1, o1, weight, start, sems = refs
    rows, width = x1.shape
    copies = block_copies(where, weight, 1, mine, theirs, sems, 1, False)
    example_copy(where, suffix, start, sems.at[0]).wait()
    values = start[...].reshape(rows, width).astype(F32)
    hat, _ = normalise(values)
    a1[...] = (hat * vec[0:1, :] + vec[1:2, :]).astype(BF)
    wait_all(copies)
    for cols in chunks(3 * width):
        qkv[:, cols] = dot(a1[...], weight[:, cols]).astype(BF)
    mask = head_mask(group)
    length = suffix.shape[1]
    shape = (TOGETHER * group, group)
    row = lax.broadcasted_iota(jnp.int32, shape, 0) % group
    col = lax.broadcasted_iota(jnp.int32, shape, 1)
    seen = (row // length == col // length) & (row >= col)
    for r in range(rows // group):
        here = slice(r * group, (r + 1) * group)
        for g in range(GROUPS):
            lanes = [slice(i * width + g * LANES, i * width + (g + 1) * LANES) for i in range(3)]
            queries = stack_heads(qkv[here, lanes[0]], mask)
            scores = dot_nt(queries, qkv[here, lanes[1]]) * SCALE
            scores = jnp.where(seen, scores, -1e30)
            powers = jnp.exp(scores - jnp.max(scores, axis=-1, keepdims=True))
            probs = (powers / jnp.sum(powers, axis=-1, keepdims=True)).astype(BF)
            p1[r * GROUPS + g] = probs
            found = dot(probs, qkv[here, lanes[2]])
            o1[here, lanes[0]] = merge_heads(found, mask).astype(BF)
    x1[...] = values + dot(o1[...], weight[:, 3 * width :])


def load_memory(pieces, target, sems, first):
    slots = pieces[0].shape[1]
    copies = []
    for d, piece in enumerate(pieces):
        copies.append(
            pltpu.make_async_copy(
                piece, target.at[:, d * slots : (d + 1) * slots, :], sems.at[first + d]
            )
        )
    for copy in copies:
        copy.start()
    return copies


def cross_forward(fast, mem, where, counts, x1, vec, *refs):
    pieces, refs = refs[:mem], refs[mem:]
    mine, refs = refs[:fast], refs[fast:]
    theirs, refs = refs[:fast], refs[fast:]
    x2, a2, q2, kv, p2, o2, weight, memory, sems = refs
    rows, width = x1.shape
    examples, total, _ = memory.shape
    length = rows // examples
    slots = total // mem
    copies = load_memory(pieces, memory, sems, 0)
    copies += block_copies(where, weight, 1, mine, theirs, sems, mem, False)
    hat, _ = normalise(x1[...])
    a2[...] = (hat * vec[2:3, :] + vec[3:4, :]).astype(BF)
    wait_all(copies)
    q2[...] = dot(a2[...], weight[:, :width]).astype(BF)
    mask = head_mask(length)
    slot = lax.broadcasted_iota(jnp.int32, (1, total), 1)
    position = ((slot // slots) ^ where[3]) * slots + slot % slots

    def one(e, carry):
        for cols in chunks(2 * width):
            kv[e, :, cols] = dot(
                memory[e], weight[:, width + cols.start : width + cols.stop]
            ).astype(BF)
        valid = position < counts[where[3] * examples + e]
        here = rows_of(e * length, length)
        for g in range(GROUPS):
            lanes = slice(g * LANES, (g + 1) * LANES)
            queries = stack_heads(q2[here, lanes], mask)
            scores = dot_nt(queries, kv[e, :, lanes]) * SCALE
            scores = jnp.where(valid, scores, -1e30)
            top = jnp.maximum(jnp.max(scores, axis=-1, keepdims=True), 0.0)
            powers = jnp.exp(scores - top)
            weight_sum = jnp.sum(powers, axis=-1, keepdims=True) + jnp.exp(-top)
            probs = (powers / weight_sum).astype(BF)
            p2[e, g] = probs
            found = dot(probs, kv[e, :, width + g * LANES : width + (g + 1) * LANES])
            o2[here, lanes] = merge_heads(found, mask).astype(BF)
        return carry

    lax.fori_loop(0, examples, one, 0)
    x2[...] = x1[...] + dot(o2[...], weight[:, 3 * width :])


def dense_first(fast, where, x2, vec, bias, cotangent, *refs):
    mine, refs = refs[:fast], refs[fast:]
    theirs, refs = refs[:fast], refs[fast:]
    a3, h, slope = refs[:3]
    out_mine, out_theirs = refs[3 : 3 + fast], refs[3 + fast : 3 + 2 * fast]
    weight, grad, cot, sems = refs[3 + 2 * fast :]
    rows, width = x2.shape
    inner = weight.shape[1]
    count = len(mine) * mine[0].shape[0] * 2
    copies = block_copies(where, weight, 1, mine, theirs, sems, 1, False)
    cot_copy = example_copy(where, cotangent, cot, sems.at[0])
    hat, _ = normalise(x2[...])
    a3[...] = (hat * vec[4:5, :] + vec[5:6, :]).astype(BF)
    cot_copy.wait()
    gy = cot[...].reshape(rows, width)
    wait_all(copies)
    for cols in chunks(inner, 512):
        u = dot(a3[...], weight[:, cols]) + bias[:, cols]
        square = u * u
        t = jnp.tanh(0.7978845608 * u * (1.0 + 0.044715 * square))
        h[:, cols] = (0.5 * u * (1.0 + t)).astype(BF)
        slope[:, cols] = 0.5 * (1.0 + t) + (0.5 * 0.7978845608) * u * (1.0 - t * t) * (
            1.0 + (3.0 * 0.044715) * square
        )
        grad[cols, :] = dot_tn(h[:, cols], gy).astype(BF)
    wait_all(block_copies(where, grad, 0, out_mine, out_theirs, sems, 1, True))


def dense_second(fast, where, x2, vec, bias_row, a3, h, slope, cotangent, *refs):
    in_mine, refs = refs[:fast], refs[fast:]
    in_theirs, refs = refs[:fast], refs[fast:]
    mine, refs = refs[:fast], refs[fast:]
    theirs, refs = refs[:fast], refs[fast:]
    y, gx2, vecs, bias_grad = refs[:4]
    out_mine, out_theirs = refs[4 : 4 + fast], refs[4 + fast : 4 + 2 * fast]
    weight_in, weight_out, grad, du, cot, sems = refs[4 + 2 * fast :]
    rows, width = x2.shape
    inner = weight_in.shape[1]
    count = len(mine) * mine[0].shape[0] * 2
    copies_out = block_copies(where, weight_out, 0, mine, theirs, sems, 1, False)
    copies_in = block_copies(where, weight_in, 1, in_mine, in_theirs, sems, 1 + count, False)
    example_copy(where, cotangent, cot, sems.at[0]).wait()
    gy = cot[...].reshape(rows, width)
    wait_all(copies_out)
    for cols in chunks(inner, 512):
        back = dot_nt(gy, weight_out[cols, :]) * slope[:, cols]
        low = back.astype(BF)
        du[:, cols] = low
        bias_grad[:, cols] = jnp.sum(low.astype(F32), axis=0, keepdims=True)
        grad[:, cols] = dot_tn(a3[...], low).astype(BF)
    copies_grad = block_copies(where, grad, 1, out_mine, out_theirs, sems, 1, True)
    result = x2[...] + dot(h[...], weight_out[...]) + vec[6:7, :]
    y[...] = result.astype(BF).reshape(y.shape)
    wait_all(copies_in)
    da3 = dot_nt(du[...], weight_in[...])
    hat, scale = normalise(x2[...])
    back, gain_grad, shift_grad = norm_back(da3, vec[4:5, :], hat, scale)
    gy_wide = gy.astype(F32)
    gx2[...] = gy_wide + back
    vecs[0:1, :] = gain_grad
    vecs[1:2, :] = shift_grad
    vecs[2:3, :] = jnp.sum(gy_wide, axis=0, keepdims=True)
    wait_all(copies_grad)


def cross_backward(fast, mem, where, x1, vec, gx2, a2, q2, o2, kv, p2, *refs):
    pieces, refs = refs[:mem], refs[mem:]
    mine, refs = refs[:fast], refs[fast:]
    theirs, refs = refs[:fast], refs[fast:]
    gx1, vecs = refs[:2]
    out_mem, refs = refs[2 : 2 + mem], refs[2 + mem :]
    out_mine, out_theirs = refs[:fast], refs[fast : 2 * fast]
    weight, memory, memory_grad, grad, dkv, do2, dq2, sems = refs[2 * fast :]
    rows, width = x1.shape
    examples, total, _ = memory.shape
    length = rows // examples
    slots = total // mem
    copies = load_memory(pieces, memory, sems, 0)
    copies += block_copies(where, weight, 1, mine, theirs, sems, mem, False)
    gc = gx2[...].astype(BF)
    wait_all(copies)
    do2[...] = dot_nt(gc, weight[:, 3 * width :]).astype(BF)
    grad[:, 3 * width :] = dot_tn(o2[...], gc).astype(BF)
    mask = head_mask(length)

    def one(e, carry):
        here = rows_of(e * length, length)
        for g in range(GROUPS):
            lanes = slice(g * LANES, (g + 1) * LANES)
            value_lanes = slice(width + g * LANES, width + (g + 1) * LANES)
            queries = stack_heads(q2[here, lanes], mask)
            grads = stack_heads(do2[here, lanes], mask)
            probs = p2[e, g]
            dp = dot_nt(grads, kv[e, :, value_lanes])
            wide = probs.astype(F32)
            row_sum = jnp.sum(wide * dp, axis=-1, keepdims=True)
            dz = (wide * (dp - row_sum)).astype(BF)
            dkv[e, :, value_lanes] = dot_tn(probs, grads).astype(BF)
            dkv[e, :, lanes] = (dot_tn(dz, queries) * SCALE).astype(BF)
            dq = merge_heads(dot(dz, kv[e, :, lanes]), mask) * SCALE
            dq2[here, lanes] = dq.astype(BF)
        memory_grad[e] = dot_nt(dkv[e], weight[:, width : 3 * width]).astype(BF)
        return carry

    lax.fori_loop(0, examples, one, 0)
    copies = []
    for d in range(mem):
        copies.append(
            pltpu.make_async_copy(
                memory_grad.at[:, d * slots : (d + 1) * slots, :], out_mem[d], sems.at[d]
            )
        )
        copies[-1].start()
    flat = memory[...].reshape(examples * total, width)
    for cols in chunks(2 * width, 512):
        part = dkv[:, :, cols].reshape(examples * total, cols.stop - cols.start)
        grad[:, width + cols.start : width + cols.stop] = dot_tn(flat, part).astype(BF)
    grad[:, :width] = dot_tn(a2[...], dq2[...]).astype(BF)
    copies += block_copies(where, grad, 1, out_mine, out_theirs, sems, mem, True)
    hat, scale = normalise(x1[...])
    back, gain_grad, shift_grad = norm_back(
        dot_nt(dq2[...], weight[:, :width]), vec[2:3, :], hat, scale
    )
    gx1[...] = gx2[...] + back
    vecs[0:1, :] = gain_grad
    vecs[1:2, :] = shift_grad
    wait_all(copies)


def self_backward(fast, group, where, suffix, vec, gx1, a1, qkv, p1, o1, *refs):
    mine, refs = refs[:fast], refs[fast:]
    theirs, refs = refs[:fast], refs[fast:]
    suffix_grad, vecs = refs[:2]
    out_mine, out_theirs = refs[2 : 2 + fast], refs[2 + fast : 2 + 2 * fast]
    weight, start, grad, dqkv, do1, sems = refs[2 + 2 * fast :]
    rows, width = gx1.shape
    copies = block_copies(where, weight, 1, mine, theirs, sems, 1, False)
    start_copy = example_copy(where, suffix, start, sems.at[0])
    gs = gx1[...].astype(BF)
    grad[:, 3 * width :] = dot_tn(o1[...], gs).astype(BF)
    wait_all(copies)
    do1[...] = dot_nt(gs, weight[:, 3 * width :]).astype(BF)
    mask = head_mask(group)
    for r in range(rows // group):
        here = slice(r * group, (r + 1) * group)
        for g in range(GROUPS):
            lanes = [slice(i * width + g * LANES, i * width + (g + 1) * LANES) for i in range(3)]
            queries = stack_heads(qkv[here, lanes[0]], mask)
            grads = stack_heads(do1[here, lanes[0]], mask)
            probs = p1[r * GROUPS + g]
            dp = dot_nt(grads, qkv[here, lanes[2]])
            wide = probs.astype(F32)
            row_sum = jnp.sum(wide * dp, axis=-1, keepdims=True)
            dz = (wide * (dp - row_sum)).astype(BF)
            dqkv[here, lanes[2]] = dot_tn(probs, grads).astype(BF)
            dqkv[here, lanes[1]] = (dot_tn(dz, queries) * SCALE).astype(BF)
            dq = merge_heads(dot(dz, qkv[here, lanes[1]]), mask) * SCALE
            dqkv[here, lanes[0]] = dq.astype(BF)
    for cols in chunks(3 * width):
        grad[:, cols] = dot_tn(a1[...], dqkv[:, cols]).astype(BF)
    copies = block_copies(where, grad, 1, out_mine, out_theirs, sems, 1, True)
    da1 = dot_nt(dqkv[...], weight[:, : 3 * width])
    start_copy.wait()
    hat, scale = normalise(start[...].reshape(rows, width).astype(F32))
    back, gain_grad, shift_grad = norm_back(da1, vec[0:1, :], hat, scale)
    suffix_grad[...] = (gx1[...] + back).astype(BF).reshape(suffix_grad.shape)
    vecs[0:1, :] = gain_grad
    vecs[1:2, :] = shift_grad
    wait_all(copies)


def run(kernel, inputs, outputs, scratch, flops, copies):
    sizes = [x for _, x in inputs] + [x for _, x in outputs]
    moved = sum(x.size * x.dtype.itemsize for x in sizes)
    return pl.pallas_call(
        kernel,
        in_specs=[spec for spec, _ in inputs],
        out_specs=[spec for spec, _ in outputs],
        out_shape=[shape for _, shape in outputs],
        scratch_shapes=scratch + [pltpu.SemaphoreType.DMA((copies,))],
        compiler_params=pltpu.CompilerParams(vmem_limit_bytes=56 * 1024 * 1024),
        cost_estimate=pl.CostEstimate(flops=flops, bytes_accessed=moved, transcendentals=0),
    )(*[x for _, x in inputs])


def shape_of(dims, dtype):
    return jax.ShapeDtypeStruct(tuple(dims), dtype)


def gather_weight(own, dim, c, slow, fast):
    half = own.shape[dim] // 2
    own = lax.dynamic_slice_in_dim(own, c * half, half, dim)
    pieces = [own] + [swap(own, "fsdp", k * fast) for k in range(1, slow)]
    near = jnp.stack(pieces)
    mine = [near] + [swap(near, "fsdp", b) for b in range(1, fast)]
    theirs = [swap(piece, "mem", 1) for piece in mine]
    return mine, theirs


def scatter_grad(mine, theirs, dim, c, across):
    fast, slow = len(mine), mine[0].shape[0]
    sent = [swap(piece, "mem", 1) for piece in theirs]

    def both(b):
        return mine[b].astype(F32) + sent[b].astype(F32)

    total = both(0)
    for b in range(1, fast):
        total = total + swap(both(b).astype(BF), "fsdp", b).astype(F32)
    final = total[0]
    for k in range(1, slow):
        final = final + swap(total[k].astype(BF), "fsdp", k * fast).astype(F32)
    k = 1
    while 2 * k < across:
        low = final.astype(BF)
        final = low.astype(F32) + swap(low, "mem", 2 * k).astype(F32)
        k *= 2
    low = final.astype(BF)
    halves = [low, swap(low, "mem", 2 * k)] if across > 1 else [low]
    others = [swap(half, "mem", 1) for half in halves]
    mine = sum(half.astype(F32) for half in halves)
    other = sum(half.astype(F32) for half in others)
    first = jnp.where(c == 0, mine, other)
    second = jnp.where(c == 0, other, mine)
    return first, second


def add_everywhere(value):
    for axis in ("mem", "fsdp"):
        k = 1
        while k < lax.axis_size(axis):
            value = value + swap(value, axis, k)
            k *= 2
    return value


def spread_rows(value, m, across):
    examples = value.shape[0]
    out = jnp.zeros((2 * across * examples,) + value.shape[1:], value.dtype)
    blocks = {0: value}
    for k in range(1, across):
        blocks[2 * k] = swap(value, "mem", 2 * k)
    for k in range(across):
        blocks[2 * k + 1] = swap(blocks[2 * k], "mem", 1)
    for d, block in blocks.items():
        out = lax.dynamic_update_slice_in_dim(out, block, (m ^ d) * examples, 0)
    return out


def per_device(
    suffix,
    memory,
    counts,
    cotangent,
    self_norm_gain,
    self_norm_bias,
    self_query,
    self_key,
    self_value,
    self_output,
    cross_norm_gain,
    cross_norm_bias,
    cross_query,
    cross_key,
    cross_value,
    cross_output,
    dense_norm_gain,
    dense_norm_bias,
    dense_in,
    dense_in_bias,
    dense_out,
    dense_out_bias,
):
    f = lax.axis_index("fsdp")
    m = lax.axis_index("mem")
    c = m % 2
    fsdp = lax.axis_size("fsdp")
    mem = lax.axis_size("mem")
    across = mem // 2
    slow, fast = fsdp_split(fsdp)
    where = jnp.stack([f // fast, f % fast, c, m]).astype(jnp.int32)
    examples = suffix.shape[0] // mem
    length = suffix.shape[1]
    width = suffix.shape[2]
    slots = memory.shape[1]
    total = mem * slots
    rows = examples * length
    inner = dense_in.shape[1]
    part = width // fsdp
    group = min(128, rows)
    blocks = 2 * fsdp

    self_all = gather_weight(
        jnp.concatenate([self_query, self_key, self_value, self_output], axis=1), 1, c, slow, fast
    )
    small = jnp.concatenate(
        [
            self_norm_gain,
            self_norm_bias,
            cross_norm_gain,
            cross_norm_bias,
            dense_norm_gain,
            dense_norm_bias,
            dense_out_bias,
            dense_in_bias,
        ]
    )[None]
    k = 1
    while k < fsdp:
        small = jnp.concatenate([small, swap(small, "fsdp", k)], axis=0)
        k *= 2
    small = jnp.take(small, jnp.arange(fsdp) ^ f, axis=0).astype(F32)
    vec = small[:, : 7 * part].reshape(fsdp, 7, part).transpose(1, 0, 2).reshape(7, width)
    bias_in = small[:, 7 * part :].reshape(1, inner)

    def my_examples(value, index):
        return lax.dynamic_slice_in_dim(value, index * examples, examples, 0)

    pieces = [my_examples(memory, m)]
    for d in range(1, mem):
        pieces.append(swap(my_examples(memory, m ^ d), "mem", d))
    cross_all = gather_weight(
        jnp.concatenate([cross_query, cross_key, cross_value, cross_output], axis=1),
        1,
        c,
        slow,
        fast,
    )
    in_all = gather_weight(dense_in, 1, c, slow, fast)
    out_all = gather_weight(dense_out, 0, c, slow, fast)

    def parts_of(weights):
        return [(ANY, piece) for side in weights for piece in side]

    def grads_like(weights):
        return [
            (ANY, shape_of(piece.shape, BF)) for side in weights for piece in side
        ]

    def two(values):
        return values[:fast], values[fast:]

    def flat(dims, dtype):
        return (VMEM, shape_of(dims, dtype))

    def scratch(*dims):
        return pltpu.VMEM(dims, BF)

    wide = (rows, width)
    attention = 2 * GROUPS * TOGETHER * LANES * rows
    x1, a1, qkv, p1, o1 = run(
        functools.partial(self_forward, fast, group),
        [(SMEM, where), (ANY, suffix), (VMEM, vec)] + parts_of(self_all),
        [
            flat(wide, F32),
            flat(wide, BF),
            flat((rows, 3 * width), BF),
            flat((rows // group * GROUPS, TOGETHER * group, group), BF),
            flat(wide, BF),
        ],
        [scratch(width, 4 * width), scratch(examples, length, width)],
        8 * rows * width * width + 2 * attention * group,
        1 + blocks,
    )
    x2, a2, q2, kv, p2, o2 = run(
        functools.partial(cross_forward, fast, mem),
        [(SMEM, where), (SMEM, counts), (VMEM, x1), (VMEM, vec)]
        + [(ANY, piece) for piece in pieces]
        + parts_of(cross_all),
        [
            flat(wide, F32),
            flat(wide, BF),
            flat(wide, BF),
            flat((examples, total, 2 * width), BF),
            flat((examples, GROUPS, TOGETHER * length, total), BF),
            flat(wide, BF),
        ],
        [scratch(width, 4 * width), scratch(examples, total, width)],
        4 * rows * width * width + 4 * examples * total * width * width + 2 * attention * total,
        mem + blocks,
    )
    a3, h, slope, *grad_out = run(
        functools.partial(dense_first, fast),
        [(SMEM, where), (VMEM, x2), (VMEM, vec), (VMEM, bias_in), (ANY, cotangent)]
        + parts_of(in_all),
        [flat(wide, BF), flat((rows, inner), BF), flat((rows, inner), F32)] + grads_like(out_all),
        [scratch(width, inner), scratch(inner, width), scratch(examples, length, width)],
        4 * rows * width * inner,
        1 + blocks,
    )
    y, gx2, vecs_dense, bias_grad, *grad_in = run(
        functools.partial(dense_second, fast),
        [(SMEM, where), (VMEM, x2), (VMEM, vec), (VMEM, bias_in), (VMEM, a3), (VMEM, h)]
        + [(VMEM, slope), (ANY, cotangent)]
        + parts_of(in_all)
        + parts_of(out_all),
        [
            flat((examples, length, width), BF),
            flat(wide, F32),
            flat((3, width), F32),
            flat((1, inner), F32),
        ]
        + grads_like(in_all),
        [
            scratch(width, inner),
            scratch(inner, width),
            scratch(width, inner),
            scratch(rows, inner),
            scratch(examples, length, width),
        ],
        8 * rows * width * inner,
        1 + 2 * blocks,
    )
    gx1, vecs_cross, *rest = run(
        functools.partial(cross_backward, fast, mem),
        [(SMEM, where), (VMEM, x1), (VMEM, vec), (VMEM, gx2), (VMEM, a2), (VMEM, q2)]
        + [(VMEM, o2), (VMEM, kv), (VMEM, p2)]
        + [(ANY, piece) for piece in pieces]
        + parts_of(cross_all),
        [flat(wide, F32), flat((2, width), F32)]
        + [(ANY, shape_of((examples, slots, width), BF))] * mem
        + grads_like(cross_all),
        [
            scratch(width, 4 * width),
            scratch(examples, total, width),
            scratch(examples, total, width),
            scratch(width, 4 * width),
            scratch(examples, total, 2 * width),
            scratch(*wide),
            scratch(*wide),
        ],
        8 * rows * width * width + 8 * examples * total * width * width + 4 * attention * total,
        mem + blocks,
    )
    mem_pieces, grad_cross = rest[:mem], rest[mem:]
    suffix_part, vecs_self, *grad_self = run(
        functools.partial(self_backward, fast, group),
        [(SMEM, where), (ANY, suffix), (VMEM, vec), (VMEM, gx1), (VMEM, a1), (VMEM, qkv)]
        + [(VMEM, p1), (VMEM, o1)]
        + parts_of(self_all),
        [flat((examples, length, width), BF), flat((2, width), F32)] + grads_like(self_all),
        [
            scratch(width, 4 * width),
            scratch(examples, length, width),
            scratch(width, 4 * width),
            scratch(rows, 3 * width),
            scratch(*wide),
        ],
        16 * rows * width * width + 4 * attention * group,
        1 + blocks,
    )

    def reduce(grads, dim):
        return scatter_grad(*two(grads), dim, c, across)

    block_output = spread_rows(y, m, across)
    grad_out = jnp.concatenate(reduce(grad_out, 0), axis=0)
    grad_in = jnp.concatenate(reduce(grad_in, 1), axis=1)
    memory_grad = jnp.zeros_like(memory)
    for d in range(mem):
        block = swap(mem_pieces[d], "mem", d) if d else mem_pieces[d]
        memory_grad = lax.dynamic_update_slice_in_dim(memory_grad, block, (m ^ d) * examples, 0)
    cross_low, cross_high = reduce(grad_cross, 1)
    self_low, self_high = reduce(grad_self, 1)
    suffix_grad = spread_rows(suffix_part, m, across)

    vectors = jnp.concatenate([vecs_self, vecs_cross, vecs_dense, bias_grad.reshape(-1, width)])
    vectors = add_everywhere(vectors)

    def vector(i):
        return lax.dynamic_slice(vectors, (i, f * part), (1, part)).reshape(part)

    return (
        block_output,
        suffix_grad,
        memory_grad,
        vector(0),
        vector(1),
        self_low[:, :width],
        self_low[:, width:],
        self_high[:, :width],
        self_high[:, width:],
        vector(2),
        vector(3),
        cross_low[:, :width],
        cross_low[:, width:],
        cross_high[:, :width],
        cross_high[:, width:],
        vector(4),
        vector(5),
        grad_in,
        lax.dynamic_slice_in_dim(vectors[7:].reshape(-1), f * (inner // fsdp), inner // fsdp, 0),
        grad_out,
        vector(6),
    )


def solution(mesh):
    rows = P("fsdp", None, None)
    matrix = P("fsdp", None)
    vector = P("fsdp")
    attention = (vector, vector, matrix, matrix, matrix, matrix)
    params = attention + attention + (vector, vector, matrix, vector, matrix, vector)
    return jax.shard_map(
        per_device,
        mesh=mesh,
        in_specs=(rows, P("fsdp", "mem", None), vector, rows) + params,
        out_specs=(rows, rows, P("fsdp", "mem", None)) + params,
        check_vma=False,
    )
```

```python
import functools

import jax
import jax.numpy as jnp
from jax import lax
from jax.experimental import pallas as pl
from jax.experimental.pallas import tpu as pltpu
from jax.sharding import PartitionSpec as P

HEADS = 12
HEAD = 64
TOGETHER = 4
GROUPS = HEADS // TOGETHER
LANES = TOGETHER * HEAD
SCALE = HEAD ** (-0.5)
BF = jnp.bfloat16
F32 = jnp.float32
ANY = pl.BlockSpec(memory_space=pl.ANY)
SMEM = pl.BlockSpec(memory_space=pltpu.SMEM)
VMEM = pl.BlockSpec(memory_space=pltpu.VMEM)


def swap(value, axis, distance):
    size = lax.axis_size(axis)
    return lax.ppermute(value, axis, [(i, i ^ distance) for i in range(size)])


def after(value, *others):
    return lax.optimization_barrier((value, *others))[0] if others else value


class Link:
    def __init__(self, depth):
        self.depth = depth
        self.done = []

    def swap(self, value, axis, distance):
        if len(self.done) >= self.depth:
            value = after(value, self.done[-self.depth])
        self.done.append(swap(value, axis, distance))
        return self.done[-1]


def fsdp_split(size):
    slow = 4 if size % 4 == 0 else 1
    return slow, size // slow


def dot(left, right):
    return jnp.dot(left, right, preferred_element_type=F32)


def dot_nt(left, right):
    return lax.dot_general(left, right, (((1,), (1,)), ((), ())), preferred_element_type=F32)


def dot_tn(left, right):
    return lax.dot_general(left, right, (((0,), (0,)), ((), ())), preferred_element_type=F32)


def rows_of(start, size):
    return pl.ds(pl.multiple_of(start, 16), size)


def block(ref, by_rows, shard, which):
    if by_rows:
        return ref.at[shard, pl.ds(which * 2, 2)]
    rows = ref.shape[1] // SHARDS[0]
    return ref.at[pl.ds(which * 2, 2), rows_of(shard * rows, rows)]


SHARDS = [0]


class Copies:
    def __init__(self, sems):
        self.sems = sems
        self.next = 0

    def start(self, source, target):
        copy = pltpu.make_async_copy(source, target, self.sems.at[self.next])
        self.next += 1
        copy.start()
        return copy


def wait_all(copies):
    for copy in copies:
        copy.wait()


def load_weight(where, whole, by_rows, weights, copies):
    own, mine, theirs = weights
    z, y, c = where[0], where[1], where[2]
    slow = mine[0].shape[0] + 1
    fast = (len(mine) + 1) // 2
    me = z * fast + y
    started = []
    rows = mine[0].shape[2]
    if by_rows:
        for j in range(4):
            started.append(copies.start(own[0].at[pl.ds(j * rows, rows)], whole.at[me, j]))
    else:
        for j in range(4):
            if len(own) == 4:
                source = own[j]
            else:
                source = own[0].at[:, pl.ds(j * whole.shape[2], whole.shape[2])]
            started.append(copies.start(source, whole.at[j, rows_of(me * rows, rows)]))
    for which, pieces in ((c, mine), (1 - c, theirs)):
        for k in range(1, slow):
            shard = (z ^ k) * fast + y
            started.append(
                copies.start(pieces[0].at[k - 1], block(whole, by_rows, shard, which))
            )
        for b in range(1, fast):
            for k in range(slow):
                shard = (z ^ k) * fast + (y ^ b)
                piece = pieces[2 * b].at[k - 1] if k else pieces[2 * b - 1]
                started.append(copies.start(piece, block(whole, by_rows, shard, which)))
    return started


def store_grad(where, whole, by_rows, near, far, theirs, copies):
    z, y, c = where[0], where[1], where[2]
    fast, slow = theirs.shape[0], theirs.shape[1]
    started = []
    for b in range(fast):
        for k in range(slow):
            shard = (z ^ k) * fast + (y ^ b)
            mine = far.at[b - 1, k] if b else near.at[k]
            started.append(copies.start(block(whole, by_rows, shard, 1 - c), theirs.at[b, k]))
            started.append(copies.start(block(whole, by_rows, shard, c), mine))
    return started


def my_examples(where, source, target, copies):
    count = target.shape[0]
    return copies.start(source.at[pl.ds(where[3] * count, count)], target)


def normalise(values):
    centred = values - jnp.mean(values, axis=-1, keepdims=True)
    scale = lax.rsqrt(jnp.mean(centred * centred, axis=-1, keepdims=True) + 1e-06)
    return centred * scale, scale


def norm_back(grad, gain, hat, scale):
    inner = grad * gain
    mean = jnp.mean(inner, axis=-1, keepdims=True)
    along = jnp.mean(inner * hat, axis=-1, keepdims=True)
    return (
        scale * (inner - mean - hat * along),
        jnp.sum(grad * hat, axis=0, keepdims=True),
        jnp.sum(grad, axis=0, keepdims=True),
    )


def head_mask(rows):
    shape = (TOGETHER * rows, LANES)
    row = lax.broadcasted_iota(jnp.int32, shape, 0) // rows
    lane = lax.broadcasted_iota(jnp.int32, shape, 1) // HEAD
    return (row == lane).astype(F32)


def stack_heads(value, mask):
    return (jnp.concatenate([value] * TOGETHER, axis=0).astype(F32) * mask).astype(BF)


def merge_heads(value, mask):
    rows = value.shape[0] // TOGETHER
    value = value * mask
    total = value[:rows]
    for h in range(1, TOGETHER):
        total = total + value[h * rows : (h + 1) * rows]
    return total


def columns(j, width):
    return slice(j * width, (j + 1) * width)


def self_forward(group, where, suffix, vec, weights, x1, a1, qkv, p1, o1, weight, start, sems):
    rows, width = x1.shape
    copies = Copies(sems)
    first = my_examples(where, suffix, start, copies)
    loads = load_weight(where, weight, False, weights, copies)
    first.wait()
    values = start[...].reshape(rows, width).astype(F32)
    hat, _ = normalise(values)
    a1[...] = (hat * vec[0:1, :] + vec[1:2, :]).astype(BF)
    wait_all(loads)
    for j in range(3):
        qkv[:, columns(j, width)] = dot(a1[...], weight[j]).astype(BF)
    mask = head_mask(group)
    length = suffix.shape[1]
    shape = (TOGETHER * group, group)
    row = lax.broadcasted_iota(jnp.int32, shape, 0) % group
    col = lax.broadcasted_iota(jnp.int32, shape, 1)
    seen = (row // length == col // length) & (row >= col)
    for r in range(rows // group):
        here = columns(r, group)
        for g in range(GROUPS):
            lanes = [slice(i * width + g * LANES, i * width + (g + 1) * LANES) for i in range(3)]
            queries = stack_heads(qkv[here, lanes[0]], mask)
            scores = dot_nt(queries, qkv[here, lanes[1]]) * SCALE
            scores = jnp.where(seen, scores, -1e30)
            powers = jnp.exp(scores - jnp.max(scores, axis=-1, keepdims=True))
            probs = (powers / jnp.sum(powers, axis=-1, keepdims=True)).astype(BF)
            p1[r * GROUPS + g] = probs
            found = dot(probs, qkv[here, lanes[2]])
            o1[here, lanes[0]] = merge_heads(found, mask).astype(BF)
    x1[...] = values + dot(o1[...], weight[3])


def cross_forward(
    where, counts, x1, vec, pieces, weights, x2, a2, q2, kv, p2, o2, weight, sems
):
    rows, width = x1.shape
    examples = pl.num_programs(0)
    e = pl.program_id(0)
    total = kv.shape[1]
    length = p2.shape[2] // TOGETHER
    slots = pieces[0].shape[1]

    @pl.when(e == 0)
    def _():
        loads = load_weight(where, weight, False, weights, Copies(sems))
        hat, _ = normalise(x1[...])
        a2[...] = (hat * vec[2:3, :] + vec[3:4, :]).astype(BF)
        wait_all(loads)
        q2[...] = dot(a2[...], weight[0]).astype(BF)

    memory = jnp.concatenate([piece[0] for piece in pieces], axis=0)
    for j in range(2):
        kv[0, :, columns(j, width)] = dot(memory, weight[1 + j]).astype(BF)
    mask = head_mask(length)
    slot = lax.broadcasted_iota(jnp.int32, (1, total), 1)
    position = ((slot // slots) ^ where[3]) * slots + slot % slots
    valid = position < counts[where[3] * examples + e]
    here = rows_of(e * length, length)
    probs = []
    for g in range(GROUPS):
        lanes = columns(g, LANES)
        queries = stack_heads(q2[here, lanes], mask)
        scores = dot_nt(queries, kv[0, :, lanes]) * SCALE
        scores = jnp.where(valid, scores, -1e30)
        top = jnp.maximum(jnp.max(scores, axis=-1, keepdims=True), 0.0)
        powers = jnp.exp(scores - top)
        weight_sum = jnp.sum(powers, axis=-1, keepdims=True) + jnp.exp(-top)
        probs.append((powers / weight_sum).astype(BF))
    for g in range(GROUPS):
        p2[0, g] = probs[g]
        found = dot(probs[g], kv[0, :, width + g * LANES : width + (g + 1) * LANES])
        o2[here, columns(g, LANES)] = merge_heads(found, mask).astype(BF)

    @pl.when(e == examples - 1)
    def _():
        x2[...] = x1[...] + dot(o2[...], weight[3])


def dense_inner(
    where, x2, vec, bias, cotangent, weights, a3, h, slope, near, far, theirs,
    weight, grad, cot, sems,
):
    rows, width = x2.shape
    copies = Copies(sems)
    cot_copy = my_examples(where, cotangent, cot, copies)
    loads = load_weight(where, weight, False, weights, copies)
    hat, _ = normalise(x2[...])
    a3[...] = (hat * vec[4:5, :] + vec[5:6, :]).astype(BF)
    cot_copy.wait()
    gy = cot[...].reshape(rows, width)
    wait_all(loads)
    flat = grad.shape[0] * grad.shape[1] * grad.shape[2]
    step = flat // grad.shape[0]
    for j in range(4):
        for half in range(2):
            cols = slice(j * width + half * 384, j * width + (half + 1) * 384)
            u = dot(a3[...], weight[j, :, half * 384 : (half + 1) * 384]) + bias[:, cols]
            square = u * u
            t = jnp.tanh(0.7978845608 * u * (1.0 + 0.044715 * square))
            h[:, cols] = (0.5 * u * (1.0 + t)).astype(BF)
            slope[:, cols] = (
                0.5 * (1.0 + t)
                + (0.5 * 0.7978845608) * u * (1.0 - t * t) * (1.0 + (3.0 * 0.044715) * square)
            ).astype(BF)
            part = dot_tn(h[:, cols], gy).astype(BF)
            per = 384 // step
            grad[cols.start // step : cols.start // step + per] = part.reshape(
                (per,) + grad.shape[1:]
            )
    wait_all(store_grad(where, grad, True, near, far, theirs, Copies(sems)))


def dense_outer(
    where, x2, vec, a3, h, slope, cotangent, weights, y, du, vecs, bias_grad, near, far, theirs,
    weight, grad, cot, sems,
):
    rows, width = x2.shape
    copies = Copies(sems)
    cot_copy = my_examples(where, cotangent, cot, copies)
    wait_all(load_weight(where, weight, True, weights, copies))
    cot_copy.wait()
    gy = cot[...].reshape(rows, width)
    shards = weight.shape[0]
    step = weight.shape[1] * weight.shape[2]
    whole = weight[...].reshape(shards * step, width)
    for j in range(4):
        cols = columns(j, width)
        low = (dot_nt(gy, whole[cols]) * slope[:, cols].astype(F32)).astype(BF)
        du[:, cols] = low
        bias_grad[:, cols] = jnp.sum(low.astype(F32), axis=0, keepdims=True)
        grad[j] = dot_tn(a3[...], low).astype(BF)
    started = store_grad(where, grad, False, near, far, theirs, Copies(sems))
    result = x2[...] + dot(h[...], whole) + vec[6:7, :]
    y[...] = result.astype(BF).reshape(y.shape)
    vecs[...] = jnp.sum(gy.astype(F32), axis=0, keepdims=True)
    wait_all(started)


def dense_back(where, x2, vec, du, cotangent, weights, gx2, vecs, weight, cot, sems):
    rows, width = x2.shape
    copies = Copies(sems)
    cot_copy = my_examples(where, cotangent, cot, copies)
    loads = load_weight(where, weight, False, weights, copies)
    hat, scale = normalise(x2[...])
    cot_copy.wait()
    wait_all(loads)
    da3 = dot_nt(du[:, columns(0, width)], weight[0])
    for j in range(1, 4):
        da3 = da3 + dot_nt(du[:, columns(j, width)], weight[j])
    back, gain_grad, shift_grad = norm_back(da3, vec[4:5, :], hat, scale)
    gx2[...] = cot[...].reshape(rows, width).astype(F32) + back
    vecs[0:1, :] = gain_grad
    vecs[1:2, :] = shift_grad


def cross_backward(
    where, x1, vec, gx2, q2, kv, p2, weights, gx1, vecs, dkv, dq2, out_mem, weight, do2, sems
):
    rows, width = x1.shape
    examples = pl.num_programs(0)
    e = pl.program_id(0)
    length = p2.shape[2] // TOGETHER
    slots = out_mem[0].shape[1]

    @pl.when(e == 0)
    def _():
        wait_all(load_weight(where, weight, False, weights, Copies(sems)))
        do2[...] = dot_nt(gx2[...].astype(BF), weight[3]).astype(BF)

    mask = head_mask(length)
    here = rows_of(e * length, length)
    for g in range(GROUPS):
        lanes = columns(g, LANES)
        value_lanes = slice(width + g * LANES, width + (g + 1) * LANES)
        queries = stack_heads(q2[here, lanes], mask)
        grads = stack_heads(do2[here, lanes], mask)
        probs = p2[0, g]
        dp = dot_nt(grads, kv[0, :, value_lanes])
        wide = probs.astype(F32)
        row_sum = jnp.sum(wide * dp, axis=-1, keepdims=True)
        dz = (wide * (dp - row_sum)).astype(BF)
        dkv[0, :, value_lanes] = dot_tn(probs, grads).astype(BF)
        dkv[0, :, lanes] = (dot_tn(dz, queries) * SCALE).astype(BF)
        dq2[here, lanes] = (merge_heads(dot(dz, kv[0, :, lanes]), mask) * SCALE).astype(BF)
    back = dot_nt(dkv[0, :, :width], weight[1]) + dot_nt(dkv[0, :, width:], weight[2])
    for d, out in enumerate(out_mem):
        out[0] = back[d * slots : (d + 1) * slots].astype(BF)

    @pl.when(e == examples - 1)
    def _():
        hat, scale = normalise(x1[...])
        back, gain_grad, shift_grad = norm_back(
            dot_nt(dq2[...], weight[0]), vec[2:3, :], hat, scale
        )
        gx1[...] = gx2[...] + back
        vecs[0:1, :] = gain_grad
        vecs[1:2, :] = shift_grad


def cross_grads(where, gx2, a2, o2, dq2, dkv, pieces, near, far, theirs, grad, memory, sems):
    rows, width = gx2.shape
    examples, total, _ = memory.shape
    slots = total // len(pieces)
    copies = Copies(sems)
    loads = [
        copies.start(piece, memory.at[:, d * slots : (d + 1) * slots, :])
        for d, piece in enumerate(pieces)
    ]
    grad[0] = dot_tn(a2[...], dq2[...]).astype(BF)
    grad[3] = dot_tn(o2[...], gx2[...].astype(BF)).astype(BF)
    wait_all(loads)
    flat = memory[...].reshape(examples * total, width)
    for j in range(2):
        part = dkv[:, :, columns(j, width)].reshape(examples * total, width)
        grad[1 + j] = dot_tn(flat, part).astype(BF)
    wait_all(store_grad(where, grad, False, near, far, theirs, Copies(sems)))


def self_backward(
    group, where, suffix, vec, gx1, a1, qkv, p1, o1, weights, suffix_grad, vecs,
    near, far, theirs, weight, start, grad, dqkv, do1, sems,
):
    rows, width = gx1.shape
    copies = Copies(sems)
    start_copy = my_examples(where, suffix, start, copies)
    loads = load_weight(where, weight, False, weights, copies)
    gs = gx1[...].astype(BF)
    grad[3] = dot_tn(o1[...], gs).astype(BF)
    wait_all(loads)
    do1[...] = dot_nt(gs, weight[3]).astype(BF)
    mask = head_mask(group)
    for r in range(rows // group):
        here = columns(r, group)
        for g in range(GROUPS):
            lanes = [slice(i * width + g * LANES, i * width + (g + 1) * LANES) for i in range(3)]
            queries = stack_heads(qkv[here, lanes[0]], mask)
            grads = stack_heads(do1[here, lanes[0]], mask)
            probs = p1[r * GROUPS + g]
            dp = dot_nt(grads, qkv[here, lanes[2]])
            wide = probs.astype(F32)
            row_sum = jnp.sum(wide * dp, axis=-1, keepdims=True)
            dz = (wide * (dp - row_sum)).astype(BF)
            dqkv[here, lanes[2]] = dot_tn(probs, grads).astype(BF)
            dqkv[here, lanes[1]] = (dot_tn(dz, queries) * SCALE).astype(BF)
            dq = merge_heads(dot(dz, qkv[here, lanes[1]]), mask) * SCALE
            dqkv[here, lanes[0]] = dq.astype(BF)
    for j in range(3):
        grad[j] = dot_tn(a1[...], dqkv[:, columns(j, width)]).astype(BF)
    start_copy.wait()
    started = store_grad(where, grad, False, near, far, theirs, Copies(sems))
    da1 = dot_nt(dqkv[:, columns(0, width)], weight[0])
    for j in range(1, 3):
        da1 = da1 + dot_nt(dqkv[:, columns(j, width)], weight[j])
    hat, scale = normalise(start[...].reshape(rows, width).astype(F32))
    back, gain_grad, shift_grad = norm_back(da1, vec[0:1, :], hat, scale)
    suffix_grad[...] = (gx1[...] + back).astype(BF).reshape(suffix_grad.shape)
    vecs[0:1, :] = gain_grad
    vecs[1:2, :] = shift_grad
    wait_all(started)


def run(kernel, inputs, outputs, scratch, flops, copies, grid=()):
    def leaf(x):
        return isinstance(x, tuple) and len(x) == 2 and isinstance(x[0], pl.BlockSpec)

    flat_in, tree_in = jax.tree.flatten(inputs, is_leaf=leaf)
    flat_out, tree_out = jax.tree.flatten(outputs, is_leaf=leaf)
    moved = sum(x.size * x.dtype.itemsize for _, x in flat_in + flat_out)

    def body(*refs):
        first, second = len(flat_in), len(flat_in) + len(flat_out)
        given = jax.tree.unflatten(tree_in, refs[:first])
        taken = jax.tree.unflatten(tree_out, refs[first:second])
        kernel(*given, *taken, *refs[second:])

    found = pl.pallas_call(
        body,
        grid=grid,
        in_specs=[spec for spec, _ in flat_in],
        out_specs=[spec for spec, _ in flat_out],
        out_shape=[shape for _, shape in flat_out],
        scratch_shapes=scratch + [pltpu.SemaphoreType.DMA((copies,))],
        compiler_params=pltpu.CompilerParams(vmem_limit_bytes=56 * 1024 * 1024),
        cost_estimate=pl.CostEstimate(flops=flops, bytes_accessed=moved, transcendentals=0),
    )(*[x for _, x in flat_in])
    return jax.tree.unflatten(tree_out, found)


def shape_of(dims, dtype):
    return jax.ShapeDtypeStruct(tuple(dims), dtype)


class Gather:
    def __init__(self, own, half, slow, fast):
        self.own, self.half, self.slow, self.fast = own, half, slow, fast
        self.near = self.far = None

    def send_own(self, link):
        self.far_own = [link.swap(self.half, "fsdp", b) for b in range(1, self.fast)]

    def send_slow(self, link):
        self.near = jnp.stack(
            [link.swap(self.half, "fsdp", k * self.fast) for k in range(1, self.slow)]
        )

    def send_fast(self, link):
        self.far = [link.swap(self.near, "fsdp", b) for b in range(1, self.fast)]

    def whole(self, *others):
        mine = [self.near]
        for far_own, far in zip(self.far_own, self.far):
            mine += [far_own, after(far, *others)]
        theirs = [swap(piece, "mem", 1) for piece in mine]
        return [[(ANY, x) for x in some] for some in (self.own, mine, theirs)]


class Scatter:
    def __init__(self, grads, slow, fast, across):
        self.near, self.far, theirs = grads
        self.slow, self.fast, self.across = slow, fast, across
        self.sent = swap(theirs, "mem", 1)

    def add_cores(self):
        self.out = [
            (self.far[b].astype(F32) + self.sent[b + 1].astype(F32)).astype(BF)
            for b in range(self.fast - 1)
        ]
        return self.out

    def send_fast(self, link):
        self.came = [link.swap(part, "fsdp", b + 1) for b, part in enumerate(self.out)]

    def add_fast(self):
        total = self.near.astype(F32) + self.sent[0].astype(F32)
        for part in self.came:
            total = total + part.astype(F32)
        self.total = total.astype(BF)
        return self.total

    def send_slow(self, link):
        self.came = [
            link.swap(self.total[k], "fsdp", k * self.fast) for k in range(1, self.slow)
        ]

    def finish(self, c):
        final = self.total[0].astype(F32)
        for part in self.came:
            final = final + part.astype(F32)
        k = 1
        while 2 * k < self.across:
            low = final.astype(BF)
            final = low.astype(F32) + swap(low, "mem", 2 * k).astype(F32)
            k *= 2
        low = final.astype(BF)
        halves = [low, swap(low, "mem", 2 * k)] if self.across > 1 else [low]
        others = [swap(half, "mem", 1) for half in halves]
        mine = sum(half.astype(F32) for half in halves)
        other = sum(half.astype(F32) for half in others)
        first = jnp.where(c == 0, mine, other)
        second = jnp.where(c == 0, other, mine)
        return [first[0], first[1], second[0], second[1]]


def add_everywhere(value):
    for axis in ("mem", "fsdp"):
        k = 1
        while k < lax.axis_size(axis):
            value = value + swap(value, axis, k)
            k *= 2
    return value


def spread_rows(value, m, across):
    examples = value.shape[0]
    out = jnp.zeros((2 * across * examples,) + value.shape[1:], value.dtype)
    blocks = {0: value}
    for k in range(1, across):
        blocks[2 * k] = swap(value, "mem", 2 * k)
    for k in range(across):
        blocks[2 * k + 1] = swap(blocks[2 * k], "mem", 1)
    for d, piece in blocks.items():
        out = lax.dynamic_update_slice_in_dim(out, piece, (m ^ d) * examples, 0)
    return out


def per_device(
    suffix,
    memory,
    counts,
    cotangent,
    self_norm_gain,
    self_norm_bias,
    self_query,
    self_key,
    self_value,
    self_output,
    cross_norm_gain,
    cross_norm_bias,
    cross_query,
    cross_key,
    cross_value,
    cross_output,
    dense_norm_gain,
    dense_norm_bias,
    dense_in,
    dense_in_bias,
    dense_out,
    dense_out_bias,
):
    f = lax.axis_index("fsdp")
    m = lax.axis_index("mem")
    c = m % 2
    fsdp = lax.axis_size("fsdp")
    mem = lax.axis_size("mem")
    across = mem // 2
    slow, fast = fsdp_split(fsdp)
    SHARDS[0] = fsdp
    where = jnp.stack([f // fast, f % fast, c, m]).astype(jnp.int32)
    examples = suffix.shape[0] // mem
    length = suffix.shape[1]
    width = suffix.shape[2]
    slots = memory.shape[1]
    total = mem * slots
    rows = examples * length
    inner = dense_in.shape[1]
    part = width // fsdp
    group = min(128, rows)
    blocks = 2 * fsdp + 4

    slow_link, fast_link = Link(3), Link(2)

    def gather(own, matrices):
        half = jnp.where(c == 0, jnp.stack(matrices[:2]), jnp.stack(matrices[2:]))
        return Gather(own, half, slow, fast)

    self_matrices = [self_query, self_key, self_value, self_output]
    cross_matrices = [cross_query, cross_key, cross_value, cross_output]
    self_gather = gather(self_matrices, self_matrices)
    cross_gather = gather(cross_matrices, cross_matrices)
    in_gather = gather([dense_in], [dense_in[:, columns(j, width)] for j in range(4)])
    out_gather = gather([dense_out], [dense_out[columns(j, part)] for j in range(4)])
    gathers = [self_gather, cross_gather, in_gather, out_gather]
    small = jnp.concatenate(
        [
            self_norm_gain,
            self_norm_bias,
            cross_norm_gain,
            cross_norm_bias,
            dense_norm_gain,
            dense_norm_bias,
            dense_out_bias,
            dense_in_bias,
        ]
    )[None]
    k = 1
    while k < fsdp:
        small = jnp.concatenate([small, swap(small, "fsdp", k)], axis=0)
        k *= 2
    small = jnp.take(small, jnp.arange(fsdp) ^ f, axis=0).astype(F32)
    vec = small[:, : 7 * part].reshape(fsdp, 7, part).transpose(1, 0, 2).reshape(7, width)
    bias_in = small[:, 7 * part :].reshape(1, inner)
    for one in gathers:
        one.send_own(fast_link)
    for one in gathers:
        one.send_slow(slow_link)
        one.send_fast(fast_link)

    def of_device(value, index):
        return lax.dynamic_slice_in_dim(value, index * examples, examples, 0)

    pieces = [of_device(memory, m)]
    for d in range(1, mem):
        pieces.append(swap(of_device(memory, m ^ d), "mem", d))

    half = (2, part, width)
    grads_like = [
        (ANY, shape_of((slow,) + half, BF)),
        (ANY, shape_of((fast - 1, slow) + half, BF)),
        (ANY, shape_of((fast, slow) + half, BF)),
    ]

    def flat(dims, dtype):
        return (VMEM, shape_of(dims, dtype))

    def per_example(value):
        dims = value.shape[1:]
        spec = pl.BlockSpec((1,) + dims, lambda e: (e,) + (0,) * len(dims))
        return (spec, value)

    def scratch(*dims):
        return pltpu.VMEM(dims, BF)

    def scatter(grads):
        return Scatter(grads, slow, fast, across)

    wide = (rows, width)
    square = scratch(4, width, width)
    attention = 2 * GROUPS * TOGETHER * LANES * rows
    product = 2 * rows * width * width
    own_rows = scratch(examples, length, width)
    self_weights = self_gather.whole()
    x1, a1, qkv, p1, o1 = run(
        functools.partial(self_forward, group),
        [(SMEM, where), (ANY, suffix), (VMEM, vec), self_weights],
        [
            flat(wide, F32),
            flat(wide, BF),
            flat((rows, 3 * width), BF),
            flat((rows // group * GROUPS, TOGETHER * group, group), BF),
            flat(wide, BF),
        ],
        [square, own_rows],
        4 * product + 2 * attention * group,
        1 + blocks,
    )
    cross_weights = cross_gather.whole(x1)
    x2, a2, q2, kv, p2, o2 = run(
        cross_forward,
        [(SMEM, where), (SMEM, counts), (VMEM, x1), (VMEM, vec)]
        + [[per_example(piece) for piece in pieces], cross_weights],
        [
            flat(wide, F32),
            flat(wide, BF),
            flat(wide, BF),
            per_example(shape_of((examples, total, 2 * width), BF)),
            per_example(shape_of((examples, GROUPS, TOGETHER * length, total), BF)),
            flat(wide, BF),
        ],
        [square],
        2 * product + 4 * examples * total * width * width + 2 * attention * total,
        blocks,
        (examples,),
    )
    in_weights = in_gather.whole(x2)
    a3, h, slope, *grads = run(
        dense_inner,
        [(SMEM, where), (VMEM, x2), (VMEM, vec), (VMEM, bias_in), (ANY, cotangent), in_weights],
        [flat(wide, BF), flat((rows, inner), BF), flat((rows, inner), BF)] + grads_like,
        [square, scratch(fsdp, 4, part, width), own_rows],
        8 * product,
        1 + blocks,
    )
    out_scatter = scatter(grads)
    link_fast, link_slow = Link(2), Link(3)
    out_sum = out_scatter.add_cores()
    out_scatter.send_fast(link_fast)
    out_weights = out_gather.whole(a3)
    y, du, vecs_y, bias_grad, *grads = run(
        dense_outer,
        [(SMEM, where), (VMEM, after(x2, *out_sum)), (VMEM, vec), (VMEM, a3), (VMEM, h)]
        + [(VMEM, slope), (ANY, cotangent), out_weights],
        [
            flat((examples, length, width), BF),
            flat((rows, inner), BF),
            flat((1, width), F32),
            flat((1, inner), F32),
        ]
        + grads_like,
        [scratch(fsdp, 4, part, width), square, own_rows],
        12 * product,
        1 + blocks,
    )
    in_scatter = scatter(grads)
    gx2, vecs_dense = run(
        dense_back,
        [(SMEM, where), (VMEM, x2), (VMEM, vec), (VMEM, du), (ANY, cotangent), in_weights],
        [flat(wide, F32), flat((2, width), F32)],
        [square, own_rows],
        4 * product,
        1 + blocks,
    )
    in_sum = in_scatter.add_cores()
    in_scatter.send_fast(link_fast)
    gx1, vecs_cross, dkv, dq2, mem_pieces = run(
        cross_backward,
        [(SMEM, where), (VMEM, x1), (VMEM, vec), (VMEM, after(gx2, *in_sum)), (VMEM, q2)]
        + [per_example(kv), per_example(p2), cross_weights],
        [
            flat(wide, F32),
            flat((2, width), F32),
            per_example(shape_of((examples, total, 2 * width), BF)),
            flat(wide, BF),
            [per_example(shape_of((examples, slots, width), BF))] * mem,
        ],
        [square, scratch(*wide)],
        2 * product + 4 * examples * total * width * width + 4 * attention * total,
        blocks,
        (examples,),
    )
    out_total = out_scatter.add_fast()
    out_scatter.send_slow(link_slow)
    grads = run(
        cross_grads,
        [(SMEM, where), (VMEM, after(gx2, out_total)), (VMEM, a2), (VMEM, o2), (VMEM, dq2)]
        + [(VMEM, dkv), [(ANY, piece) for piece in pieces]],
        grads_like,
        [square, scratch(examples, total, width)],
        2 * product + 4 * examples * total * width * width,
        max(mem, blocks),
    )
    cross_scatter = scatter(grads)
    cross_sum = cross_scatter.add_cores()
    cross_scatter.send_fast(link_fast)
    suffix_part, vecs_self, *grads = run(
        functools.partial(self_backward, group),
        [(SMEM, where), (ANY, suffix), (VMEM, vec), (VMEM, after(gx1, *cross_sum)), (VMEM, a1)]
        + [(VMEM, qkv), (VMEM, p1), (VMEM, o1), self_weights],
        [flat((examples, length, width), BF), flat((2, width), F32)] + grads_like,
        [square, own_rows, square, scratch(rows, 3 * width), scratch(*wide)],
        8 * product + 4 * attention * group,
        1 + blocks,
    )
    self_scatter = scatter(grads)
    self_scatter.add_cores()
    self_scatter.send_fast(link_fast)
    for one in (in_scatter, cross_scatter, self_scatter):
        one.add_fast()
        one.send_slow(link_slow)

    block_output = spread_rows(y, m, across)
    grad_out = jnp.concatenate(out_scatter.finish(c), axis=0)
    grad_in = jnp.concatenate(in_scatter.finish(c), axis=1)
    memory_grad = jnp.zeros_like(memory)
    for d in range(mem):
        piece = swap(mem_pieces[d], "mem", d) if d else mem_pieces[d]
        memory_grad = lax.dynamic_update_slice_in_dim(memory_grad, piece, (m ^ d) * examples, 0)
    grad_cross = cross_scatter.finish(c)
    suffix_grad = spread_rows(suffix_part, m, across)
    vectors = jnp.concatenate(
        [vecs_self, vecs_cross, vecs_dense, vecs_y, bias_grad.reshape(-1, width)]
    )
    vectors = add_everywhere(vectors)
    grad_self = self_scatter.finish(c)

    def vector(i):
        return lax.dynamic_slice(vectors, (i, f * part), (1, part)).reshape(part)

    return (
        block_output,
        suffix_grad,
        memory_grad,
        vector(0),
        vector(1),
        *grad_self,
        vector(2),
        vector(3),
        *grad_cross,
        vector(4),
        vector(5),
        grad_in,
        lax.dynamic_slice_in_dim(vectors[7:].reshape(-1), f * (inner // fsdp), inner // fsdp, 0),
        grad_out,
        vector(6),
    )


def solution(mesh):
    rows = P("fsdp", None, None)
    matrix = P("fsdp", None)
    vector = P("fsdp")
    attention = (vector, vector, matrix, matrix, matrix, matrix)
    params = attention + attention + (vector, vector, matrix, vector, matrix, vector)
    return jax.shard_map(
        per_device,
        mesh=mesh,
        in_specs=(rows, P("fsdp", "mem", None), vector, rows) + params,
        out_specs=(rows, rows, P("fsdp", "mem", None)) + params,
        check_vma=False,
    )
```

```python
import functools

import jax
import jax.numpy as jnp
from jax import lax
from jax.experimental import pallas as pl
from jax.experimental.pallas import tpu as pltpu
from jax.sharding import PartitionSpec as P

HEADS = 12
HEAD = 64
TOGETHER = 4
GROUPS = HEADS // TOGETHER
LANES = TOGETHER * HEAD
SCALE = HEAD ** (-0.5)
BF = jnp.bfloat16
F32 = jnp.float32
ANY = pl.BlockSpec(memory_space=pl.ANY)
SMEM = pl.BlockSpec(memory_space=pltpu.SMEM)
VMEM = pl.BlockSpec(memory_space=pltpu.VMEM)


def swap(value, axis, distance):
    size = lax.axis_size(axis)
    return lax.ppermute(value, axis, [(i, i ^ distance) for i in range(size)])


def after(value, *others):
    return lax.optimization_barrier((value, *others))[0] if others else value


class Link:
    def __init__(self, depth):
        self.depth = depth
        self.done = []

    def swap(self, value, axis, distance):
        if len(self.done) >= self.depth:
            value = after(value, self.done[-self.depth])
        self.done.append(swap(value, axis, distance))
        return self.done[-1]


def fsdp_split(size):
    slow = 4 if size % 4 == 0 else 1
    return slow, size // slow


def dot(left, right):
    return jnp.dot(left, right, preferred_element_type=F32)


def dot_nt(left, right):
    return lax.dot_general(left, right, (((1,), (1,)), ((), ())), preferred_element_type=F32)


def dot_tn(left, right):
    return lax.dot_general(left, right, (((0,), (0,)), ((), ())), preferred_element_type=F32)


def rows_of(start, size):
    return pl.ds(pl.multiple_of(start, 16), size)


def block(ref, by_rows, shard, which):
    if by_rows:
        return ref.at[shard, pl.ds(which * 2, 2)]
    rows = ref.shape[1] // SHARDS[0]
    return ref.at[pl.ds(which * 2, 2), rows_of(shard * rows, rows)]


SHARDS = [0]


class Copies:
    def __init__(self, sems):
        self.sems = sems
        self.next = 0

    def start(self, source, target):
        copy = pltpu.make_async_copy(source, target, self.sems.at[self.next])
        self.next += 1
        copy.start()
        return copy


def wait_all(copies):
    for copy in copies:
        copy.wait()


def load_weight(where, whole, by_rows, weights, copies):
    own, mine, theirs = weights
    z, y, c = where[0], where[1], where[2]
    slow = mine[0].shape[0] + 1
    fast = (len(mine) + 1) // 2
    me = z * fast + y
    started = []
    rows = mine[0].shape[2]
    if by_rows:
        for j in range(4):
            started.append(copies.start(own[0].at[pl.ds(j * rows, rows)], whole.at[me, j]))
    else:
        for j in range(4):
            if len(own) == 4:
                source = own[j]
            else:
                source = own[0].at[:, pl.ds(j * whole.shape[2], whole.shape[2])]
            started.append(copies.start(source, whole.at[j, rows_of(me * rows, rows)]))
    for which, pieces in ((c, mine), (1 - c, theirs)):
        for k in range(1, slow):
            shard = (z ^ k) * fast + y
            started.append(
                copies.start(pieces[0].at[k - 1], block(whole, by_rows, shard, which))
            )
        for b in range(1, fast):
            for k in range(slow):
                shard = (z ^ k) * fast + (y ^ b)
                piece = pieces[2 * b].at[k - 1] if k else pieces[2 * b - 1]
                started.append(copies.start(piece, block(whole, by_rows, shard, which)))
    return started


def store_grad(where, whole, by_rows, near, far, theirs, copies):
    z, y, c = where[0], where[1], where[2]
    fast, slow = theirs.shape[0], theirs.shape[1]
    started = []
    for b in range(fast):
        for k in range(slow):
            shard = (z ^ k) * fast + (y ^ b)
            mine = far.at[b - 1, k] if b else near.at[k]
            started.append(copies.start(block(whole, by_rows, shard, 1 - c), theirs.at[b, k]))
            started.append(copies.start(block(whole, by_rows, shard, c), mine))
    return started


def my_examples(where, source, target, copies):
    count = target.shape[0]
    return copies.start(source.at[pl.ds(where[3] * count, count)], target)


def normalise(values):
    centred = values - jnp.mean(values, axis=-1, keepdims=True)
    scale = lax.rsqrt(jnp.mean(centred * centred, axis=-1, keepdims=True) + 1e-06)
    return centred * scale, scale


def norm_back(grad, gain, hat, scale):
    inner = grad * gain
    mean = jnp.mean(inner, axis=-1, keepdims=True)
    along = jnp.mean(inner * hat, axis=-1, keepdims=True)
    return (
        scale * (inner - mean - hat * along),
        jnp.sum(grad * hat, axis=0, keepdims=True),
        jnp.sum(grad, axis=0, keepdims=True),
    )


def head_mask(rows):
    shape = (TOGETHER * rows, LANES)
    row = lax.broadcasted_iota(jnp.int32, shape, 0) // rows
    lane = lax.broadcasted_iota(jnp.int32, shape, 1) // HEAD
    return (row == lane).astype(F32)


def stack_heads(value, mask):
    return (jnp.concatenate([value] * TOGETHER, axis=0).astype(F32) * mask).astype(BF)


def merge_heads(value, mask):
    rows = value.shape[0] // TOGETHER
    value = value * mask
    total = value[:rows]
    for h in range(1, TOGETHER):
        total = total + value[h * rows : (h + 1) * rows]
    return total


def columns(j, width):
    return slice(j * width, (j + 1) * width)


def self_forward(group, where, suffix, vec, weights, x1, a1, qkv, p1, o1, weight, start, sems):
    rows, width = x1.shape
    copies = Copies(sems)
    first = my_examples(where, suffix, start, copies)
    loads = load_weight(where, weight, False, weights, copies)
    first.wait()
    values = start[...].reshape(rows, width).astype(F32)
    hat, _ = normalise(values)
    a1[...] = (hat * vec[0:1, :] + vec[1:2, :]).astype(BF)
    wait_all(loads)
    for j in range(3):
        qkv[:, columns(j, width)] = dot(a1[...], weight[j]).astype(BF)
    mask = head_mask(group)
    length = suffix.shape[1]
    shape = (TOGETHER * group, group)
    row = lax.broadcasted_iota(jnp.int32, shape, 0) % group
    col = lax.broadcasted_iota(jnp.int32, shape, 1)
    seen = (row // length == col // length) & (row >= col)
    for r in range(rows // group):
        here = columns(r, group)
        for g in range(GROUPS):
            lanes = [slice(i * width + g * LANES, i * width + (g + 1) * LANES) for i in range(3)]
            queries = stack_heads(qkv[here, lanes[0]], mask)
            scores = dot_nt(queries, qkv[here, lanes[1]]) * SCALE
            scores = jnp.where(seen, scores, -1e30)
            powers = jnp.exp(scores - jnp.max(scores, axis=-1, keepdims=True))
            probs = (powers / jnp.sum(powers, axis=-1, keepdims=True)).astype(BF)
            p1[r * GROUPS + g] = probs
            found = dot(probs, qkv[here, lanes[2]])
            o1[here, lanes[0]] = merge_heads(found, mask).astype(BF)
    x1[...] = values + dot(o1[...], weight[3])


def cross_forward(
    where, counts, x1, vec, pieces, weights, x2, a2, q2, kv, p2, o2, weight, sems
):
    rows, width = x1.shape
    examples = pl.num_programs(0)
    e = pl.program_id(0)
    total = kv.shape[1]
    length = p2.shape[2] // TOGETHER
    slots = pieces[0].shape[1]

    @pl.when(e == 0)
    def _():
        loads = load_weight(where, weight, False, weights, Copies(sems))
        hat, _ = normalise(x1[...])
        a2[...] = (hat * vec[2:3, :] + vec[3:4, :]).astype(BF)
        wait_all(loads)
        q2[...] = dot(a2[...], weight[0]).astype(BF)

    memory = jnp.concatenate([piece[0] for piece in pieces], axis=0)
    for j in range(2):
        kv[0, :, columns(j, width)] = dot(memory, weight[1 + j]).astype(BF)
    mask = head_mask(length)
    slot = lax.broadcasted_iota(jnp.int32, (1, total), 1)
    position = ((slot // slots) ^ where[3]) * slots + slot % slots
    valid = position < counts[where[3] * examples + e]
    here = rows_of(e * length, length)
    probs = []
    for g in range(GROUPS):
        lanes = columns(g, LANES)
        queries = stack_heads(q2[here, lanes], mask)
        scores = dot_nt(queries, kv[0, :, lanes]) * SCALE
        scores = jnp.where(valid, scores, -1e30)
        top = jnp.maximum(jnp.max(scores, axis=-1, keepdims=True), 0.0)
        powers = jnp.exp(scores - top)
        weight_sum = jnp.sum(powers, axis=-1, keepdims=True) + jnp.exp(-top)
        probs.append((powers / weight_sum).astype(BF))
    for g in range(GROUPS):
        p2[0, g] = probs[g]
        found = dot(probs[g], kv[0, :, width + g * LANES : width + (g + 1) * LANES])
        o2[here, columns(g, LANES)] = merge_heads(found, mask).astype(BF)

    @pl.when(e == examples - 1)
    def _():
        x2[...] = x1[...] + dot(o2[...], weight[3])


def dense_inner(
    where, x2, vec, bias, cotangent, weights, a3, h, slope, near, far, theirs,
    weight, grad, cot, sems,
):
    rows, width = x2.shape
    copies = Copies(sems)
    cot_copy = my_examples(where, cotangent, cot, copies)
    loads = load_weight(where, weight, False, weights, copies)
    hat, _ = normalise(x2[...])
    a3[...] = (hat * vec[4:5, :] + vec[5:6, :]).astype(BF)
    cot_copy.wait()
    gy = cot[...].reshape(rows, width)
    wait_all(loads)
    flat = grad.shape[0] * grad.shape[1] * grad.shape[2]
    step = flat // grad.shape[0]
    for j in range(4):
        for half in range(2):
            cols = slice(j * width + half * 384, j * width + (half + 1) * 384)
            u = dot(a3[...], weight[j, :, half * 384 : (half + 1) * 384]) + bias[:, cols]
            square = u * u
            t = jnp.tanh(0.7978845608 * u * (1.0 + 0.044715 * square))
            h[:, cols] = (0.5 * u * (1.0 + t)).astype(BF)
            slope[:, cols] = (
                0.5 * (1.0 + t)
                + (0.5 * 0.7978845608) * u * (1.0 - t * t) * (1.0 + (3.0 * 0.044715) * square)
            ).astype(BF)
            part = dot_tn(h[:, cols], gy).astype(BF)
            per = 384 // step
            grad[cols.start // step : cols.start // step + per] = part.reshape(
                (per,) + grad.shape[1:]
            )
    wait_all(store_grad(where, grad, True, near, far, theirs, Copies(sems)))


def dense_outer(
    where, x2, vec, a3, h, slope, cotangent, weights, y, du, vecs, bias_grad, near, far, theirs,
    weight, grad, cot, sems,
):
    rows, width = x2.shape
    copies = Copies(sems)
    cot_copy = my_examples(where, cotangent, cot, copies)
    wait_all(load_weight(where, weight, True, weights, copies))
    cot_copy.wait()
    gy = cot[...].reshape(rows, width)
    shards = weight.shape[0]
    step = weight.shape[1] * weight.shape[2]
    whole = weight[...].reshape(shards * step, width)
    for j in range(4):
        cols = columns(j, width)
        low = (dot_nt(gy, whole[cols]) * slope[:, cols].astype(F32)).astype(BF)
        du[:, cols] = low
        bias_grad[:, cols] = jnp.sum(low.astype(F32), axis=0, keepdims=True)
        grad[j] = dot_tn(a3[...], low).astype(BF)
    started = store_grad(where, grad, False, near, far, theirs, Copies(sems))
    result = x2[...] + dot(h[...], whole) + vec[6:7, :]
    y[...] = result.astype(BF).reshape(y.shape)
    vecs[...] = jnp.sum(gy.astype(F32), axis=0, keepdims=True)
    wait_all(started)


def dense_back(where, x2, vec, du, cotangent, weights, gx2, vecs, weight, cot, sems):
    rows, width = x2.shape
    copies = Copies(sems)
    cot_copy = my_examples(where, cotangent, cot, copies)
    loads = load_weight(where, weight, False, weights, copies)
    hat, scale = normalise(x2[...])
    cot_copy.wait()
    wait_all(loads)
    da3 = dot_nt(du[:, columns(0, width)], weight[0])
    for j in range(1, 4):
        da3 = da3 + dot_nt(du[:, columns(j, width)], weight[j])
    back, gain_grad, shift_grad = norm_back(da3, vec[4:5, :], hat, scale)
    gx2[...] = cot[...].reshape(rows, width).astype(F32) + back
    vecs[0:1, :] = gain_grad
    vecs[1:2, :] = shift_grad


def cross_backward(
    where, x1, vec, gx2, q2, kv, p2, weights, gx1, vecs, dkv, dq2, out_mem, weight, do2, sems
):
    rows, width = x1.shape
    examples = pl.num_programs(0)
    e = pl.program_id(0)
    length = p2.shape[2] // TOGETHER
    slots = out_mem[0].shape[1]

    @pl.when(e == 0)
    def _():
        wait_all(load_weight(where, weight, False, weights, Copies(sems)))
        do2[...] = dot_nt(gx2[...].astype(BF), weight[3]).astype(BF)

    mask = head_mask(length)
    here = rows_of(e * length, length)
    for g in range(GROUPS):
        lanes = columns(g, LANES)
        value_lanes = slice(width + g * LANES, width + (g + 1) * LANES)
        queries = stack_heads(q2[here, lanes], mask)
        grads = stack_heads(do2[here, lanes], mask)
        probs = p2[0, g]
        dp = dot_nt(grads, kv[0, :, value_lanes])
        wide = probs.astype(F32)
        row_sum = jnp.sum(wide * dp, axis=-1, keepdims=True)
        dz = (wide * (dp - row_sum)).astype(BF)
        dkv[0, :, value_lanes] = dot_tn(probs, grads).astype(BF)
        dkv[0, :, lanes] = (dot_tn(dz, queries) * SCALE).astype(BF)
        dq2[here, lanes] = (merge_heads(dot(dz, kv[0, :, lanes]), mask) * SCALE).astype(BF)
    back = dot_nt(dkv[0, :, :width], weight[1]) + dot_nt(dkv[0, :, width:], weight[2])
    for d, out in enumerate(out_mem):
        out[0] = back[d * slots : (d + 1) * slots].astype(BF)

    @pl.when(e == examples - 1)
    def _():
        hat, scale = normalise(x1[...])
        back, gain_grad, shift_grad = norm_back(
            dot_nt(dq2[...], weight[0]), vec[2:3, :], hat, scale
        )
        gx1[...] = gx2[...] + back
        vecs[0:1, :] = gain_grad
        vecs[1:2, :] = shift_grad


def cross_grads(where, gx2, a2, o2, dq2, dkv, pieces, near, far, theirs, grad, memory, sems):
    rows, width = gx2.shape
    examples, total, _ = memory.shape
    slots = total // len(pieces)
    copies = Copies(sems)
    loads = [
        copies.start(piece, memory.at[:, d * slots : (d + 1) * slots, :])
        for d, piece in enumerate(pieces)
    ]
    grad[0] = dot_tn(a2[...], dq2[...]).astype(BF)
    grad[3] = dot_tn(o2[...], gx2[...].astype(BF)).astype(BF)
    wait_all(loads)
    flat = memory[...].reshape(examples * total, width)
    for j in range(2):
        part = dkv[:, :, columns(j, width)].reshape(examples * total, width)
        grad[1 + j] = dot_tn(flat, part).astype(BF)
    wait_all(store_grad(where, grad, False, near, far, theirs, Copies(sems)))


def self_backward(
    group, where, suffix, vec, gx1, a1, qkv, p1, o1, weights, suffix_grad, vecs,
    near, far, theirs, weight, start, grad, dqkv, do1, sems,
):
    rows, width = gx1.shape
    copies = Copies(sems)
    start_copy = my_examples(where, suffix, start, copies)
    loads = load_weight(where, weight, False, weights, copies)
    gs = gx1[...].astype(BF)
    grad[3] = dot_tn(o1[...], gs).astype(BF)
    wait_all(loads)
    do1[...] = dot_nt(gs, weight[3]).astype(BF)
    mask = head_mask(group)
    for r in range(rows // group):
        here = columns(r, group)
        for g in range(GROUPS):
            lanes = [slice(i * width + g * LANES, i * width + (g + 1) * LANES) for i in range(3)]
            queries = stack_heads(qkv[here, lanes[0]], mask)
            grads = stack_heads(do1[here, lanes[0]], mask)
            probs = p1[r * GROUPS + g]
            dp = dot_nt(grads, qkv[here, lanes[2]])
            wide = probs.astype(F32)
            row_sum = jnp.sum(wide * dp, axis=-1, keepdims=True)
            dz = (wide * (dp - row_sum)).astype(BF)
            dqkv[here, lanes[2]] = dot_tn(probs, grads).astype(BF)
            dqkv[here, lanes[1]] = (dot_tn(dz, queries) * SCALE).astype(BF)
            dq = merge_heads(dot(dz, qkv[here, lanes[1]]), mask) * SCALE
            dqkv[here, lanes[0]] = dq.astype(BF)
    for j in range(3):
        grad[j] = dot_tn(a1[...], dqkv[:, columns(j, width)]).astype(BF)
    start_copy.wait()
    started = store_grad(where, grad, False, near, far, theirs, Copies(sems))
    da1 = dot_nt(dqkv[:, columns(0, width)], weight[0])
    for j in range(1, 3):
        da1 = da1 + dot_nt(dqkv[:, columns(j, width)], weight[j])
    hat, scale = normalise(start[...].reshape(rows, width).astype(F32))
    back, gain_grad, shift_grad = norm_back(da1, vec[0:1, :], hat, scale)
    suffix_grad[...] = (gx1[...] + back).astype(BF).reshape(suffix_grad.shape)
    vecs[0:1, :] = gain_grad
    vecs[1:2, :] = shift_grad
    wait_all(started)


def run(kernel, inputs, outputs, scratch, copies, grid=()):
    def leaf(x):
        return isinstance(x, tuple) and len(x) == 2 and isinstance(x[0], pl.BlockSpec)

    flat_in, tree_in = jax.tree.flatten(inputs, is_leaf=leaf)
    flat_out, tree_out = jax.tree.flatten(outputs, is_leaf=leaf)

    def body(*refs):
        first, second = len(flat_in), len(flat_in) + len(flat_out)
        given = jax.tree.unflatten(tree_in, refs[:first])
        taken = jax.tree.unflatten(tree_out, refs[first:second])
        kernel(*given, *taken, *refs[second:])

    found = pl.pallas_call(
        body,
        grid=grid,
        in_specs=[spec for spec, _ in flat_in],
        out_specs=[spec for spec, _ in flat_out],
        out_shape=[shape for _, shape in flat_out],
        scratch_shapes=scratch + [pltpu.SemaphoreType.DMA((copies,))],
        compiler_params=pltpu.CompilerParams(vmem_limit_bytes=56 * 1024 * 1024),
        cost_estimate=pl.CostEstimate(
            flops=0, bytes_accessed=0, transcendentals=0
        ),
    )(*[x for _, x in flat_in])
    return jax.tree.unflatten(tree_out, found)


def shape_of(dims, dtype):
    return jax.ShapeDtypeStruct(tuple(dims), dtype)


class Gather:
    def __init__(self, own, half, slow, fast):
        self.own, self.half, self.slow, self.fast = own, half, slow, fast
        self.far_own = self.far_other = self.near = self.far = None

    def send_slow(self, *others):
        half = after(self.half, *others)
        self.came = [swap(half, "fsdp", k * self.fast) for k in range(1, self.slow)]

    def send_fast(self, *others):
        self.near = jnp.stack([after(piece, *others) for piece in self.came])
        self.near_other = swap(self.near, "mem", 1)
        self.far = [swap(self.near, "fsdp", b) for b in range(1, self.fast)]

    def whole(self):
        far_other = [swap(piece, "mem", 1) for piece in self.far]
        mine, theirs = [self.near], [self.near_other]
        for b in range(self.fast - 1):
            mine += [self.far_own[b], self.far[b]]
            theirs += [self.far_other[b], far_other[b]]
        return [[(ANY, x) for x in some] for some in (self.own, mine, theirs)]


class Scatter:
    def __init__(self, grads, slow, fast, *others):
        self.near, self.far, theirs = grads
        self.slow, self.fast = slow, fast
        self.sent = swap(after(theirs, *others), "mem", 1)

    def add_cores(self):
        self.out = [
            (self.far[b].astype(F32) + self.sent[b + 1].astype(F32)).astype(BF)
            for b in range(self.fast - 1)
        ]
        return self.out

    def send_fast(self, link):
        self.came = [link.swap(part, "fsdp", b + 1) for b, part in enumerate(self.out)]

    def add_fast(self, *others):
        total = after(self.near, *others).astype(F32) + self.sent[0].astype(F32)
        for part in self.came:
            total = total + part.astype(F32)
        self.total = total.astype(BF)
        return self.total

    def send_slow(self, link):
        self.came = [
            link.swap(self.total[k], "fsdp", k * self.fast) for k in range(1, self.slow)
        ]

    def add_slow(self, *others):
        final = after(self.total, *others)[0].astype(F32)
        for part in self.came:
            final = final + part.astype(F32)
        return final


def add_replicas(value, across, c):
    k = 1
    while 2 * k < across:
        low = value.astype(BF)
        value = low.astype(F32) + swap(low, "mem", 2 * k).astype(F32)
        k *= 2
    low = value.astype(BF)
    halves = [low, swap(low, "mem", 2 * k)] if across > 1 else [low]
    others = [swap(half, "mem", 1) for half in halves]
    mine = sum(half.astype(F32) for half in halves)
    other = sum(half.astype(F32) for half in others)
    first = jnp.where(c == 0, mine, other)
    second = jnp.where(c == 0, other, mine)
    return [
        [first[2 * i], first[2 * i + 1], second[2 * i], second[2 * i + 1]] for i in range(2)
    ]


def add_everywhere(value):
    for axis in ("mem", "fsdp"):
        k = 1
        while k < lax.axis_size(axis):
            value = value + swap(value, axis, k)
            k *= 2
    return value


def spread_rows(value, m, across):
    examples = value.shape[0]
    out = jnp.zeros((2 * across * examples,) + value.shape[1:], value.dtype)
    blocks = {0: value}
    for k in range(1, across):
        blocks[2 * k] = swap(value, "mem", 2 * k)
    for k in range(across):
        blocks[2 * k + 1] = swap(blocks[2 * k], "mem", 1)
    for d, piece in blocks.items():
        out = lax.dynamic_update_slice_in_dim(out, piece, (m ^ d) * examples, 0)
    return out


def per_device(
    suffix,
    memory,
    counts,
    cotangent,
    self_norm_gain,
    self_norm_bias,
    self_query,
    self_key,
    self_value,
    self_output,
    cross_norm_gain,
    cross_norm_bias,
    cross_query,
    cross_key,
    cross_value,
    cross_output,
    dense_norm_gain,
    dense_norm_bias,
    dense_in,
    dense_in_bias,
    dense_out,
    dense_out_bias,
):
    f = lax.axis_index("fsdp")
    m = lax.axis_index("mem")
    c = m % 2
    fsdp = lax.axis_size("fsdp")
    mem = lax.axis_size("mem")
    across = mem // 2
    slow, fast = fsdp_split(fsdp)
    SHARDS[0] = fsdp
    where = jnp.stack([f // fast, f % fast, c, m]).astype(jnp.int32)
    examples = suffix.shape[0] // mem
    length = suffix.shape[1]
    width = suffix.shape[2]
    slots = memory.shape[1]
    total = mem * slots
    rows = examples * length
    inner = dense_in.shape[1]
    part = width // fsdp
    group = min(128, rows)
    blocks = 2 * fsdp + 4

    def gather(own, matrices):
        half = jnp.where(c == 0, jnp.stack(matrices[:2]), jnp.stack(matrices[2:]))
        return Gather(own, half, slow, fast)

    self_matrices = [self_query, self_key, self_value, self_output]
    cross_matrices = [cross_query, cross_key, cross_value, cross_output]
    self_gather = gather(self_matrices, self_matrices)
    cross_gather = gather(cross_matrices, cross_matrices)
    in_gather = gather([dense_in], [dense_in[:, columns(j, width)] for j in range(4)])
    out_gather = gather([dense_out], [dense_out[columns(j, part)] for j in range(4)])
    gathers = [self_gather, cross_gather, in_gather, out_gather]
    small = jnp.concatenate(
        [
            self_norm_gain,
            self_norm_bias,
            cross_norm_gain,
            cross_norm_bias,
            dense_norm_gain,
            dense_norm_bias,
            dense_out_bias,
            dense_in_bias,
        ]
    )[None]
    halves = jnp.stack([one.half for one in gathers])
    near_small = jnp.concatenate([small] + [swap(small, "fsdp", b) for b in range(1, fast)])
    far_own = [swap(halves, "fsdp", b) for b in range(1, fast)]

    def of_device(value, index):
        return lax.dynamic_slice_in_dim(value, index * examples, examples, 0)

    pieces = [of_device(memory, m)]
    for d in range(1, mem):
        pieces.append(swap(of_device(memory, m ^ d), "mem", d))

    self_gather.send_slow()
    sent = [*self_gather.came, *far_own, near_small]
    self_gather.send_fast(*sent)
    cross_gather.send_slow(*sent)
    far_other = [swap(after(piece, *sent), "mem", 1) for piece in far_own]
    for i, one in enumerate(gathers):
        one.far_own = [piece[i] for piece in far_own]
        one.far_other = [piece[i] for piece in far_other]
    near_small = after(near_small, *sent)
    small = jnp.concatenate(
        [near_small] + [swap(near_small, "fsdp", k * fast) for k in range(1, slow)]
    )
    small = jnp.take(small, jnp.arange(fsdp) ^ f, axis=0).astype(F32)
    vec = small[:, : 7 * part].reshape(fsdp, 7, part).transpose(1, 0, 2).reshape(7, width)
    bias_in = small[:, 7 * part :].reshape(1, inner)
    sent = [*self_gather.far, *cross_gather.came, *pieces[1:], vec]
    self_gather.far = [after(piece, *sent) for piece in self_gather.far]
    self_weights = self_gather.whole()
    cross_gather.send_fast(*self_gather.far)
    in_gather.send_slow(*self_gather.far)

    half = (2, part, width)
    grads_like = [
        (ANY, shape_of((slow,) + half, BF)),
        (ANY, shape_of((fast - 1, slow) + half, BF)),
        (ANY, shape_of((fast, slow) + half, BF)),
    ]

    def flat(dims, dtype):
        return (VMEM, shape_of(dims, dtype))

    def per_example(value):
        dims = value.shape[1:]
        spec = pl.BlockSpec((1,) + dims, lambda e: (e,) + (0,) * len(dims))
        return (spec, value)

    def scratch(*dims):
        return pltpu.VMEM(dims, BF)

    def scatter(grads, *others):
        return Scatter(grads, slow, fast, *others)

    wide = (rows, width)
    square = scratch(4, width, width)
    own_rows = scratch(examples, length, width)
    x1, a1, qkv, p1, o1 = run(
        functools.partial(self_forward, group),
        [(SMEM, where), (ANY, suffix), (VMEM, vec), self_weights],
        [
            flat(wide, F32),
            flat(wide, BF),
            flat((rows, 3 * width), BF),
            flat((rows // group * GROUPS, TOGETHER * group, group), BF),
            flat(wide, BF),
        ],
        [square, own_rows],
        1 + blocks,
    )
    cross_gather.far = [after(piece, x1, *in_gather.came) for piece in cross_gather.far]
    cross_weights = cross_gather.whole()
    in_gather.send_fast(*cross_gather.far)
    out_gather.send_slow(*cross_gather.far)
    x2, a2, q2, kv, p2, o2 = run(
        cross_forward,
        [(SMEM, where), (SMEM, counts), (VMEM, x1), (VMEM, vec)]
        + [[per_example(piece) for piece in pieces], cross_weights],
        [
            flat(wide, F32),
            flat(wide, BF),
            flat(wide, BF),
            per_example(shape_of((examples, total, 2 * width), BF)),
            per_example(shape_of((examples, GROUPS, TOGETHER * length, total), BF)),
            flat(wide, BF),
        ],
        [square],
        blocks,
        (examples,),
    )
    in_gather.far = [after(piece, x2, *out_gather.came) for piece in in_gather.far]
    in_weights = in_gather.whole()
    out_gather.send_fast(*in_gather.far)
    a3, h, slope, *grads = run(
        dense_inner,
        [(SMEM, where), (VMEM, x2), (VMEM, vec), (VMEM, bias_in), (ANY, cotangent), in_weights],
        [flat(wide, BF), flat((rows, inner), BF), flat((rows, inner), BF)] + grads_like,
        [square, scratch(fsdp, 4, part, width), own_rows],
        1 + blocks,
    )
    link_fast, link_slow = Link(2), Link(3)
    out_gather.far = [after(piece, a3) for piece in out_gather.far]
    out_weights = out_gather.whole()
    out_scatter = scatter(grads, *out_gather.far)
    out_sum = out_scatter.add_cores()
    out_scatter.send_fast(link_fast)
    y, du, vecs_y, bias_grad, *grads = run(
        dense_outer,
        [(SMEM, where), (VMEM, after(x2, *out_sum)), (VMEM, vec), (VMEM, a3), (VMEM, h)]
        + [(VMEM, slope), (ANY, cotangent), out_weights],
        [
            flat((examples, length, width), BF),
            flat((rows, inner), BF),
            flat((1, width), F32),
            flat((1, inner), F32),
        ]
        + grads_like,
        [scratch(fsdp, 4, part, width), square, own_rows],
        1 + blocks,
    )
    in_grads = grads
    gx2, vecs_dense = run(
        dense_back,
        [(SMEM, where), (VMEM, x2), (VMEM, vec), (VMEM, du), (ANY, cotangent), in_weights],
        [flat(wide, F32), flat((2, width), F32)],
        [square, own_rows],
        1 + blocks,
    )
    out_total = out_scatter.add_fast(gx2)
    out_scatter.send_slow(link_slow)
    in_scatter = scatter(in_grads, out_total)
    in_sum = in_scatter.add_cores()
    in_scatter.send_fast(link_fast)
    gx1, vecs_cross, dkv, dq2, mem_pieces = run(
        cross_backward,
        [(SMEM, where), (VMEM, x1), (VMEM, vec), (VMEM, after(gx2, out_total, *in_sum)), (VMEM, q2)]
        + [per_example(kv), per_example(p2), cross_weights],
        [
            flat(wide, F32),
            flat((2, width), F32),
            per_example(shape_of((examples, total, 2 * width), BF)),
            flat(wide, BF),
            [per_example(shape_of((examples, slots, width), BF))] * mem,
        ],
        [square, scratch(*wide)],
        blocks,
        (examples,),
    )
    out_final = out_scatter.add_slow(gx1)
    grads = run(
        cross_grads,
        [(SMEM, where), (VMEM, after(gx2, out_final)), (VMEM, a2), (VMEM, o2), (VMEM, dq2)]
        + [(VMEM, dkv), [(ANY, piece) for piece in pieces]],
        grads_like,
        [square, scratch(examples, total, width)],
        max(mem, blocks),
    )
    in_total = in_scatter.add_fast()
    in_scatter.send_slow(link_slow)
    cross_scatter = scatter(grads, in_total)
    cross_sum = cross_scatter.add_cores()
    cross_scatter.send_fast(link_fast)
    gx1 = after(gx1, *cross_sum)
    suffix_part, vecs_self, *grads = run(
        functools.partial(self_backward, group),
        [(SMEM, where), (ANY, suffix), (VMEM, vec), (VMEM, gx1), (VMEM, a1)]
        + [(VMEM, qkv), (VMEM, p1), (VMEM, o1), self_weights],
        [flat((examples, length, width), BF), flat((2, width), F32)] + grads_like,
        [square, own_rows, square, scratch(rows, 3 * width), scratch(*wide)],
        1 + blocks,
    )
    cross_total = cross_scatter.add_fast(suffix_part)
    cross_scatter.send_slow(link_slow)
    in_final = in_scatter.add_slow(suffix_part)
    self_scatter = scatter(grads, cross_total, in_final)
    self_sum = self_scatter.add_cores()
    self_scatter.send_fast(link_fast)
    self_total = self_scatter.add_fast()
    self_scatter.send_slow(link_slow)
    mem_pieces = [after(mem_pieces[0], self_total)] + [
        after(swap(mem_pieces[d], "mem", d), self_total) for d in range(1, mem)
    ]
    suffix_part, vecs_self = after(suffix_part, self_total), after(vecs_self, self_total)

    def finish(*some):
        return add_replicas(jnp.concatenate(some), across, c)

    block_output = after(spread_rows(y, m, across), self_total)
    grad_out, grad_in = finish(after(out_final, self_total), in_final)
    grad_out = jnp.concatenate(grad_out, axis=0)
    grad_in = jnp.concatenate(grad_in, axis=1)
    memory_grad = jnp.zeros_like(memory)
    for d in range(mem):
        memory_grad = lax.dynamic_update_slice_in_dim(
            memory_grad, mem_pieces[d], (m ^ d) * examples, 0
        )
    suffix_grad = spread_rows(suffix_part, m, across)
    vectors = jnp.concatenate(
        [vecs_self, vecs_cross, vecs_dense, vecs_y, bias_grad.reshape(-1, width)]
    )
    vectors = add_everywhere(vectors)
    grad_cross, grad_self = finish(cross_scatter.add_slow(), self_scatter.add_slow())

    def vector(i):
        return lax.dynamic_slice(vectors, (i, f * part), (1, part)).reshape(part)

    return (
        block_output,
        suffix_grad,
        memory_grad,
        vector(0),
        vector(1),
        *grad_self,
        vector(2),
        vector(3),
        *grad_cross,
        vector(4),
        vector(5),
        grad_in,
        lax.dynamic_slice_in_dim(vectors[7:].reshape(-1), f * (inner // fsdp), inner // fsdp, 0),
        grad_out,
        vector(6),
    )


def solution(mesh):
    rows = P("fsdp", None, None)
    matrix = P("fsdp", None)
    vector = P("fsdp")
    attention = (vector, vector, matrix, matrix, matrix, matrix)
    params = attention + attention + (vector, vector, matrix, vector, matrix, vector)
    return jax.shard_map(
        per_device,
        mesh=mesh,
        in_specs=(rows, P("fsdp", "mem", None), vector, rows) + params,
        out_specs=(rows, rows, P("fsdp", "mem", None)) + params,
        check_vma=False,
    )
```

```python
import functools

import jax
import jax.numpy as jnp
from jax import lax
from jax.experimental import pallas as pl
from jax.experimental.pallas import tpu as pltpu
from jax.sharding import PartitionSpec as P

HEADS = 12
HEAD = 64
TOGETHER = 4
GROUPS = HEADS // TOGETHER
LANES = TOGETHER * HEAD
SCALE = HEAD ** (-0.5)
BF = jnp.bfloat16
F32 = jnp.float32
ANY = pl.BlockSpec(memory_space=pl.ANY)
SMEM = pl.BlockSpec(memory_space=pltpu.SMEM)
VMEM = pl.BlockSpec(memory_space=pltpu.VMEM)


def swap(value, axis, distance):
    size = lax.axis_size(axis)
    return lax.ppermute(value, axis, [(i, i ^ distance) for i in range(size)])


def after(value, *others):
    return lax.optimization_barrier((value, *others))[0] if others else value


def fsdp_split(size):
    slow = 4 if size % 4 == 0 else 1
    return slow, size // slow


def dot(left, right):
    return jnp.dot(left, right, preferred_element_type=F32)


def dot_nt(left, right):
    return lax.dot_general(left, right, (((1,), (1,)), ((), ())), preferred_element_type=F32)


def dot_tn(left, right):
    return lax.dot_general(left, right, (((0,), (0,)), ((), ())), preferred_element_type=F32)


def rows_of(start, size):
    return pl.ds(pl.multiple_of(start, 16), size)


def block(ref, by_rows, shard, which):
    if by_rows:
        return ref.at[shard, pl.ds(which * 2, 2)]
    rows = ref.shape[1] // SHARDS[0]
    return ref.at[pl.ds(which * 2, 2), rows_of(shard * rows, rows)]


SHARDS = [0]


class Copies:
    def __init__(self, sems):
        self.sems = sems
        self.next = 0

    def start(self, source, target):
        copy = pltpu.make_async_copy(source, target, self.sems.at[self.next])
        self.next += 1
        copy.start()
        return copy


def wait_all(copies):
    for copy in copies:
        copy.wait()


def load_weight(where, whole, by_rows, weights, copies):
    index, own, mine, theirs = weights
    z, y, c = where[0], where[1], where[2]
    slow = mine[0].shape[0] + 1
    fast = (len(mine) + 1) // 2
    me = z * fast + y
    started = []
    rows = mine[0].shape[2]
    if by_rows:
        for j in range(4):
            started.append(copies.start(own[0].at[pl.ds(j * rows, rows)], whole.at[me, j]))
    else:
        for j in range(4):
            if len(own) == 4:
                source = own[j]
            else:
                source = own[0].at[:, pl.ds(j * whole.shape[2], whole.shape[2])]
            started.append(copies.start(source, whole.at[j, rows_of(me * rows, rows)]))
    for which, pieces in ((c, mine), (1 - c, theirs)):
        for k in range(1, slow):
            shard = (z ^ k) * fast + y
            started.append(
                copies.start(pieces[0].at[k - 1], block(whole, by_rows, shard, which))
            )
        for b in range(1, fast):
            for k in range(slow):
                shard = (z ^ k) * fast + (y ^ b)
                piece = pieces[2 * b].at[k - 1] if k else pieces[2 * b - 1].at[index]
                started.append(copies.start(piece, block(whole, by_rows, shard, which)))
    return started


def store_grad(where, whole, by_rows, near, far, theirs, copies):
    z, y, c = where[0], where[1], where[2]
    fast, slow = theirs.shape[0], theirs.shape[1]
    started = []
    for b in range(fast):
        for k in range(slow):
            shard = (z ^ k) * fast + (y ^ b)
            mine = far.at[b - 1, k] if b else near.at[k]
            started.append(copies.start(block(whole, by_rows, shard, 1 - c), theirs.at[b, k]))
            started.append(copies.start(block(whole, by_rows, shard, c), mine))
    return started


def my_examples(where, source, target, copies):
    count = target.shape[0]
    return copies.start(source.at[pl.ds(where[3] * count, count)], target)


def normalise(values):
    centred = values - jnp.mean(values, axis=-1, keepdims=True)
    scale = lax.rsqrt(jnp.mean(centred * centred, axis=-1, keepdims=True) + 1e-06)
    return centred * scale, scale


def norm_back(grad, gain, hat, scale):
    inner = grad * gain
    mean = jnp.mean(inner, axis=-1, keepdims=True)
    along = jnp.mean(inner * hat, axis=-1, keepdims=True)
    return (
        scale * (inner - mean - hat * along),
        jnp.sum(grad * hat, axis=0, keepdims=True),
        jnp.sum(grad, axis=0, keepdims=True),
    )


def head_mask(rows):
    shape = (TOGETHER * rows, LANES)
    row = lax.broadcasted_iota(jnp.int32, shape, 0) // rows
    lane = lax.broadcasted_iota(jnp.int32, shape, 1) // HEAD
    return (row == lane).astype(F32)


def stack_heads(value, mask):
    return (jnp.concatenate([value] * TOGETHER, axis=0).astype(F32) * mask).astype(BF)


def merge_heads(value, mask):
    rows = value.shape[0] // TOGETHER
    value = value * mask
    total = value[:rows]
    for h in range(1, TOGETHER):
        total = total + value[h * rows : (h + 1) * rows]
    return total


def columns(j, width):
    return slice(j * width, (j + 1) * width)


def self_forward(group, where, suffix, vec, weights, x1, a1, qkv, p1, o1, weight, start, sems):
    rows, width = x1.shape
    copies = Copies(sems)
    first = my_examples(where, suffix, start, copies)
    loads = load_weight(where, weight, False, weights, copies)
    first.wait()
    values = start[...].reshape(rows, width).astype(F32)
    hat, _ = normalise(values)
    a1[...] = (hat * vec[0:1, :] + vec[1:2, :]).astype(BF)
    wait_all(loads)
    for j in range(3):
        qkv[:, columns(j, width)] = dot(a1[...], weight[j]).astype(BF)
    mask = head_mask(group)
    length = suffix.shape[1]
    shape = (TOGETHER * group, group)
    row = lax.broadcasted_iota(jnp.int32, shape, 0) % group
    col = lax.broadcasted_iota(jnp.int32, shape, 1)
    seen = (row // length == col // length) & (row >= col)
    for r in range(rows // group):
        here = columns(r, group)
        for g in range(GROUPS):
            lanes = [slice(i * width + g * LANES, i * width + (g + 1) * LANES) for i in range(3)]
            queries = stack_heads(qkv[here, lanes[0]], mask)
            scores = dot_nt(queries, qkv[here, lanes[1]]) * SCALE
            scores = jnp.where(seen, scores, -1e30)
            powers = jnp.exp(scores - jnp.max(scores, axis=-1, keepdims=True))
            probs = (powers / jnp.sum(powers, axis=-1, keepdims=True)).astype(BF)
            p1[r * GROUPS + g] = probs
            found = dot(probs, qkv[here, lanes[2]])
            o1[here, lanes[0]] = merge_heads(found, mask).astype(BF)
    x1[...] = values + dot(o1[...], weight[3])


def cross_forward(
    where, counts, x1, vec, memory, weights, x2, a2, q2, kv, p2, o2, weight, sems
):
    rows, width = x1.shape
    examples = pl.num_programs(0)
    e = pl.program_id(0)
    total = kv.shape[1]
    length = p2.shape[2] // TOGETHER

    @pl.when(e == 0)
    def _():
        loads = load_weight(where, weight, False, weights, Copies(sems))
        hat, _ = normalise(x1[...])
        a2[...] = (hat * vec[2:3, :] + vec[3:4, :]).astype(BF)
        wait_all(loads)
        q2[...] = dot(a2[...], weight[0]).astype(BF)

    tokens = memory[...].reshape(total, width)
    for j in range(2):
        kv[0, :, columns(j, width)] = dot(tokens, weight[1 + j]).astype(BF)
    mask = head_mask(length)
    position = lax.broadcasted_iota(jnp.int32, (1, total), 1)
    valid = position < counts[where[3] * examples + e]
    here = rows_of(e * length, length)
    probs = []
    for g in range(GROUPS):
        lanes = columns(g, LANES)
        queries = stack_heads(q2[here, lanes], mask)
        scores = dot_nt(queries, kv[0, :, lanes]) * SCALE
        scores = jnp.where(valid, scores, -1e30)
        top = jnp.maximum(jnp.max(scores, axis=-1, keepdims=True), 0.0)
        powers = jnp.exp(scores - top)
        weight_sum = jnp.sum(powers, axis=-1, keepdims=True) + jnp.exp(-top)
        probs.append((powers / weight_sum).astype(BF))
    for g in range(GROUPS):
        p2[0, g] = probs[g]
        found = dot(probs[g], kv[0, :, width + g * LANES : width + (g + 1) * LANES])
        o2[here, columns(g, LANES)] = merge_heads(found, mask).astype(BF)

    @pl.when(e == examples - 1)
    def _():
        x2[...] = x1[...] + dot(o2[...], weight[3])


def dense_inner(
    where, x2, vec, bias, cotangent, weights, a3, h, slope, near, far, theirs,
    weight, grad, cot, sems,
):
    rows, width = x2.shape
    copies = Copies(sems)
    cot_copy = my_examples(where, cotangent, cot, copies)
    loads = load_weight(where, weight, False, weights, copies)
    hat, _ = normalise(x2[...])
    a3[...] = (hat * vec[4:5, :] + vec[5:6, :]).astype(BF)
    cot_copy.wait()
    gy = cot[...].reshape(rows, width)
    wait_all(loads)
    flat = grad.shape[0] * grad.shape[1] * grad.shape[2]
    step = flat // grad.shape[0]
    for j in range(4):
        for half in range(2):
            cols = slice(j * width + half * 384, j * width + (half + 1) * 384)
            u = dot(a3[...], weight[j, :, half * 384 : (half + 1) * 384]) + bias[:, cols]
            square = u * u
            t = jnp.tanh(0.7978845608 * u * (1.0 + 0.044715 * square))
            h[:, cols] = (0.5 * u * (1.0 + t)).astype(BF)
            slope[:, cols] = (
                0.5 * (1.0 + t)
                + (0.5 * 0.7978845608) * u * (1.0 - t * t) * (1.0 + (3.0 * 0.044715) * square)
            ).astype(BF)
            part = dot_tn(h[:, cols], gy).astype(BF)
            per = 384 // step
            grad[cols.start // step : cols.start // step + per] = part.reshape(
                (per,) + grad.shape[1:]
            )
    wait_all(store_grad(where, grad, True, near, far, theirs, Copies(sems)))


def dense_outer(
    where, x2, vec, a3, h, slope, cotangent, weights, y, du, vecs, bias_grad, near, far, theirs,
    weight, grad, cot, sems,
):
    rows, width = x2.shape
    copies = Copies(sems)
    cot_copy = my_examples(where, cotangent, cot, copies)
    wait_all(load_weight(where, weight, True, weights, copies))
    cot_copy.wait()
    gy = cot[...].reshape(rows, width)
    shards = weight.shape[0]
    step = weight.shape[1] * weight.shape[2]
    whole = weight[...].reshape(shards * step, width)
    for j in range(4):
        cols = columns(j, width)
        low = (dot_nt(gy, whole[cols]) * slope[:, cols].astype(F32)).astype(BF)
        du[:, cols] = low
        bias_grad[:, cols] = jnp.sum(low.astype(F32), axis=0, keepdims=True)
        grad[j] = dot_tn(a3[...], low).astype(BF)
    started = store_grad(where, grad, False, near, far, theirs, Copies(sems))
    result = x2[...] + dot(h[...], whole) + vec[6:7, :]
    y[...] = result.astype(BF).reshape(y.shape)
    vecs[...] = jnp.sum(gy.astype(F32), axis=0, keepdims=True)
    wait_all(started)


def dense_back(where, x2, vec, du, cotangent, weights, gx2, vecs, weight, cot, sems):
    rows, width = x2.shape
    copies = Copies(sems)
    cot_copy = my_examples(where, cotangent, cot, copies)
    loads = load_weight(where, weight, False, weights, copies)
    hat, scale = normalise(x2[...])
    cot_copy.wait()
    wait_all(loads)
    da3 = dot_nt(du[:, columns(0, width)], weight[0])
    for j in range(1, 4):
        da3 = da3 + dot_nt(du[:, columns(j, width)], weight[j])
    back, gain_grad, shift_grad = norm_back(da3, vec[4:5, :], hat, scale)
    gx2[...] = cot[...].reshape(rows, width).astype(F32) + back
    vecs[0:1, :] = gain_grad
    vecs[1:2, :] = shift_grad


def cross_backward(
    where, x1, vec, gx2, q2, kv, p2, weights, gx1, vecs, dkv, dq2, out_mem, weight, do2, sems
):
    rows, width = x1.shape
    examples = pl.num_programs(0)
    e = pl.program_id(0)
    length = p2.shape[2] // TOGETHER

    @pl.when(e == 0)
    def _():
        wait_all(load_weight(where, weight, False, weights, Copies(sems)))
        do2[...] = dot_nt(gx2[...].astype(BF), weight[3]).astype(BF)

    mask = head_mask(length)
    here = rows_of(e * length, length)
    for g in range(GROUPS):
        lanes = columns(g, LANES)
        value_lanes = slice(width + g * LANES, width + (g + 1) * LANES)
        queries = stack_heads(q2[here, lanes], mask)
        grads = stack_heads(do2[here, lanes], mask)
        probs = p2[0, g]
        dp = dot_nt(grads, kv[0, :, value_lanes])
        wide = probs.astype(F32)
        row_sum = jnp.sum(wide * dp, axis=-1, keepdims=True)
        dz = (wide * (dp - row_sum)).astype(BF)
        dkv[0, :, value_lanes] = dot_tn(probs, grads).astype(BF)
        dkv[0, :, lanes] = (dot_tn(dz, queries) * SCALE).astype(BF)
        dq2[here, lanes] = (merge_heads(dot(dz, kv[0, :, lanes]), mask) * SCALE).astype(BF)
    back = dot_nt(dkv[0, :, :width], weight[1]) + dot_nt(dkv[0, :, width:], weight[2])
    out_mem[...] = back.astype(BF).reshape(out_mem.shape)

    @pl.when(e == examples - 1)
    def _():
        hat, scale = normalise(x1[...])
        back, gain_grad, shift_grad = norm_back(
            dot_nt(dq2[...], weight[0]), vec[2:3, :], hat, scale
        )
        gx1[...] = gx2[...] + back
        vecs[0:1, :] = gain_grad
        vecs[1:2, :] = shift_grad


def cross_grads(
    where, gx2, a2, o2, dq2, dkv, all_memory, near, far, theirs, grad, memory, sems
):
    rows, width = gx2.shape
    examples, total, _ = memory.shape
    mem, _, slots, _ = all_memory.shape
    copies = Copies(sems)
    loads = [
        copies.start(all_memory.at[d], memory.at[:, d * slots : (d + 1) * slots, :])
        for d in range(mem)
    ]
    grad[0] = dot_tn(a2[...], dq2[...]).astype(BF)
    grad[3] = dot_tn(o2[...], gx2[...].astype(BF)).astype(BF)
    wait_all(loads)
    flat = memory[...].reshape(examples * total, width)
    for j in range(2):
        part = dkv[:, :, columns(j, width)].reshape(examples * total, width)
        grad[1 + j] = dot_tn(flat, part).astype(BF)
    wait_all(store_grad(where, grad, False, near, far, theirs, Copies(sems)))


def self_backward(
    group, where, suffix, vec, gx1, a1, qkv, p1, o1, parts, weights, suffix_grad, vecs,
    near, far, theirs, weight, start, grad, dqkv, do1, sems,
):
    rows, width = gx1.shape
    copies = Copies(sems)
    start_copy = my_examples(where, suffix, start, copies)
    loads = load_weight(where, weight, False, weights, copies)
    gs = gx1[...].astype(BF)
    grad[3] = dot_tn(o1[...], gs).astype(BF)
    wait_all(loads)
    do1[...] = dot_nt(gs, weight[3]).astype(BF)
    mask = head_mask(group)
    for r in range(rows // group):
        here = columns(r, group)
        for g in range(GROUPS):
            lanes = [slice(i * width + g * LANES, i * width + (g + 1) * LANES) for i in range(3)]
            queries = stack_heads(qkv[here, lanes[0]], mask)
            grads = stack_heads(do1[here, lanes[0]], mask)
            probs = p1[r * GROUPS + g]
            dp = dot_nt(grads, qkv[here, lanes[2]])
            wide = probs.astype(F32)
            row_sum = jnp.sum(wide * dp, axis=-1, keepdims=True)
            dz = (wide * (dp - row_sum)).astype(BF)
            dqkv[here, lanes[2]] = dot_tn(probs, grads).astype(BF)
            dqkv[here, lanes[1]] = (dot_tn(dz, queries) * SCALE).astype(BF)
            dq = merge_heads(dot(dz, qkv[here, lanes[1]]), mask) * SCALE
            dqkv[here, lanes[0]] = dq.astype(BF)
    for j in range(3):
        grad[j] = dot_tn(a1[...], dqkv[:, columns(j, width)]).astype(BF)
    start_copy.wait()
    started = store_grad(where, grad, False, near, far, theirs, Copies(sems))
    da1 = dot_nt(dqkv[:, columns(0, width)], weight[0])
    for j in range(1, 3):
        da1 = da1 + dot_nt(dqkv[:, columns(j, width)], weight[j])
    hat, scale = normalise(start[...].reshape(rows, width).astype(F32))
    back, gain_grad, shift_grad = norm_back(da1, vec[0:1, :], hat, scale)
    suffix_grad[...] = (gx1[...] + back).astype(BF).reshape(suffix_grad.shape)
    found = [gain_grad, shift_grad]
    for ref in parts:
        for r in range(ref.shape[0]):
            found += [ref[r : r + 1, columns(j, width)] for j in range(ref.shape[1] // width)]
    found.append(jnp.zeros((vecs.shape[0] - len(found), width), F32))
    vecs[...] = jnp.concatenate(found, axis=0).astype(BF)
    wait_all(started)


def run(kernel, inputs, outputs, scratch, copies, grid=()):
    def leaf(x):
        return isinstance(x, tuple) and len(x) == 2 and isinstance(x[0], pl.BlockSpec)

    flat_in, tree_in = jax.tree.flatten(inputs, is_leaf=leaf)
    fixed = {i: x for i, x in enumerate(flat_in) if isinstance(x, int)}
    flat_in = [x for x in flat_in if not isinstance(x, int)]
    flat_out, tree_out = jax.tree.flatten(outputs, is_leaf=leaf)

    def body(*refs):
        first, second = len(flat_in), len(flat_in) + len(flat_out)
        leaves = list(refs[:first])
        for i, x in fixed.items():
            leaves.insert(i, x)
        given = jax.tree.unflatten(tree_in, leaves)
        taken = jax.tree.unflatten(tree_out, refs[first:second])
        kernel(*given, *taken, *refs[second:])

    found = pl.pallas_call(
        body,
        grid=grid,
        in_specs=[spec for spec, _ in flat_in],
        out_specs=[spec for spec, _ in flat_out],
        out_shape=[shape for _, shape in flat_out],
        scratch_shapes=scratch + [pltpu.SemaphoreType.DMA((copies,))],
        compiler_params=pltpu.CompilerParams(vmem_limit_bytes=56 * 1024 * 1024),
        cost_estimate=pl.CostEstimate(
            flops=0, bytes_accessed=0, transcendentals=0
        ),
    )(*[x for _, x in flat_in])
    return jax.tree.unflatten(tree_out, found)


def shape_of(dims, dtype):
    return jax.ShapeDtypeStruct(tuple(dims), dtype)


class Gather:
    def __init__(self, index, own, half, slow, fast):
        self.index, self.own, self.half, self.slow, self.fast = index, own, half, slow, fast

    def send_slow(self, *others):
        half = after(self.half, *others)
        self.came = [swap(half, "fsdp", k * self.fast) for k in range(1, self.slow)]

    def send_fast(self, *others):
        self.near = jnp.stack([after(piece, *others) for piece in self.came])
        self.near_other = swap(self.near, "mem", 1)
        self.far = [swap(self.near, "fsdp", b) for b in range(1, self.fast)]

    def whole(self):
        far_other = [swap(piece, "mem", 1) for piece in self.far]
        mine, theirs = [self.near], [self.near_other]
        for b in range(self.fast - 1):
            mine += [self.far_own[b], self.far[b]]
            theirs += [self.far_other[b], far_other[b]]
        return [self.index] + [[(ANY, x) for x in some] for some in (self.own, mine, theirs)]


class Scatter:
    def __init__(self, grads, slow, fast, *others, vectors=None):
        self.near, self.far, theirs = grads
        self.slow, self.fast, self.vectors = slow, fast, vectors
        theirs = after(theirs, *others)
        self.unit = theirs.shape[2:]
        if vectors is None:
            self.sent = swap(theirs, "mem", 1)
        else:
            self.sent, came = self.unpack(swap(self.pack(theirs), "mem", 1), theirs.shape)
            self.vectors = vectors.astype(F32) + came

    def pack(self, value):
        if self.vectors is None:
            return value
        width = value.shape[-1]
        return jnp.concatenate([value.reshape(-1, width), self.vectors.astype(BF)])

    def unpack(self, value, shape):
        if self.vectors is None:
            return value, 0.0
        rows = value.shape[0] - self.vectors.shape[0]
        return value[:rows].reshape(shape), value[rows:].astype(F32)

    def add_cores(self):
        self.out = [
            self.pack((self.far[b].astype(F32) + self.sent[b + 1].astype(F32)).astype(BF))
            for b in range(self.fast - 1)
        ]
        return self.out

    def send_fast(self):
        self.came = [swap(part, "fsdp", b + 1) for b, part in enumerate(self.out)]

    def add_fast(self, *others):
        total = after(self.near, *others).astype(F32) + self.sent[0].astype(F32)
        vectors = 0.0 if self.vectors is None else self.vectors.astype(BF).astype(F32)
        for part in self.came:
            part, more = self.unpack(part, total.shape)
            total = total + part.astype(F32)
            vectors = vectors + more
        self.total = total.astype(BF)
        if self.vectors is not None:
            self.vectors = vectors
        return self.total

    def send_slow(self):
        self.came = [
            swap(self.pack(self.total[k]), "fsdp", k * self.fast) for k in range(1, self.slow)
        ]

    def add_slow(self, *others):
        held = (self.total, self.vectors, self.came, others)
        total, vectors, came, _ = lax.optimization_barrier(held)
        final = total[0].astype(F32)
        vectors = 0.0 if vectors is None else vectors.astype(BF).astype(F32)
        for part in came:
            part, more = self.unpack(part, final.shape)
            final = final + part.astype(F32)
            vectors = vectors + more
        if self.vectors is not None:
            self.vectors = vectors
        return final


def add_replicas(value, across, c, vectors=None):
    value = value.astype(F32).reshape(-1, value.shape[-1])
    rows = value.shape[0]
    if vectors is not None:
        value = jnp.concatenate([value, vectors])
    k = 1
    while 2 * k < across:
        low = value.astype(BF)
        value = low.astype(F32) + swap(low, "mem", 2 * k).astype(F32)
        k *= 2
    low = value.astype(BF)
    halves = [low, swap(low, "mem", 2 * k)] if across > 1 else [low]
    others = [swap(half[:rows], "mem", 1) for half in halves]
    mine = sum(half.astype(F32) for half in halves)
    other = sum(half.astype(F32) for half in others).reshape(4, -1, value.shape[-1])
    vectors, mine = mine[rows:], mine[:rows].reshape(other.shape)
    first = jnp.where(c == 0, mine, other)
    second = jnp.where(c == 0, other, mine)
    pairs = [[first[2 * i], first[2 * i + 1], second[2 * i], second[2 * i + 1]] for i in range(2)]
    return *pairs, vectors


def place_rows(where, pieces, *refs):
    outs, (scratch, sems) = refs[:-2], refs[-2:]
    examples = pieces[0].shape[1]
    copies = Copies(sems)
    loads = [copies.start(piece, scratch.at[d]) for d, piece in enumerate(pieces)]
    stores = []
    for d, load in enumerate(loads):
        load.wait()
        for i, out in enumerate(outs):
            target = out.at[pl.ds((where[3] ^ d) * examples, examples)]
            stores.append(copies.start(scratch.at[d, i], target))
    wait_all(stores)


def spread_rows(where, values, mem):
    value = jnp.stack(values)
    blocks = [None] * mem
    blocks[0] = value
    for d in range(2, mem, 2):
        blocks[d] = swap(value, "mem", d)
    for d in range(0, mem, 2):
        blocks[d + 1] = swap(blocks[d], "mem", 1)
    whole = shape_of((mem * value.shape[1],) + value.shape[2:], BF)
    return run(
        place_rows,
        [(SMEM, where), [(ANY, piece) for piece in blocks]],
        [(ANY, whole)] * len(values),
        [pltpu.VMEM((mem,) + value.shape, BF)],
        mem * (1 + len(values)),
    )


def per_device(
    suffix,
    memory,
    counts,
    cotangent,
    self_norm_gain,
    self_norm_bias,
    self_query,
    self_key,
    self_value,
    self_output,
    cross_norm_gain,
    cross_norm_bias,
    cross_query,
    cross_key,
    cross_value,
    cross_output,
    dense_norm_gain,
    dense_norm_bias,
    dense_in,
    dense_in_bias,
    dense_out,
    dense_out_bias,
):
    f = lax.axis_index("fsdp")
    m = lax.axis_index("mem")
    c = m % 2
    fsdp = lax.axis_size("fsdp")
    mem = lax.axis_size("mem")
    across = mem // 2
    slow, fast = fsdp_split(fsdp)
    SHARDS[0] = fsdp
    where = jnp.stack([f // fast, f % fast, c, m]).astype(jnp.int32)
    examples = suffix.shape[0] // mem
    length = suffix.shape[1]
    width = suffix.shape[2]
    slots = memory.shape[1]
    total = mem * slots
    rows = examples * length
    inner = dense_in.shape[1]
    part = width // fsdp
    group = min(128, rows)
    blocks = 2 * fsdp + 4

    def gather(index, own, matrices):
        half = jnp.where(c == 0, jnp.stack(matrices[:2]), jnp.stack(matrices[2:]))
        return Gather(index, own, half, slow, fast)

    self_matrices = [self_query, self_key, self_value, self_output]
    cross_matrices = [cross_query, cross_key, cross_value, cross_output]
    self_gather = gather(0, self_matrices, self_matrices)
    cross_gather = gather(1, cross_matrices, cross_matrices)
    in_gather = gather(2, [dense_in], [dense_in[:, columns(j, width)] for j in range(4)])
    out_gather = gather(3, [dense_out], [dense_out[columns(j, part)] for j in range(4)])
    gathers = [self_gather, cross_gather, in_gather, out_gather]
    small = jnp.concatenate(
        [
            self_norm_gain,
            self_norm_bias,
            cross_norm_gain,
            cross_norm_bias,
            dense_norm_gain,
            dense_norm_bias,
            dense_out_bias,
            dense_in_bias,
        ]
    )[None]
    halves = jnp.stack([one.half for one in gathers])
    near_small = jnp.concatenate([small] + [swap(small, "fsdp", b) for b in range(1, fast)])
    far_own = [swap(after(halves, near_small), "fsdp", b) for b in range(1, fast)]

    def exchange(value):
        blocks = value.reshape((mem, examples) + value.shape[1:])
        return lax.all_to_all(blocks, "mem", 0, 0, tiled=True)

    all_memory = exchange(memory)

    self_gather.send_slow()
    sent = [*self_gather.came, *far_own, near_small]
    self_gather.send_fast(*sent)
    cross_gather.send_slow(*sent)
    far_other = [swap(after(piece, *sent), "mem", 1) for piece in far_own]
    for one in gathers:
        one.far_own, one.far_other = far_own, far_other
    near_small = after(near_small, *sent)
    small = jnp.concatenate(
        [near_small] + [swap(near_small, "fsdp", k * fast) for k in range(1, slow)]
    )
    small = jnp.take(small, jnp.arange(fsdp) ^ f, axis=0).astype(F32)
    vec = small[:, : 7 * part].reshape(fsdp, 7, part).transpose(1, 0, 2).reshape(7, width)
    bias_in = small[:, 7 * part :].reshape(1, inner)
    sent = [*self_gather.far, *cross_gather.came, all_memory, vec]
    self_gather.far = [after(piece, *sent) for piece in self_gather.far]
    self_weights = self_gather.whole()
    cross_gather.send_fast(*self_gather.far)
    in_gather.send_slow(*self_gather.far)

    half = (2, part, width)
    grads_like = [
        (ANY, shape_of((slow,) + half, BF)),
        (ANY, shape_of((fast - 1, slow) + half, BF)),
        (ANY, shape_of((fast, slow) + half, BF)),
    ]

    def flat(dims, dtype):
        return (VMEM, shape_of(dims, dtype))

    def per_example(value):
        dims = value.shape[1:]
        spec = pl.BlockSpec((1,) + dims, lambda e: (e,) + (0,) * len(dims))
        return (spec, value)

    def slots_of_example(value):
        spec = pl.BlockSpec((mem, 1, slots, width), lambda e: (0, e, 0, 0))
        return (spec, value)

    def scratch(*dims):
        return pltpu.VMEM(dims, BF)

    def scatter(grads, *others, vectors=None):
        return Scatter(grads, slow, fast, *others, vectors=vectors)

    wide = (rows, width)
    square = scratch(4, width, width)
    own_rows = scratch(examples, length, width)
    x1, a1, qkv, p1, o1 = run(
        functools.partial(self_forward, group),
        [(SMEM, where), (ANY, suffix), (VMEM, vec), self_weights],
        [
            flat(wide, F32),
            flat(wide, BF),
            flat((rows, 3 * width), BF),
            flat((rows // group * GROUPS, TOGETHER * group, group), BF),
            flat(wide, BF),
        ],
        [square, own_rows],
        1 + blocks,
    )
    cross_gather.far = [after(piece, x1, *in_gather.came) for piece in cross_gather.far]
    cross_weights = cross_gather.whole()
    in_gather.send_fast(*cross_gather.far)
    out_gather.send_slow(*cross_gather.far)
    x2, a2, q2, kv, p2, o2 = run(
        cross_forward,
        [(SMEM, where), (SMEM, counts), (VMEM, x1), (VMEM, vec)]
        + [slots_of_example(all_memory), cross_weights],
        [
            flat(wide, F32),
            flat(wide, BF),
            flat(wide, BF),
            per_example(shape_of((examples, total, 2 * width), BF)),
            per_example(shape_of((examples, GROUPS, TOGETHER * length, total), BF)),
            flat(wide, BF),
        ],
        [square],
        blocks,
        (examples,),
    )
    in_gather.far = [after(piece, x2, *out_gather.came) for piece in in_gather.far]
    in_weights = in_gather.whole()
    out_gather.send_fast(*in_gather.far)
    a3, h, slope, *grads = run(
        dense_inner,
        [(SMEM, where), (VMEM, x2), (VMEM, vec), (VMEM, bias_in), (ANY, cotangent), in_weights],
        [flat(wide, BF), flat((rows, inner), BF), flat((rows, inner), BF)] + grads_like,
        [square, scratch(fsdp, 4, part, width), own_rows],
        1 + blocks,
    )
    out_gather.far = [after(piece, a3) for piece in out_gather.far]
    out_weights = out_gather.whole()
    out_scatter = scatter(grads, *out_gather.far)
    out_sum = out_scatter.add_cores()
    out_scatter.send_fast()
    y, du, vecs_y, bias_grad, *grads = run(
        dense_outer,
        [(SMEM, where), (VMEM, after(x2, *out_sum)), (VMEM, vec), (VMEM, a3), (VMEM, h)]
        + [(VMEM, slope), (ANY, cotangent), out_weights],
        [
            flat((examples, length, width), BF),
            flat((rows, inner), BF),
            flat((1, width), F32),
            flat((1, inner), F32),
        ]
        + grads_like,
        [scratch(fsdp, 4, part, width), square, own_rows],
        1 + blocks,
    )
    in_grads = grads
    gx2, vecs_dense = run(
        dense_back,
        [(SMEM, where), (VMEM, x2), (VMEM, vec), (VMEM, du), (ANY, cotangent), in_weights],
        [flat(wide, F32), flat((2, width), F32)],
        [square, own_rows],
        1 + blocks,
    )
    out_total = out_scatter.add_fast(gx2)
    out_scatter.send_slow()
    in_scatter = scatter(in_grads, out_total)
    in_sum = in_scatter.add_cores()
    in_scatter.send_fast()
    gx1, vecs_cross, dkv, dq2, grad_memory = run(
        cross_backward,
        [(SMEM, where), (VMEM, x1), (VMEM, vec), (VMEM, after(gx2, out_total, *in_sum)), (VMEM, q2)]
        + [per_example(kv), per_example(p2), cross_weights],
        [
            flat(wide, F32),
            flat((2, width), F32),
            per_example(shape_of((examples, total, 2 * width), BF)),
            flat(wide, BF),
            slots_of_example(shape_of((mem, examples, slots, width), BF)),
        ],
        [square, scratch(*wide)],
        blocks,
        (examples,),
    )
    out_final = out_scatter.add_slow(gx1)
    grads = run(
        cross_grads,
        [(SMEM, where), (VMEM, after(gx2, out_final)), (VMEM, a2), (VMEM, o2), (VMEM, dq2)]
        + [(VMEM, dkv), (ANY, all_memory)],
        grads_like,
        [square, scratch(examples, total, width)],
        max(mem, blocks),
    )
    in_total = in_scatter.add_fast()
    in_scatter.send_slow()
    cross_scatter = scatter(grads, in_total)
    cross_sum = cross_scatter.add_cores()
    cross_scatter.send_fast()
    gx1 = after(gx1, *cross_sum)
    suffix_part, vecs_self, *grads = run(
        functools.partial(self_backward, group),
        [(SMEM, where), (ANY, suffix), (VMEM, vec), (VMEM, gx1), (VMEM, a1)]
        + [(VMEM, qkv), (VMEM, p1), (VMEM, o1)]
        + [[(VMEM, x) for x in (vecs_cross, vecs_dense, vecs_y, bias_grad)], self_weights],
        [flat((examples, length, width), BF), flat((16, width), BF)] + grads_like,
        [square, own_rows, square, scratch(rows, 3 * width), scratch(*wide)],
        1 + blocks,
    )
    cross_total = cross_scatter.add_fast(suffix_part)
    cross_scatter.send_slow()
    in_final = in_scatter.add_slow(suffix_part)
    self_scatter = scatter(grads, cross_total, in_final, vectors=vecs_self)
    self_sum = self_scatter.add_cores()
    self_scatter.send_fast()
    self_total = self_scatter.add_fast()
    self_scatter.send_slow()
    memory_grad = exchange(after(grad_memory, *self_sum).reshape(memory.shape))
    memory_grad = after(memory_grad.reshape(memory.shape), self_total)
    suffix_part = after(suffix_part, self_total)

    grad_out, grad_in, _ = add_replicas(
        jnp.stack([after(out_final, self_total), in_final]), across, c
    )
    grad_out = jnp.concatenate(grad_out, axis=0)
    grad_in = jnp.concatenate(grad_in, axis=1)
    block_output, suffix_grad = spread_rows(where, [y, suffix_part], mem)
    self_final = self_scatter.add_slow(block_output, grad_in, memory_grad)
    finals = jnp.stack([cross_scatter.add_slow(self_total), self_final])
    grad_cross, grad_self, vectors = add_replicas(finals, across, c, self_scatter.vectors)

    def vector(i):
        return lax.dynamic_slice(vectors, (i, f * part), (1, part)).reshape(part)

    return (
        block_output,
        suffix_grad,
        memory_grad,
        vector(0),
        vector(1),
        *grad_self,
        vector(2),
        vector(3),
        *grad_cross,
        vector(4),
        vector(5),
        grad_in,
        lax.dynamic_slice_in_dim(vectors[7:11].reshape(-1), f * (inner // fsdp), inner // fsdp, 0),
        grad_out,
        vector(6),
    )


def solution(mesh):
    rows = P("fsdp", None, None)
    matrix = P("fsdp", None)
    vector = P("fsdp")
    attention = (vector, vector, matrix, matrix, matrix, matrix)
    params = attention + attention + (vector, vector, matrix, vector, matrix, vector)
    return jax.shard_map(
        per_device,
        mesh=mesh,
        in_specs=(rows, P("fsdp", "mem", None), vector, rows) + params,
        out_specs=(rows, rows, P("fsdp", "mem", None)) + params,
        check_vma=False,
    )
```

```python
import functools

import jax
import jax.numpy as jnp
from jax import lax
from jax.experimental import pallas as pl
from jax.experimental.pallas import tpu as pltpu
from jax.sharding import PartitionSpec as P

HEADS = 12
HEAD = 64
TOGETHER = 4
GROUPS = HEADS // TOGETHER
LANES = TOGETHER * HEAD
SCALE = HEAD ** (-0.5)
BF = jnp.bfloat16
F32 = jnp.float32
ANY = pl.BlockSpec(memory_space=pl.ANY)
SMEM = pl.BlockSpec(memory_space=pltpu.SMEM)
VMEM = pl.BlockSpec(memory_space=pltpu.VMEM)


def swap(value, axis, distance):
    size = lax.axis_size(axis)
    return lax.ppermute(value, axis, [(i, i ^ distance) for i in range(size)])


def after(value, *others):
    return lax.optimization_barrier((value, *others))[0] if others else value


def fsdp_split(size):
    slow = 4 if size % 4 == 0 else 1
    return slow, size // slow


def dot(left, right):
    return jnp.dot(left, right, preferred_element_type=F32)


def dot_nt(left, right):
    return lax.dot_general(left, right, (((1,), (1,)), ((), ())), preferred_element_type=F32)


def dot_tn(left, right):
    return lax.dot_general(left, right, (((0,), (0,)), ((), ())), preferred_element_type=F32)


def rows_of(start, size):
    return pl.ds(pl.multiple_of(start, 16), size)


def block(ref, by_rows, shard, which):
    if by_rows:
        return ref.at[shard, pl.ds(which * 2, 2)]
    rows = ref.shape[1] // SHARDS[0]
    return ref.at[pl.ds(which * 2, 2), rows_of(shard * rows, rows)]


SHARDS = [0]


class Copies:
    def __init__(self, sems):
        self.sems = sems
        self.next = 0

    def start(self, source, target):
        copy = pltpu.make_async_copy(source, target, self.sems.at[self.next])
        self.next += 1
        copy.start()
        return copy


def wait_all(copies):
    for copy in copies:
        copy.wait()


def load_weight(where, whole, by_rows, weights, copies):
    y, c = where[1], where[2]
    started = []
    for which, pieces in ((c, weights[0]), (1 - c, weights[1])):
        fast = len(pieces)
        for b, piece in enumerate(pieces):
            for k in range(piece.shape[0]):
                target = block(whole, by_rows, k * fast + (y ^ b), which)
                started.append(copies.start(piece.at[k], target))
    return started


def store_grad(where, whole, by_rows, near, far, theirs, copies):
    y, c = where[1], where[2]
    fast, slow = theirs.shape[0], theirs.shape[1]
    started = []
    for b in range(fast):
        for k in range(slow):
            shard = k * fast + (y ^ b)
            mine = far.at[b - 1, k] if b else near.at[k]
            started.append(copies.start(block(whole, by_rows, shard, 1 - c), theirs.at[b, k]))
            started.append(copies.start(block(whole, by_rows, shard, c), mine))
    return started


def my_examples(where, source, target, copies):
    count = target.shape[0]
    return copies.start(source.at[pl.ds(where[3] * count, count)], target)


def normalise(values):
    centred = values - jnp.mean(values, axis=-1, keepdims=True)
    scale = lax.rsqrt(jnp.mean(centred * centred, axis=-1, keepdims=True) + 1e-06)
    return centred * scale, scale


def norm_back(grad, gain, hat, scale):
    inner = grad * gain
    mean = jnp.mean(inner, axis=-1, keepdims=True)
    along = jnp.mean(inner * hat, axis=-1, keepdims=True)
    return (
        scale * (inner - mean - hat * along),
        jnp.sum(grad * hat, axis=0, keepdims=True),
        jnp.sum(grad, axis=0, keepdims=True),
    )


def head_mask(rows):
    shape = (TOGETHER * rows, LANES)
    row = lax.broadcasted_iota(jnp.int32, shape, 0) // rows
    lane = lax.broadcasted_iota(jnp.int32, shape, 1) // HEAD
    return (row == lane).astype(F32)


def stack_heads(value, mask):
    return (jnp.concatenate([value] * TOGETHER, axis=0).astype(F32) * mask).astype(BF)


def merge_heads(value, mask):
    rows = value.shape[0] // TOGETHER
    value = value * mask
    total = value[:rows]
    for h in range(1, TOGETHER):
        total = total + value[h * rows : (h + 1) * rows]
    return total


def columns(j, width):
    return slice(j * width, (j + 1) * width)


def self_forward(
    group, where, suffix, small, weights, x1, a1, qkv, p1, o1, vec, weight, start, sems
):
    rows, width = x1.shape
    copies = Copies(sems)
    first = my_examples(where, suffix, start, copies)
    loads = load_weight(where, weight, False, weights, copies)
    fast = len(weights[0])
    part = width // small.shape[0]
    lane = lax.broadcasted_iota(jnp.int32, (128, width), 0)
    place = lax.broadcasted_iota(jnp.int32, (128, width), 1) - lane
    together = jnp.zeros(vec.shape, F32)
    for i in range(small.shape[0]):
        shard = i // fast * fast + (where[1] ^ (i % fast))
        chosen = ((place == shard * part) & (lane < part)).astype(F32).astype(BF)
        together = together + dot(small[i], chosen)
    vec[...] = together
    first.wait()
    values = start[...].reshape(rows, width).astype(F32)
    hat, _ = normalise(values)
    a1[...] = (hat * vec[0:1, :] + vec[1:2, :]).astype(BF)
    wait_all(loads)
    for j in range(3):
        qkv[:, columns(j, width)] = dot(a1[...], weight[j]).astype(BF)
    mask = head_mask(group)
    length = suffix.shape[1]
    shape = (TOGETHER * group, group)
    row = lax.broadcasted_iota(jnp.int32, shape, 0) % group
    col = lax.broadcasted_iota(jnp.int32, shape, 1)
    seen = (row // length == col // length) & (row >= col)
    for r in range(rows // group):
        here = columns(r, group)
        for g in range(GROUPS):
            lanes = [slice(i * width + g * LANES, i * width + (g + 1) * LANES) for i in range(3)]
            queries = stack_heads(qkv[here, lanes[0]], mask)
            scores = dot_nt(queries, qkv[here, lanes[1]]) * SCALE
            scores = jnp.where(seen, scores, -1e30)
            powers = jnp.exp(scores - jnp.max(scores, axis=-1, keepdims=True))
            probs = (powers / jnp.sum(powers, axis=-1, keepdims=True)).astype(BF)
            p1[r * GROUPS + g] = probs
            found = dot(probs, qkv[here, lanes[2]])
            o1[here, lanes[0]] = merge_heads(found, mask).astype(BF)
    x1[...] = values + dot(o1[...], weight[3])


def cross_forward(
    where, counts, x1, vec, memory, weights, x2, a2, q2, kv, p2, o2, weight, sems
):
    rows, width = x1.shape
    examples = pl.num_programs(0)
    e = pl.program_id(0)
    total = kv.shape[1]
    length = p2.shape[2] // TOGETHER

    @pl.when(e == 0)
    def _():
        loads = load_weight(where, weight, False, weights, Copies(sems))
        hat, _ = normalise(x1[...])
        a2[...] = (hat * vec[2:3, :] + vec[3:4, :]).astype(BF)
        wait_all(loads)
        q2[...] = dot(a2[...], weight[0]).astype(BF)

    tokens = memory[...].reshape(total, width)
    for j in range(2):
        kv[0, :, columns(j, width)] = dot(tokens, weight[1 + j]).astype(BF)
    mask = head_mask(length)
    position = lax.broadcasted_iota(jnp.int32, (1, total), 1)
    valid = position < counts[where[3] * examples + e]
    here = rows_of(e * length, length)
    probs = []
    for g in range(GROUPS):
        lanes = columns(g, LANES)
        queries = stack_heads(q2[here, lanes], mask)
        scores = dot_nt(queries, kv[0, :, lanes]) * SCALE
        scores = jnp.where(valid, scores, -1e30)
        top = jnp.maximum(jnp.max(scores, axis=-1, keepdims=True), 0.0)
        powers = jnp.exp(scores - top)
        weight_sum = jnp.sum(powers, axis=-1, keepdims=True) + jnp.exp(-top)
        probs.append((powers / weight_sum).astype(BF))
    for g in range(GROUPS):
        p2[0, g] = probs[g]
        found = dot(probs[g], kv[0, :, width + g * LANES : width + (g + 1) * LANES])
        o2[here, columns(g, LANES)] = merge_heads(found, mask).astype(BF)

    @pl.when(e == examples - 1)
    def _():
        x2[...] = x1[...] + dot(o2[...], weight[3])


def dense_inner(
    where, x2, vec, bias, cotangent, weights, a3, h, slope, near, far, theirs,
    weight, grad, cot, sems,
):
    rows, width = x2.shape
    copies = Copies(sems)
    cot_copy = my_examples(where, cotangent, cot, copies)
    loads = load_weight(where, weight, False, weights, copies)
    hat, _ = normalise(x2[...])
    a3[...] = (hat * vec[4:5, :] + vec[5:6, :]).astype(BF)
    cot_copy.wait()
    gy = cot[...].reshape(rows, width)
    wait_all(loads)
    flat = grad.shape[0] * grad.shape[1] * grad.shape[2]
    step = flat // grad.shape[0]
    for j in range(4):
        for half in range(2):
            cols = slice(j * width + half * 384, j * width + (half + 1) * 384)
            u = dot(a3[...], weight[j, :, half * 384 : (half + 1) * 384]) + bias[:, cols]
            square = u * u
            t = jnp.tanh(0.7978845608 * u * (1.0 + 0.044715 * square))
            h[:, cols] = (0.5 * u * (1.0 + t)).astype(BF)
            slope[:, cols] = (
                0.5 * (1.0 + t)
                + (0.5 * 0.7978845608) * u * (1.0 - t * t) * (1.0 + (3.0 * 0.044715) * square)
            ).astype(BF)
            part = dot_tn(h[:, cols], gy).astype(BF)
            per = 384 // step
            grad[cols.start // step : cols.start // step + per] = part.reshape(
                (per,) + grad.shape[1:]
            )
    wait_all(store_grad(where, grad, True, near, far, theirs, Copies(sems)))


def dense_outer(
    where, x2, vec, a3, h, slope, cotangent, weights, y, du, vecs, bias_grad, near, far, theirs,
    weight, grad, cot, sems,
):
    rows, width = x2.shape
    copies = Copies(sems)
    cot_copy = my_examples(where, cotangent, cot, copies)
    wait_all(load_weight(where, weight, True, weights, copies))
    cot_copy.wait()
    gy = cot[...].reshape(rows, width)
    shards = weight.shape[0]
    step = weight.shape[1] * weight.shape[2]
    whole = weight[...].reshape(shards * step, width)
    for j in range(4):
        cols = columns(j, width)
        low = (dot_nt(gy, whole[cols]) * slope[:, cols].astype(F32)).astype(BF)
        du[:, cols] = low
        bias_grad[:, cols] = jnp.sum(low.astype(F32), axis=0, keepdims=True)
        grad[j] = dot_tn(a3[...], low).astype(BF)
    started = store_grad(where, grad, False, near, far, theirs, Copies(sems))
    result = x2[...] + dot(h[...], whole) + vec[6:7, :]
    y[...] = result.astype(BF).reshape(y.shape)
    vecs[...] = jnp.sum(gy.astype(F32), axis=0, keepdims=True)
    wait_all(started)


def dense_back(where, x2, vec, du, cotangent, weights, gx2, vecs, weight, cot, sems):
    rows, width = x2.shape
    copies = Copies(sems)
    cot_copy = my_examples(where, cotangent, cot, copies)
    loads = load_weight(where, weight, False, weights, copies)
    hat, scale = normalise(x2[...])
    cot_copy.wait()
    wait_all(loads)
    da3 = dot_nt(du[:, columns(0, width)], weight[0])
    for j in range(1, 4):
        da3 = da3 + dot_nt(du[:, columns(j, width)], weight[j])
    back, gain_grad, shift_grad = norm_back(da3, vec[4:5, :], hat, scale)
    gx2[...] = cot[...].reshape(rows, width).astype(F32) + back
    vecs[0:1, :] = gain_grad
    vecs[1:2, :] = shift_grad


def cross_backward(
    where, x1, vec, gx2, q2, kv, p2, weights, gx1, vecs, dkv, dq2, out_mem, weight, do2, sems
):
    rows, width = x1.shape
    examples = pl.num_programs(0)
    e = pl.program_id(0)
    length = p2.shape[2] // TOGETHER

    @pl.when(e == 0)
    def _():
        wait_all(load_weight(where, weight, False, weights, Copies(sems)))
        do2[...] = dot_nt(gx2[...].astype(BF), weight[3]).astype(BF)

    mask = head_mask(length)
    here = rows_of(e * length, length)
    for g in range(GROUPS):
        lanes = columns(g, LANES)
        value_lanes = slice(width + g * LANES, width + (g + 1) * LANES)
        queries = stack_heads(q2[here, lanes], mask)
        grads = stack_heads(do2[here, lanes], mask)
        probs = p2[0, g]
        dp = dot_nt(grads, kv[0, :, value_lanes])
        wide = probs.astype(F32)
        row_sum = jnp.sum(wide * dp, axis=-1, keepdims=True)
        dz = (wide * (dp - row_sum)).astype(BF)
        dkv[0, :, value_lanes] = dot_tn(probs, grads).astype(BF)
        dkv[0, :, lanes] = (dot_tn(dz, queries) * SCALE).astype(BF)
        dq2[here, lanes] = (merge_heads(dot(dz, kv[0, :, lanes]), mask) * SCALE).astype(BF)
    back = dot_nt(dkv[0, :, :width], weight[1]) + dot_nt(dkv[0, :, width:], weight[2])
    out_mem[...] = back.astype(BF).reshape(out_mem.shape)

    @pl.when(e == examples - 1)
    def _():
        hat, scale = normalise(x1[...])
        back, gain_grad, shift_grad = norm_back(
            dot_nt(dq2[...], weight[0]), vec[2:3, :], hat, scale
        )
        gx1[...] = gx2[...] + back
        vecs[0:1, :] = gain_grad
        vecs[1:2, :] = shift_grad


def cross_grads(
    where, gx2, a2, o2, dq2, dkv, all_memory, near, far, theirs, grad, memory, sems
):
    rows, width = gx2.shape
    examples, total, _ = memory.shape
    mem, _, slots, _ = all_memory.shape
    copies = Copies(sems)
    loads = [
        copies.start(all_memory.at[d], memory.at[:, d * slots : (d + 1) * slots, :])
        for d in range(mem)
    ]
    grad[0] = dot_tn(a2[...], dq2[...]).astype(BF)
    grad[3] = dot_tn(o2[...], gx2[...].astype(BF)).astype(BF)
    wait_all(loads)
    flat = memory[...].reshape(examples * total, width)
    for j in range(2):
        part = dkv[:, :, columns(j, width)].reshape(examples * total, width)
        grad[1 + j] = dot_tn(flat, part).astype(BF)
    wait_all(store_grad(where, grad, False, near, far, theirs, Copies(sems)))


def self_backward(
    group, where, suffix, vec, gx1, a1, qkv, p1, o1, parts, weights, suffix_grad, vecs,
    near, far, theirs, weight, start, grad, dqkv, do1, sems,
):
    rows, width = gx1.shape
    copies = Copies(sems)
    start_copy = my_examples(where, suffix, start, copies)
    loads = load_weight(where, weight, False, weights, copies)
    gs = gx1[...].astype(BF)
    grad[3] = dot_tn(o1[...], gs).astype(BF)
    wait_all(loads)
    do1[...] = dot_nt(gs, weight[3]).astype(BF)
    mask = head_mask(group)
    for r in range(rows // group):
        here = columns(r, group)
        for g in range(GROUPS):
            lanes = [slice(i * width + g * LANES, i * width + (g + 1) * LANES) for i in range(3)]
            queries = stack_heads(qkv[here, lanes[0]], mask)
            grads = stack_heads(do1[here, lanes[0]], mask)
            probs = p1[r * GROUPS + g]
            dp = dot_nt(grads, qkv[here, lanes[2]])
            wide = probs.astype(F32)
            row_sum = jnp.sum(wide * dp, axis=-1, keepdims=True)
            dz = (wide * (dp - row_sum)).astype(BF)
            dqkv[here, lanes[2]] = dot_tn(probs, grads).astype(BF)
            dqkv[here, lanes[1]] = (dot_tn(dz, queries) * SCALE).astype(BF)
            dq = merge_heads(dot(dz, qkv[here, lanes[1]]), mask) * SCALE
            dqkv[here, lanes[0]] = dq.astype(BF)
    for j in range(3):
        grad[j] = dot_tn(a1[...], dqkv[:, columns(j, width)]).astype(BF)
    start_copy.wait()
    started = store_grad(where, grad, False, near, far, theirs, Copies(sems))
    da1 = dot_nt(dqkv[:, columns(0, width)], weight[0])
    for j in range(1, 3):
        da1 = da1 + dot_nt(dqkv[:, columns(j, width)], weight[j])
    hat, scale = normalise(start[...].reshape(rows, width).astype(F32))
    back, gain_grad, shift_grad = norm_back(da1, vec[0:1, :], hat, scale)
    suffix_grad[...] = (gx1[...] + back).astype(BF).reshape(suffix_grad.shape)
    found = [gain_grad, shift_grad]
    for ref in parts:
        for r in range(ref.shape[0]):
            found += [ref[r : r + 1, columns(j, width)] for j in range(ref.shape[1] // width)]
    found.append(jnp.zeros((vecs.shape[0] - len(found), width), F32))
    vecs[...] = jnp.concatenate(found, axis=0).astype(BF)
    wait_all(started)


def run(kernel, inputs, outputs, scratch, copies, grid=()):
    def leaf(x):
        return isinstance(x, tuple) and len(x) == 2 and isinstance(x[0], pl.BlockSpec)

    flat_in, tree_in = jax.tree.flatten(inputs, is_leaf=leaf)
    flat_out, tree_out = jax.tree.flatten(outputs, is_leaf=leaf)

    def body(*refs):
        first, second = len(flat_in), len(flat_in) + len(flat_out)
        given = jax.tree.unflatten(tree_in, refs[:first])
        taken = jax.tree.unflatten(tree_out, refs[first:second])
        kernel(*given, *taken, *refs[second:])

    found = pl.pallas_call(
        body,
        grid=grid,
        in_specs=[spec for spec, _ in flat_in],
        out_specs=[spec for spec, _ in flat_out],
        out_shape=[shape for _, shape in flat_out],
        scratch_shapes=scratch + [pltpu.SemaphoreType.DMA((copies,))],
        compiler_params=pltpu.CompilerParams(vmem_limit_bytes=56 * 1024 * 1024),
        cost_estimate=pl.CostEstimate(
            flops=0, bytes_accessed=0, transcendentals=0
        ),
    )(*[x for _, x in flat_in])
    return jax.tree.unflatten(tree_out, found)


def shape_of(dims, dtype):
    return jax.ShapeDtypeStruct(tuple(dims), dtype)


def over_slow(value, slow, fast):
    groups = [[k * fast + b for k in range(slow)] for b in range(fast)]
    return lax.all_to_all(value, "fsdp", 0, 0, axis_index_groups=groups, tiled=True)


class Gather:
    def __init__(self, half, slow, fast):
        self.half, self.slow, self.fast = half, slow, fast

    def send_slow(self, *others):
        half = after(self.half, *others)
        half = jnp.broadcast_to(half[None], (self.slow,) + half.shape)
        self.near = over_slow(half, self.slow, self.fast)

    def send_fast(self, *others):
        self.near = after(self.near, *others)
        self.near_other = swap(self.near, "mem", 1)
        self.far = [swap(self.near, "fsdp", b) for b in range(1, self.fast)]

    def whole(self):
        mine = [self.near] + self.far
        theirs = [self.near_other] + [swap(piece, "mem", 1) for piece in self.far]
        return [[(ANY, x) for x in some] for some in (mine, theirs)]


class Scatter:
    def __init__(self, grads, slow, fast, *others, vectors=None):
        self.near, self.far, theirs = grads
        self.slow, self.fast, self.vectors = slow, fast, vectors
        theirs = after(theirs, *others)
        self.unit = theirs.shape[2:]
        if vectors is None:
            self.sent = swap(theirs, "mem", 1)
        else:
            self.sent, came = self.unpack(swap(self.pack(theirs), "mem", 1), theirs.shape)
            self.vectors = vectors.astype(F32) + came

    def pack(self, value):
        if self.vectors is None:
            return value
        width = value.shape[-1]
        return jnp.concatenate([value.reshape(-1, width), self.vectors.astype(BF)])

    def unpack(self, value, shape):
        if self.vectors is None:
            return value, 0.0
        rows = value.shape[0] - self.vectors.shape[0]
        return value[:rows].reshape(shape), value[rows:].astype(F32)

    def add_cores(self):
        self.out = [
            self.pack((self.far[b].astype(F32) + self.sent[b + 1].astype(F32)).astype(BF))
            for b in range(self.fast - 1)
        ]
        return self.out

    def send_fast(self):
        self.came = [swap(part, "fsdp", b + 1) for b, part in enumerate(self.out)]

    def add_fast(self, *others):
        total = after(self.near, *others).astype(F32) + self.sent[0].astype(F32)
        vectors = 0.0 if self.vectors is None else self.vectors.astype(BF).astype(F32)
        for part in self.came:
            part, more = self.unpack(part, total.shape)
            total = total + part.astype(F32)
            vectors = vectors + more
        self.total = total.astype(BF).reshape(self.slow, -1, total.shape[-1])
        if self.vectors is not None:
            low = jnp.broadcast_to(vectors.astype(BF), (self.slow,) + vectors.shape)
            self.total = jnp.concatenate([self.total, low], axis=1)
        return self.total

    def send_slow(self):
        self.came = over_slow(self.total, self.slow, self.fast)

    def add_slow(self, *others):
        return jnp.sum(after(self.came, *others).astype(F32), axis=0)


def add_replicas(value, rows, across, c):
    k = 1
    while 2 * k < across:
        low = value.astype(BF)
        value = low.astype(F32) + swap(low, "mem", 2 * k).astype(F32)
        k *= 2
    low = value.astype(BF)
    halves = [low, swap(low, "mem", 2 * k)] if across > 1 else [low]
    others = [swap(half[: 2 * rows], "mem", 1) for half in halves]
    mine = sum(half.astype(F32) for half in halves)
    other = sum(half.astype(F32) for half in others)
    vectors, mine = mine[2 * rows :], mine[: 2 * rows]
    first = jnp.where(c == 0, mine, other)
    second = jnp.where(c == 0, other, mine)
    return [first[:rows], first[rows:], second[:rows], second[rows:]], vectors


def place_rows(where, pieces, *refs):
    outs, (scratch, sems) = refs[:-2], refs[-2:]
    examples = pieces[0].shape[1]
    copies = Copies(sems)
    loads = [copies.start(piece, scratch.at[d]) for d, piece in enumerate(pieces)]
    stores = []
    for d, load in enumerate(loads):
        load.wait()
        for i, out in enumerate(outs):
            target = out.at[pl.ds((where[3] ^ d) * examples, examples)]
            stores.append(copies.start(scratch.at[d, i], target))
    wait_all(stores)


def spread_rows(where, values, mem):
    value = jnp.stack(values)
    blocks = [None] * mem
    blocks[0] = value
    for d in range(2, mem, 2):
        blocks[d] = swap(value, "mem", d)
    for d in range(0, mem, 2):
        blocks[d + 1] = swap(blocks[d], "mem", 1)
    whole = shape_of((mem * value.shape[1],) + value.shape[2:], BF)
    return run(
        place_rows,
        [(SMEM, where), [(ANY, piece) for piece in blocks]],
        [(ANY, whole)] * len(values),
        [pltpu.VMEM((mem,) + value.shape, BF)],
        mem * (1 + len(values)),
    )


def per_device(
    suffix,
    memory,
    counts,
    cotangent,
    self_norm_gain,
    self_norm_bias,
    self_query,
    self_key,
    self_value,
    self_output,
    cross_norm_gain,
    cross_norm_bias,
    cross_query,
    cross_key,
    cross_value,
    cross_output,
    dense_norm_gain,
    dense_norm_bias,
    dense_in,
    dense_in_bias,
    dense_out,
    dense_out_bias,
):
    f = lax.axis_index("fsdp")
    m = lax.axis_index("mem")
    c = m % 2
    fsdp = lax.axis_size("fsdp")
    mem = lax.axis_size("mem")
    across = mem // 2
    slow, fast = fsdp_split(fsdp)
    SHARDS[0] = fsdp
    where = jnp.stack([f // fast, f % fast, c, m]).astype(jnp.int32)
    examples = suffix.shape[0] // mem
    length = suffix.shape[1]
    width = suffix.shape[2]
    slots = memory.shape[1]
    total = mem * slots
    rows = examples * length
    inner = dense_in.shape[1]
    part = width // fsdp
    group = min(128, rows)
    blocks = 2 * fsdp

    def gather(matrices):
        half = jnp.where(c == 0, jnp.stack(matrices[:2]), jnp.stack(matrices[2:]))
        return Gather(half, slow, fast)

    self_gather = gather([self_query, self_key, self_value, self_output])
    cross_gather = gather([cross_query, cross_key, cross_value, cross_output])
    in_gather = gather([dense_in[:, columns(j, width)] for j in range(4)])
    out_gather = gather([dense_out[columns(j, part)] for j in range(4)])
    small = [
        self_norm_gain,
        self_norm_bias,
        cross_norm_gain,
        cross_norm_bias,
        dense_norm_gain,
        dense_norm_bias,
        dense_out_bias,
    ]
    small += [dense_in_bias[columns(j, part)] for j in range(4)]
    small = sum(
        jnp.pad(value[None], ((i, 15 - i), (0, 128 - part))) for i, value in enumerate(small)
    )

    def exchange(value):
        blocks = value.reshape((mem, examples) + value.shape[1:])
        return lax.all_to_all(blocks, "mem", 0, 0, tiled=True)

    all_memory = exchange(memory)
    small = jnp.concatenate([small] + [swap(small, "fsdp", b) for b in range(1, fast)])
    self_gather.send_slow()
    sent = [self_gather.near, small]
    self_gather.send_fast(*sent)
    cross_gather.send_slow(*sent)
    small = after(small, *sent)
    small = over_slow(jnp.broadcast_to(small[None], (slow,) + small.shape), slow, fast)
    small = small.reshape(slow * fast, 16, 128)
    sent = [*self_gather.far, cross_gather.near, all_memory, small]
    self_gather.far = [after(piece, *sent) for piece in self_gather.far]
    self_weights = self_gather.whole()
    cross_gather.send_fast(*self_gather.far)
    in_gather.send_slow(*self_gather.far)

    half = (2, part, width)
    grads_like = [
        (ANY, shape_of((slow,) + half, BF)),
        (ANY, shape_of((fast - 1, slow) + half, BF)),
        (ANY, shape_of((fast, slow) + half, BF)),
    ]

    def flat(dims, dtype):
        return (VMEM, shape_of(dims, dtype))

    def per_example(value):
        dims = value.shape[1:]
        spec = pl.BlockSpec((1,) + dims, lambda e: (e,) + (0,) * len(dims))
        return (spec, value)

    def slots_of_example(value):
        spec = pl.BlockSpec((mem, 1, slots, width), lambda e: (0, e, 0, 0))
        return (spec, value)

    def scratch(*dims):
        return pltpu.VMEM(dims, BF)

    def scatter(grads, *others, vectors=None):
        return Scatter(grads, slow, fast, *others, vectors=vectors)

    wide = (rows, width)
    square = scratch(4, width, width)
    own_rows = scratch(examples, length, width)
    x1, a1, qkv, p1, o1, vec = run(
        functools.partial(self_forward, group),
        [(SMEM, where), (ANY, suffix), (VMEM, small), self_weights],
        [
            flat(wide, F32),
            flat(wide, BF),
            flat((rows, 3 * width), BF),
            flat((rows // group * GROUPS, TOGETHER * group, group), BF),
            flat(wide, BF),
            flat((16, width), F32),
        ],
        [square, own_rows],
        1 + blocks,
    )
    cross_gather.far = [after(piece, x1, in_gather.near) for piece in cross_gather.far]
    cross_weights = cross_gather.whole()
    in_gather.send_fast(*cross_gather.far)
    out_gather.send_slow(*cross_gather.far)
    x2, a2, q2, kv, p2, o2 = run(
        cross_forward,
        [(SMEM, where), (SMEM, counts), (VMEM, x1), (VMEM, vec)]
        + [slots_of_example(all_memory), cross_weights],
        [
            flat(wide, F32),
            flat(wide, BF),
            flat(wide, BF),
            per_example(shape_of((examples, total, 2 * width), BF)),
            per_example(shape_of((examples, GROUPS, TOGETHER * length, total), BF)),
            flat(wide, BF),
        ],
        [square],
        blocks,
        (examples,),
    )
    bias_in = after(small, x1).reshape(slow, fast, 16, 128)[:, :, 7:11, :part].astype(F32)
    order = jnp.arange(fast) ^ (f % fast)
    bias_in = jnp.take(bias_in, order, axis=1).reshape(1, inner)
    in_gather.far = [after(piece, x2, out_gather.near) for piece in in_gather.far]
    in_weights = in_gather.whole()
    out_gather.send_fast(*in_gather.far)
    a3, h, slope, *grads = run(
        dense_inner,
        [(SMEM, where), (VMEM, x2), (VMEM, vec), (VMEM, bias_in), (ANY, cotangent), in_weights],
        [flat(wide, BF), flat((rows, inner), BF), flat((rows, inner), BF)] + grads_like,
        [square, scratch(fsdp, 4, part, width), own_rows],
        1 + blocks,
    )
    out_gather.far = [after(piece, a3) for piece in out_gather.far]
    out_weights = out_gather.whole()
    out_scatter = scatter(grads, *out_gather.far)
    out_sum = out_scatter.add_cores()
    out_scatter.send_fast()
    y, du, vecs_y, bias_grad, *grads = run(
        dense_outer,
        [(SMEM, where), (VMEM, after(x2, *out_sum)), (VMEM, vec), (VMEM, a3), (VMEM, h)]
        + [(VMEM, slope), (ANY, cotangent), out_weights],
        [
            flat((examples, length, width), BF),
            flat((rows, inner), BF),
            flat((1, width), F32),
            flat((1, inner), F32),
        ]
        + grads_like,
        [scratch(fsdp, 4, part, width), square, own_rows],
        1 + blocks,
    )
    in_grads = grads
    gx2, vecs_dense = run(
        dense_back,
        [(SMEM, where), (VMEM, x2), (VMEM, vec), (VMEM, du), (ANY, cotangent), in_weights],
        [flat(wide, F32), flat((2, width), F32)],
        [square, own_rows],
        1 + blocks,
    )
    out_total = out_scatter.add_fast(gx2)
    out_scatter.send_slow()
    in_scatter = scatter(in_grads, out_total)
    in_sum = in_scatter.add_cores()
    in_scatter.send_fast()
    gx1, vecs_cross, dkv, dq2, grad_memory = run(
        cross_backward,
        [(SMEM, where), (VMEM, x1), (VMEM, vec), (VMEM, after(gx2, out_total, *in_sum)), (VMEM, q2)]
        + [per_example(kv), per_example(p2), cross_weights],
        [
            flat(wide, F32),
            flat((2, width), F32),
            per_example(shape_of((examples, total, 2 * width), BF)),
            flat(wide, BF),
            slots_of_example(shape_of((mem, examples, slots, width), BF)),
        ],
        [square, scratch(*wide)],
        blocks,
        (examples,),
    )
    out_final = out_scatter.add_slow(gx1)
    memory_grad = exchange(grad_memory.reshape(memory.shape)).reshape(memory.shape)
    grads = run(
        cross_grads,
        [(SMEM, where), (VMEM, after(gx2, out_final)), (VMEM, a2), (VMEM, o2), (VMEM, dq2)]
        + [(VMEM, dkv), (ANY, all_memory)],
        grads_like,
        [square, scratch(examples, total, width)],
        max(mem, blocks),
    )
    in_total = in_scatter.add_fast()
    in_scatter.send_slow()
    cross_scatter = scatter(grads, in_total)
    cross_sum = cross_scatter.add_cores()
    cross_scatter.send_fast()
    gx1 = after(gx1, *cross_sum)
    suffix_part, vecs_self, *grads = run(
        functools.partial(self_backward, group),
        [(SMEM, where), (ANY, suffix), (VMEM, vec), (VMEM, gx1), (VMEM, a1)]
        + [(VMEM, qkv), (VMEM, p1), (VMEM, o1)]
        + [[(VMEM, x) for x in (vecs_cross, vecs_dense, vecs_y, bias_grad)], self_weights],
        [flat((examples, length, width), BF), flat((16, width), BF)] + grads_like,
        [square, own_rows, square, scratch(rows, 3 * width), scratch(*wide)],
        1 + blocks,
    )
    cross_total = cross_scatter.add_fast(suffix_part)
    cross_scatter.send_slow()
    in_final = in_scatter.add_slow(suffix_part)
    self_scatter = scatter(grads, cross_total, in_final, memory_grad, vectors=vecs_self)
    self_sum = self_scatter.add_cores()
    self_scatter.send_fast()
    suffix_part = after(suffix_part, *self_sum)
    self_total = self_scatter.add_fast()
    self_scatter.send_slow()

    def finish(value):
        return add_replicas(value, part, across, c)

    grad_out, _ = finish(after(out_final, *self_sum))
    grad_in, _ = finish(after(in_final, *self_sum))
    grad_cross, _ = finish(cross_scatter.add_slow(self_total))
    block_output, suffix_grad = spread_rows(where, [y, suffix_part], mem)
    grad_out = jnp.concatenate(grad_out, axis=0)
    grad_in = jnp.concatenate(grad_in, axis=1)
    grad_self, vectors = finish(
        self_scatter.add_slow(block_output, grad_in, grad_out, *grad_cross)
    )

    def vector(i):
        return lax.dynamic_slice(vectors, (i, f * part), (1, part)).reshape(part)

    return (
        block_output,
        suffix_grad,
        memory_grad,
        vector(0),
        vector(1),
        *grad_self,
        vector(2),
        vector(3),
        *grad_cross,
        vector(4),
        vector(5),
        grad_in,
        lax.dynamic_slice_in_dim(vectors[7:11].reshape(-1), f * (inner // fsdp), inner // fsdp, 0),
        grad_out,
        vector(6),
    )


def solution(mesh):
    rows = P("fsdp", None, None)
    matrix = P("fsdp", None)
    vector = P("fsdp")
    attention = (vector, vector, matrix, matrix, matrix, matrix)
    params = attention + attention + (vector, vector, matrix, vector, matrix, vector)
    return jax.shard_map(
        per_device,
        mesh=mesh,
        in_specs=(rows, P("fsdp", "mem", None), vector, rows) + params,
        out_specs=(rows, rows, P("fsdp", "mem", None)) + params,
        check_vma=False,
    )
```

```python
import functools

import jax
import jax.numpy as jnp
from jax import lax
from jax.experimental import pallas as pl
from jax.experimental.pallas import tpu as pltpu
from jax.sharding import PartitionSpec as P

HEADS = 12
HEAD = 64
TOGETHER = 4
GROUPS = HEADS // TOGETHER
LANES = TOGETHER * HEAD
SCALE = HEAD ** (-0.5)
BF = jnp.bfloat16
F32 = jnp.float32
ANY = pl.BlockSpec(memory_space=pl.ANY)
SMEM = pl.BlockSpec(memory_space=pltpu.SMEM)
VMEM = pl.BlockSpec(memory_space=pltpu.VMEM)


def swap(value, axis, distance):
    size = lax.axis_size(axis)
    return lax.ppermute(value, axis, [(i, i ^ distance) for i in range(size)])


def after(value, *others):
    return lax.optimization_barrier((value, *others))[0] if others else value


def fsdp_split(size):
    slow = 4 if size % 4 == 0 else 1
    return slow, size // slow


def dot(left, right):
    return jnp.dot(left, right, preferred_element_type=F32)


def dot_nt(left, right):
    return lax.dot_general(left, right, (((1,), (1,)), ((), ())), preferred_element_type=F32)


def dot_tn(left, right):
    return lax.dot_general(left, right, (((0,), (0,)), ((), ())), preferred_element_type=F32)


def rows_of(start, size):
    return pl.ds(pl.multiple_of(start, 16), size)


def block(ref, by_rows, shard, which):
    if by_rows:
        return ref.at[shard, pl.ds(which * 2, 2)]
    rows = ref.shape[1] // SHARDS[0]
    return ref.at[pl.ds(which * 2, 2), rows_of(shard * rows, rows)]


SHARDS = [0]


class Copies:
    def __init__(self, sems):
        self.sems = sems
        self.next = 0

    def start(self, source, target):
        copy = pltpu.make_async_copy(source, target, self.sems.at[self.next])
        self.next += 1
        copy.start()
        return copy


def wait_all(copies):
    for copy in copies:
        copy.wait()


def load_weight(where, whole, by_rows, weights, copies):
    z, y, c = where[0], where[1], where[2]
    started = []
    for which, pieces in ((c, weights[0]), (1 - c, weights[1])):
        fast = len(pieces)
        for b, piece in enumerate(pieces):
            for k in range(piece.shape[0]):
                target = block(whole, by_rows, (z ^ k) * fast + (y ^ b), which)
                started.append(copies.start(piece.at[k], target))
    return started


def load_dense(where, whole, by_rows, weights, copies):
    c = where[2]
    started = []
    for which, shards in ((c, weights[0]), (1 - c, weights[1])):
        for shard in range(shards.shape[0]):
            source = shards.at[shard, pl.ds(2 if by_rows else 0, 2)]
            started.append(copies.start(source, block(whole, by_rows, shard, which)))
    return started


def store_grad(where, whole, near, far, theirs, copies):
    z, y, c = where[0], where[1], where[2]
    fast, slow = len(theirs), near.shape[0]
    started = []
    for b in range(fast):
        for k in range(slow):
            shard = (z ^ k) * fast + (y ^ b)
            mine = far.at[b - 1, k] if b else near.at[k]
            started.append(copies.start(block(whole, False, shard, 1 - c), theirs[b].at[k]))
            started.append(copies.start(block(whole, False, shard, c), mine))
    return started


def store_dense(where, whole, by_rows, mine, theirs, copies):
    c = where[2]
    started = []
    for shard in range(mine.shape[0]):
        started.append(copies.start(block(whole, by_rows, shard, 1 - c), theirs.at[shard]))
        started.append(copies.start(block(whole, by_rows, shard, c), mine.at[shard]))
    return started


def my_examples(where, source, target, copies):
    count = target.shape[0]
    return copies.start(source.at[pl.ds(where[3] * count, count)], target)


def normalise(values):
    centred = values - jnp.mean(values, axis=-1, keepdims=True)
    scale = lax.rsqrt(jnp.mean(centred * centred, axis=-1, keepdims=True) + 1e-06)
    return centred * scale, scale


def norm_back(grad, gain, hat, scale):
    inner = grad * gain
    mean = jnp.mean(inner, axis=-1, keepdims=True)
    along = jnp.mean(inner * hat, axis=-1, keepdims=True)
    return (
        scale * (inner - mean - hat * along),
        jnp.sum(grad * hat, axis=0, keepdims=True),
        jnp.sum(grad, axis=0, keepdims=True),
    )


def head_mask(rows):
    shape = (TOGETHER * rows, LANES)
    row = lax.broadcasted_iota(jnp.int32, shape, 0) // rows
    lane = lax.broadcasted_iota(jnp.int32, shape, 1) // HEAD
    return (row == lane).astype(F32)


def stack_heads(value, mask):
    return (jnp.concatenate([value] * TOGETHER, axis=0).astype(F32) * mask).astype(BF)


def merge_heads(value, mask):
    rows = value.shape[0] // TOGETHER
    value = value * mask
    total = value[:rows]
    for h in range(1, TOGETHER):
        total = total + value[h * rows : (h + 1) * rows]
    return total


def columns(j, width):
    return slice(j * width, (j + 1) * width)


def self_forward(
    group, where, suffix, small, weights, x1, a1, qkv, p1, o1, vec, weight, start, sems
):
    rows, width = x1.shape
    copies = Copies(sems)
    first = my_examples(where, suffix, start, copies)
    loads = load_weight(where, weight, False, weights, copies)
    fast = len(weights[0])
    part = width // small.shape[0]
    lane = lax.broadcasted_iota(jnp.int32, (128, width), 0)
    place = lax.broadcasted_iota(jnp.int32, (128, width), 1) - lane
    together = jnp.zeros(vec.shape, F32)
    for i in range(small.shape[0]):
        shard = (where[0] ^ (i // fast)) * fast + (where[1] ^ (i % fast))
        chosen = ((place == shard * part) & (lane < part)).astype(F32).astype(BF)
        together = together + dot(small[i], chosen)
    vec[...] = together
    first.wait()
    values = start[...].reshape(rows, width).astype(F32)
    hat, _ = normalise(values)
    a1[...] = (hat * vec[0:1, :] + vec[1:2, :]).astype(BF)
    wait_all(loads)
    for j in range(3):
        qkv[:, columns(j, width)] = dot(a1[...], weight[j]).astype(BF)
    mask = head_mask(group)
    length = suffix.shape[1]
    shape = (TOGETHER * group, group)
    row = lax.broadcasted_iota(jnp.int32, shape, 0) % group
    col = lax.broadcasted_iota(jnp.int32, shape, 1)
    seen = (row // length == col // length) & (row >= col)
    for r in range(rows // group):
        here = columns(r, group)
        for g in range(GROUPS):
            lanes = [slice(i * width + g * LANES, i * width + (g + 1) * LANES) for i in range(3)]
            queries = stack_heads(qkv[here, lanes[0]], mask)
            scores = dot_nt(queries, qkv[here, lanes[1]]) * SCALE
            scores = jnp.where(seen, scores, -1e30)
            powers = jnp.exp(scores - jnp.max(scores, axis=-1, keepdims=True))
            probs = (powers / jnp.sum(powers, axis=-1, keepdims=True)).astype(BF)
            p1[r * GROUPS + g] = probs
            found = dot(probs, qkv[here, lanes[2]])
            o1[here, lanes[0]] = merge_heads(found, mask).astype(BF)
    x1[...] = values + dot(o1[...], weight[3])


def cross_forward(
    where, counts, x1, vec, memory, weights, x2, a2, q2, kv, p2, o2, weight, sems
):
    rows, width = x1.shape
    examples = pl.num_programs(0)
    e = pl.program_id(0)
    total = kv.shape[1]
    length = p2.shape[2] // TOGETHER

    @pl.when(e == 0)
    def _():
        loads = load_weight(where, weight, False, weights, Copies(sems))
        hat, _ = normalise(x1[...])
        a2[...] = (hat * vec[2:3, :] + vec[3:4, :]).astype(BF)
        wait_all(loads)
        q2[...] = dot(a2[...], weight[0]).astype(BF)

    tokens = memory[...].reshape(total, width)
    for j in range(2):
        kv[0, :, columns(j, width)] = dot(tokens, weight[1 + j]).astype(BF)
    mask = head_mask(length)
    position = lax.broadcasted_iota(jnp.int32, (1, total), 1)
    valid = position < counts[where[3] * examples + e]
    here = rows_of(e * length, length)
    probs = []
    for g in range(GROUPS):
        lanes = columns(g, LANES)
        queries = stack_heads(q2[here, lanes], mask)
        scores = dot_nt(queries, kv[0, :, lanes]) * SCALE
        scores = jnp.where(valid, scores, -1e30)
        top = jnp.maximum(jnp.max(scores, axis=-1, keepdims=True), 0.0)
        powers = jnp.exp(scores - top)
        weight_sum = jnp.sum(powers, axis=-1, keepdims=True) + jnp.exp(-top)
        probs.append((powers / weight_sum).astype(BF))
    for g in range(GROUPS):
        p2[0, g] = probs[g]
        found = dot(probs[g], kv[0, :, width + g * LANES : width + (g + 1) * LANES])
        o2[here, columns(g, LANES)] = merge_heads(found, mask).astype(BF)

    @pl.when(e == examples - 1)
    def _():
        x2[...] = x1[...] + dot(o2[...], weight[3])


def dense_inner(
    where, x2, vec, bias, cotangent, weights, a3, h, slope, mine, theirs,
    weight, grad, cot, sems,
):
    rows, width = x2.shape
    copies = Copies(sems)
    cot_copy = my_examples(where, cotangent, cot, copies)
    loads = load_dense(where, weight, False, weights, copies)
    hat, _ = normalise(x2[...])
    a3[...] = (hat * vec[4:5, :] + vec[5:6, :]).astype(BF)
    cot_copy.wait()
    gy = cot[...].reshape(rows, width)
    wait_all(loads)
    flat = grad.shape[0] * grad.shape[1] * grad.shape[2]
    step = flat // grad.shape[0]
    for j in range(4):
        for half in range(2):
            cols = slice(j * width + half * 384, j * width + (half + 1) * 384)
            u = dot(a3[...], weight[j, :, half * 384 : (half + 1) * 384]) + bias[:, cols]
            square = u * u
            t = jnp.tanh(0.7978845608 * u * (1.0 + 0.044715 * square))
            h[:, cols] = (0.5 * u * (1.0 + t)).astype(BF)
            slope[:, cols] = (
                0.5 * (1.0 + t)
                + (0.5 * 0.7978845608) * u * (1.0 - t * t) * (1.0 + (3.0 * 0.044715) * square)
            ).astype(BF)
            part = dot_tn(h[:, cols], gy).astype(BF)
            per = 384 // step
            grad[cols.start // step : cols.start // step + per] = part.reshape(
                (per,) + grad.shape[1:]
            )
    wait_all(store_dense(where, grad, True, mine, theirs, Copies(sems)))


def dense_outer(
    where, x2, vec, a3, h, slope, cotangent, weights, y, du, vecs, bias_grad, mine, theirs,
    weight, grad, cot, sems,
):
    rows, width = x2.shape
    copies = Copies(sems)
    cot_copy = my_examples(where, cotangent, cot, copies)
    wait_all(load_dense(where, weight, True, weights, copies))
    cot_copy.wait()
    gy = cot[...].reshape(rows, width)
    shards = weight.shape[0]
    step = weight.shape[1] * weight.shape[2]
    whole = weight[...].reshape(shards * step, width)
    for j in range(4):
        cols = columns(j, width)
        low = (dot_nt(gy, whole[cols]) * slope[:, cols].astype(F32)).astype(BF)
        du[:, cols] = low
        bias_grad[:, cols] = jnp.sum(low.astype(F32), axis=0, keepdims=True)
        grad[j] = dot_tn(a3[...], low).astype(BF)
    started = store_dense(where, grad, False, mine, theirs, Copies(sems))
    result = x2[...] + dot(h[...], whole) + vec[6:7, :]
    y[...] = result.astype(BF).reshape(y.shape)
    vecs[...] = jnp.sum(gy.astype(F32), axis=0, keepdims=True)
    wait_all(started)


def dense_back(where, x2, vec, du, cotangent, weights, gx2, vecs, weight, cot, sems):
    rows, width = x2.shape
    copies = Copies(sems)
    cot_copy = my_examples(where, cotangent, cot, copies)
    loads = load_dense(where, weight, False, weights, copies)
    hat, scale = normalise(x2[...])
    cot_copy.wait()
    wait_all(loads)
    da3 = dot_nt(du[:, columns(0, width)], weight[0])
    for j in range(1, 4):
        da3 = da3 + dot_nt(du[:, columns(j, width)], weight[j])
    back, gain_grad, shift_grad = norm_back(da3, vec[4:5, :], hat, scale)
    gx2[...] = cot[...].reshape(rows, width).astype(F32) + back
    vecs[0:1, :] = gain_grad
    vecs[1:2, :] = shift_grad


def cross_backward(
    where, x1, vec, gx2, q2, kv, p2, weights, gx1, vecs, dkv, dq2, out_mem, weight, do2, sems
):
    rows, width = x1.shape
    examples = pl.num_programs(0)
    e = pl.program_id(0)
    length = p2.shape[2] // TOGETHER

    @pl.when(e == 0)
    def _():
        wait_all(load_weight(where, weight, False, weights, Copies(sems)))
        do2[...] = dot_nt(gx2[...].astype(BF), weight[3]).astype(BF)

    mask = head_mask(length)
    here = rows_of(e * length, length)
    for g in range(GROUPS):
        lanes = columns(g, LANES)
        value_lanes = slice(width + g * LANES, width + (g + 1) * LANES)
        queries = stack_heads(q2[here, lanes], mask)
        grads = stack_heads(do2[here, lanes], mask)
        probs = p2[0, g]
        dp = dot_nt(grads, kv[0, :, value_lanes])
        wide = probs.astype(F32)
        row_sum = jnp.sum(wide * dp, axis=-1, keepdims=True)
        dz = (wide * (dp - row_sum)).astype(BF)
        dkv[0, :, value_lanes] = dot_tn(probs, grads).astype(BF)
        dkv[0, :, lanes] = (dot_tn(dz, queries) * SCALE).astype(BF)
        dq2[here, lanes] = (merge_heads(dot(dz, kv[0, :, lanes]), mask) * SCALE).astype(BF)
    back = dot_nt(dkv[0, :, :width], weight[1]) + dot_nt(dkv[0, :, width:], weight[2])
    out_mem[...] = back.astype(BF).reshape(out_mem.shape)

    @pl.when(e == examples - 1)
    def _():
        hat, scale = normalise(x1[...])
        back, gain_grad, shift_grad = norm_back(
            dot_nt(dq2[...], weight[0]), vec[2:3, :], hat, scale
        )
        gx1[...] = gx2[...] + back
        vecs[0:1, :] = gain_grad
        vecs[1:2, :] = shift_grad


def cross_grads(
    where, gx2, a2, o2, dq2, dkv, all_memory, near, far, theirs, grad, memory, sems
):
    rows, width = gx2.shape
    examples, total, _ = memory.shape
    mem, _, slots, _ = all_memory.shape
    copies = Copies(sems)
    loads = [
        copies.start(all_memory.at[d], memory.at[:, d * slots : (d + 1) * slots, :])
        for d in range(mem)
    ]
    grad[0] = dot_tn(a2[...], dq2[...]).astype(BF)
    grad[3] = dot_tn(o2[...], gx2[...].astype(BF)).astype(BF)
    wait_all(loads)
    flat = memory[...].reshape(examples * total, width)
    for j in range(2):
        part = dkv[:, :, columns(j, width)].reshape(examples * total, width)
        grad[1 + j] = dot_tn(flat, part).astype(BF)
    wait_all(store_grad(where, grad, near, far, theirs, Copies(sems)))


def self_backward(
    group, where, suffix, vec, gx1, a1, qkv, p1, o1, parts, weights, suffix_grad, vecs,
    near, far, theirs, weight, start, grad, dqkv, do1, sems,
):
    rows, width = gx1.shape
    copies = Copies(sems)
    start_copy = my_examples(where, suffix, start, copies)
    loads = load_weight(where, weight, False, weights, copies)
    gs = gx1[...].astype(BF)
    grad[3] = dot_tn(o1[...], gs).astype(BF)
    wait_all(loads)
    do1[...] = dot_nt(gs, weight[3]).astype(BF)
    mask = head_mask(group)
    for r in range(rows // group):
        here = columns(r, group)
        for g in range(GROUPS):
            lanes = [slice(i * width + g * LANES, i * width + (g + 1) * LANES) for i in range(3)]
            queries = stack_heads(qkv[here, lanes[0]], mask)
            grads = stack_heads(do1[here, lanes[0]], mask)
            probs = p1[r * GROUPS + g]
            dp = dot_nt(grads, qkv[here, lanes[2]])
            wide = probs.astype(F32)
            row_sum = jnp.sum(wide * dp, axis=-1, keepdims=True)
            dz = (wide * (dp - row_sum)).astype(BF)
            dqkv[here, lanes[2]] = dot_tn(probs, grads).astype(BF)
            dqkv[here, lanes[1]] = (dot_tn(dz, queries) * SCALE).astype(BF)
            dq = merge_heads(dot(dz, qkv[here, lanes[1]]), mask) * SCALE
            dqkv[here, lanes[0]] = dq.astype(BF)
    for j in range(3):
        grad[j] = dot_tn(a1[...], dqkv[:, columns(j, width)]).astype(BF)
    start_copy.wait()
    started = store_grad(where, grad, near, far, theirs, Copies(sems))
    da1 = dot_nt(dqkv[:, columns(0, width)], weight[0])
    for j in range(1, 3):
        da1 = da1 + dot_nt(dqkv[:, columns(j, width)], weight[j])
    hat, scale = normalise(start[...].reshape(rows, width).astype(F32))
    back, gain_grad, shift_grad = norm_back(da1, vec[0:1, :], hat, scale)
    suffix_grad[...] = (gx1[...] + back).astype(BF).reshape(suffix_grad.shape)
    found = [gain_grad, shift_grad]
    for ref in parts:
        for r in range(ref.shape[0]):
            found += [ref[r : r + 1, columns(j, width)] for j in range(ref.shape[1] // width)]
    found.append(jnp.zeros((vecs.shape[0] - len(found), width), F32))
    vecs[...] = jnp.concatenate(found, axis=0).astype(BF)
    wait_all(started)


def run(kernel, inputs, outputs, scratch, copies, grid=()):
    def leaf(x):
        return isinstance(x, tuple) and len(x) == 2 and isinstance(x[0], pl.BlockSpec)

    flat_in, tree_in = jax.tree.flatten(inputs, is_leaf=leaf)
    flat_out, tree_out = jax.tree.flatten(outputs, is_leaf=leaf)

    def body(*refs):
        first, second = len(flat_in), len(flat_in) + len(flat_out)
        given = jax.tree.unflatten(tree_in, refs[:first])
        taken = jax.tree.unflatten(tree_out, refs[first:second])
        kernel(*given, *taken, *refs[second:])

    found = pl.pallas_call(
        body,
        grid=grid,
        in_specs=[spec for spec, _ in flat_in],
        out_specs=[spec for spec, _ in flat_out],
        out_shape=[shape for _, shape in flat_out],
        scratch_shapes=scratch + [pltpu.SemaphoreType.DMA((copies,))],
        compiler_params=pltpu.CompilerParams(vmem_limit_bytes=56 * 1024 * 1024),
        cost_estimate=pl.CostEstimate(
            flops=0, bytes_accessed=0, transcendentals=0
        ),
    )(*[x for _, x in flat_in])
    return jax.tree.unflatten(tree_out, found)


def shape_of(dims, dtype):
    return jax.ShapeDtypeStruct(tuple(dims), dtype)


def gather_slow(value, slow, fast):
    return jnp.stack([value] + [swap(value, "fsdp", k * fast) for k in range(1, slow)])


class Gather:
    def __init__(self, half, slow, fast):
        self.half, self.slow, self.fast = half, slow, fast

    def send_slow(self, *others):
        self.near = gather_slow(after(self.half, *others), self.slow, self.fast)

    def send_fast(self, *others):
        self.near = after(self.near, *others)
        self.near_other = swap(self.near, "mem", 1)
        self.far = [swap(self.near, "fsdp", b) for b in range(1, self.fast)]

    def whole(self):
        mine = [self.near] + self.far
        theirs = [self.near_other] + [swap(piece, "mem", 1) for piece in self.far]
        return [[(ANY, x) for x in some] for some in (mine, theirs)]


class Scatter:
    def __init__(self, grads, slow, fast, *others, vectors=None):
        self.near, self.far, theirs = grads
        self.slow, self.fast, self.vectors = slow, fast, vectors
        theirs = [after(part, *others) for part in theirs]
        self.sent = [None] * fast
        for b in range(1, fast):
            self.sent[b] = swap(theirs[b] if b > 1 else self.pack(theirs[b]), "mem", 1)
        self.sent[0] = swap(theirs[0], "mem", 1)
        if vectors is not None:
            self.sent[1], came = self.unpack(self.sent[1], theirs[1].shape)
            self.vectors = vectors.astype(F32) + came

    def pack(self, value):
        if self.vectors is None:
            return value
        width = value.shape[-1]
        return jnp.concatenate([value.reshape(-1, width), self.vectors.astype(BF)])

    def unpack(self, value, shape):
        if self.vectors is None:
            return value, 0.0
        rows = value.shape[0] - self.vectors.shape[0]
        return value[:rows].reshape(shape), value[rows:].astype(F32)

    def add_cores(self):
        self.out = [
            self.pack((self.far[b].astype(F32) + self.sent[b + 1].astype(F32)).astype(BF))
            for b in range(self.fast - 1)
        ]
        return self.out

    def send_fast(self):
        self.came = [swap(part, "fsdp", b + 1) for b, part in enumerate(self.out)]

    def add_fast(self, *others):
        total = after(self.near, *others).astype(F32) + self.sent[0].astype(F32)
        vectors = 0.0 if self.vectors is None else self.vectors.astype(BF).astype(F32)
        for part in self.came:
            part, more = self.unpack(part, total.shape)
            total = total + part.astype(F32)
            vectors = vectors + more
        self.total = total.astype(BF).reshape(self.slow, -1, total.shape[-1])
        if self.vectors is not None:
            low = jnp.broadcast_to(vectors.astype(BF), (self.slow,) + vectors.shape)
            self.total = jnp.concatenate([self.total, low], axis=1)
        return self.total

    def send_slow(self):
        self.came = [swap(self.total[k], "fsdp", k * self.fast) for k in range(1, self.slow)]

    def add_slow(self, *others):
        total, came, _ = lax.optimization_barrier((self.total, self.came, others))
        return sum(part.astype(F32) for part in [total[0], *came])


def add_replicas(value, rows, across, c):
    k = 1
    while 2 * k < across:
        low = value.astype(BF)
        value = low.astype(F32) + swap(low, "mem", 2 * k).astype(F32)
        k *= 2
    low = value.astype(BF)
    halves = [low, swap(low, "mem", 2 * k)] if across > 1 else [low]
    others = [swap(half[: 2 * rows], "mem", 1) for half in halves]
    mine = sum(half.astype(F32) for half in halves)
    other = sum(half.astype(F32) for half in others)
    vectors, mine = mine[2 * rows :], mine[: 2 * rows]
    first = jnp.where(c == 0, mine, other)
    second = jnp.where(c == 0, other, mine)
    return [first[:rows], first[rows:], second[:rows], second[rows:]], vectors


def place_rows(where, pieces, *refs):
    outs, (scratch, sems) = refs[:-2], refs[-2:]
    examples = pieces[0].shape[1]
    copies = Copies(sems)
    loads = [copies.start(piece, scratch.at[d]) for d, piece in enumerate(pieces)]
    stores = []
    for d, load in enumerate(loads):
        load.wait()
        for i, out in enumerate(outs):
            target = out.at[pl.ds((where[3] ^ d) * examples, examples)]
            stores.append(copies.start(scratch.at[d, i], target))
    wait_all(stores)


def spread_rows(where, values, mem):
    value = jnp.stack(values)
    blocks = [None] * mem
    blocks[0] = value
    for d in range(2, mem, 2):
        blocks[d] = swap(value, "mem", d)
    for d in range(0, mem, 2):
        blocks[d + 1] = swap(blocks[d], "mem", 1)
    whole = shape_of((mem * value.shape[1],) + value.shape[2:], BF)
    return run(
        place_rows,
        [(SMEM, where), [(ANY, piece) for piece in blocks]],
        [(ANY, whole)] * len(values),
        [pltpu.VMEM((mem,) + value.shape, BF)],
        mem * (1 + len(values)),
    )


def per_device(
    suffix,
    memory,
    counts,
    cotangent,
    self_norm_gain,
    self_norm_bias,
    self_query,
    self_key,
    self_value,
    self_output,
    cross_norm_gain,
    cross_norm_bias,
    cross_query,
    cross_key,
    cross_value,
    cross_output,
    dense_norm_gain,
    dense_norm_bias,
    dense_in,
    dense_in_bias,
    dense_out,
    dense_out_bias,
):
    f = lax.axis_index("fsdp")
    m = lax.axis_index("mem")
    c = m % 2
    fsdp = lax.axis_size("fsdp")
    mem = lax.axis_size("mem")
    across = mem // 2
    slow, fast = fsdp_split(fsdp)
    SHARDS[0] = fsdp
    where = jnp.stack([f // fast, f % fast, c, m]).astype(jnp.int32)
    examples = suffix.shape[0] // mem
    length = suffix.shape[1]
    width = suffix.shape[2]
    slots = memory.shape[1]
    total = mem * slots
    rows = examples * length
    inner = dense_in.shape[1]
    part = width // fsdp
    group = min(128, rows)
    blocks = 2 * fsdp

    def gather(matrices):
        half = jnp.where(c == 0, jnp.stack(matrices[:2]), jnp.stack(matrices[2:]))
        return Gather(half, slow, fast)

    self_gather = gather([self_query, self_key, self_value, self_output])
    cross_gather = gather([cross_query, cross_key, cross_value, cross_output])
    dense = [
        [dense_in[:, columns(2 * i + j, width)] for j in range(2)]
        + [dense_out[columns(2 * i + j, part)] for j in range(2)]
        for i in range(2)
    ]
    dense = jnp.where(c == 0, jnp.stack(dense[0]), jnp.stack(dense[1]))
    dense_mine = lax.all_gather(dense, "fsdp")
    small = [
        self_norm_gain,
        self_norm_bias,
        cross_norm_gain,
        cross_norm_bias,
        dense_norm_gain,
        dense_norm_bias,
        dense_out_bias,
    ]
    small += [dense_in_bias[columns(j, part)] for j in range(4)]
    small = sum(
        jnp.pad(value[None], ((i, 15 - i), (0, 128 - part))) for i, value in enumerate(small)
    )

    def exchange(value):
        blocks = value.reshape((mem, examples) + value.shape[1:])
        return lax.all_to_all(blocks, "mem", 0, 0, tiled=True)

    all_memory = exchange(memory)
    small = jnp.concatenate([small] + [swap(small, "fsdp", b) for b in range(1, fast)])
    self_gather.send_slow()
    sent = [self_gather.near, small]
    self_gather.send_fast(*sent)
    cross_gather.send_slow(*sent)
    small = after(small, *sent)
    small = gather_slow(small, slow, fast).reshape(slow * fast, 16, 128)
    sent = [*self_gather.far, cross_gather.near, all_memory, small]
    self_gather.far = [after(piece, *sent) for piece in self_gather.far]
    self_weights = self_gather.whole()
    cross_gather.send_fast(*self_gather.far)

    half = (2, part, width)
    grads_like = [
        (ANY, shape_of((slow,) + half, BF)),
        (ANY, shape_of((fast - 1, slow) + half, BF)),
        [(ANY, shape_of((slow,) + half, BF))] * fast,
    ]

    dense_like = [(ANY, shape_of((fsdp,) + half, BF))] * 2

    def flat(dims, dtype):
        return (VMEM, shape_of(dims, dtype))

    def per_example(value):
        dims = value.shape[1:]
        spec = pl.BlockSpec((1,) + dims, lambda e: (e,) + (0,) * len(dims))
        return (spec, value)

    def slots_of_example(value):
        spec = pl.BlockSpec((mem, 1, slots, width), lambda e: (0, e, 0, 0))
        return (spec, value)

    def scratch(*dims):
        return pltpu.VMEM(dims, BF)

    def scatter(grads, *others, vectors=None):
        return Scatter(grads, slow, fast, *others, vectors=vectors)

    wide = (rows, width)
    square = scratch(4, width, width)
    own_rows = scratch(examples, length, width)
    x1, a1, qkv, p1, o1, vec = run(
        functools.partial(self_forward, group),
        [(SMEM, where), (ANY, suffix), (VMEM, small), self_weights],
        [
            flat(wide, F32),
            flat(wide, BF),
            flat((rows, 3 * width), BF),
            flat((rows // group * GROUPS, TOGETHER * group, group), BF),
            flat(wide, BF),
            flat((16, width), F32),
        ],
        [square, own_rows],
        1 + blocks,
    )
    cross_gather.far = [after(piece, x1) for piece in cross_gather.far]
    cross_weights = cross_gather.whole()
    x2, a2, q2, kv, p2, o2 = run(
        cross_forward,
        [(SMEM, where), (SMEM, counts), (VMEM, x1), (VMEM, vec)]
        + [slots_of_example(all_memory), cross_weights],
        [
            flat(wide, F32),
            flat(wide, BF),
            flat(wide, BF),
            per_example(shape_of((examples, total, 2 * width), BF)),
            per_example(shape_of((examples, GROUPS, TOGETHER * length, total), BF)),
            flat(wide, BF),
        ],
        [square],
        blocks,
        (examples,),
    )
    bias_in = jnp.take(after(small, x1)[:, 7:11, :part], jnp.arange(fsdp) ^ f, axis=0)
    bias_in = bias_in.astype(F32).reshape(1, inner)
    dense_mine = after(dense_mine, x2)
    dense_weights = [(ANY, dense_mine), (ANY, swap(dense_mine, "mem", 1))]
    a3, h, slope, *grads = run(
        dense_inner,
        [(SMEM, where), (VMEM, x2), (VMEM, vec), (VMEM, bias_in), (ANY, cotangent), dense_weights],
        [flat(wide, BF), flat((rows, inner), BF), flat((rows, inner), BF)] + dense_like,
        [square, scratch(fsdp, 4, part, width), own_rows],
        1 + blocks,
    )
    def add_cores(grads, *others):
        mine, theirs = grads
        return mine.astype(F32) + swap(after(theirs, *others), "mem", 1).astype(F32)

    out_sum = add_cores(grads).astype(BF)
    y, du, vecs_y, bias_grad, *grads = run(
        dense_outer,
        [(SMEM, where), (VMEM, after(x2, out_sum)), (VMEM, vec), (VMEM, a3), (VMEM, h)]
        + [(VMEM, slope), (ANY, cotangent), dense_weights],
        [
            flat((examples, length, width), BF),
            flat((rows, inner), BF),
            flat((1, width), F32),
            flat((1, inner), F32),
        ]
        + dense_like,
        [scratch(fsdp, 4, part, width), square, own_rows],
        1 + blocks,
    )
    in_grads = grads
    gx2, vecs_dense = run(
        dense_back,
        [(SMEM, where), (VMEM, x2), (VMEM, vec), (VMEM, du), (ANY, cotangent), dense_weights],
        [flat(wide, F32), flat((2, width), F32)],
        [square, own_rows],
        1 + blocks,
    )
    dense_grads = jnp.concatenate([out_sum, add_cores(in_grads, gx2).astype(BF)], axis=1)
    dense_sum = lax.psum_scatter(dense_grads, "fsdp", scatter_dimension=0)
    gx1, vecs_cross, dkv, dq2, grad_memory = run(
        cross_backward,
        [(SMEM, where), (VMEM, x1), (VMEM, vec), (VMEM, after(gx2, dense_grads)), (VMEM, q2)]
        + [per_example(kv), per_example(p2), cross_weights],
        [
            flat(wide, F32),
            flat((2, width), F32),
            per_example(shape_of((examples, total, 2 * width), BF)),
            flat(wide, BF),
            slots_of_example(shape_of((mem, examples, slots, width), BF)),
        ],
        [square, scratch(*wide)],
        blocks,
        (examples,),
    )
    memory_grad = exchange(grad_memory.reshape(memory.shape)).reshape(memory.shape)
    grads = run(
        cross_grads,
        [(SMEM, where), (VMEM, gx2), (VMEM, a2), (VMEM, o2), (VMEM, dq2)]
        + [(VMEM, dkv), (ANY, all_memory)],
        grads_like,
        [square, scratch(examples, total, width)],
        max(mem, blocks),
    )
    cross_grads_out = grads
    suffix_part, vecs_self, *grads = run(
        functools.partial(self_backward, group),
        [(SMEM, where), (ANY, suffix), (VMEM, vec), (VMEM, gx1), (VMEM, a1)]
        + [(VMEM, qkv), (VMEM, p1), (VMEM, o1)]
        + [[(VMEM, x) for x in (vecs_cross, vecs_dense, vecs_y, bias_grad)], self_weights],
        [flat((examples, length, width), BF), flat((16, width), BF)] + grads_like,
        [square, own_rows, square, scratch(rows, 3 * width), scratch(*wide)],
        1 + blocks,
    )
    cross_scatter = scatter(cross_grads_out, suffix_part)
    self_scatter = scatter(grads, memory_grad, vectors=vecs_self)
    cross_scatter.add_cores()
    cross_scatter.send_fast()
    self_scatter.add_cores()
    self_scatter.send_fast()
    cross_scatter.add_fast(dense_sum)
    cross_scatter.send_slow()
    self_total = self_scatter.add_fast()
    self_scatter.send_slow()

    def finish(value, rows):
        return add_replicas(value, rows, across, c)

    grad_cross, _ = finish(cross_scatter.add_slow(self_total), part)
    block_output, suffix_grad = spread_rows(where, [y, after(suffix_part, self_total)], mem)
    dense_sum = after(dense_sum, self_total).reshape(4 * part, width)
    (out_low, in_low, out_high, in_high), _ = finish(dense_sum, 2 * part)
    grad_in = jnp.concatenate([in_low[:part], in_low[part:], in_high[:part], in_high[part:]], axis=1)
    grad_out = jnp.concatenate([out_low, out_high])
    grad_self, vectors = finish(
        self_scatter.add_slow(block_output, grad_in, grad_out, *grad_cross), part
    )

    def vector(i):
        return lax.dynamic_slice(vectors, (i, f * part), (1, part)).reshape(part)

    return (
        block_output,
        suffix_grad,
        memory_grad,
        vector(0),
        vector(1),
        *grad_self,
        vector(2),
        vector(3),
        *grad_cross,
        vector(4),
        vector(5),
        grad_in,
        lax.dynamic_slice_in_dim(vectors[7:11].reshape(-1), f * (inner // fsdp), inner // fsdp, 0),
        grad_out,
        vector(6),
    )


def solution(mesh):
    rows = P("fsdp", None, None)
    matrix = P("fsdp", None)
    vector = P("fsdp")
    attention = (vector, vector, matrix, matrix, matrix, matrix)
    params = attention + attention + (vector, vector, matrix, vector, matrix, vector)
    return jax.shard_map(
        per_device,
        mesh=mesh,
        in_specs=(rows, P("fsdp", "mem", None), vector, rows) + params,
        out_specs=(rows, rows, P("fsdp", "mem", None)) + params,
        check_vma=False,
    )
```

```python
import functools

import jax
import jax.numpy as jnp
from jax import lax
from jax.experimental import pallas as pl
from jax.experimental.pallas import tpu as pltpu
from jax.sharding import PartitionSpec as P

HEADS = 12
HEAD = 64
TOGETHER = 4
GROUPS = HEADS // TOGETHER
LANES = TOGETHER * HEAD
SCALE = HEAD ** (-0.5)
BF = jnp.bfloat16
F32 = jnp.float32
ANY = pl.BlockSpec(memory_space=pl.ANY)
SMEM = pl.BlockSpec(memory_space=pltpu.SMEM)
VMEM = pl.BlockSpec(memory_space=pltpu.VMEM)


def swap(value, axis, distance):
    size = lax.axis_size(axis)
    return lax.ppermute(value, axis, [(i, i ^ distance) for i in range(size)])


def after(value, *others):
    return lax.optimization_barrier((value, *others))[0] if others else value


def fsdp_split(size):
    slow = 4 if size % 4 == 0 else 1
    return slow, size // slow


def dot(left, right):
    return jnp.dot(left, right, preferred_element_type=F32)


def dot_nt(left, right):
    return lax.dot_general(left, right, (((1,), (1,)), ((), ())), preferred_element_type=F32)


def dot_tn(left, right):
    return lax.dot_general(left, right, (((0,), (0,)), ((), ())), preferred_element_type=F32)


def rows_of(start, size):
    return pl.ds(pl.multiple_of(start, 16), size)


def block(ref, by_rows, shard, which):
    if by_rows:
        return ref.at[shard, pl.ds(which * 2, 2)]
    rows = ref.shape[1] // SHARDS[0]
    return ref.at[pl.ds(which * 2, 2), rows_of(shard * rows, rows)]


SHARDS = [0]


class Copies:
    def __init__(self, sems):
        self.sems = sems
        self.next = 0

    def start(self, source, target):
        copy = pltpu.make_async_copy(source, target, self.sems.at[self.next])
        self.next += 1
        copy.start()
        return copy


def wait_all(copies):
    for copy in copies:
        copy.wait()


def load_weight(where, whole, weights, copies):
    z, y, c = where[0], where[1], where[2]
    rows = whole.shape[1] // SHARDS[0]
    started = []
    for which, pieces in ((c, weights[0]), (1 - c, weights[1])):
        fast = len(pieces)
        for b, piece in enumerate(pieces):
            for k in range(piece.shape[0]):
                shard = (z ^ k) * fast + (y ^ b)
                for i in range(2):
                    source = piece.at[k, pl.ds(i * rows, rows)]
                    target = whole.at[2 * which + i, rows_of(shard * rows, rows)]
                    started.append(copies.start(source, target))
    return started


def load_dense(where, whole, by_rows, weights, copies):
    c = where[2]
    started = []
    for which, shards in ((c, weights[0]), (1 - c, weights[1])):
        for shard in range(shards.shape[0]):
            source = shards.at[shard, pl.ds(2 if by_rows else 0, 2)]
            started.append(copies.start(source, block(whole, by_rows, shard, which)))
    return started


def store_grad(where, whole, near, far, theirs, copies, absolute=False):
    z, y, c = where[0], where[1], where[2]
    if absolute:
        z = 0
    fast, slow = len(theirs), near.shape[0]
    started = []
    for b in range(fast):
        for k in range(slow):
            shard = (z ^ k) * fast + (y ^ b)
            mine = far.at[b - 1, k] if b else near.at[k]
            started.append(copies.start(block(whole, False, shard, 1 - c), theirs[b].at[k]))
            started.append(copies.start(block(whole, False, shard, c), mine))
    return started


def store_dense(where, whole, by_rows, mine, theirs, copies):
    c = where[2]
    started = []
    for shard in range(mine.shape[0]):
        started.append(copies.start(block(whole, by_rows, shard, 1 - c), theirs.at[shard]))
        started.append(copies.start(block(whole, by_rows, shard, c), mine.at[shard]))
    return started


def my_examples(where, source, target, copies):
    count = target.shape[0]
    return copies.start(source.at[pl.ds(where[3] * count, count)], target)


def normalise(values):
    centred = values - jnp.mean(values, axis=-1, keepdims=True)
    scale = lax.rsqrt(jnp.mean(centred * centred, axis=-1, keepdims=True) + 1e-06)
    return centred * scale, scale


def norm_back(grad, gain, hat, scale):
    inner = grad * gain
    mean = jnp.mean(inner, axis=-1, keepdims=True)
    along = jnp.mean(inner * hat, axis=-1, keepdims=True)
    return (
        scale * (inner - mean - hat * along),
        jnp.sum(grad * hat, axis=0, keepdims=True),
        jnp.sum(grad, axis=0, keepdims=True),
    )


def head_mask(rows):
    shape = (TOGETHER * rows, LANES)
    row = lax.broadcasted_iota(jnp.int32, shape, 0) // rows
    lane = lax.broadcasted_iota(jnp.int32, shape, 1) // HEAD
    return (row == lane).astype(F32)


def stack_heads(value, mask):
    return (jnp.concatenate([value] * TOGETHER, axis=0).astype(F32) * mask).astype(BF)


def merge_heads(value, mask):
    rows = value.shape[0] // TOGETHER
    value = value * mask
    total = value[:rows]
    for h in range(1, TOGETHER):
        total = total + value[h * rows : (h + 1) * rows]
    return total


def columns(j, width):
    return slice(j * width, (j + 1) * width)


def self_forward(
    group, where, suffix, weights, x1, a1, qkv, p1, o1, vec, weight, start, small, sems
):
    rows, width = x1.shape
    copies = Copies(sems)
    first = my_examples(where, suffix, start, copies)
    fast, slow = len(weights[0]), weights[0][0].shape[0]
    part = width // (fast * slow)
    vectors = []
    for b, piece in enumerate(weights[0]):
        for k in range(slow):
            source = piece.at[k, pl.ds(2 * part, 16), pl.ds(0, 128)]
            vectors.append(copies.start(source, small.at[b * slow + k]))
    loads = load_weight(where, weight, weights, copies)
    wait_all(vectors)
    lane = lax.broadcasted_iota(jnp.int32, (128, width), 0)
    place = lax.broadcasted_iota(jnp.int32, (128, width), 1) - lane
    together = jnp.zeros(vec.shape, F32)
    for i in range(fast * slow):
        shard = (where[0] ^ (i % slow)) * fast + (where[1] ^ (i // slow))
        chosen = ((place == shard * part) & (lane < part)).astype(F32).astype(BF)
        together = together + dot(small[i], chosen)
    vec[...] = together
    first.wait()
    values = start[...].reshape(rows, width).astype(F32)
    hat, _ = normalise(values)
    a1[...] = (hat * vec[0:1, :] + vec[1:2, :]).astype(BF)
    wait_all(loads)
    for j in range(3):
        qkv[:, columns(j, width)] = dot(a1[...], weight[j]).astype(BF)
    mask = head_mask(group)
    length = suffix.shape[1]
    shape = (TOGETHER * group, group)
    row = lax.broadcasted_iota(jnp.int32, shape, 0) % group
    col = lax.broadcasted_iota(jnp.int32, shape, 1)
    seen = (row // length == col // length) & (row >= col)
    for r in range(rows // group):
        here = columns(r, group)
        for g in range(GROUPS):
            lanes = [slice(i * width + g * LANES, i * width + (g + 1) * LANES) for i in range(3)]
            queries = stack_heads(qkv[here, lanes[0]], mask)
            scores = dot_nt(queries, qkv[here, lanes[1]]) * SCALE
            scores = jnp.where(seen, scores, -1e30)
            powers = jnp.exp(scores - jnp.max(scores, axis=-1, keepdims=True))
            probs = (powers / jnp.sum(powers, axis=-1, keepdims=True)).astype(BF)
            p1[r * GROUPS + g] = probs
            found = dot(probs, qkv[here, lanes[2]])
            o1[here, lanes[0]] = merge_heads(found, mask).astype(BF)
    x1[...] = values + dot(o1[...], weight[3])


def cross_forward(
    where, counts, x1, vec, memory, weights, x2, a2, q2, kv, p2, o2, weight, sems
):
    rows, width = x1.shape
    examples = pl.num_programs(0)
    e = pl.program_id(0)
    total = kv.shape[1]
    length = p2.shape[2] // TOGETHER

    @pl.when(e == 0)
    def _():
        loads = load_weight(where, weight, weights, Copies(sems))
        hat, _ = normalise(x1[...])
        a2[...] = (hat * vec[2:3, :] + vec[3:4, :]).astype(BF)
        wait_all(loads)
        q2[...] = dot(a2[...], weight[0]).astype(BF)

    tokens = memory[...].reshape(total, width)
    for j in range(2):
        kv[0, :, columns(j, width)] = dot(tokens, weight[1 + j]).astype(BF)
    mask = head_mask(length)
    position = lax.broadcasted_iota(jnp.int32, (1, total), 1)
    valid = position < counts[where[3] * examples + e]
    here = rows_of(e * length, length)
    probs = []
    for g in range(GROUPS):
        lanes = columns(g, LANES)
        queries = stack_heads(q2[here, lanes], mask)
        scores = dot_nt(queries, kv[0, :, lanes]) * SCALE
        scores = jnp.where(valid, scores, -1e30)
        top = jnp.maximum(jnp.max(scores, axis=-1, keepdims=True), 0.0)
        powers = jnp.exp(scores - top)
        weight_sum = jnp.sum(powers, axis=-1, keepdims=True) + jnp.exp(-top)
        probs.append((powers / weight_sum).astype(BF))
    for g in range(GROUPS):
        p2[0, g] = probs[g]
        found = dot(probs[g], kv[0, :, width + g * LANES : width + (g + 1) * LANES])
        o2[here, columns(g, LANES)] = merge_heads(found, mask).astype(BF)

    @pl.when(e == examples - 1)
    def _():
        x2[...] = x1[...] + dot(o2[...], weight[3])


def dense_inner(
    where, x2, vec, bias, cotangent, weights, a3, h, slope, mine, theirs,
    weight, grad, cot, sems,
):
    rows, width = x2.shape
    copies = Copies(sems)
    cot_copy = my_examples(where, cotangent, cot, copies)
    loads = load_dense(where, weight, False, weights, copies)
    hat, _ = normalise(x2[...])
    a3[...] = (hat * vec[4:5, :] + vec[5:6, :]).astype(BF)
    cot_copy.wait()
    gy = cot[...].reshape(rows, width)
    wait_all(loads)
    flat = grad.shape[0] * grad.shape[1] * grad.shape[2]
    step = flat // grad.shape[0]
    for j in range(4):
        for half in range(2):
            cols = slice(j * width + half * 384, j * width + (half + 1) * 384)
            u = dot(a3[...], weight[j, :, half * 384 : (half + 1) * 384]) + bias[:, cols]
            square = u * u
            t = jnp.tanh(0.7978845608 * u * (1.0 + 0.044715 * square))
            h[:, cols] = (0.5 * u * (1.0 + t)).astype(BF)
            slope[:, cols] = (
                0.5 * (1.0 + t)
                + (0.5 * 0.7978845608) * u * (1.0 - t * t) * (1.0 + (3.0 * 0.044715) * square)
            ).astype(BF)
            part = dot_tn(h[:, cols], gy).astype(BF)
            per = 384 // step
            grad[cols.start // step : cols.start // step + per] = part.reshape(
                (per,) + grad.shape[1:]
            )
    wait_all(store_dense(where, grad, True, mine, theirs, Copies(sems)))


def dense_outer(
    where, x2, vec, a3, h, slope, cotangent, weights, y, du, vecs, bias_grad, mine, theirs,
    weight, grad, cot, sems,
):
    rows, width = x2.shape
    copies = Copies(sems)
    cot_copy = my_examples(where, cotangent, cot, copies)
    wait_all(load_dense(where, weight, True, weights, copies))
    cot_copy.wait()
    gy = cot[...].reshape(rows, width)
    shards = weight.shape[0]
    step = weight.shape[1] * weight.shape[2]
    whole = weight[...].reshape(shards * step, width)
    for j in range(4):
        cols = columns(j, width)
        low = (dot_nt(gy, whole[cols]) * slope[:, cols].astype(F32)).astype(BF)
        du[:, cols] = low
        bias_grad[:, cols] = jnp.sum(low.astype(F32), axis=0, keepdims=True)
        grad[j] = dot_tn(a3[...], low).astype(BF)
    started = store_dense(where, grad, False, mine, theirs, Copies(sems))
    result = x2[...] + dot(h[...], whole) + vec[6:7, :]
    y[...] = result.astype(BF).reshape(y.shape)
    vecs[...] = jnp.sum(gy.astype(F32), axis=0, keepdims=True)
    wait_all(started)


def dense_back(where, x2, vec, du, cotangent, weights, gx2, vecs, weight, cot, sems):
    rows, width = x2.shape
    copies = Copies(sems)
    cot_copy = my_examples(where, cotangent, cot, copies)
    loads = load_dense(where, weight, False, weights, copies)
    hat, scale = normalise(x2[...])
    cot_copy.wait()
    wait_all(loads)
    da3 = dot_nt(du[:, columns(0, width)], weight[0])
    for j in range(1, 4):
        da3 = da3 + dot_nt(du[:, columns(j, width)], weight[j])
    back, gain_grad, shift_grad = norm_back(da3, vec[4:5, :], hat, scale)
    gx2[...] = cot[...].reshape(rows, width).astype(F32) + back
    vecs[0:1, :] = gain_grad
    vecs[1:2, :] = shift_grad


def cross_backward(
    where, x1, vec, gx2, q2, kv, p2, weights, gx1, vecs, dkv, dq2, out_mem, weight, do2, moved, sems
):
    rows, width = x1.shape
    examples = pl.num_programs(0)
    e = pl.program_id(0)
    length = p2.shape[2] // TOGETHER

    @pl.when(e == 0)
    def _():
        wait_all(load_weight(where, weight, weights, Copies(sems)))
        do2[...] = dot_nt(gx2[...].astype(BF), weight[3]).astype(BF)

    mask = head_mask(length)
    here = rows_of(e * length, length)
    for g in range(GROUPS):
        lanes = columns(g, LANES)
        value_lanes = slice(width + g * LANES, width + (g + 1) * LANES)
        queries = stack_heads(q2[here, lanes], mask)
        grads = stack_heads(do2[here, lanes], mask)
        probs = p2[0, g]
        dp = dot_nt(grads, kv[0, :, value_lanes])
        wide = probs.astype(F32)
        row_sum = jnp.sum(wide * dp, axis=-1, keepdims=True)
        dz = (wide * (dp - row_sum)).astype(BF)
        dkv[0, :, value_lanes] = dot_tn(probs, grads).astype(BF)
        dkv[0, :, lanes] = (dot_tn(dz, queries) * SCALE).astype(BF)
        dq2[here, lanes] = (merge_heads(dot(dz, kv[0, :, lanes]), mask) * SCALE).astype(BF)
    back = dot_nt(dkv[0, :, :width], weight[1]) + dot_nt(dkv[0, :, width:], weight[2])
    moved[...] = back.astype(BF)
    for d, out in enumerate(out_mem):
        slots = out.shape[1]
        out[0] = moved[rows_of((where[3] ^ d) * slots, slots), :]

    @pl.when(e == examples - 1)
    def _():
        hat, scale = normalise(x1[...])
        back, gain_grad, shift_grad = norm_back(
            dot_nt(dq2[...], weight[0]), vec[2:3, :], hat, scale
        )
        gx1[...] = gx2[...] + back
        vecs[0:1, :] = gain_grad
        vecs[1:2, :] = shift_grad


def cross_grads(
    where, gx2, a2, o2, dq2, dkv, all_memory, near, far, theirs, grad, memory, sems
):
    rows, width = gx2.shape
    examples, total, _ = memory.shape
    mem, _, slots, _ = all_memory.shape
    copies = Copies(sems)
    loads = [
        copies.start(all_memory.at[d], memory.at[:, d * slots : (d + 1) * slots, :])
        for d in range(mem)
    ]
    grad[0] = dot_tn(a2[...], dq2[...]).astype(BF)
    grad[3] = dot_tn(o2[...], gx2[...].astype(BF)).astype(BF)
    wait_all(loads)
    flat = memory[...].reshape(examples * total, width)
    for j in range(2):
        part = dkv[:, :, columns(j, width)].reshape(examples * total, width)
        grad[1 + j] = dot_tn(flat, part).astype(BF)
    wait_all(store_grad(where, grad, near, far, theirs, Copies(sems)))


def self_backward(
    group, where, suffix, vec, gx1, a1, qkv, p1, o1, parts, weights, suffix_grad, vecs,
    near, far, theirs, weight, start, grad, dqkv, do1, sems,
):
    rows, width = gx1.shape
    copies = Copies(sems)
    start_copy = my_examples(where, suffix, start, copies)
    loads = load_weight(where, weight, weights, copies)
    gs = gx1[...].astype(BF)
    grad[3] = dot_tn(o1[...], gs).astype(BF)
    wait_all(loads)
    do1[...] = dot_nt(gs, weight[3]).astype(BF)
    mask = head_mask(group)
    for r in range(rows // group):
        here = columns(r, group)
        for g in range(GROUPS):
            lanes = [slice(i * width + g * LANES, i * width + (g + 1) * LANES) for i in range(3)]
            queries = stack_heads(qkv[here, lanes[0]], mask)
            grads = stack_heads(do1[here, lanes[0]], mask)
            probs = p1[r * GROUPS + g]
            dp = dot_nt(grads, qkv[here, lanes[2]])
            wide = probs.astype(F32)
            row_sum = jnp.sum(wide * dp, axis=-1, keepdims=True)
            dz = (wide * (dp - row_sum)).astype(BF)
            dqkv[here, lanes[2]] = dot_tn(probs, grads).astype(BF)
            dqkv[here, lanes[1]] = (dot_tn(dz, queries) * SCALE).astype(BF)
            dq = merge_heads(dot(dz, qkv[here, lanes[1]]), mask) * SCALE
            dqkv[here, lanes[0]] = dq.astype(BF)
    for j in range(3):
        grad[j] = dot_tn(a1[...], dqkv[:, columns(j, width)]).astype(BF)
    start_copy.wait()
    started = store_grad(where, grad, near, far, theirs, Copies(sems), True)
    da1 = dot_nt(dqkv[:, columns(0, width)], weight[0])
    for j in range(1, 3):
        da1 = da1 + dot_nt(dqkv[:, columns(j, width)], weight[j])
    hat, scale = normalise(start[...].reshape(rows, width).astype(F32))
    back, gain_grad, shift_grad = norm_back(da1, vec[0:1, :], hat, scale)
    suffix_grad[...] = (gx1[...] + back).astype(BF).reshape(suffix_grad.shape)
    found = [gain_grad, shift_grad]
    for ref in parts:
        for r in range(ref.shape[0]):
            found += [ref[r : r + 1, columns(j, width)] for j in range(ref.shape[1] // width)]
    found.append(jnp.zeros((vecs.shape[0] - len(found), width), F32))
    vecs[...] = jnp.concatenate(found, axis=0).astype(BF)
    wait_all(started)


def run(kernel, inputs, outputs, scratch, copies, grid=()):
    def leaf(x):
        return isinstance(x, tuple) and len(x) == 2 and isinstance(x[0], pl.BlockSpec)

    flat_in, tree_in = jax.tree.flatten(inputs, is_leaf=leaf)
    flat_out, tree_out = jax.tree.flatten(outputs, is_leaf=leaf)

    def body(*refs):
        first, second = len(flat_in), len(flat_in) + len(flat_out)
        given = jax.tree.unflatten(tree_in, refs[:first])
        taken = jax.tree.unflatten(tree_out, refs[first:second])
        kernel(*given, *taken, *refs[second:])

    found = pl.pallas_call(
        body,
        grid=grid,
        in_specs=[spec for spec, _ in flat_in],
        out_specs=[spec for spec, _ in flat_out],
        out_shape=[shape for _, shape in flat_out],
        scratch_shapes=scratch + [pltpu.SemaphoreType.DMA((copies,))],
        compiler_params=pltpu.CompilerParams(vmem_limit_bytes=56 * 1024 * 1024),
        cost_estimate=pl.CostEstimate(
            flops=0, bytes_accessed=0, transcendentals=0
        ),
    )(*[x for _, x in flat_in])
    return jax.tree.unflatten(tree_out, found)


def shape_of(dims, dtype):
    return jax.ShapeDtypeStruct(tuple(dims), dtype)


def over_slow(value, slow, fast):
    groups = [[k * fast + b for k in range(slow)] for b in range(fast)]
    return lax.all_to_all(value, "fsdp", 0, 0, axis_index_groups=groups, tiled=True)


def gather_slow(value, slow, fast):
    return jnp.stack([value] + [swap(value, "fsdp", k * fast) for k in range(1, slow)])


class Gather:
    def __init__(self, half, slow, fast):
        self.half, self.slow, self.fast = half, slow, fast

    def send_slow(self, *others):
        self.near = gather_slow(after(self.half, *others), self.slow, self.fast)

    def send_fast(self, *others):
        self.near = after(self.near, *others)
        self.near_other = swap(self.near, "mem", 1)
        self.far = [swap(self.near, "fsdp", b) for b in range(1, self.fast)]

    def whole(self):
        mine = [self.near] + self.far
        theirs = [self.near_other] + [swap(piece, "mem", 1) for piece in self.far]
        return mine, theirs

    @staticmethod
    def refs(weights):
        return [[(ANY, x) for x in some] for some in weights]


class Scatter:
    def __init__(self, grads, slow, fast, *others, vectors=None):
        self.near, self.far, theirs = grads
        self.slow, self.fast, self.vectors = slow, fast, vectors
        theirs = [after(part, *others) for part in theirs]
        self.sent = [None] * fast
        for b in range(1, fast):
            self.sent[b] = swap(theirs[b] if b > 1 else self.pack(theirs[b]), "mem", 1)
        self.sent[0] = swap(theirs[0], "mem", 1)
        if vectors is not None:
            self.sent[1], came = self.unpack(self.sent[1], theirs[1].shape)
            self.vectors = vectors.astype(F32) + came

    def pack(self, value):
        if self.vectors is None:
            return value
        width = value.shape[-1]
        return jnp.concatenate([value.reshape(-1, width), self.vectors.astype(BF)])

    def unpack(self, value, shape):
        if self.vectors is None:
            return value, 0.0
        rows = value.shape[0] - self.vectors.shape[0]
        return value[:rows].reshape(shape), value[rows:].astype(F32)

    def add_cores(self):
        self.out = [
            self.pack((self.far[b].astype(F32) + self.sent[b + 1].astype(F32)).astype(BF))
            for b in range(self.fast - 1)
        ]
        return self.out

    def send_fast(self):
        self.came = [swap(part, "fsdp", b + 1) for b, part in enumerate(self.out)]

    def add_fast(self, *others):
        total = after(self.near, *others).astype(F32) + self.sent[0].astype(F32)
        vectors = 0.0 if self.vectors is None else self.vectors.astype(BF).astype(F32)
        for part in self.came:
            part, more = self.unpack(part, total.shape)
            total = total + part.astype(F32)
            vectors = vectors + more
        self.total = total.astype(BF).reshape(self.slow, -1, total.shape[-1])
        if self.vectors is not None:
            low = jnp.broadcast_to(vectors.astype(BF), (self.slow,) + vectors.shape)
            self.total = jnp.concatenate([self.total, low], axis=1)
        return self.total

    def send_slow(self, absolute=False):
        if absolute:
            came = over_slow(self.total, self.slow, self.fast)
            self.came = [came[k] for k in range(self.slow)]
        else:
            self.came = [swap(self.total[k], "fsdp", k * self.fast) for k in range(1, self.slow)]
            self.came.append(self.total[0])

    def add_slow(self, *others):
        came, _ = lax.optimization_barrier((self.came, others))
        return sum(part.astype(F32) for part in came)


def add_replicas(value, rows, across, c):
    k = 1
    while 2 * k < across:
        low = value.astype(BF)
        value = low.astype(F32) + swap(low, "mem", 2 * k).astype(F32)
        k *= 2
    low = value.astype(BF)
    halves = [low, swap(low, "mem", 2 * k)] if across > 1 else [low]
    others = [swap(half[: 2 * rows], "mem", 1) for half in halves]
    mine = sum(half.astype(F32) for half in halves)
    other = sum(half.astype(F32) for half in others)
    vectors, mine = mine[2 * rows :], mine[: 2 * rows]
    first = jnp.where(c == 0, mine, other)
    second = jnp.where(c == 0, other, mine)
    return [first[:rows], first[rows:], second[:rows], second[rows:]], vectors


def place_rows(where, pieces, mem_pieces, outs, memory_out, scratch, mem_scratch, sems):
    examples = pieces[0].shape[1]
    copies = Copies(sems)
    loads = [copies.start(piece, scratch.at[d]) for d, piece in enumerate(pieces)]
    mem_loads = [copies.start(piece, mem_scratch.at[d]) for d, piece in enumerate(mem_pieces)]
    stores = []
    for d, load in enumerate(loads):
        load.wait()
        place = pl.ds((where[3] ^ d) * examples, examples)
        for i, out in enumerate(outs):
            stores.append(copies.start(scratch.at[d, i], out.at[place]))
    for d, load in enumerate(mem_loads):
        load.wait()
        place = pl.ds((where[3] ^ d) * examples, examples)
        stores.append(copies.start(mem_scratch.at[d], memory_out.at[place]))
    wait_all(stores)


def spread_rows(where, values, mem_pieces):
    mem = len(mem_pieces)
    value = jnp.stack(values)
    blocks = [None] * mem
    blocks[0] = value
    for d in range(2, mem, 2):
        blocks[d] = swap(value, "mem", d)
    for d in range(0, mem, 2):
        blocks[d + 1] = swap(blocks[d], "mem", 1)
    whole = shape_of((mem * value.shape[1],) + value.shape[2:], BF)
    memory_whole = shape_of((mem * value.shape[1],) + mem_pieces[0].shape[1:], BF)
    return run(
        place_rows,
        [(SMEM, where), [(ANY, piece) for piece in blocks], [(ANY, x) for x in mem_pieces]],
        [[(ANY, whole)] * len(values), (ANY, memory_whole)],
        [pltpu.VMEM((mem,) + value.shape, BF), pltpu.VMEM((mem,) + mem_pieces[0].shape, BF)],
        mem * (3 + len(values)),
    )


def per_device(
    suffix,
    memory,
    counts,
    cotangent,
    self_norm_gain,
    self_norm_bias,
    self_query,
    self_key,
    self_value,
    self_output,
    cross_norm_gain,
    cross_norm_bias,
    cross_query,
    cross_key,
    cross_value,
    cross_output,
    dense_norm_gain,
    dense_norm_bias,
    dense_in,
    dense_in_bias,
    dense_out,
    dense_out_bias,
):
    f = lax.axis_index("fsdp")
    m = lax.axis_index("mem")
    c = m % 2
    fsdp = lax.axis_size("fsdp")
    mem = lax.axis_size("mem")
    across = mem // 2
    slow, fast = fsdp_split(fsdp)
    SHARDS[0] = fsdp
    where = jnp.stack([f // fast, f % fast, c, m]).astype(jnp.int32)
    examples = suffix.shape[0] // mem
    length = suffix.shape[1]
    width = suffix.shape[2]
    slots = memory.shape[1]
    total = mem * slots
    rows = examples * length
    inner = dense_in.shape[1]
    part = width // fsdp
    group = min(128, rows)
    blocks = 4 * fsdp

    def gather(matrices, *others):
        halves = [jnp.concatenate(matrices[:2]), jnp.concatenate(matrices[2:])]
        half = jnp.concatenate([jnp.where(c == 0, *halves), *others])
        return Gather(half, slow, fast)

    cross_gather = gather([cross_query, cross_key, cross_value, cross_output])
    dense = [
        [dense_in[:, columns(2 * i + j, width)] for j in range(2)]
        + [dense_out[columns(2 * i + j, part)] for j in range(2)]
        for i in range(2)
    ]
    dense = jnp.where(c == 0, jnp.stack(dense[0]), jnp.stack(dense[1]))
    dense_mine = lax.all_gather(dense, "fsdp")
    small = [
        self_norm_gain,
        self_norm_bias,
        cross_norm_gain,
        cross_norm_bias,
        dense_norm_gain,
        dense_norm_bias,
        dense_out_bias,
    ]
    small += [dense_in_bias[columns(j, part)] for j in range(4)]
    small = sum(
        jnp.pad(value[None], ((i, 15 - i), (0, width - part))) for i, value in enumerate(small)
    )
    self_gather = gather([self_query, self_key, self_value, self_output], small)

    def exchange(value):
        blocks = value.reshape((mem, examples) + value.shape[1:])
        return lax.all_to_all(blocks, "mem", 0, 0, tiled=True)

    all_memory = exchange(memory)
    self_gather.send_slow()
    sent = [self_gather.near]
    self_gather.send_fast(*sent)
    cross_gather.send_slow(*sent)
    sent = [*self_gather.far, cross_gather.near, all_memory]
    self_gather.far = [after(piece, *sent) for piece in self_gather.far]
    self_weights = self_gather.whole()
    cross_gather.send_fast(*self_gather.far)

    half = (2, part, width)
    grads_like = [
        (ANY, shape_of((slow,) + half, BF)),
        (ANY, shape_of((fast - 1, slow) + half, BF)),
        [(ANY, shape_of((slow,) + half, BF))] * fast,
    ]

    dense_like = [(ANY, shape_of((fsdp,) + half, BF))] * 2

    def flat(dims, dtype):
        return (VMEM, shape_of(dims, dtype))

    def per_example(value):
        dims = value.shape[1:]
        spec = pl.BlockSpec((1,) + dims, lambda e: (e,) + (0,) * len(dims))
        return (spec, value)

    def slots_of_example(value):
        spec = pl.BlockSpec((mem, 1, slots, width), lambda e: (0, e, 0, 0))
        return (spec, value)

    def scratch(*dims):
        return pltpu.VMEM(dims, BF)

    def scatter(grads, *others, vectors=None):
        return Scatter(grads, slow, fast, *others, vectors=vectors)

    wide = (rows, width)
    square = scratch(4, width, width)
    own_rows = scratch(examples, length, width)
    x1, a1, qkv, p1, o1, vec = run(
        functools.partial(self_forward, group),
        [(SMEM, where), (ANY, suffix), Gather.refs(self_weights)],
        [
            flat(wide, F32),
            flat(wide, BF),
            flat((rows, 3 * width), BF),
            flat((rows // group * GROUPS, TOGETHER * group, group), BF),
            flat(wide, BF),
            flat((16, width), F32),
        ],
        [square, own_rows, scratch(fsdp, 16, 128)],
        1 + fsdp + blocks,
    )
    cross_gather.far = [after(piece, x1) for piece in cross_gather.far]
    cross_weights = Gather.refs(cross_gather.whole())
    x2, a2, q2, kv, p2, o2 = run(
        cross_forward,
        [(SMEM, where), (SMEM, counts), (VMEM, x1), (VMEM, vec)]
        + [slots_of_example(all_memory), cross_weights],
        [
            flat(wide, F32),
            flat(wide, BF),
            flat(wide, BF),
            per_example(shape_of((examples, total, 2 * width), BF)),
            per_example(shape_of((examples, GROUPS, TOGETHER * length, total), BF)),
            flat(wide, BF),
        ],
        [square],
        blocks,
        (examples,),
    )
    small = [after(piece, x1)[:, 2 * part + 7 : 2 * part + 11, :part] for piece in self_weights[0]]
    order = jnp.arange(fsdp) ^ f
    bias_in = jnp.take(jnp.concatenate(small), order % fast * slow + order // fast, axis=0)
    bias_in = bias_in.astype(F32).reshape(1, inner)
    dense_mine = after(dense_mine, x2)
    dense_weights = [(ANY, dense_mine), (ANY, swap(dense_mine, "mem", 1))]
    a3, h, slope, *grads = run(
        dense_inner,
        [(SMEM, where), (VMEM, x2), (VMEM, vec), (VMEM, bias_in), (ANY, cotangent), dense_weights],
        [flat(wide, BF), flat((rows, inner), BF), flat((rows, inner), BF)] + dense_like,
        [square, scratch(fsdp, 4, part, width), own_rows],
        1 + blocks,
    )
    def add_cores(grads, *others):
        mine, theirs = grads
        return mine.astype(F32) + swap(after(theirs, *others), "mem", 1).astype(F32)

    out_sum = add_cores(grads).astype(BF)
    y, du, vecs_y, bias_grad, *grads = run(
        dense_outer,
        [(SMEM, where), (VMEM, after(x2, out_sum)), (VMEM, vec), (VMEM, a3), (VMEM, h)]
        + [(VMEM, slope), (ANY, cotangent), dense_weights],
        [
            flat((examples, length, width), BF),
            flat((rows, inner), BF),
            flat((1, width), F32),
            flat((1, inner), F32),
        ]
        + dense_like,
        [scratch(fsdp, 4, part, width), square, own_rows],
        1 + blocks,
    )
    in_grads = grads
    gx2, vecs_dense = run(
        dense_back,
        [(SMEM, where), (VMEM, x2), (VMEM, vec), (VMEM, du), (ANY, cotangent), dense_weights],
        [flat(wide, F32), flat((2, width), F32)],
        [square, own_rows],
        1 + blocks,
    )
    dense_grads = jnp.concatenate([out_sum, add_cores(in_grads, gx2).astype(BF)], axis=1)
    dense_sum = lax.psum_scatter(dense_grads, "fsdp", scatter_dimension=0)
    gx1, vecs_cross, dkv, dq2, grad_memory = run(
        cross_backward,
        [(SMEM, where), (VMEM, x1), (VMEM, vec), (VMEM, after(gx2, dense_grads)), (VMEM, q2)]
        + [per_example(kv), per_example(p2), cross_weights],
        [
            flat(wide, F32),
            flat((2, width), F32),
            per_example(shape_of((examples, total, 2 * width), BF)),
            flat(wide, BF),
            [per_example(shape_of((examples, slots, width), BF))] * mem,
        ],
        [square, scratch(*wide), scratch(total, width)],
        blocks,
        (examples,),
    )
    mem_pieces = grad_memory[:1] + [swap(grad_memory[d], "mem", d) for d in range(1, mem)]
    grads = run(
        cross_grads,
        [(SMEM, where), (VMEM, gx2), (VMEM, a2), (VMEM, o2), (VMEM, dq2)]
        + [(VMEM, dkv), (ANY, all_memory)],
        grads_like,
        [square, scratch(examples, total, width)],
        max(mem, blocks),
    )
    cross_grads_out = grads
    suffix_part, vecs_self, *grads = run(
        functools.partial(self_backward, group),
        [(SMEM, where), (ANY, suffix), (VMEM, vec), (VMEM, gx1), (VMEM, a1)]
        + [(VMEM, qkv), (VMEM, p1), (VMEM, o1)]
        + [[(VMEM, x) for x in (vecs_cross, vecs_dense, vecs_y, bias_grad)], Gather.refs(self_weights)],
        [flat((examples, length, width), BF), flat((16, width), BF)] + grads_like,
        [square, own_rows, square, scratch(rows, 3 * width), scratch(*wide)],
        1 + blocks,
    )
    cross_scatter = scatter(cross_grads_out, suffix_part)
    self_scatter = scatter(grads, vectors=vecs_self)
    cross_scatter.add_cores()
    cross_scatter.send_fast()
    self_scatter.add_cores()
    self_scatter.send_fast()
    cross_scatter.add_fast(dense_sum)
    cross_scatter.send_slow()
    self_total = self_scatter.add_fast()
    self_scatter.send_slow(True)

    def finish(value, rows):
        return add_replicas(value, rows, across, c)

    grad_cross, _ = finish(cross_scatter.add_slow(self_total), part)
    suffix_part = after(suffix_part, self_total)
    (block_output, suffix_grad), memory_grad = spread_rows(where, [y, suffix_part], mem_pieces)
    dense_sum = after(dense_sum, self_total).reshape(4 * part, width)
    (out_low, in_low, out_high, in_high), _ = finish(dense_sum, 2 * part)
    grad_in = jnp.concatenate([in_low[:part], in_low[part:], in_high[:part], in_high[part:]], axis=1)
    grad_out = jnp.concatenate([out_low, out_high])
    grad_self, vectors = finish(
        self_scatter.add_slow(block_output, grad_in, grad_out, *grad_cross), part
    )

    def vector(i):
        return lax.dynamic_slice(vectors, (i, f * part), (1, part)).reshape(part)

    return (
        block_output,
        suffix_grad,
        memory_grad,
        vector(0),
        vector(1),
        *grad_self,
        vector(2),
        vector(3),
        *grad_cross,
        vector(4),
        vector(5),
        grad_in,
        lax.dynamic_slice_in_dim(vectors[7:11].reshape(-1), f * (inner // fsdp), inner // fsdp, 0),
        grad_out,
        vector(6),
    )


def solution(mesh):
    rows = P("fsdp", None, None)
    matrix = P("fsdp", None)
    vector = P("fsdp")
    attention = (vector, vector, matrix, matrix, matrix, matrix)
    params = attention + attention + (vector, vector, matrix, vector, matrix, vector)
    return jax.shard_map(
        per_device,
        mesh=mesh,
        in_specs=(rows, P("fsdp", "mem", None), vector, rows) + params,
        out_specs=(rows, rows, P("fsdp", "mem", None)) + params,
        check_vma=False,
    )
```

```python
import functools

import jax
import jax.numpy as jnp
from jax import lax
from jax.experimental import pallas as pl
from jax.experimental.pallas import tpu as pltpu
from jax.sharding import PartitionSpec as P

HEADS = 12
HEAD = 64
TOGETHER = 4
GROUPS = HEADS // TOGETHER
LANES = TOGETHER * HEAD
SCALE = HEAD ** (-0.5)
BF = jnp.bfloat16
F32 = jnp.float32
ANY = pl.BlockSpec(memory_space=pl.ANY)
SMEM = pl.BlockSpec(memory_space=pltpu.SMEM)
VMEM = pl.BlockSpec(memory_space=pltpu.VMEM)


def swap(value, axis, distance):
    size = lax.axis_size(axis)
    return lax.ppermute(value, axis, [(i, i ^ distance) for i in range(size)])


def after(value, *others):
    return lax.optimization_barrier((value, *others))[0] if others else value


def fsdp_split(size):
    slow = 4 if size % 4 == 0 else 1
    return slow, size // slow


def dot(left, right):
    return jnp.dot(left, right, preferred_element_type=F32)


def dot_nt(left, right):
    return lax.dot_general(left, right, (((1,), (1,)), ((), ())), preferred_element_type=F32)


def dot_tn(left, right):
    return lax.dot_general(left, right, (((0,), (0,)), ((), ())), preferred_element_type=F32)


def rows_of(start, size):
    return pl.ds(pl.multiple_of(start, 16), size)


def block(ref, by_rows, shard, which):
    if by_rows:
        return ref.at[shard, pl.ds(which * 2, 2)]
    rows = ref.shape[1] // SHARDS[0]
    return ref.at[pl.ds(which * 2, 2), rows_of(shard * rows, rows)]


SHARDS = [0]


class Copies:
    def __init__(self, sems):
        self.sems = sems
        self.next = 0

    def start(self, source, target):
        copy = pltpu.make_async_copy(source, target, self.sems.at[self.next])
        self.next += 1
        copy.start()
        return copy


def wait_all(copies):
    for copy in copies:
        copy.wait()


def load_weight(where, whole, weights, copies, by_rows=False):
    z, y, c = where[0], where[1], where[2]
    rows = whole.shape[2] if by_rows else whole.shape[1] // SHARDS[0]
    started = []
    for which, pieces in ((c, weights[0]), (1 - c, weights[1])):
        fast = len(pieces)
        for b, piece in enumerate(pieces):
            for k in range(piece.shape[0]):
                shard = (z ^ k) * fast + (y ^ b)
                for i in range(2):
                    source = piece.at[k, pl.ds(i * rows, rows)]
                    if by_rows:
                        target = whole.at[shard, 2 * which + i]
                    else:
                        target = whole.at[2 * which + i, rows_of(shard * rows, rows)]
                    started.append(copies.start(source, target))
    return started


def store_grad(where, whole, near, far, theirs, copies, by_rows=False):
    y, c = where[1], where[2]
    fast, slow = len(theirs), near.shape[0]
    started = []
    for b in range(fast):
        for k in range(slow):
            shard = k * fast + (y ^ b)
            mine = far.at[b - 1, k] if b else near.at[k]
            started.append(copies.start(block(whole, by_rows, shard, 1 - c), theirs[b].at[k]))
            started.append(copies.start(block(whole, by_rows, shard, c), mine))
    return started


def my_examples(where, source, target, copies):
    count = target.shape[0]
    return copies.start(source.at[pl.ds(where[3] * count, count)], target)


def normalise(values):
    centred = values - jnp.mean(values, axis=-1, keepdims=True)
    scale = lax.rsqrt(jnp.mean(centred * centred, axis=-1, keepdims=True) + 1e-06)
    return centred * scale, scale


def norm_back(grad, gain, hat, scale):
    inner = grad * gain
    mean = jnp.mean(inner, axis=-1, keepdims=True)
    along = jnp.mean(inner * hat, axis=-1, keepdims=True)
    return (
        scale * (inner - mean - hat * along),
        jnp.sum(grad * hat, axis=0, keepdims=True),
        jnp.sum(grad, axis=0, keepdims=True),
    )


def head_mask(rows):
    shape = (TOGETHER * rows, LANES)
    row = lax.broadcasted_iota(jnp.int32, shape, 0) // rows
    lane = lax.broadcasted_iota(jnp.int32, shape, 1) // HEAD
    return (row == lane).astype(F32)


def stack_heads(value, mask):
    return (jnp.concatenate([value] * TOGETHER, axis=0).astype(F32) * mask).astype(BF)


def merge_heads(value, mask):
    rows = value.shape[0] // TOGETHER
    value = value * mask
    total = value[:rows]
    for h in range(1, TOGETHER):
        total = total + value[h * rows : (h + 1) * rows]
    return total


def columns(j, width):
    return slice(j * width, (j + 1) * width)


def self_forward(
    group, where, suffix, weights, x1, a1, qkv, p1, o1, vec, weight, start, small, sems
):
    rows, width = x1.shape
    copies = Copies(sems)
    first = my_examples(where, suffix, start, copies)
    fast, slow = len(weights[0]), weights[0][0].shape[0]
    part = width // (fast * slow)
    vectors = []
    for b, piece in enumerate(weights[0]):
        for k in range(slow):
            source = piece.at[k, pl.ds(2 * part, 16), pl.ds(0, 128)]
            vectors.append(copies.start(source, small.at[b * slow + k]))
    loads = load_weight(where, weight, weights, copies)
    wait_all(vectors)
    lane = lax.broadcasted_iota(jnp.int32, (128, width), 0)
    place = lax.broadcasted_iota(jnp.int32, (128, width), 1) - lane
    together = jnp.zeros(vec.shape, F32)
    for i in range(fast * slow):
        shard = (where[0] ^ (i % slow)) * fast + (where[1] ^ (i // slow))
        chosen = ((place == shard * part) & (lane < part)).astype(F32).astype(BF)
        together = together + dot(small[i], chosen)
    vec[...] = together
    first.wait()
    values = start[...].reshape(rows, width).astype(F32)
    hat, _ = normalise(values)
    a1[...] = (hat * vec[0:1, :] + vec[1:2, :]).astype(BF)
    wait_all(loads)
    for j in range(3):
        qkv[:, columns(j, width)] = dot(a1[...], weight[j]).astype(BF)
    mask = head_mask(group)
    length = suffix.shape[1]
    shape = (TOGETHER * group, group)
    row = lax.broadcasted_iota(jnp.int32, shape, 0) % group
    col = lax.broadcasted_iota(jnp.int32, shape, 1)
    seen = (row // length == col // length) & (row >= col)
    for r in range(rows // group):
        here = columns(r, group)
        for g in range(GROUPS):
            lanes = [slice(i * width + g * LANES, i * width + (g + 1) * LANES) for i in range(3)]
            queries = stack_heads(qkv[here, lanes[0]], mask)
            scores = dot_nt(queries, qkv[here, lanes[1]]) * SCALE
            scores = jnp.where(seen, scores, -1e30)
            powers = jnp.exp(scores - jnp.max(scores, axis=-1, keepdims=True))
            probs = (powers / jnp.sum(powers, axis=-1, keepdims=True)).astype(BF)
            p1[r * GROUPS + g] = probs
            found = dot(probs, qkv[here, lanes[2]])
            o1[here, lanes[0]] = merge_heads(found, mask).astype(BF)
    x1[...] = values + dot(o1[...], weight[3])


def cross_forward(
    where, counts, x1, vec, memory, weights, x2, a2, q2, kv, p2, o2, weight, sems
):
    rows, width = x1.shape
    examples = pl.num_programs(0)
    e = pl.program_id(0)
    total = kv.shape[1]
    length = p2.shape[2] // TOGETHER

    @pl.when(e == 0)
    def _():
        loads = load_weight(where, weight, weights, Copies(sems))
        hat, _ = normalise(x1[...])
        a2[...] = (hat * vec[2:3, :] + vec[3:4, :]).astype(BF)
        wait_all(loads)
        q2[...] = dot(a2[...], weight[0]).astype(BF)

    tokens = memory[...].reshape(total, width)
    for j in range(2):
        kv[0, :, columns(j, width)] = dot(tokens, weight[1 + j]).astype(BF)
    mask = head_mask(length)
    position = lax.broadcasted_iota(jnp.int32, (1, total), 1)
    valid = position < counts[where[3] * examples + e]
    here = rows_of(e * length, length)
    probs = []
    for g in range(GROUPS):
        lanes = columns(g, LANES)
        queries = stack_heads(q2[here, lanes], mask)
        scores = dot_nt(queries, kv[0, :, lanes]) * SCALE
        scores = jnp.where(valid, scores, -1e30)
        top = jnp.maximum(jnp.max(scores, axis=-1, keepdims=True), 0.0)
        powers = jnp.exp(scores - top)
        weight_sum = jnp.sum(powers, axis=-1, keepdims=True) + jnp.exp(-top)
        probs.append((powers / weight_sum).astype(BF))
    for g in range(GROUPS):
        p2[0, g] = probs[g]
        found = dot(probs[g], kv[0, :, width + g * LANES : width + (g + 1) * LANES])
        o2[here, columns(g, LANES)] = merge_heads(found, mask).astype(BF)

    @pl.when(e == examples - 1)
    def _():
        x2[...] = x1[...] + dot(o2[...], weight[3])


def dense_inner(
    where, x2, vec, bias, cotangent, weights, a3, h, slope, near, far, theirs,
    weight, grad, cot, sems,
):
    rows, width = x2.shape
    copies = Copies(sems)
    cot_copy = my_examples(where, cotangent, cot, copies)
    loads = load_weight(where, weight, weights, copies)
    hat, _ = normalise(x2[...])
    a3[...] = (hat * vec[4:5, :] + vec[5:6, :]).astype(BF)
    cot_copy.wait()
    gy = cot[...].reshape(rows, width)
    wait_all(loads)
    flat = grad.shape[0] * grad.shape[1] * grad.shape[2]
    step = flat // grad.shape[0]
    for j in range(4):
        for half in range(2):
            cols = slice(j * width + half * 384, j * width + (half + 1) * 384)
            u = dot(a3[...], weight[j, :, half * 384 : (half + 1) * 384]) + bias[:, cols]
            square = u * u
            t = jnp.tanh(0.7978845608 * u * (1.0 + 0.044715 * square))
            h[:, cols] = (0.5 * u * (1.0 + t)).astype(BF)
            slope[:, cols] = (
                0.5 * (1.0 + t)
                + (0.5 * 0.7978845608) * u * (1.0 - t * t) * (1.0 + (3.0 * 0.044715) * square)
            ).astype(BF)
            part = dot_tn(h[:, cols], gy).astype(BF)
            per = 384 // step
            grad[cols.start // step : cols.start // step + per] = part.reshape(
                (per,) + grad.shape[1:]
            )
    wait_all(store_grad(where, grad, near, far, theirs, Copies(sems), True))


def dense_outer(
    where, x2, vec, a3, h, slope, cotangent, weights, y, du, vecs, bias_grad, near, far, theirs,
    weight, grad, cot, sems,
):
    rows, width = x2.shape
    copies = Copies(sems)
    cot_copy = my_examples(where, cotangent, cot, copies)
    wait_all(load_weight(where, weight, weights, copies, True))
    cot_copy.wait()
    gy = cot[...].reshape(rows, width)
    shards = weight.shape[0]
    step = weight.shape[1] * weight.shape[2]
    whole = weight[...].reshape(shards * step, width)
    for j in range(4):
        cols = columns(j, width)
        low = (dot_nt(gy, whole[cols]) * slope[:, cols].astype(F32)).astype(BF)
        du[:, cols] = low
        bias_grad[:, cols] = jnp.sum(low.astype(F32), axis=0, keepdims=True)
        grad[j] = dot_tn(a3[...], low).astype(BF)
    started = store_grad(where, grad, near, far, theirs, Copies(sems))
    result = x2[...] + dot(h[...], whole) + vec[6:7, :]
    y[...] = result.astype(BF).reshape(y.shape)
    vecs[...] = jnp.sum(gy.astype(F32), axis=0, keepdims=True)
    wait_all(started)


def dense_back(where, x2, vec, du, cotangent, weights, gx2, vecs, weight, cot, sems):
    rows, width = x2.shape
    copies = Copies(sems)
    cot_copy = my_examples(where, cotangent, cot, copies)
    loads = load_weight(where, weight, weights, copies)
    hat, scale = normalise(x2[...])
    cot_copy.wait()
    wait_all(loads)
    da3 = dot_nt(du[:, columns(0, width)], weight[0])
    for j in range(1, 4):
        da3 = da3 + dot_nt(du[:, columns(j, width)], weight[j])
    back, gain_grad, shift_grad = norm_back(da3, vec[4:5, :], hat, scale)
    gx2[...] = cot[...].reshape(rows, width).astype(F32) + back
    vecs[0:1, :] = gain_grad
    vecs[1:2, :] = shift_grad


def cross_backward(
    where, x1, vec, gx2, q2, kv, p2, weights, gx1, vecs, dkv, dq2, out_mem, weight, do2, moved, sems
):
    rows, width = x1.shape
    examples = pl.num_programs(0)
    e = pl.program_id(0)
    length = p2.shape[2] // TOGETHER

    @pl.when(e == 0)
    def _():
        wait_all(load_weight(where, weight, weights, Copies(sems)))
        do2[...] = dot_nt(gx2[...].astype(BF), weight[3]).astype(BF)

    mask = head_mask(length)
    here = rows_of(e * length, length)
    for g in range(GROUPS):
        lanes = columns(g, LANES)
        value_lanes = slice(width + g * LANES, width + (g + 1) * LANES)
        queries = stack_heads(q2[here, lanes], mask)
        grads = stack_heads(do2[here, lanes], mask)
        probs = p2[0, g]
        dp = dot_nt(grads, kv[0, :, value_lanes])
        wide = probs.astype(F32)
        row_sum = jnp.sum(wide * dp, axis=-1, keepdims=True)
        dz = (wide * (dp - row_sum)).astype(BF)
        dkv[0, :, value_lanes] = dot_tn(probs, grads).astype(BF)
        dkv[0, :, lanes] = (dot_tn(dz, queries) * SCALE).astype(BF)
        dq2[here, lanes] = (merge_heads(dot(dz, kv[0, :, lanes]), mask) * SCALE).astype(BF)
    back = dot_nt(dkv[0, :, :width], weight[1]) + dot_nt(dkv[0, :, width:], weight[2])
    moved[...] = back.astype(BF)
    for d, out in enumerate(out_mem):
        slots = out.shape[1]
        out[0] = moved[rows_of((where[3] ^ d) * slots, slots), :]

    @pl.when(e == examples - 1)
    def _():
        hat, scale = normalise(x1[...])
        back, gain_grad, shift_grad = norm_back(
            dot_nt(dq2[...], weight[0]), vec[2:3, :], hat, scale
        )
        gx1[...] = gx2[...] + back
        vecs[0:1, :] = gain_grad
        vecs[1:2, :] = shift_grad


def cross_grads(
    where, gx2, a2, o2, dq2, dkv, all_memory, near, far, theirs, grad, memory, sems
):
    rows, width = gx2.shape
    examples, total, _ = memory.shape
    mem, _, slots, _ = all_memory.shape
    copies = Copies(sems)
    loads = [
        copies.start(all_memory.at[d], memory.at[:, d * slots : (d + 1) * slots, :])
        for d in range(mem)
    ]
    grad[0] = dot_tn(a2[...], dq2[...]).astype(BF)
    grad[3] = dot_tn(o2[...], gx2[...].astype(BF)).astype(BF)
    wait_all(loads)
    flat = memory[...].reshape(examples * total, width)
    for j in range(2):
        part = dkv[:, :, columns(j, width)].reshape(examples * total, width)
        grad[1 + j] = dot_tn(flat, part).astype(BF)
    wait_all(store_grad(where, grad, near, far, theirs, Copies(sems)))


def self_backward(
    group, where, suffix, vec, gx1, a1, qkv, p1, o1, parts, weights, suffix_grad, vecs,
    near, far, theirs, weight, start, grad, dqkv, do1, sems,
):
    rows, width = gx1.shape
    copies = Copies(sems)
    start_copy = my_examples(where, suffix, start, copies)
    loads = load_weight(where, weight, weights, copies)
    gs = gx1[...].astype(BF)
    grad[3] = dot_tn(o1[...], gs).astype(BF)
    wait_all(loads)
    do1[...] = dot_nt(gs, weight[3]).astype(BF)
    mask = head_mask(group)
    for r in range(rows // group):
        here = columns(r, group)
        for g in range(GROUPS):
            lanes = [slice(i * width + g * LANES, i * width + (g + 1) * LANES) for i in range(3)]
            queries = stack_heads(qkv[here, lanes[0]], mask)
            grads = stack_heads(do1[here, lanes[0]], mask)
            probs = p1[r * GROUPS + g]
            dp = dot_nt(grads, qkv[here, lanes[2]])
            wide = probs.astype(F32)
            row_sum = jnp.sum(wide * dp, axis=-1, keepdims=True)
            dz = (wide * (dp - row_sum)).astype(BF)
            dqkv[here, lanes[2]] = dot_tn(probs, grads).astype(BF)
            dqkv[here, lanes[1]] = (dot_tn(dz, queries) * SCALE).astype(BF)
            dq = merge_heads(dot(dz, qkv[here, lanes[1]]), mask) * SCALE
            dqkv[here, lanes[0]] = dq.astype(BF)
    for j in range(3):
        grad[j] = dot_tn(a1[...], dqkv[:, columns(j, width)]).astype(BF)
    start_copy.wait()
    started = store_grad(where, grad, near, far, theirs, Copies(sems))
    da1 = dot_nt(dqkv[:, columns(0, width)], weight[0])
    for j in range(1, 3):
        da1 = da1 + dot_nt(dqkv[:, columns(j, width)], weight[j])
    hat, scale = normalise(start[...].reshape(rows, width).astype(F32))
    back, gain_grad, shift_grad = norm_back(da1, vec[0:1, :], hat, scale)
    suffix_grad[...] = (gx1[...] + back).astype(BF).reshape(suffix_grad.shape)
    found = [gain_grad, shift_grad]
    for ref in parts:
        for r in range(ref.shape[0]):
            found += [ref[r : r + 1, columns(j, width)] for j in range(ref.shape[1] // width)]
    found.append(jnp.zeros((vecs.shape[0] - len(found), width), F32))
    vecs[...] = jnp.concatenate(found, axis=0).astype(BF)
    wait_all(started)


def run(kernel, inputs, outputs, scratch, copies, grid=()):
    def leaf(x):
        return isinstance(x, tuple) and len(x) == 2 and isinstance(x[0], pl.BlockSpec)

    flat_in, tree_in = jax.tree.flatten(inputs, is_leaf=leaf)
    flat_out, tree_out = jax.tree.flatten(outputs, is_leaf=leaf)

    def body(*refs):
        first, second = len(flat_in), len(flat_in) + len(flat_out)
        given = jax.tree.unflatten(tree_in, refs[:first])
        taken = jax.tree.unflatten(tree_out, refs[first:second])
        kernel(*given, *taken, *refs[second:])

    found = pl.pallas_call(
        body,
        grid=grid,
        in_specs=[spec for spec, _ in flat_in],
        out_specs=[spec for spec, _ in flat_out],
        out_shape=[shape for _, shape in flat_out],
        scratch_shapes=scratch + [pltpu.SemaphoreType.DMA((copies,))],
        compiler_params=pltpu.CompilerParams(vmem_limit_bytes=56 * 1024 * 1024),
        cost_estimate=pl.CostEstimate(
            flops=0, bytes_accessed=0, transcendentals=0
        ),
    )(*[x for _, x in flat_in])
    return jax.tree.unflatten(tree_out, found)


def shape_of(dims, dtype):
    return jax.ShapeDtypeStruct(tuple(dims), dtype)


def over_slow(value, slow, fast):
    groups = [[k * fast + b for k in range(slow)] for b in range(fast)]
    return lax.all_to_all(value, "fsdp", 0, 0, axis_index_groups=groups, tiled=True)


class Gather:
    def __init__(self, half, slow, fast):
        self.half, self.slow, self.fast = half, slow, fast

    def send_slow(self, *others):
        half = after(self.half, *others)
        self.came = [half] + [swap(half, "fsdp", k * self.fast) for k in range(1, self.slow)]

    def send_fast(self, *others):
        self.near = jnp.stack([after(piece, *others) for piece in self.came])
        self.near_other = swap(self.near, "mem", 1)
        self.far = [swap(self.near, "fsdp", b) for b in range(1, self.fast)]

    def whole(self):
        mine = [self.near] + self.far
        theirs = [self.near_other] + [swap(piece, "mem", 1) for piece in self.far]
        return mine, theirs

    @staticmethod
    def refs(weights):
        return [[(ANY, x) for x in some] for some in weights]


class Scatter:
    def __init__(self, grads, slow, fast, *others, vectors=None):
        self.near, self.far, theirs = grads
        self.slow, self.fast, self.vectors = slow, fast, vectors
        theirs = [after(part, *others) for part in theirs]
        self.sent = [None] * fast
        for b in range(1, fast):
            self.sent[b] = swap(theirs[b] if b > 1 else self.pack(theirs[b]), "mem", 1)
        self.sent[0] = swap(theirs[0], "mem", 1)
        if vectors is not None:
            self.sent[1], came = self.unpack(self.sent[1], theirs[1].shape)
            self.vectors = vectors.astype(F32) + came

    def pack(self, value):
        if self.vectors is None:
            return value
        width = value.shape[-1]
        return jnp.concatenate([value.reshape(-1, width), self.vectors.astype(BF)])

    def unpack(self, value, shape):
        if self.vectors is None:
            return value, 0.0
        rows = value.shape[0] - self.vectors.shape[0]
        return value[:rows].reshape(shape), value[rows:].astype(F32)

    def add_cores(self):
        self.out = [
            self.pack((self.far[b].astype(F32) + self.sent[b + 1].astype(F32)).astype(BF))
            for b in range(self.fast - 1)
        ]
        return self.out

    def send_fast(self):
        self.came = [swap(part, "fsdp", b + 1) for b, part in enumerate(self.out)]

    def add_fast(self, *others):
        total = after(self.near, *others).astype(F32) + self.sent[0].astype(F32)
        vectors = 0.0 if self.vectors is None else self.vectors.astype(BF).astype(F32)
        for part in self.came:
            part, more = self.unpack(part, total.shape)
            total = total + part.astype(F32)
            vectors = vectors + more
        self.total = total.astype(BF).reshape(self.slow, -1, total.shape[-1])
        if self.vectors is not None:
            low = jnp.broadcast_to(vectors.astype(BF), (self.slow,) + vectors.shape)
            self.total = jnp.concatenate([self.total, low], axis=1)
        return self.total

    def send_slow(self):
        self.came = over_slow(self.total, self.slow, self.fast)

    def add_slow(self, *others):
        return jnp.sum(after(self.came, *others).astype(F32), axis=0)


class Replicas:
    def __init__(self, value, rows, across):
        self.rows = rows
        k = 1
        while 2 * k < across:
            low = value.astype(BF)
            value = low.astype(F32) + swap(low, "mem", 2 * k).astype(F32)
            k *= 2
        low = value.astype(BF)
        self.halves = [low, swap(low, "mem", 2 * k)] if across > 1 else [low]
        self.others = [swap(half[: 2 * rows], "mem", 1) for half in self.halves]

    def combine(self, c, *others):
        rows = self.rows
        halves, others, _ = lax.optimization_barrier((self.halves, self.others, others))
        mine = sum(half.astype(F32) for half in halves)
        other = sum(half.astype(F32) for half in others)
        vectors, mine = mine[2 * rows :], mine[: 2 * rows]
        first = jnp.where(c == 0, mine, other)
        second = jnp.where(c == 0, other, mine)
        return [first[:rows], first[rows:], second[:rows], second[rows:]], vectors


def place_rows(where, near, far, mem_pieces, outs, memory_out, scratch, mem_scratch, sems):
    examples = mem_pieces[0].shape[0]
    copies = Copies(sems)
    loads = []
    for i, pieces in enumerate(near):
        for d, piece in enumerate(pieces):
            loads.append((copies.start(piece, scratch.at[i, 2 * d]), i, 2 * d))
            loads.append((copies.start(far[i].at[d], scratch.at[i, 2 * d + 1]), i, 2 * d + 1))
    mem_loads = [copies.start(piece, mem_scratch.at[d]) for d, piece in enumerate(mem_pieces)]
    stores = []
    for load, i, d in loads:
        load.wait()
        target = outs[i].at[pl.ds((where[3] ^ d) * examples, examples)]
        stores.append(copies.start(scratch.at[i, d], target))
    for d, load in enumerate(mem_loads):
        load.wait()
        target = memory_out.at[pl.ds((where[3] ^ d) * examples, examples)]
        stores.append(copies.start(mem_scratch.at[d], target))
    wait_all(stores)


def spread_across(value, mem):
    return [value] + [swap(value, "mem", d) for d in range(2, mem, 2)]


def place(where, values, mem_pieces):
    mem = len(mem_pieces)
    far = [swap(jnp.stack(value), "mem", 1) for value in values]
    piece, mem_piece = values[0][0], mem_pieces[0]
    whole = shape_of((mem * piece.shape[0],) + piece.shape[1:], BF)
    memory_whole = shape_of((mem * mem_piece.shape[0],) + mem_piece.shape[1:], BF)
    return run(
        place_rows,
        [(SMEM, where), [[(ANY, x) for x in value] for value in values]]
        + [[(ANY, x) for x in far], [(ANY, x) for x in mem_pieces]],
        [[(ANY, whole)] * len(values), (ANY, memory_whole)],
        [
            pltpu.VMEM((len(values), mem) + piece.shape, BF),
            pltpu.VMEM((mem,) + mem_piece.shape, BF),
        ],
        2 * mem * (1 + len(values)),
    )


def per_device(
    suffix,
    memory,
    counts,
    cotangent,
    self_norm_gain,
    self_norm_bias,
    self_query,
    self_key,
    self_value,
    self_output,
    cross_norm_gain,
    cross_norm_bias,
    cross_query,
    cross_key,
    cross_value,
    cross_output,
    dense_norm_gain,
    dense_norm_bias,
    dense_in,
    dense_in_bias,
    dense_out,
    dense_out_bias,
):
    f = lax.axis_index("fsdp")
    m = lax.axis_index("mem")
    c = m % 2
    fsdp = lax.axis_size("fsdp")
    mem = lax.axis_size("mem")
    across = mem // 2
    slow, fast = fsdp_split(fsdp)
    SHARDS[0] = fsdp
    where = jnp.stack([f // fast, f % fast, c, m]).astype(jnp.int32)
    examples = suffix.shape[0] // mem
    length = suffix.shape[1]
    width = suffix.shape[2]
    slots = memory.shape[1]
    total = mem * slots
    rows = examples * length
    inner = dense_in.shape[1]
    part = width // fsdp
    group = min(128, rows)
    blocks = 4 * fsdp

    def gather(matrices, *others):
        halves = [jnp.concatenate(matrices[:2]), jnp.concatenate(matrices[2:])]
        half = jnp.concatenate([jnp.where(c == 0, *halves), *others])
        return Gather(half, slow, fast)

    cross_gather = gather([cross_query, cross_key, cross_value, cross_output])
    in_gather = gather([dense_in[:, columns(j, width)] for j in range(4)])
    out_gather = gather([dense_out[columns(j, part)] for j in range(4)])
    small = [
        self_norm_gain,
        self_norm_bias,
        cross_norm_gain,
        cross_norm_bias,
        dense_norm_gain,
        dense_norm_bias,
        dense_out_bias,
    ]
    small += [dense_in_bias[columns(j, part)] for j in range(4)]
    small = sum(
        jnp.pad(value[None], ((i, 15 - i), (0, width - part))) for i, value in enumerate(small)
    )
    self_gather = gather([self_query, self_key, self_value, self_output], small)

    def exchange(value):
        blocks = value.reshape((mem, examples) + value.shape[1:])
        return lax.all_to_all(blocks, "mem", 0, 0, tiled=True)

    all_memory = exchange(memory)
    self_gather.send_slow()
    sent = self_gather.came
    self_gather.send_fast(*sent)
    cross_gather.send_slow(*sent)
    sent = [*self_gather.far, *cross_gather.came, all_memory]
    self_gather.far = [after(piece, *sent) for piece in self_gather.far]
    self_weights = self_gather.whole()
    cross_gather.send_fast(*self_gather.far)
    in_gather.send_slow(*self_gather.far)

    half = (2, part, width)
    grads_like = [
        (ANY, shape_of((slow,) + half, BF)),
        (ANY, shape_of((fast - 1, slow) + half, BF)),
        [(ANY, shape_of((slow,) + half, BF))] * fast,
    ]

    def flat(dims, dtype):
        return (VMEM, shape_of(dims, dtype))

    def per_example(value):
        dims = value.shape[1:]
        spec = pl.BlockSpec((1,) + dims, lambda e: (e,) + (0,) * len(dims))
        return (spec, value)

    def slots_of_example(value):
        spec = pl.BlockSpec((mem, 1, slots, width), lambda e: (0, e, 0, 0))
        return (spec, value)

    def scratch(*dims):
        return pltpu.VMEM(dims, BF)

    def scatter(grads, *others, vectors=None):
        return Scatter(grads, slow, fast, *others, vectors=vectors)

    wide = (rows, width)
    square = scratch(4, width, width)
    own_rows = scratch(examples, length, width)
    x1, a1, qkv, p1, o1, vec = run(
        functools.partial(self_forward, group),
        [(SMEM, where), (ANY, suffix), Gather.refs(self_weights)],
        [
            flat(wide, F32),
            flat(wide, BF),
            flat((rows, 3 * width), BF),
            flat((rows // group * GROUPS, TOGETHER * group, group), BF),
            flat(wide, BF),
            flat((16, width), F32),
        ],
        [square, own_rows, scratch(fsdp, 16, 128)],
        1 + fsdp + blocks,
    )
    cross_gather.far = [after(piece, x1, *in_gather.came) for piece in cross_gather.far]
    cross_weights = Gather.refs(cross_gather.whole())
    in_gather.send_fast(*cross_gather.far)
    out_gather.send_slow(*cross_gather.far)
    x2, a2, q2, kv, p2, o2 = run(
        cross_forward,
        [(SMEM, where), (SMEM, counts), (VMEM, x1), (VMEM, vec)]
        + [slots_of_example(all_memory), cross_weights],
        [
            flat(wide, F32),
            flat(wide, BF),
            flat(wide, BF),
            per_example(shape_of((examples, total, 2 * width), BF)),
            per_example(shape_of((examples, GROUPS, TOGETHER * length, total), BF)),
            flat(wide, BF),
        ],
        [square],
        blocks,
        (examples,),
    )
    small = [after(piece, x1)[:, 2 * part + 7 : 2 * part + 11, :part] for piece in self_weights[0]]
    order = jnp.arange(fsdp) ^ f
    bias_in = jnp.take(jnp.concatenate(small), order % fast * slow + order // fast, axis=0)
    bias_in = bias_in.astype(F32).reshape(1, inner)
    in_gather.far = [after(piece, x2, *out_gather.came) for piece in in_gather.far]
    in_weights = Gather.refs(in_gather.whole())
    out_gather.send_fast(*in_gather.far)
    a3, h, slope, *grads = run(
        dense_inner,
        [(SMEM, where), (VMEM, x2), (VMEM, vec), (VMEM, bias_in), (ANY, cotangent), in_weights],
        [flat(wide, BF), flat((rows, inner), BF), flat((rows, inner), BF)] + grads_like,
        [square, scratch(fsdp, 4, part, width), own_rows],
        1 + blocks,
    )
    out_gather.far = [after(piece, a3) for piece in out_gather.far]
    out_weights = Gather.refs(out_gather.whole())
    out_scatter = scatter(grads, *out_gather.far)
    out_sum = out_scatter.add_cores()
    out_scatter.send_fast()
    y, du, vecs_y, bias_grad, *grads = run(
        dense_outer,
        [(SMEM, where), (VMEM, after(x2, *out_sum)), (VMEM, vec), (VMEM, a3), (VMEM, h)]
        + [(VMEM, slope), (ANY, cotangent), out_weights],
        [
            flat((examples, length, width), BF),
            flat((rows, inner), BF),
            flat((1, width), F32),
            flat((1, inner), F32),
        ]
        + grads_like,
        [scratch(fsdp, 4, part, width), square, own_rows],
        1 + blocks,
    )
    in_grads = grads
    gx2, vecs_dense = run(
        dense_back,
        [(SMEM, where), (VMEM, x2), (VMEM, vec), (VMEM, du), (ANY, cotangent), in_weights],
        [flat(wide, F32), flat((2, width), F32)],
        [square, own_rows],
        1 + blocks,
    )
    out_total = out_scatter.add_fast(gx2)
    out_scatter.send_slow()
    in_scatter = scatter(in_grads, out_total)
    in_sum = in_scatter.add_cores()
    in_scatter.send_fast()
    gx1, vecs_cross, dkv, dq2, grad_memory = run(
        cross_backward,
        [(SMEM, where), (VMEM, x1), (VMEM, vec), (VMEM, after(gx2, out_total, *in_sum)), (VMEM, q2)]
        + [per_example(kv), per_example(p2), cross_weights],
        [
            flat(wide, F32),
            flat((2, width), F32),
            per_example(shape_of((examples, total, 2 * width), BF)),
            flat(wide, BF),
            [per_example(shape_of((examples, slots, width), BF))] * mem,
        ],
        [square, scratch(*wide), scratch(total, width)],
        blocks,
        (examples,),
    )
    out_final = out_scatter.add_slow(gx1)
    mem_pieces = grad_memory[:1] + [swap(grad_memory[d], "mem", d) for d in range(1, mem)]
    grads = run(
        cross_grads,
        [(SMEM, where), (VMEM, after(gx2, out_final)), (VMEM, a2), (VMEM, o2), (VMEM, dq2)]
        + [(VMEM, dkv), (ANY, all_memory)],
        grads_like,
        [square, scratch(examples, total, width)],
        max(mem, blocks),
    )
    in_total = in_scatter.add_fast()
    in_scatter.send_slow()
    cross_scatter = scatter(grads, in_total)
    cross_sum = cross_scatter.add_cores()
    cross_scatter.send_fast()
    gx1 = after(gx1, *cross_sum)
    suffix_part, vecs_self, *grads = run(
        functools.partial(self_backward, group),
        [(SMEM, where), (ANY, suffix), (VMEM, vec), (VMEM, gx1), (VMEM, a1)]
        + [(VMEM, qkv), (VMEM, p1), (VMEM, o1)]
        + [[(VMEM, x) for x in (vecs_cross, vecs_dense, vecs_y, bias_grad)], Gather.refs(self_weights)],
        [flat((examples, length, width), BF), flat((16, width), BF)] + grads_like,
        [square, own_rows, square, scratch(rows, 3 * width), scratch(*wide)],
        1 + blocks,
    )
    cross_total = cross_scatter.add_fast(suffix_part)
    cross_scatter.send_slow()
    in_final = in_scatter.add_slow(suffix_part)
    others = [cross_total, in_final]
    self_scatter = scatter(grads, *others, vectors=vecs_self)
    self_sum = self_scatter.add_cores()
    self_scatter.send_fast()
    self_total = self_scatter.add_fast(*mem_pieces[1:3])
    self_scatter.send_slow()

    dense_sum = after(jnp.concatenate([out_final, in_final]), self_total)
    dense_sum = Replicas(dense_sum, 2 * part, across)
    cross_sum = Replicas(cross_scatter.add_slow(self_total), part, across)
    y_rows = spread_across(after(y, self_total), mem)
    suffix_part = spread_across(after(suffix_part, self_total), mem)
    (block_output, suffix_grad), memory_grad = place(where, [y_rows, suffix_part], mem_pieces)
    (out_low, in_low, out_high, in_high), _ = dense_sum.combine(c, self_total)
    grad_in = jnp.concatenate([in_low[:part], in_low[part:], in_high[:part], in_high[part:]], axis=1)
    grad_out = jnp.concatenate([out_low, out_high])
    grad_cross, _ = cross_sum.combine(c)
    self_final = self_scatter.add_slow(block_output, grad_in, grad_out, *grad_cross)
    grad_self, vectors = Replicas(self_final, part, across).combine(c)

    def vector(i):
        return lax.dynamic_slice(vectors, (i, f * part), (1, part)).reshape(part)

    return (
        block_output,
        suffix_grad,
        memory_grad,
        vector(0),
        vector(1),
        *grad_self,
        vector(2),
        vector(3),
        *grad_cross,
        vector(4),
        vector(5),
        grad_in,
        lax.dynamic_slice_in_dim(vectors[7:11].reshape(-1), f * (inner // fsdp), inner // fsdp, 0),
        grad_out,
        vector(6),
    )


def solution(mesh):
    rows = P("fsdp", None, None)
    matrix = P("fsdp", None)
    vector = P("fsdp")
    attention = (vector, vector, matrix, matrix, matrix, matrix)
    params = attention + attention + (vector, vector, matrix, vector, matrix, vector)
    return jax.shard_map(
        per_device,
        mesh=mesh,
        in_specs=(rows, P("fsdp", "mem", None), vector, rows) + params,
        out_specs=(rows, rows, P("fsdp", "mem", None)) + params,
        check_vma=False,
    )
```

```python
import functools

import jax
import jax.numpy as jnp
from jax import lax
from jax.experimental import pallas as pl
from jax.experimental.pallas import tpu as pltpu
from jax.sharding import PartitionSpec as P

HEADS = 12
HEAD = 64
TOGETHER = 4
GROUPS = HEADS // TOGETHER
LANES = TOGETHER * HEAD
SCALE = HEAD ** (-0.5)
BF = jnp.bfloat16
F32 = jnp.float32
ANY = pl.BlockSpec(memory_space=pl.ANY)
SMEM = pl.BlockSpec(memory_space=pltpu.SMEM)
VMEM = pl.BlockSpec(memory_space=pltpu.VMEM)


def swap(value, axis, distance):
    size = lax.axis_size(axis)
    return lax.ppermute(value, axis, [(i, i ^ distance) for i in range(size)])


def after(value, *others):
    return lax.optimization_barrier((value, *others))[0] if others else value


def fsdp_split(size):
    slow = 4 if size % 4 == 0 else 1
    return slow, size // slow


def dot(left, right):
    return jnp.dot(left, right, preferred_element_type=F32)


def dot_nt(left, right):
    return lax.dot_general(left, right, (((1,), (1,)), ((), ())), preferred_element_type=F32)


def dot_tn(left, right):
    return lax.dot_general(left, right, (((0,), (0,)), ((), ())), preferred_element_type=F32)


def rows_of(start, size):
    return pl.ds(pl.multiple_of(start, 16), size)


def block(ref, by_rows, shard, which):
    if by_rows:
        return ref.at[shard, pl.ds(which * 2, 2)]
    rows = ref.shape[1] // SHARDS[0]
    return ref.at[pl.ds(which * 2, 2), rows_of(shard * rows, rows)]


SHARDS = [0]


class Copies:
    def __init__(self, sems):
        self.sems = sems
        self.next = 0

    def start(self, source, target):
        copy = pltpu.make_async_copy(source, target, self.sems.at[self.next])
        self.next += 1
        copy.start()
        return copy


def wait_all(copies):
    for copy in copies:
        copy.wait()


def load_weight(where, whole, weights, copies, by_rows=False):
    z, y, c = where[0], where[1], where[2]
    rows = whole.shape[2] if by_rows else whole.shape[1] // SHARDS[0]
    started = []
    for which, pieces in ((c, weights[0]), (1 - c, weights[1])):
        fast = len(pieces)
        for b, piece in enumerate(pieces):
            for k in range(piece.shape[0]):
                shard = (z ^ k) * fast + (y ^ b)
                for i in range(2):
                    source = piece.at[k, pl.ds(i * rows, rows)]
                    if by_rows:
                        target = whole.at[shard, 2 * which + i]
                    else:
                        target = whole.at[2 * which + i, rows_of(shard * rows, rows)]
                    started.append(copies.start(source, target))
    return started


def store_grad(where, whole, near, far, theirs, copies, by_rows=False):
    y, c = where[1], where[2]
    fast, slow = len(theirs), near.shape[0]
    started = []
    for b in range(fast):
        for k in range(slow):
            shard = k * fast + (y ^ b)
            mine = far.at[b - 1, k] if b else near.at[k]
            started.append(copies.start(block(whole, by_rows, shard, 1 - c), theirs[b].at[k]))
            started.append(copies.start(block(whole, by_rows, shard, c), mine))
    return started


def my_examples(where, source, target, copies):
    count = target.shape[0]
    return copies.start(source.at[pl.ds(where[3] * count, count)], target)


def normalise(values):
    centred = values - jnp.mean(values, axis=-1, keepdims=True)
    scale = lax.rsqrt(jnp.mean(centred * centred, axis=-1, keepdims=True) + 1e-06)
    return centred * scale, scale


def norm_back(grad, gain, hat, scale):
    inner = grad * gain
    mean = jnp.mean(inner, axis=-1, keepdims=True)
    along = jnp.mean(inner * hat, axis=-1, keepdims=True)
    return (
        scale * (inner - mean - hat * along),
        jnp.sum(grad * hat, axis=0, keepdims=True),
        jnp.sum(grad, axis=0, keepdims=True),
    )


def head_mask(rows):
    shape = (TOGETHER * rows, LANES)
    row = lax.broadcasted_iota(jnp.int32, shape, 0) // rows
    lane = lax.broadcasted_iota(jnp.int32, shape, 1) // HEAD
    return (row == lane).astype(F32)


def stack_heads(value, mask):
    return (jnp.concatenate([value] * TOGETHER, axis=0).astype(F32) * mask).astype(BF)


def merge_heads(value, mask):
    rows = value.shape[0] // TOGETHER
    value = value * mask
    total = value[:rows]
    for h in range(1, TOGETHER):
        total = total + value[h * rows : (h + 1) * rows]
    return total


def columns(j, width):
    return slice(j * width, (j + 1) * width)


def self_forward(
    group, where, suffix, weights, x1, a1, qkv, p1, o1, vec, weight, start, small, sems
):
    rows, width = x1.shape
    copies = Copies(sems)
    first = my_examples(where, suffix, start, copies)
    fast, slow = len(weights[0]), weights[0][0].shape[0]
    part = width // (fast * slow)
    vectors = []
    for b, piece in enumerate(weights[0]):
        for k in range(slow):
            source = piece.at[k, pl.ds(2 * part, 16), pl.ds(0, 128)]
            vectors.append(copies.start(source, small.at[b * slow + k]))
    loads = load_weight(where, weight, weights, copies)
    wait_all(vectors)
    lane = lax.broadcasted_iota(jnp.int32, (128, width), 0)
    place = lax.broadcasted_iota(jnp.int32, (128, width), 1) - lane
    together = jnp.zeros(vec.shape, F32)
    for i in range(fast * slow):
        shard = (where[0] ^ (i % slow)) * fast + (where[1] ^ (i // slow))
        chosen = ((place == shard * part) & (lane < part)).astype(F32).astype(BF)
        together = together + dot(small[i], chosen)
    vec[...] = together
    first.wait()
    values = start[...].reshape(rows, width).astype(F32)
    hat, _ = normalise(values)
    a1[...] = (hat * vec[0:1, :] + vec[1:2, :]).astype(BF)
    wait_all(loads)
    for j in range(3):
        qkv[:, columns(j, width)] = dot(a1[...], weight[j]).astype(BF)
    mask = head_mask(group)
    length = suffix.shape[1]
    shape = (TOGETHER * group, group)
    row = lax.broadcasted_iota(jnp.int32, shape, 0) % group
    col = lax.broadcasted_iota(jnp.int32, shape, 1)
    seen = (row // length == col // length) & (row >= col)
    for r in range(rows // group):
        here = columns(r, group)
        for g in range(GROUPS):
            lanes = [slice(i * width + g * LANES, i * width + (g + 1) * LANES) for i in range(3)]
            queries = stack_heads(qkv[here, lanes[0]], mask)
            scores = dot_nt(queries, qkv[here, lanes[1]]) * SCALE
            scores = jnp.where(seen, scores, -1e30)
            powers = jnp.exp(scores - jnp.max(scores, axis=-1, keepdims=True))
            probs = (powers / jnp.sum(powers, axis=-1, keepdims=True)).astype(BF)
            p1[r * GROUPS + g] = probs
            found = dot(probs, qkv[here, lanes[2]])
            o1[here, lanes[0]] = merge_heads(found, mask).astype(BF)
    x1[...] = values + dot(o1[...], weight[3])


def cross_forward(
    where, counts, x1, vec, memory, weights, x2, a2, q2, kv, p2, o2, weight, sems
):
    rows, width = x1.shape
    examples = pl.num_programs(0)
    e = pl.program_id(0)
    total = kv.shape[1]
    length = p2.shape[2] // TOGETHER

    @pl.when(e == 0)
    def _():
        loads = load_weight(where, weight, weights, Copies(sems))
        hat, _ = normalise(x1[...])
        a2[...] = (hat * vec[2:3, :] + vec[3:4, :]).astype(BF)
        wait_all(loads)
        q2[...] = dot(a2[...], weight[0]).astype(BF)

    tokens = memory[...].reshape(total, width)
    for j in range(2):
        kv[0, :, columns(j, width)] = dot(tokens, weight[1 + j]).astype(BF)
    mask = head_mask(length)
    position = lax.broadcasted_iota(jnp.int32, (1, total), 1)
    valid = position < counts[where[3] * examples + e]
    here = rows_of(e * length, length)
    probs = []
    for g in range(GROUPS):
        lanes = columns(g, LANES)
        queries = stack_heads(q2[here, lanes], mask)
        scores = dot_nt(queries, kv[0, :, lanes]) * SCALE
        scores = jnp.where(valid, scores, -1e30)
        top = jnp.maximum(jnp.max(scores, axis=-1, keepdims=True), 0.0)
        powers = jnp.exp(scores - top)
        weight_sum = jnp.sum(powers, axis=-1, keepdims=True) + jnp.exp(-top)
        probs.append((powers / weight_sum).astype(BF))
    for g in range(GROUPS):
        p2[0, g] = probs[g]
        found = dot(probs[g], kv[0, :, width + g * LANES : width + (g + 1) * LANES])
        o2[here, columns(g, LANES)] = merge_heads(found, mask).astype(BF)

    @pl.when(e == examples - 1)
    def _():
        x2[...] = x1[...] + dot(o2[...], weight[3])


def dense_inner(
    where, x2, vec, bias, cotangent, weights, a3, h, slope, near, far, theirs,
    weight, grad, cot, sems,
):
    rows, width = x2.shape
    copies = Copies(sems)
    cot_copy = my_examples(where, cotangent, cot, copies)
    loads = load_weight(where, weight, weights, copies)
    hat, _ = normalise(x2[...])
    a3[...] = (hat * vec[4:5, :] + vec[5:6, :]).astype(BF)
    cot_copy.wait()
    gy = cot[...].reshape(rows, width)
    wait_all(loads)
    flat = grad.shape[0] * grad.shape[1] * grad.shape[2]
    step = flat // grad.shape[0]
    for j in range(4):
        for half in range(2):
            cols = slice(j * width + half * 384, j * width + (half + 1) * 384)
            u = dot(a3[...], weight[j, :, half * 384 : (half + 1) * 384]) + bias[:, cols]
            square = u * u
            t = jnp.tanh(0.7978845608 * u * (1.0 + 0.044715 * square))
            h[:, cols] = (0.5 * u * (1.0 + t)).astype(BF)
            slope[:, cols] = (
                0.5 * (1.0 + t)
                + (0.5 * 0.7978845608) * u * (1.0 - t * t) * (1.0 + (3.0 * 0.044715) * square)
            ).astype(BF)
            part = dot_tn(h[:, cols], gy).astype(BF)
            per = 384 // step
            grad[cols.start // step : cols.start // step + per] = part.reshape(
                (per,) + grad.shape[1:]
            )
    wait_all(store_grad(where, grad, near, far, theirs, Copies(sems), True))


def dense_outer(
    where, x2, vec, a3, h, slope, cotangent, weights, y, du, vecs, bias_grad, near, far, theirs,
    weight, grad, cot, sems,
):
    rows, width = x2.shape
    copies = Copies(sems)
    cot_copy = my_examples(where, cotangent, cot, copies)
    wait_all(load_weight(where, weight, weights, copies, True))
    cot_copy.wait()
    gy = cot[...].reshape(rows, width)
    shards = weight.shape[0]
    step = weight.shape[1] * weight.shape[2]
    whole = weight[...].reshape(shards * step, width)
    for j in range(4):
        cols = columns(j, width)
        low = (dot_nt(gy, whole[cols]) * slope[:, cols].astype(F32)).astype(BF)
        du[:, cols] = low
        bias_grad[:, cols] = jnp.sum(low.astype(F32), axis=0, keepdims=True)
        grad[j] = dot_tn(a3[...], low).astype(BF)
    started = store_grad(where, grad, near, far, theirs, Copies(sems))
    result = x2[...] + dot(h[...], whole) + vec[6:7, :]
    y[...] = result.astype(BF).reshape(y.shape)
    vecs[...] = jnp.sum(gy.astype(F32), axis=0, keepdims=True)
    wait_all(started)


def dense_back(where, x2, vec, du, cotangent, weights, gx2, vecs, weight, cot, sems):
    rows, width = x2.shape
    copies = Copies(sems)
    cot_copy = my_examples(where, cotangent, cot, copies)
    loads = load_weight(where, weight, weights, copies)
    hat, scale = normalise(x2[...])
    cot_copy.wait()
    wait_all(loads)
    da3 = dot_nt(du[:, columns(0, width)], weight[0])
    for j in range(1, 4):
        da3 = da3 + dot_nt(du[:, columns(j, width)], weight[j])
    back, gain_grad, shift_grad = norm_back(da3, vec[4:5, :], hat, scale)
    gx2[...] = cot[...].reshape(rows, width).astype(F32) + back
    vecs[0:1, :] = gain_grad
    vecs[1:2, :] = shift_grad


def cross_backward(
    where, x1, vec, gx2, q2, kv, p2, weights, gx1, vecs, dkv, dq2, out_mem, weight, do2, moved, sems
):
    rows, width = x1.shape
    examples = pl.num_programs(0)
    e = pl.program_id(0)
    length = p2.shape[2] // TOGETHER

    @pl.when(e == 0)
    def _():
        wait_all(load_weight(where, weight, weights, Copies(sems)))
        do2[...] = dot_nt(gx2[...].astype(BF), weight[3]).astype(BF)

    mask = head_mask(length)
    here = rows_of(e * length, length)
    for g in range(GROUPS):
        lanes = columns(g, LANES)
        value_lanes = slice(width + g * LANES, width + (g + 1) * LANES)
        queries = stack_heads(q2[here, lanes], mask)
        grads = stack_heads(do2[here, lanes], mask)
        probs = p2[0, g]
        dp = dot_nt(grads, kv[0, :, value_lanes])
        wide = probs.astype(F32)
        row_sum = jnp.sum(wide * dp, axis=-1, keepdims=True)
        dz = (wide * (dp - row_sum)).astype(BF)
        dkv[0, :, value_lanes] = dot_tn(probs, grads).astype(BF)
        dkv[0, :, lanes] = (dot_tn(dz, queries) * SCALE).astype(BF)
        dq2[here, lanes] = (merge_heads(dot(dz, kv[0, :, lanes]), mask) * SCALE).astype(BF)
    back = dot_nt(dkv[0, :, :width], weight[1]) + dot_nt(dkv[0, :, width:], weight[2])
    moved[...] = back.astype(BF)
    for d, out in enumerate(out_mem):
        slots = out.shape[1]
        out[0] = moved[rows_of((where[3] ^ d) * slots, slots), :]

    @pl.when(e == examples - 1)
    def _():
        hat, scale = normalise(x1[...])
        back, gain_grad, shift_grad = norm_back(
            dot_nt(dq2[...], weight[0]), vec[2:3, :], hat, scale
        )
        gx1[...] = gx2[...] + back
        vecs[0:1, :] = gain_grad
        vecs[1:2, :] = shift_grad


def cross_grads(
    where, gx2, a2, o2, dq2, dkv, all_memory, near, far, theirs, grad, memory, sems
):
    rows, width = gx2.shape
    examples, total, _ = memory.shape
    mem, _, slots, _ = all_memory.shape
    copies = Copies(sems)
    loads = [
        copies.start(all_memory.at[d], memory.at[:, d * slots : (d + 1) * slots, :])
        for d in range(mem)
    ]
    grad[0] = dot_tn(a2[...], dq2[...]).astype(BF)
    grad[3] = dot_tn(o2[...], gx2[...].astype(BF)).astype(BF)
    wait_all(loads)
    flat = memory[...].reshape(examples * total, width)
    for j in range(2):
        part = dkv[:, :, columns(j, width)].reshape(examples * total, width)
        grad[1 + j] = dot_tn(flat, part).astype(BF)
    wait_all(store_grad(where, grad, near, far, theirs, Copies(sems)))


def self_backward(
    group, where, suffix, vec, gx1, a1, qkv, p1, o1, parts, weights, suffix_grad, vecs,
    near, far, theirs, weight, start, grad, dqkv, do1, sems,
):
    rows, width = gx1.shape
    copies = Copies(sems)
    start_copy = my_examples(where, suffix, start, copies)
    loads = load_weight(where, weight, weights, copies)
    gs = gx1[...].astype(BF)
    grad[3] = dot_tn(o1[...], gs).astype(BF)
    wait_all(loads)
    do1[...] = dot_nt(gs, weight[3]).astype(BF)
    mask = head_mask(group)
    for r in range(rows // group):
        here = columns(r, group)
        for g in range(GROUPS):
            lanes = [slice(i * width + g * LANES, i * width + (g + 1) * LANES) for i in range(3)]
            queries = stack_heads(qkv[here, lanes[0]], mask)
            grads = stack_heads(do1[here, lanes[0]], mask)
            probs = p1[r * GROUPS + g]
            dp = dot_nt(grads, qkv[here, lanes[2]])
            wide = probs.astype(F32)
            row_sum = jnp.sum(wide * dp, axis=-1, keepdims=True)
            dz = (wide * (dp - row_sum)).astype(BF)
            dqkv[here, lanes[2]] = dot_tn(probs, grads).astype(BF)
            dqkv[here, lanes[1]] = (dot_tn(dz, queries) * SCALE).astype(BF)
            dq = merge_heads(dot(dz, qkv[here, lanes[1]]), mask) * SCALE
            dqkv[here, lanes[0]] = dq.astype(BF)
    for j in range(3):
        grad[j] = dot_tn(a1[...], dqkv[:, columns(j, width)]).astype(BF)
    start_copy.wait()
    started = store_grad(where, grad, near, far, theirs, Copies(sems))
    da1 = dot_nt(dqkv[:, columns(0, width)], weight[0])
    for j in range(1, 3):
        da1 = da1 + dot_nt(dqkv[:, columns(j, width)], weight[j])
    hat, scale = normalise(start[...].reshape(rows, width).astype(F32))
    back, gain_grad, shift_grad = norm_back(da1, vec[0:1, :], hat, scale)
    suffix_grad[...] = (gx1[...] + back).astype(BF).reshape(suffix_grad.shape)
    found = [gain_grad, shift_grad]
    for ref in parts:
        for r in range(ref.shape[0]):
            found += [ref[r : r + 1, columns(j, width)] for j in range(ref.shape[1] // width)]
    found.append(jnp.zeros((vecs.shape[0] - len(found), width), F32))
    vecs[...] = jnp.concatenate(found, axis=0).astype(BF)
    wait_all(started)


def run(kernel, inputs, outputs, scratch, copies, grid=()):
    def leaf(x):
        return isinstance(x, tuple) and len(x) == 2 and isinstance(x[0], pl.BlockSpec)

    flat_in, tree_in = jax.tree.flatten(inputs, is_leaf=leaf)
    flat_out, tree_out = jax.tree.flatten(outputs, is_leaf=leaf)

    def body(*refs):
        first, second = len(flat_in), len(flat_in) + len(flat_out)
        given = jax.tree.unflatten(tree_in, refs[:first])
        taken = jax.tree.unflatten(tree_out, refs[first:second])
        kernel(*given, *taken, *refs[second:])

    found = pl.pallas_call(
        body,
        grid=grid,
        in_specs=[spec for spec, _ in flat_in],
        out_specs=[spec for spec, _ in flat_out],
        out_shape=[shape for _, shape in flat_out],
        scratch_shapes=scratch + [pltpu.SemaphoreType.DMA((copies,))],
        compiler_params=pltpu.CompilerParams(vmem_limit_bytes=56 * 1024 * 1024),
        cost_estimate=pl.CostEstimate(
            flops=0, bytes_accessed=0, transcendentals=0
        ),
    )(*[x for _, x in flat_in])
    return jax.tree.unflatten(tree_out, found)


def shape_of(dims, dtype):
    return jax.ShapeDtypeStruct(tuple(dims), dtype)


def over_slow(value, slow, fast):
    groups = [[k * fast + b for k in range(slow)] for b in range(fast)]
    return lax.all_to_all(value, "fsdp", 0, 0, axis_index_groups=groups, tiled=True)


class Gather:
    def __init__(self, half, slow, fast):
        self.half, self.slow, self.fast = half, slow, fast

    def send_slow(self, *others):
        half = after(self.half, *others)
        self.came = [half] + [swap(half, "fsdp", k * self.fast) for k in range(1, self.slow)]

    def send_fast(self, *others):
        self.near = jnp.stack([after(piece, *others) for piece in self.came])
        self.near_other = swap(self.near, "mem", 1)
        self.far = [swap(self.near, "fsdp", b) for b in range(1, self.fast)]

    def whole(self):
        mine = [self.near] + self.far
        theirs = [self.near_other] + [swap(piece, "mem", 1) for piece in self.far]
        return mine, theirs

    @staticmethod
    def refs(weights):
        return [[(ANY, x) for x in some] for some in weights]


class Scatter:
    def __init__(self, grads, slow, fast, *others, vectors=None):
        self.near, self.far, theirs = grads
        self.slow, self.fast, self.vectors = slow, fast, vectors
        theirs = [after(part, *others) for part in theirs]
        self.sent = [None] * fast
        for b in range(1, fast):
            self.sent[b] = swap(theirs[b] if b > 1 else self.pack(theirs[b]), "mem", 1)
        self.sent[0] = swap(theirs[0], "mem", 1)
        if vectors is not None:
            self.sent[1], came = self.unpack(self.sent[1], theirs[1].shape)
            self.vectors = vectors.astype(F32) + came

    def pack(self, value):
        if self.vectors is None:
            return value
        width = value.shape[-1]
        return jnp.concatenate([value.reshape(-1, width), self.vectors.astype(BF)])

    def unpack(self, value, shape):
        if self.vectors is None:
            return value, 0.0
        rows = value.shape[0] - self.vectors.shape[0]
        return value[:rows].reshape(shape), value[rows:].astype(F32)

    def add_cores(self):
        self.out = [
            self.pack((self.far[b].astype(F32) + self.sent[b + 1].astype(F32)).astype(BF))
            for b in range(self.fast - 1)
        ]
        return self.out

    def send_fast(self):
        self.came = [swap(part, "fsdp", b + 1) for b, part in enumerate(self.out)]

    def add_fast(self, *others):
        total = after(self.near, *others).astype(F32) + self.sent[0].astype(F32)
        vectors = 0.0 if self.vectors is None else self.vectors.astype(BF).astype(F32)
        for part in self.came:
            part, more = self.unpack(part, total.shape)
            total = total + part.astype(F32)
            vectors = vectors + more
        self.total = total.astype(BF).reshape(self.slow, -1, total.shape[-1])
        if self.vectors is not None:
            low = jnp.broadcast_to(vectors.astype(BF), (self.slow,) + vectors.shape)
            self.total = jnp.concatenate([self.total, low], axis=1)
        return self.total

    def send_slow(self):
        self.came = over_slow(self.total, self.slow, self.fast)

    def add_slow(self, *others):
        return jnp.sum(after(self.came, *others).astype(F32), axis=0)


class Replicas:
    def __init__(self, value, rows, across):
        self.rows = rows
        k = 1
        while 2 * k < across:
            low = value.astype(BF)
            value = low.astype(F32) + swap(low, "mem", 2 * k).astype(F32)
            k *= 2
        low = value.astype(BF)
        self.halves = [low, swap(low, "mem", 2 * k)] if across > 1 else [low]

    def swap_cores(self, *others):
        halves, _ = lax.optimization_barrier((self.halves, others))
        self.others = [swap(half[: 2 * self.rows], "mem", 1) for half in halves]

    def combine(self, c):
        rows = self.rows
        other = sum(half.astype(F32) for half in self.others)
        mine = sum(half.astype(F32) for half in self.halves)
        vectors, mine = mine[2 * rows :], mine[: 2 * rows]
        first = jnp.where(c == 0, mine, other)
        second = jnp.where(c == 0, other, mine)
        return [first[:rows], first[rows:], second[:rows], second[rows:]], vectors


def place_rows(where, blocks, outs, scratch, sems):
    copies = Copies(sems)
    loads = []
    for i, (even, odd) in enumerate(blocks):
        for d, piece in enumerate(even):
            loads.append((copies.start(piece, scratch.at[i, 2 * d]), i, 2 * d))
            loads.append((copies.start(odd.at[d], scratch.at[i, 2 * d + 1]), i, 2 * d + 1))
    examples = scratch.shape[2]
    stores = []
    for load, i, d in loads:
        load.wait()
        target = outs[i].at[pl.ds((where[3] ^ d) * examples, examples)]
        stores.append(copies.start(scratch.at[i, d], target))
    wait_all(stores)


def place_memory(where, pieces, out, scratch, sems):
    examples = pieces[0].shape[0]
    copies = Copies(sems)
    loads = [copies.start(piece, scratch.at[d]) for d, piece in enumerate(pieces)]
    stores = []
    for d, load in enumerate(loads):
        load.wait()
        target = out.at[pl.ds((where[3] ^ d) * examples, examples)]
        stores.append(copies.start(scratch.at[d], target))
    wait_all(stores)


def spread_across(value, mem):
    return [value] + [swap(value, "mem", d) for d in range(2, mem, 2)]


def per_device(
    suffix,
    memory,
    counts,
    cotangent,
    self_norm_gain,
    self_norm_bias,
    self_query,
    self_key,
    self_value,
    self_output,
    cross_norm_gain,
    cross_norm_bias,
    cross_query,
    cross_key,
    cross_value,
    cross_output,
    dense_norm_gain,
    dense_norm_bias,
    dense_in,
    dense_in_bias,
    dense_out,
    dense_out_bias,
):
    f = lax.axis_index("fsdp")
    m = lax.axis_index("mem")
    c = m % 2
    fsdp = lax.axis_size("fsdp")
    mem = lax.axis_size("mem")
    across = mem // 2
    slow, fast = fsdp_split(fsdp)
    SHARDS[0] = fsdp
    where = jnp.stack([f // fast, f % fast, c, m]).astype(jnp.int32)
    examples = suffix.shape[0] // mem
    length = suffix.shape[1]
    width = suffix.shape[2]
    slots = memory.shape[1]
    total = mem * slots
    rows = examples * length
    inner = dense_in.shape[1]
    part = width // fsdp
    group = min(128, rows)
    blocks = 4 * fsdp

    def gather(matrices, *others):
        halves = [jnp.concatenate(matrices[:2]), jnp.concatenate(matrices[2:])]
        half = jnp.concatenate([jnp.where(c == 0, *halves), *others])
        return Gather(half, slow, fast)

    cross_gather = gather([cross_query, cross_key, cross_value, cross_output])
    in_gather = gather([dense_in[:, columns(j, width)] for j in range(4)])
    out_gather = gather([dense_out[columns(j, part)] for j in range(4)])
    small = [
        self_norm_gain,
        self_norm_bias,
        cross_norm_gain,
        cross_norm_bias,
        dense_norm_gain,
        dense_norm_bias,
        dense_out_bias,
    ]
    small += [dense_in_bias[columns(j, part)] for j in range(4)]
    small = sum(
        jnp.pad(value[None], ((i, 15 - i), (0, width - part))) for i, value in enumerate(small)
    )
    self_gather = gather([self_query, self_key, self_value, self_output], small)

    def exchange(value):
        blocks = value.reshape((mem, examples) + value.shape[1:])
        return lax.all_to_all(blocks, "mem", 0, 0, tiled=True)

    all_memory = exchange(memory)
    self_gather.send_slow()
    sent = self_gather.came
    self_gather.send_fast(*sent)
    cross_gather.send_slow(*sent)
    sent = [*self_gather.far, *cross_gather.came, all_memory]
    self_gather.far = [after(piece, *sent) for piece in self_gather.far]
    self_weights = self_gather.whole()
    cross_gather.send_fast(*self_gather.far)
    in_gather.send_slow(*self_gather.far)

    half = (2, part, width)
    grads_like = [
        (ANY, shape_of((slow,) + half, BF)),
        (ANY, shape_of((fast - 1, slow) + half, BF)),
        [(ANY, shape_of((slow,) + half, BF))] * fast,
    ]

    def flat(dims, dtype):
        return (VMEM, shape_of(dims, dtype))

    def per_example(value):
        dims = value.shape[1:]
        spec = pl.BlockSpec((1,) + dims, lambda e: (e,) + (0,) * len(dims))
        return (spec, value)

    def slots_of_example(value):
        spec = pl.BlockSpec((mem, 1, slots, width), lambda e: (0, e, 0, 0))
        return (spec, value)

    def scratch(*dims):
        return pltpu.VMEM(dims, BF)

    def scatter(grads, *others, vectors=None):
        return Scatter(grads, slow, fast, *others, vectors=vectors)

    wide = (rows, width)
    square = scratch(4, width, width)
    own_rows = scratch(examples, length, width)
    x1, a1, qkv, p1, o1, vec = run(
        functools.partial(self_forward, group),
        [(SMEM, where), (ANY, suffix), Gather.refs(self_weights)],
        [
            flat(wide, F32),
            flat(wide, BF),
            flat((rows, 3 * width), BF),
            flat((rows // group * GROUPS, TOGETHER * group, group), BF),
            flat(wide, BF),
            flat((16, width), F32),
        ],
        [square, own_rows, scratch(fsdp, 16, 128)],
        1 + fsdp + blocks,
    )
    cross_gather.far = [after(piece, x1, *in_gather.came) for piece in cross_gather.far]
    cross_weights = Gather.refs(cross_gather.whole())
    in_gather.send_fast(*cross_gather.far)
    out_gather.send_slow(*cross_gather.far)
    x2, a2, q2, kv, p2, o2 = run(
        cross_forward,
        [(SMEM, where), (SMEM, counts), (VMEM, x1), (VMEM, vec)]
        + [slots_of_example(all_memory), cross_weights],
        [
            flat(wide, F32),
            flat(wide, BF),
            flat(wide, BF),
            per_example(shape_of((examples, total, 2 * width), BF)),
            per_example(shape_of((examples, GROUPS, TOGETHER * length, total), BF)),
            flat(wide, BF),
        ],
        [square],
        blocks,
        (examples,),
    )
    small = [after(piece, x1)[:, 2 * part + 7 : 2 * part + 11, :part] for piece in self_weights[0]]
    order = jnp.arange(fsdp) ^ f
    bias_in = jnp.take(jnp.concatenate(small), order % fast * slow + order // fast, axis=0)
    bias_in = bias_in.astype(F32).reshape(1, inner)
    in_gather.far = [after(piece, x2, *out_gather.came) for piece in in_gather.far]
    in_weights = Gather.refs(in_gather.whole())
    out_gather.send_fast(*in_gather.far)
    a3, h, slope, *grads = run(
        dense_inner,
        [(SMEM, where), (VMEM, x2), (VMEM, vec), (VMEM, bias_in), (ANY, cotangent), in_weights],
        [flat(wide, BF), flat((rows, inner), BF), flat((rows, inner), BF)] + grads_like,
        [square, scratch(fsdp, 4, part, width), own_rows],
        1 + blocks,
    )
    out_gather.far = [after(piece, a3) for piece in out_gather.far]
    out_weights = Gather.refs(out_gather.whole())
    out_scatter = scatter(grads, *out_gather.far)
    out_sum = out_scatter.add_cores()
    out_scatter.send_fast()
    y, du, vecs_y, bias_grad, *grads = run(
        dense_outer,
        [(SMEM, where), (VMEM, after(x2, *out_sum)), (VMEM, vec), (VMEM, a3), (VMEM, h)]
        + [(VMEM, slope), (ANY, cotangent), out_weights],
        [
            flat((examples, length, width), BF),
            flat((rows, inner), BF),
            flat((1, width), F32),
            flat((1, inner), F32),
        ]
        + grads_like,
        [scratch(fsdp, 4, part, width), square, own_rows],
        1 + blocks,
    )
    in_grads = grads
    gx2, vecs_dense = run(
        dense_back,
        [(SMEM, where), (VMEM, x2), (VMEM, vec), (VMEM, du), (ANY, cotangent), in_weights],
        [flat(wide, F32), flat((2, width), F32)],
        [square, own_rows],
        1 + blocks,
    )
    out_total = out_scatter.add_fast(gx2)
    out_scatter.send_slow()
    in_scatter = scatter(in_grads, out_total)
    in_sum = in_scatter.add_cores()
    in_scatter.send_fast()
    gx1, vecs_cross, dkv, dq2, grad_memory = run(
        cross_backward,
        [(SMEM, where), (VMEM, x1), (VMEM, vec), (VMEM, after(gx2, out_total, *in_sum)), (VMEM, q2)]
        + [per_example(kv), per_example(p2), cross_weights],
        [
            flat(wide, F32),
            flat((2, width), F32),
            per_example(shape_of((examples, total, 2 * width), BF)),
            flat(wide, BF),
            [per_example(shape_of((examples, slots, width), BF))] * mem,
        ],
        [square, scratch(*wide), scratch(total, width)],
        blocks,
        (examples,),
    )
    out_final = out_scatter.add_slow(gx1)
    mem_pieces = grad_memory[:1] + [swap(grad_memory[d], "mem", d) for d in range(1, mem)]
    grads = run(
        cross_grads,
        [(SMEM, where), (VMEM, after(gx2, out_final)), (VMEM, a2), (VMEM, o2), (VMEM, dq2)]
        + [(VMEM, dkv), (ANY, all_memory)],
        grads_like,
        [square, scratch(examples, total, width)],
        max(mem, blocks),
    )
    in_total = in_scatter.add_fast()
    in_scatter.send_slow()
    cross_scatter = scatter(grads, in_total, *mem_pieces[1:3])
    cross_sum = cross_scatter.add_cores()
    cross_scatter.send_fast()
    gx1 = after(gx1, *cross_sum)
    suffix_part, vecs_self, *grads = run(
        functools.partial(self_backward, group),
        [(SMEM, where), (ANY, suffix), (VMEM, vec), (VMEM, gx1), (VMEM, a1)]
        + [(VMEM, qkv), (VMEM, p1), (VMEM, o1)]
        + [[(VMEM, x) for x in (vecs_cross, vecs_dense, vecs_y, bias_grad)], Gather.refs(self_weights)],
        [flat((examples, length, width), BF), flat((16, width), BF)] + grads_like,
        [square, own_rows, square, scratch(rows, 3 * width), scratch(*wide)],
        1 + blocks,
    )
    self_scatter = scatter(grads, *mem_pieces[3:4], vectors=vecs_self)
    self_sum = self_scatter.add_cores()
    self_scatter.send_fast()
    cross_scatter.add_fast(*self_sum)
    cross_scatter.send_slow()
    dense_sum = jnp.concatenate([out_final, in_scatter.add_slow(*self_sum)])
    dense_sum = Replicas(dense_sum, 2 * part, across)
    y_rows = spread_across(after(y, *self_sum), mem)
    self_total = self_scatter.add_fast(*dense_sum.halves, *y_rows)
    self_scatter.send_slow()
    cross_sum = Replicas(cross_scatter.add_slow(self_total), part, across)
    suffix_rows = spread_across(after(suffix_part, self_total), mem)
    y_rows = [after(value, self_total) for value in y_rows]
    y_far = swap(jnp.stack(y_rows), "mem", 1)
    dense_sum.swap_cores(self_total)
    mem_pieces = [after(value, self_total) for value in mem_pieces]
    (memory_grad,) = run(
        place_memory,
        [(SMEM, where), [(ANY, value) for value in mem_pieces]],
        [(ANY, shape_of(memory.shape, BF))],
        [scratch(mem, examples, slots, width)],
        2 * mem,
    )
    sent = [*cross_sum.halves, *suffix_rows, *dense_sum.others, y_far, memory_grad]
    self_final = Replicas(self_scatter.add_slow(*sent), part, across)
    cross_sum.swap_cores(self_final.halves[0])
    suffix_rows = [after(value, self_final.halves[0]) for value in suffix_rows]
    suffix_far = swap(jnp.stack(suffix_rows), "mem", 1)
    blocks = [([(ANY, x) for x in y_rows], (ANY, y_far))]
    blocks += [([(ANY, x) for x in suffix_rows], (ANY, suffix_far))]
    ((block_output, suffix_grad),) = run(
        place_rows,
        [(SMEM, where), blocks],
        [[(ANY, shape_of(suffix.shape, BF))] * 2],
        [scratch(2, mem, examples, length, width)],
        4 * mem,
    )
    self_final.swap_cores(block_output)
    (out_low, in_low, out_high, in_high), _ = dense_sum.combine(c)
    grad_in = jnp.concatenate([in_low[:part], in_low[part:], in_high[:part], in_high[part:]], axis=1)
    grad_out = jnp.concatenate([out_low, out_high])
    grad_cross, _ = cross_sum.combine(c)
    grad_self, vectors = self_final.combine(c)

    def vector(i):
        return lax.dynamic_slice(vectors, (i, f * part), (1, part)).reshape(part)

    return (
        block_output,
        suffix_grad,
        memory_grad,
        vector(0),
        vector(1),
        *grad_self,
        vector(2),
        vector(3),
        *grad_cross,
        vector(4),
        vector(5),
        grad_in,
        lax.dynamic_slice_in_dim(vectors[7:11].reshape(-1), f * (inner // fsdp), inner // fsdp, 0),
        grad_out,
        vector(6),
    )


def solution(mesh):
    rows = P("fsdp", None, None)
    matrix = P("fsdp", None)
    vector = P("fsdp")
    attention = (vector, vector, matrix, matrix, matrix, matrix)
    params = attention + attention + (vector, vector, matrix, vector, matrix, vector)
    return jax.shard_map(
        per_device,
        mesh=mesh,
        in_specs=(rows, P("fsdp", "mem", None), vector, rows) + params,
        out_specs=(rows, rows, P("fsdp", "mem", None)) + params,
        check_vma=False,
    )
```

```python
import functools

import jax
import jax.numpy as jnp
from jax import lax
from jax.experimental import pallas as pl
from jax.experimental.pallas import tpu as pltpu
from jax.sharding import PartitionSpec as P

HEADS = 12
HEAD = 64
TOGETHER = 4
GROUPS = HEADS // TOGETHER
LANES = TOGETHER * HEAD
SCALE = HEAD ** (-0.5)
BF = jnp.bfloat16
F32 = jnp.float32
ANY = pl.BlockSpec(memory_space=pl.ANY)
SMEM = pl.BlockSpec(memory_space=pltpu.SMEM)
VMEM = pl.BlockSpec(memory_space=pltpu.VMEM)


def swap(value, axis, distance):
    size = lax.axis_size(axis)
    return lax.ppermute(value, axis, [(i, i ^ distance) for i in range(size)])


def after(value, *others):
    return lax.optimization_barrier((value, *others))[0] if others else value


def fsdp_split(size):
    slow = 4 if size % 4 == 0 else 1
    return slow, size // slow


def dot(left, right):
    return jnp.dot(left, right, preferred_element_type=F32)


def dot_nt(left, right):
    return lax.dot_general(left, right, (((1,), (1,)), ((), ())), preferred_element_type=F32)


def dot_tn(left, right):
    return lax.dot_general(left, right, (((0,), (0,)), ((), ())), preferred_element_type=F32)


def rows_of(start, size):
    return pl.ds(pl.multiple_of(start, 16), size)


def block(ref, by_rows, shard, which):
    if by_rows:
        return ref.at[shard, pl.ds(which * 2, 2)]
    rows = ref.shape[1] // SHARDS[0]
    return ref.at[pl.ds(which * 2, 2), rows_of(shard * rows, rows)]


SHARDS = [0]


class Copies:
    def __init__(self, sems):
        self.sems = sems
        self.next = 0

    def start(self, source, target):
        copy = pltpu.make_async_copy(source, target, self.sems.at[self.next])
        self.next += 1
        copy.start()
        return copy


def wait_all(copies):
    for copy in copies:
        copy.wait()


def load_weight(where, whole, weights, copies, by_rows=False):
    z, y, c = where[0], where[1], where[2]
    rows = whole.shape[2] if by_rows else whole.shape[1] // SHARDS[0]
    started = []
    for which, pieces in ((c, weights[0]), (1 - c, weights[1])):
        fast = len(pieces)
        for b, piece in enumerate(pieces):
            for k in range(piece.shape[0]):
                shard = (z ^ k) * fast + (y ^ b)
                for i in range(2):
                    source = piece.at[k, pl.ds(i * rows, rows)]
                    if by_rows:
                        target = whole.at[shard, 2 * which + i]
                    else:
                        target = whole.at[2 * which + i, rows_of(shard * rows, rows)]
                    started.append(copies.start(source, target))
    return started


def store_grad(where, whole, near, far, theirs, copies, by_rows=False):
    y, c = where[1], where[2]
    slow, cut = near.shape[0], near.shape[0] // 2
    fast = (len(theirs) + 1) // 2
    started = []
    for b in range(fast):
        for k in range(slow):
            shard = k * fast + (y ^ b)
            mine = far.at[b - 1, k] if b else near.at[k]
            other = theirs[2 * b - 1 + k // cut].at[k % cut] if b else theirs[0].at[k]
            started.append(copies.start(block(whole, by_rows, shard, 1 - c), other))
            started.append(copies.start(block(whole, by_rows, shard, c), mine))
    return started


def my_examples(where, source, target, copies):
    count = target.shape[0]
    return copies.start(source.at[pl.ds(where[3] * count, count)], target)


def normalise(values):
    centred = values - jnp.mean(values, axis=-1, keepdims=True)
    scale = lax.rsqrt(jnp.mean(centred * centred, axis=-1, keepdims=True) + 1e-06)
    return centred * scale, scale


def norm_back(grad, gain, hat, scale):
    inner = grad * gain
    mean = jnp.mean(inner, axis=-1, keepdims=True)
    along = jnp.mean(inner * hat, axis=-1, keepdims=True)
    return (
        scale * (inner - mean - hat * along),
        jnp.sum(grad * hat, axis=0, keepdims=True),
        jnp.sum(grad, axis=0, keepdims=True),
    )


def head_mask(rows):
    shape = (TOGETHER * rows, LANES)
    row = lax.broadcasted_iota(jnp.int32, shape, 0) // rows
    lane = lax.broadcasted_iota(jnp.int32, shape, 1) // HEAD
    return (row == lane).astype(F32)


def stack_heads(value, mask):
    return (jnp.concatenate([value] * TOGETHER, axis=0).astype(F32) * mask).astype(BF)


def merge_heads(value, mask):
    rows = value.shape[0] // TOGETHER
    value = value * mask
    total = value[:rows]
    for h in range(1, TOGETHER):
        total = total + value[h * rows : (h + 1) * rows]
    return total


def columns(j, width):
    return slice(j * width, (j + 1) * width)


def self_forward(
    group, where, suffix, weights, x1, a1, qkv, p1, o1, vec, weight, start, small, sems
):
    rows, width = x1.shape
    copies = Copies(sems)
    first = my_examples(where, suffix, start, copies)
    fast, slow = len(weights[0]), weights[0][0].shape[0]
    part = width // (fast * slow)
    vectors = []
    for b, piece in enumerate(weights[0]):
        for k in range(slow):
            source = piece.at[k, pl.ds(2 * part, 16), pl.ds(0, 128)]
            vectors.append(copies.start(source, small.at[b * slow + k]))
    loads = load_weight(where, weight, weights, copies)
    wait_all(vectors)
    lane = lax.broadcasted_iota(jnp.int32, (128, width), 0)
    place = lax.broadcasted_iota(jnp.int32, (128, width), 1) - lane
    together = jnp.zeros(vec.shape, F32)
    for i in range(fast * slow):
        shard = (where[0] ^ (i % slow)) * fast + (where[1] ^ (i // slow))
        chosen = ((place == shard * part) & (lane < part)).astype(F32).astype(BF)
        together = together + dot(small[i], chosen)
    vec[...] = together
    first.wait()
    values = start[...].reshape(rows, width).astype(F32)
    hat, _ = normalise(values)
    a1[...] = (hat * vec[0:1, :] + vec[1:2, :]).astype(BF)
    wait_all(loads)
    for j in range(3):
        qkv[:, columns(j, width)] = dot(a1[...], weight[j]).astype(BF)
    mask = head_mask(group)
    length = suffix.shape[1]
    shape = (TOGETHER * group, group)
    row = lax.broadcasted_iota(jnp.int32, shape, 0) % group
    col = lax.broadcasted_iota(jnp.int32, shape, 1)
    seen = (row // length == col // length) & (row >= col)
    for r in range(rows // group):
        here = columns(r, group)
        for g in range(GROUPS):
            lanes = [slice(i * width + g * LANES, i * width + (g + 1) * LANES) for i in range(3)]
            queries = stack_heads(qkv[here, lanes[0]], mask)
            scores = dot_nt(queries, qkv[here, lanes[1]]) * SCALE
            scores = jnp.where(seen, scores, -1e30)
            powers = jnp.exp(scores - jnp.max(scores, axis=-1, keepdims=True))
            probs = (powers / jnp.sum(powers, axis=-1, keepdims=True)).astype(BF)
            p1[r * GROUPS + g] = probs
            found = dot(probs, qkv[here, lanes[2]])
            o1[here, lanes[0]] = merge_heads(found, mask).astype(BF)
    x1[...] = values + dot(o1[...], weight[3])


def cross_forward(
    where, counts, x1, vec, memory, weights, x2, a2, q2, kv, p2, o2, weight, sems
):
    rows, width = x1.shape
    examples = pl.num_programs(0)
    e = pl.program_id(0)
    total = kv.shape[1]
    length = p2.shape[2] // TOGETHER

    @pl.when(e == 0)
    def _():
        loads = load_weight(where, weight, weights, Copies(sems))
        hat, _ = normalise(x1[...])
        a2[...] = (hat * vec[2:3, :] + vec[3:4, :]).astype(BF)
        wait_all(loads)
        q2[...] = dot(a2[...], weight[0]).astype(BF)

    tokens = memory[...].reshape(total, width)
    for j in range(2):
        kv[0, :, columns(j, width)] = dot(tokens, weight[1 + j]).astype(BF)
    mask = head_mask(length)
    position = lax.broadcasted_iota(jnp.int32, (1, total), 1)
    valid = position < counts[where[3] * examples + e]
    here = rows_of(e * length, length)
    probs = []
    for g in range(GROUPS):
        lanes = columns(g, LANES)
        queries = stack_heads(q2[here, lanes], mask)
        scores = dot_nt(queries, kv[0, :, lanes]) * SCALE
        scores = jnp.where(valid, scores, -1e30)
        top = jnp.maximum(jnp.max(scores, axis=-1, keepdims=True), 0.0)
        powers = jnp.exp(scores - top)
        weight_sum = jnp.sum(powers, axis=-1, keepdims=True) + jnp.exp(-top)
        probs.append((powers / weight_sum).astype(BF))
    for g in range(GROUPS):
        p2[0, g] = probs[g]
        found = dot(probs[g], kv[0, :, width + g * LANES : width + (g + 1) * LANES])
        o2[here, columns(g, LANES)] = merge_heads(found, mask).astype(BF)

    @pl.when(e == examples - 1)
    def _():
        x2[...] = x1[...] + dot(o2[...], weight[3])


def dense_inner(
    where, x2, vec, bias, cotangent, weights, a3, h, slope, near, far, theirs,
    weight, grad, cot, sems,
):
    rows, width = x2.shape
    copies = Copies(sems)
    cot_copy = my_examples(where, cotangent, cot, copies)
    loads = load_weight(where, weight, weights, copies)
    hat, _ = normalise(x2[...])
    a3[...] = (hat * vec[4:5, :] + vec[5:6, :]).astype(BF)
    cot_copy.wait()
    gy = cot[...].reshape(rows, width)
    wait_all(loads)
    flat = grad.shape[0] * grad.shape[1] * grad.shape[2]
    step = flat // grad.shape[0]
    for j in range(4):
        for half in range(2):
            cols = slice(j * width + half * 384, j * width + (half + 1) * 384)
            u = dot(a3[...], weight[j, :, half * 384 : (half + 1) * 384]) + bias[:, cols]
            square = u * u
            t = jnp.tanh(0.7978845608 * u * (1.0 + 0.044715 * square))
            h[:, cols] = (0.5 * u * (1.0 + t)).astype(BF)
            slope[:, cols] = (
                0.5 * (1.0 + t)
                + (0.5 * 0.7978845608) * u * (1.0 - t * t) * (1.0 + (3.0 * 0.044715) * square)
            ).astype(BF)
            part = dot_tn(h[:, cols], gy).astype(BF)
            per = 384 // step
            grad[cols.start // step : cols.start // step + per] = part.reshape(
                (per,) + grad.shape[1:]
            )
    wait_all(store_grad(where, grad, near, far, theirs, Copies(sems), True))


def dense_outer(
    where, x2, vec, a3, h, slope, cotangent, weights, y, du, vecs, bias_grad, near, far, theirs,
    weight, grad, cot, sems,
):
    rows, width = x2.shape
    copies = Copies(sems)
    cot_copy = my_examples(where, cotangent, cot, copies)
    wait_all(load_weight(where, weight, weights, copies, True))
    cot_copy.wait()
    gy = cot[...].reshape(rows, width)
    shards = weight.shape[0]
    step = weight.shape[1] * weight.shape[2]
    whole = weight[...].reshape(shards * step, width)
    for j in range(4):
        cols = columns(j, width)
        low = (dot_nt(gy, whole[cols]) * slope[:, cols].astype(F32)).astype(BF)
        du[:, cols] = low
        bias_grad[:, cols] = jnp.sum(low.astype(F32), axis=0, keepdims=True)
        grad[j] = dot_tn(a3[...], low).astype(BF)
    started = store_grad(where, grad, near, far, theirs, Copies(sems))
    result = x2[...] + dot(h[...], whole) + vec[6:7, :]
    y[...] = result.astype(BF).reshape(y.shape)
    vecs[...] = jnp.sum(gy.astype(F32), axis=0, keepdims=True)
    wait_all(started)


def dense_back(where, x2, vec, du, cotangent, weights, gx2, vecs, weight, cot, sems):
    rows, width = x2.shape
    copies = Copies(sems)
    cot_copy = my_examples(where, cotangent, cot, copies)
    loads = load_weight(where, weight, weights, copies)
    hat, scale = normalise(x2[...])
    cot_copy.wait()
    wait_all(loads)
    da3 = dot_nt(du[:, columns(0, width)], weight[0])
    for j in range(1, 4):
        da3 = da3 + dot_nt(du[:, columns(j, width)], weight[j])
    back, gain_grad, shift_grad = norm_back(da3, vec[4:5, :], hat, scale)
    gx2[...] = cot[...].reshape(rows, width).astype(F32) + back
    vecs[0:1, :] = gain_grad
    vecs[1:2, :] = shift_grad


def cross_backward(
    where, x1, vec, gx2, q2, kv, p2, weights, gx1, vecs, dkv, dq2, out_mem, weight, do2, moved, sems
):
    rows, width = x1.shape
    examples = pl.num_programs(0)
    e = pl.program_id(0)
    length = p2.shape[2] // TOGETHER

    @pl.when(e == 0)
    def _():
        wait_all(load_weight(where, weight, weights, Copies(sems)))
        do2[...] = dot_nt(gx2[...].astype(BF), weight[3]).astype(BF)

    mask = head_mask(length)
    here = rows_of(e * length, length)
    for g in range(GROUPS):
        lanes = columns(g, LANES)
        value_lanes = slice(width + g * LANES, width + (g + 1) * LANES)
        queries = stack_heads(q2[here, lanes], mask)
        grads = stack_heads(do2[here, lanes], mask)
        probs = p2[0, g]
        dp = dot_nt(grads, kv[0, :, value_lanes])
        wide = probs.astype(F32)
        row_sum = jnp.sum(wide * dp, axis=-1, keepdims=True)
        dz = (wide * (dp - row_sum)).astype(BF)
        dkv[0, :, value_lanes] = dot_tn(probs, grads).astype(BF)
        dkv[0, :, lanes] = (dot_tn(dz, queries) * SCALE).astype(BF)
        dq2[here, lanes] = (merge_heads(dot(dz, kv[0, :, lanes]), mask) * SCALE).astype(BF)
    back = dot_nt(dkv[0, :, :width], weight[1]) + dot_nt(dkv[0, :, width:], weight[2])
    moved[...] = back.astype(BF)
    for d, out in enumerate(out_mem):
        slots = out.shape[1]
        out[0] = moved[rows_of((where[3] ^ d) * slots, slots), :]

    @pl.when(e == examples - 1)
    def _():
        hat, scale = normalise(x1[...])
        back, gain_grad, shift_grad = norm_back(
            dot_nt(dq2[...], weight[0]), vec[2:3, :], hat, scale
        )
        gx1[...] = gx2[...] + back
        vecs[0:1, :] = gain_grad
        vecs[1:2, :] = shift_grad


def cross_grads(
    where, gx2, a2, o2, dq2, dkv, all_memory, near, far, theirs, grad, memory, sems
):
    rows, width = gx2.shape
    examples, total, _ = memory.shape
    mem, _, slots, _ = all_memory.shape
    copies = Copies(sems)
    loads = [
        copies.start(all_memory.at[d], memory.at[:, d * slots : (d + 1) * slots, :])
        for d in range(mem)
    ]
    grad[0] = dot_tn(a2[...], dq2[...]).astype(BF)
    grad[3] = dot_tn(o2[...], gx2[...].astype(BF)).astype(BF)
    wait_all(loads)
    flat = memory[...].reshape(examples * total, width)
    for j in range(2):
        part = dkv[:, :, columns(j, width)].reshape(examples * total, width)
        grad[1 + j] = dot_tn(flat, part).astype(BF)
    wait_all(store_grad(where, grad, near, far, theirs, Copies(sems)))


def self_backward(
    group, where, suffix, vec, gx1, a1, qkv, p1, o1, parts, weights, suffix_grad, vecs,
    near, far, theirs, weight, start, grad, dqkv, do1, sems,
):
    rows, width = gx1.shape
    copies = Copies(sems)
    start_copy = my_examples(where, suffix, start, copies)
    loads = load_weight(where, weight, weights, copies)
    gs = gx1[...].astype(BF)
    grad[3] = dot_tn(o1[...], gs).astype(BF)
    wait_all(loads)
    do1[...] = dot_nt(gs, weight[3]).astype(BF)
    mask = head_mask(group)
    for r in range(rows // group):
        here = columns(r, group)
        for g in range(GROUPS):
            lanes = [slice(i * width + g * LANES, i * width + (g + 1) * LANES) for i in range(3)]
            queries = stack_heads(qkv[here, lanes[0]], mask)
            grads = stack_heads(do1[here, lanes[0]], mask)
            probs = p1[r * GROUPS + g]
            dp = dot_nt(grads, qkv[here, lanes[2]])
            wide = probs.astype(F32)
            row_sum = jnp.sum(wide * dp, axis=-1, keepdims=True)
            dz = (wide * (dp - row_sum)).astype(BF)
            dqkv[here, lanes[2]] = dot_tn(probs, grads).astype(BF)
            dqkv[here, lanes[1]] = (dot_tn(dz, queries) * SCALE).astype(BF)
            dq = merge_heads(dot(dz, qkv[here, lanes[1]]), mask) * SCALE
            dqkv[here, lanes[0]] = dq.astype(BF)
    for j in range(3):
        grad[j] = dot_tn(a1[...], dqkv[:, columns(j, width)]).astype(BF)
    start_copy.wait()
    started = store_grad(where, grad, near, far, theirs, Copies(sems))
    da1 = dot_nt(dqkv[:, columns(0, width)], weight[0])
    for j in range(1, 3):
        da1 = da1 + dot_nt(dqkv[:, columns(j, width)], weight[j])
    hat, scale = normalise(start[...].reshape(rows, width).astype(F32))
    back, gain_grad, shift_grad = norm_back(da1, vec[0:1, :], hat, scale)
    suffix_grad[...] = (gx1[...] + back).astype(BF).reshape(suffix_grad.shape)
    found = [gain_grad, shift_grad]
    for ref in parts:
        for r in range(ref.shape[0]):
            found += [ref[r : r + 1, columns(j, width)] for j in range(ref.shape[1] // width)]
    found.append(jnp.zeros((vecs.shape[0] - len(found), width), F32))
    vecs[...] = jnp.concatenate(found, axis=0).astype(BF)
    wait_all(started)


def run(kernel, inputs, outputs, scratch, copies, grid=()):
    def leaf(x):
        return isinstance(x, tuple) and len(x) == 2 and isinstance(x[0], pl.BlockSpec)

    flat_in, tree_in = jax.tree.flatten(inputs, is_leaf=leaf)
    flat_out, tree_out = jax.tree.flatten(outputs, is_leaf=leaf)

    def body(*refs):
        first, second = len(flat_in), len(flat_in) + len(flat_out)
        given = jax.tree.unflatten(tree_in, refs[:first])
        taken = jax.tree.unflatten(tree_out, refs[first:second])
        kernel(*given, *taken, *refs[second:])

    found = pl.pallas_call(
        body,
        grid=grid,
        in_specs=[spec for spec, _ in flat_in],
        out_specs=[spec for spec, _ in flat_out],
        out_shape=[shape for _, shape in flat_out],
        scratch_shapes=scratch + [pltpu.SemaphoreType.DMA((copies,))],
        compiler_params=pltpu.CompilerParams(vmem_limit_bytes=56 * 1024 * 1024),
        cost_estimate=pl.CostEstimate(
            flops=0, bytes_accessed=0, transcendentals=0
        ),
    )(*[x for _, x in flat_in])
    return jax.tree.unflatten(tree_out, found)


def shape_of(dims, dtype):
    return jax.ShapeDtypeStruct(tuple(dims), dtype)


def over_slow(value, slow, fast):
    groups = [[k * fast + b for k in range(slow)] for b in range(fast)]
    return lax.all_to_all(value, "fsdp", 0, 0, axis_index_groups=groups, tiled=True)


class Gather:
    def __init__(self, half, slow, fast):
        self.half, self.slow, self.fast = half, slow, fast

    def send_slow(self, *others):
        half = after(self.half, *others)
        self.came = [half] + [swap(half, "fsdp", k * self.fast) for k in range(1, self.slow)]

    def send_fast(self, *others):
        self.near = jnp.stack([after(piece, *others) for piece in self.came])
        self.near_other = swap(self.near, "mem", 1)
        self.far = [swap(self.near, "fsdp", b) for b in range(1, self.fast)]

    def whole(self):
        mine = [self.near] + self.far
        theirs = [self.near_other] + [swap(piece, "mem", 1) for piece in self.far]
        return mine, theirs

    @staticmethod
    def refs(weights):
        return [[(ANY, x) for x in some] for some in weights]


class Scatter:
    def __init__(self, grads, slow, fast, *others, vectors=None):
        self.near, self.far, theirs = grads
        self.slow, self.fast, self.vectors = slow, fast, vectors
        theirs = [after(part, *others) for part in theirs]
        far = [swap(part, "mem", 1) for part in theirs[1:]]
        far = [jnp.concatenate(far[2 * b : 2 * b + 2]) for b in range(fast - 1)]
        self.sent = [swap(theirs[0], "mem", 1)] + far
        if vectors is not None:
            self.vectors = vectors.astype(F32) + swap(vectors, "mem", 1).astype(F32)

    def add_cores(self):
        self.out = [
            (self.far[b].astype(F32) + self.sent[b + 1].astype(F32)).astype(BF)
            for b in range(self.fast - 1)
        ]
        return self.out

    def send_fast(self):
        self.came = [swap(part, "fsdp", b + 1) for b, part in enumerate(self.out)]
        if self.vectors is not None:
            low = self.vectors.astype(BF)
            came = [swap(low, "fsdp", b) for b in range(1, self.fast)]
            self.vectors = sum(part.astype(F32) for part in [low, *came])

    def add_fast(self, *others):
        total = after(self.near, *others).astype(F32) + self.sent[0].astype(F32)
        for part in self.came:
            total = total + part.astype(F32)
        self.total = total.astype(BF).reshape(self.slow, -1, total.shape[-1])
        if self.vectors is not None:
            low = self.vectors.astype(BF)
            low = jnp.broadcast_to(low, (self.slow,) + low.shape)
            self.total = jnp.concatenate([self.total, low], axis=1)
        return self.total

    def send_slow(self):
        self.came = over_slow(self.total, self.slow, self.fast)

    def add_slow(self, *others):
        return jnp.sum(after(self.came, *others).astype(F32), axis=0)


class Replicas:
    def __init__(self, value, rows, across):
        self.rows = rows
        k = 1
        while 2 * k < across:
            low = value.astype(BF)
            value = low.astype(F32) + swap(low, "mem", 2 * k).astype(F32)
            k *= 2
        low = value.astype(BF)
        self.halves = [low, swap(low, "mem", 2 * k)] if across > 1 else [low]

    def swap_cores(self, *others):
        halves, _ = lax.optimization_barrier((self.halves, others))
        self.others = [swap(half[: 2 * self.rows], "mem", 1) for half in halves]

    def combine(self, c):
        rows = self.rows
        other = sum(half.astype(F32) for half in self.others)
        mine = sum(half.astype(F32) for half in self.halves)
        vectors, mine = mine[2 * rows :], mine[: 2 * rows]
        first = jnp.where(c == 0, mine, other)
        second = jnp.where(c == 0, other, mine)
        return [first[:rows], first[rows:], second[:rows], second[rows:]], vectors


def place_rows(where, blocks, outs, scratch, sems):
    copies = Copies(sems)
    loads = []
    for i, (even, odd) in enumerate(blocks):
        for d, piece in enumerate(even):
            loads.append((copies.start(piece, scratch.at[i, 2 * d]), i, 2 * d))
            loads.append((copies.start(odd.at[d], scratch.at[i, 2 * d + 1]), i, 2 * d + 1))
    examples = scratch.shape[2]
    stores = []
    for load, i, d in loads:
        load.wait()
        target = outs[i].at[pl.ds((where[3] ^ d) * examples, examples)]
        stores.append(copies.start(scratch.at[i, d], target))
    wait_all(stores)


def place_memory(where, pieces, out, scratch, sems):
    examples = pieces[0].shape[0]
    copies = Copies(sems)
    loads = [copies.start(piece, scratch.at[d]) for d, piece in enumerate(pieces)]
    stores = []
    for d, load in enumerate(loads):
        load.wait()
        target = out.at[pl.ds((where[3] ^ d) * examples, examples)]
        stores.append(copies.start(scratch.at[d], target))
    wait_all(stores)


def spread_across(value, mem):
    return [value] + [swap(value, "mem", d) for d in range(2, mem, 2)]


def per_device(
    suffix,
    memory,
    counts,
    cotangent,
    self_norm_gain,
    self_norm_bias,
    self_query,
    self_key,
    self_value,
    self_output,
    cross_norm_gain,
    cross_norm_bias,
    cross_query,
    cross_key,
    cross_value,
    cross_output,
    dense_norm_gain,
    dense_norm_bias,
    dense_in,
    dense_in_bias,
    dense_out,
    dense_out_bias,
):
    f = lax.axis_index("fsdp")
    m = lax.axis_index("mem")
    c = m % 2
    fsdp = lax.axis_size("fsdp")
    mem = lax.axis_size("mem")
    across = mem // 2
    slow, fast = fsdp_split(fsdp)
    SHARDS[0] = fsdp
    where = jnp.stack([f // fast, f % fast, c, m]).astype(jnp.int32)
    examples = suffix.shape[0] // mem
    length = suffix.shape[1]
    width = suffix.shape[2]
    slots = memory.shape[1]
    total = mem * slots
    rows = examples * length
    inner = dense_in.shape[1]
    part = width // fsdp
    group = min(128, rows)
    blocks = 4 * fsdp

    def gather(matrices, *others):
        halves = [jnp.concatenate(matrices[:2]), jnp.concatenate(matrices[2:])]
        half = jnp.concatenate([jnp.where(c == 0, *halves), *others])
        return Gather(half, slow, fast)

    cross_gather = gather([cross_query, cross_key, cross_value, cross_output])
    in_gather = gather([dense_in[:, columns(j, width)] for j in range(4)])
    out_gather = gather([dense_out[columns(j, part)] for j in range(4)])
    small = [
        self_norm_gain,
        self_norm_bias,
        cross_norm_gain,
        cross_norm_bias,
        dense_norm_gain,
        dense_norm_bias,
        dense_out_bias,
    ]
    small += [dense_in_bias[columns(j, part)] for j in range(4)]
    small = sum(
        jnp.pad(value[None], ((i, 15 - i), (0, width - part))) for i, value in enumerate(small)
    )
    self_gather = gather([self_query, self_key, self_value, self_output], small)

    def exchange(value):
        blocks = value.reshape((mem, examples) + value.shape[1:])
        return lax.all_to_all(blocks, "mem", 0, 0, tiled=True)

    all_memory = exchange(memory)
    self_gather.send_slow()
    sent = self_gather.came
    self_gather.send_fast(*sent)
    cross_gather.send_slow(*sent)
    sent = [*self_gather.far, *cross_gather.came, all_memory]
    self_gather.far = [after(piece, *sent) for piece in self_gather.far]
    self_weights = self_gather.whole()
    cross_gather.send_fast(*self_gather.far)
    in_gather.send_slow(*self_gather.far)

    half = (2, part, width)
    grads_like = [
        (ANY, shape_of((slow,) + half, BF)),
        (ANY, shape_of((fast - 1, slow) + half, BF)),
        [(ANY, shape_of((slow,) + half, BF))]
        + [(ANY, shape_of((slow // 2,) + half, BF))] * (2 * fast - 2),
    ]

    def flat(dims, dtype):
        return (VMEM, shape_of(dims, dtype))

    def per_example(value):
        dims = value.shape[1:]
        spec = pl.BlockSpec((1,) + dims, lambda e: (e,) + (0,) * len(dims))
        return (spec, value)

    def slots_of_example(value):
        spec = pl.BlockSpec((mem, 1, slots, width), lambda e: (0, e, 0, 0))
        return (spec, value)

    def scratch(*dims):
        return pltpu.VMEM(dims, BF)

    def scatter(grads, *others, vectors=None):
        return Scatter(grads, slow, fast, *others, vectors=vectors)

    wide = (rows, width)
    square = scratch(4, width, width)
    own_rows = scratch(examples, length, width)
    x1, a1, qkv, p1, o1, vec = run(
        functools.partial(self_forward, group),
        [(SMEM, where), (ANY, suffix), Gather.refs(self_weights)],
        [
            flat(wide, F32),
            flat(wide, BF),
            flat((rows, 3 * width), BF),
            flat((rows // group * GROUPS, TOGETHER * group, group), BF),
            flat(wide, BF),
            flat((16, width), F32),
        ],
        [square, own_rows, scratch(fsdp, 16, 128)],
        1 + fsdp + blocks,
    )
    cross_gather.far = [after(piece, x1, *in_gather.came) for piece in cross_gather.far]
    cross_weights = Gather.refs(cross_gather.whole())
    in_gather.send_fast(*cross_gather.far)
    out_gather.send_slow(*cross_gather.far)
    x2, a2, q2, kv, p2, o2 = run(
        cross_forward,
        [(SMEM, where), (SMEM, counts), (VMEM, x1), (VMEM, vec)]
        + [slots_of_example(all_memory), cross_weights],
        [
            flat(wide, F32),
            flat(wide, BF),
            flat(wide, BF),
            per_example(shape_of((examples, total, 2 * width), BF)),
            per_example(shape_of((examples, GROUPS, TOGETHER * length, total), BF)),
            flat(wide, BF),
        ],
        [square],
        blocks,
        (examples,),
    )
    small = [after(piece, x1)[:, 2 * part + 7 : 2 * part + 11, :part] for piece in self_weights[0]]
    order = jnp.arange(fsdp) ^ f
    bias_in = jnp.take(jnp.concatenate(small), order % fast * slow + order // fast, axis=0)
    bias_in = bias_in.astype(F32).reshape(1, inner)
    in_gather.far = [after(piece, x2, *out_gather.came) for piece in in_gather.far]
    in_weights = Gather.refs(in_gather.whole())
    out_gather.send_fast(*in_gather.far)
    a3, h, slope, *grads = run(
        dense_inner,
        [(SMEM, where), (VMEM, x2), (VMEM, vec), (VMEM, bias_in), (ANY, cotangent), in_weights],
        [flat(wide, BF), flat((rows, inner), BF), flat((rows, inner), BF)] + grads_like,
        [square, scratch(fsdp, 4, part, width), own_rows],
        1 + blocks,
    )
    out_gather.far = [after(piece, a3) for piece in out_gather.far]
    out_weights = Gather.refs(out_gather.whole())
    out_scatter = scatter(grads, *out_gather.far)
    out_sum = out_scatter.add_cores()
    out_scatter.send_fast()
    y, du, vecs_y, bias_grad, *grads = run(
        dense_outer,
        [(SMEM, where), (VMEM, after(x2, *out_sum)), (VMEM, vec), (VMEM, a3), (VMEM, h)]
        + [(VMEM, slope), (ANY, cotangent), out_weights],
        [
            flat((examples, length, width), BF),
            flat((rows, inner), BF),
            flat((1, width), F32),
            flat((1, inner), F32),
        ]
        + grads_like,
        [scratch(fsdp, 4, part, width), square, own_rows],
        1 + blocks,
    )
    in_grads = grads
    gx2, vecs_dense = run(
        dense_back,
        [(SMEM, where), (VMEM, x2), (VMEM, vec), (VMEM, du), (ANY, cotangent), in_weights],
        [flat(wide, F32), flat((2, width), F32)],
        [square, own_rows],
        1 + blocks,
    )
    in_scatter = scatter(in_grads, gx2)
    in_sum = in_scatter.add_cores()
    in_scatter.send_fast()
    out_total = out_scatter.add_fast(*in_sum)
    out_scatter.send_slow()
    gx1, vecs_cross, dkv, dq2, grad_memory = run(
        cross_backward,
        [(SMEM, where), (VMEM, x1), (VMEM, vec), (VMEM, after(gx2, out_total, *in_sum)), (VMEM, q2)]
        + [per_example(kv), per_example(p2), cross_weights],
        [
            flat(wide, F32),
            flat((2, width), F32),
            per_example(shape_of((examples, total, 2 * width), BF)),
            flat(wide, BF),
            [per_example(shape_of((examples, slots, width), BF))] * mem,
        ],
        [square, scratch(*wide), scratch(total, width)],
        blocks,
        (examples,),
    )
    out_final = out_scatter.add_slow(gx1)
    mem_pieces = grad_memory[:1] + [swap(grad_memory[d], "mem", d) for d in range(1, mem)]
    grads = run(
        cross_grads,
        [(SMEM, where), (VMEM, after(gx2, out_final)), (VMEM, a2), (VMEM, o2), (VMEM, dq2)]
        + [(VMEM, dkv), (ANY, all_memory)],
        grads_like,
        [square, scratch(examples, total, width)],
        max(mem, blocks),
    )
    in_total = in_scatter.add_fast()
    in_scatter.send_slow()
    cross_scatter = scatter(grads, in_total, *mem_pieces[1:3])
    cross_sum = cross_scatter.add_cores()
    cross_scatter.send_fast()
    gx1 = after(gx1, *cross_sum)
    suffix_part, vecs_self, *grads = run(
        functools.partial(self_backward, group),
        [(SMEM, where), (ANY, suffix), (VMEM, vec), (VMEM, gx1), (VMEM, a1)]
        + [(VMEM, qkv), (VMEM, p1), (VMEM, o1)]
        + [[(VMEM, x) for x in (vecs_cross, vecs_dense, vecs_y, bias_grad)], Gather.refs(self_weights)],
        [flat((examples, length, width), BF), flat((16, width), BF)] + grads_like,
        [square, own_rows, square, scratch(rows, 3 * width), scratch(*wide)],
        1 + blocks,
    )
    in_final = in_scatter.add_slow(suffix_part)
    cross_total = cross_scatter.add_fast(suffix_part)
    cross_scatter.send_slow()
    self_scatter = scatter(grads, in_final, cross_total, vectors=vecs_self)
    self_sum = self_scatter.add_cores()
    self_scatter.send_fast()
    dense_sum = after(jnp.concatenate([out_final, in_final]), *self_sum)
    dense_sum = Replicas(dense_sum, 2 * part, across)
    y_rows = spread_across(after(y, *self_sum), mem)
    self_total = self_scatter.add_fast(*dense_sum.halves, *y_rows)
    self_scatter.send_slow()
    cross_sum = Replicas(cross_scatter.add_slow(self_total), part, across)
    suffix_rows = spread_across(after(suffix_part, self_total), mem)
    y_rows = [after(value, self_total) for value in y_rows]
    y_far = swap(jnp.stack(y_rows), "mem", 1)
    dense_sum.swap_cores(self_total)
    mem_pieces = [after(value, self_total) for value in mem_pieces]
    (memory_grad,) = run(
        place_memory,
        [(SMEM, where), [(ANY, value) for value in mem_pieces]],
        [(ANY, shape_of(memory.shape, BF))],
        [scratch(mem, examples, slots, width)],
        2 * mem,
    )
    cross_sum.swap_cores()
    suffix_far = swap(jnp.stack(suffix_rows), "mem", 1)
    blocks = [([(ANY, x) for x in y_rows], (ANY, y_far))]
    blocks += [([(ANY, x) for x in suffix_rows], (ANY, suffix_far))]
    ((block_output, suffix_grad),) = run(
        place_rows,
        [(SMEM, where), blocks],
        [[(ANY, shape_of(suffix.shape, BF))] * 2],
        [scratch(2, mem, examples, length, width)],
        4 * mem,
    )
    (out_low, in_low, out_high, in_high), _ = dense_sum.combine(c)
    grad_in = jnp.concatenate([in_low[:part], in_low[part:], in_high[:part], in_high[part:]], axis=1)
    grad_out = jnp.concatenate([out_low, out_high])
    grad_cross, _ = cross_sum.combine(c)
    done = [grad_in, grad_out, *grad_cross, block_output, memory_grad]
    self_final = Replicas(self_scatter.add_slow(*done), part, across)
    self_final.swap_cores()
    grad_self, vectors = self_final.combine(c)

    def vector(i):
        return lax.dynamic_slice(vectors, (i, f * part), (1, part)).reshape(part)

    return (
        block_output,
        suffix_grad,
        memory_grad,
        vector(0),
        vector(1),
        *grad_self,
        vector(2),
        vector(3),
        *grad_cross,
        vector(4),
        vector(5),
        grad_in,
        lax.dynamic_slice_in_dim(vectors[7:11].reshape(-1), f * (inner // fsdp), inner // fsdp, 0),
        grad_out,
        vector(6),
    )


def solution(mesh):
    rows = P("fsdp", None, None)
    matrix = P("fsdp", None)
    vector = P("fsdp")
    attention = (vector, vector, matrix, matrix, matrix, matrix)
    params = attention + attention + (vector, vector, matrix, vector, matrix, vector)
    return jax.shard_map(
        per_device,
        mesh=mesh,
        in_specs=(rows, P("fsdp", "mem", None), vector, rows) + params,
        out_specs=(rows, rows, P("fsdp", "mem", None)) + params,
        check_vma=False,
    )
```

```python
import functools

import jax
import jax.numpy as jnp
from jax import lax
from jax.experimental import pallas as pl
from jax.experimental.pallas import tpu as pltpu
from jax.sharding import PartitionSpec as P

HEADS = 12
HEAD = 64
TOGETHER = 4
GROUPS = HEADS // TOGETHER
LANES = TOGETHER * HEAD
SCALE = HEAD ** (-0.5)
BF = jnp.bfloat16
F32 = jnp.float32
ANY = pl.BlockSpec(memory_space=pl.ANY)
SMEM = pl.BlockSpec(memory_space=pltpu.SMEM)
VMEM = pl.BlockSpec(memory_space=pltpu.VMEM)


def swap(value, axis, distance):
    size = lax.axis_size(axis)
    return lax.ppermute(value, axis, [(i, i ^ distance) for i in range(size)])


def after(value, *others):
    return lax.optimization_barrier((value, *others))[0] if others else value


def fsdp_split(size):
    slow = 4 if size % 4 == 0 else 1
    return slow, size // slow


def dot(left, right):
    return jnp.dot(left, right, preferred_element_type=F32)


def dot_nt(left, right):
    return lax.dot_general(left, right, (((1,), (1,)), ((), ())), preferred_element_type=F32)


def dot_tn(left, right):
    return lax.dot_general(left, right, (((0,), (0,)), ((), ())), preferred_element_type=F32)


def rows_of(start, size):
    return pl.ds(pl.multiple_of(start, 16), size)


def block(ref, by_rows, shard, which):
    if by_rows:
        return ref.at[shard, pl.ds(which * 2, 2)]
    rows = ref.shape[1] // SHARDS[0]
    return ref.at[pl.ds(which * 2, 2), rows_of(shard * rows, rows)]


SHARDS = [0]


class Copies:
    def __init__(self, sems):
        self.sems = sems
        self.next = 0

    def start(self, source, target):
        copy = pltpu.make_async_copy(source, target, self.sems.at[self.next])
        self.next += 1
        copy.start()
        return copy


def wait_all(copies):
    for copy in copies:
        copy.wait()


def load_weight(where, whole, weights, copies, by_rows=False):
    z, y, c = where[0], where[1], where[2]
    rows = whole.shape[2] if by_rows else whole.shape[1] // SHARDS[0]
    started = []
    for which, pieces in ((c, weights[0]), (1 - c, weights[1])):
        fast = len(pieces)
        for b, piece in enumerate(pieces):
            for k in range(piece.shape[0]):
                shard = (z ^ k) * fast + (y ^ b)
                for i in range(2):
                    source = piece.at[k, pl.ds(i * rows, rows)]
                    if by_rows:
                        target = whole.at[shard, 2 * which + i]
                    else:
                        target = whole.at[2 * which + i, rows_of(shard * rows, rows)]
                    started.append(copies.start(source, target))
    return started


def store_grad(where, whole, near, far, theirs, copies, by_rows=False):
    y, c = where[1], where[2]
    slow, cut = near.shape[0], near.shape[0] // 2
    fast = (len(theirs) + 1) // 2
    started = []
    for b in range(fast):
        for k in range(slow):
            shard = k * fast + (y ^ b)
            mine = far.at[b - 1, k] if b else near.at[k]
            other = theirs[2 * b - 1 + k // cut].at[k % cut] if b else theirs[0].at[k]
            started.append(copies.start(block(whole, by_rows, shard, 1 - c), other))
            started.append(copies.start(block(whole, by_rows, shard, c), mine))
    return started


def my_examples(where, source, target, copies):
    count = target.shape[0]
    return copies.start(source.at[pl.ds(where[3] * count, count)], target)


def normalise(values):
    centred = values - jnp.mean(values, axis=-1, keepdims=True)
    scale = lax.rsqrt(jnp.mean(centred * centred, axis=-1, keepdims=True) + 1e-06)
    return centred * scale, scale


def norm_back(grad, gain, hat, scale):
    inner = grad * gain
    mean = jnp.mean(inner, axis=-1, keepdims=True)
    along = jnp.mean(inner * hat, axis=-1, keepdims=True)
    return (
        scale * (inner - mean - hat * along),
        jnp.sum(grad * hat, axis=0, keepdims=True),
        jnp.sum(grad, axis=0, keepdims=True),
    )


def head_mask(rows):
    shape = (TOGETHER * rows, LANES)
    row = lax.broadcasted_iota(jnp.int32, shape, 0) // rows
    lane = lax.broadcasted_iota(jnp.int32, shape, 1) // HEAD
    return (row == lane).astype(F32)


def stack_heads(value, mask):
    return (jnp.concatenate([value] * TOGETHER, axis=0).astype(F32) * mask).astype(BF)


def merge_heads(value, mask):
    rows = value.shape[0] // TOGETHER
    value = value * mask
    total = value[:rows]
    for h in range(1, TOGETHER):
        total = total + value[h * rows : (h + 1) * rows]
    return total


def columns(j, width):
    return slice(j * width, (j + 1) * width)


def self_forward(
    group, where, suffix, weights, x1, a1, qkv, p1, o1, vec, weight, start, small, sems
):
    rows, width = x1.shape
    copies = Copies(sems)
    first = my_examples(where, suffix, start, copies)
    fast, slow = len(weights[0]), weights[0][0].shape[0]
    part = width // (fast * slow)
    vectors = []
    for b, piece in enumerate(weights[0]):
        for k in range(slow):
            source = piece.at[k, pl.ds(2 * part, 16), pl.ds(0, 128)]
            vectors.append(copies.start(source, small.at[b * slow + k]))
    loads = load_weight(where, weight, weights, copies)
    wait_all(vectors)
    lane = lax.broadcasted_iota(jnp.int32, (128, width), 0)
    place = lax.broadcasted_iota(jnp.int32, (128, width), 1) - lane
    together = jnp.zeros(vec.shape, F32)
    for i in range(fast * slow):
        shard = (where[0] ^ (i % slow)) * fast + (where[1] ^ (i // slow))
        chosen = ((place == shard * part) & (lane < part)).astype(F32).astype(BF)
        together = together + dot(small[i], chosen)
    vec[...] = together
    first.wait()
    values = start[...].reshape(rows, width).astype(F32)
    hat, _ = normalise(values)
    a1[...] = (hat * vec[0:1, :] + vec[1:2, :]).astype(BF)
    wait_all(loads)
    for j in range(3):
        qkv[:, columns(j, width)] = dot(a1[...], weight[j]).astype(BF)
    mask = head_mask(group)
    length = suffix.shape[1]
    shape = (TOGETHER * group, group)
    row = lax.broadcasted_iota(jnp.int32, shape, 0) % group
    col = lax.broadcasted_iota(jnp.int32, shape, 1)
    seen = (row // length == col // length) & (row >= col)
    for r in range(rows // group):
        here = columns(r, group)
        for g in range(GROUPS):
            lanes = [slice(i * width + g * LANES, i * width + (g + 1) * LANES) for i in range(3)]
            queries = stack_heads(qkv[here, lanes[0]], mask)
            scores = dot_nt(queries, qkv[here, lanes[1]]) * SCALE
            scores = jnp.where(seen, scores, -1e30)
            powers = jnp.exp(scores - jnp.max(scores, axis=-1, keepdims=True))
            probs = (powers / jnp.sum(powers, axis=-1, keepdims=True)).astype(BF)
            p1[r * GROUPS + g] = probs
            found = dot(probs, qkv[here, lanes[2]])
            o1[here, lanes[0]] = merge_heads(found, mask).astype(BF)
    x1[...] = values + dot(o1[...], weight[3])


def cross_forward(
    where, counts, x1, vec, memory, weights, x2, a2, q2, kv, p2, o2, weight, sems
):
    rows, width = x1.shape
    examples = pl.num_programs(0)
    e = pl.program_id(0)
    total = kv.shape[1]
    length = p2.shape[2] // TOGETHER

    @pl.when(e == 0)
    def _():
        loads = load_weight(where, weight, weights, Copies(sems))
        hat, _ = normalise(x1[...])
        a2[...] = (hat * vec[2:3, :] + vec[3:4, :]).astype(BF)
        wait_all(loads)
        q2[...] = dot(a2[...], weight[0]).astype(BF)

    tokens = memory[...].reshape(total, width)
    for j in range(2):
        kv[0, :, columns(j, width)] = dot(tokens, weight[1 + j]).astype(BF)
    mask = head_mask(length)
    position = lax.broadcasted_iota(jnp.int32, (1, total), 1)
    valid = position < counts[where[3] * examples + e]
    here = rows_of(e * length, length)
    probs = []
    for g in range(GROUPS):
        lanes = columns(g, LANES)
        queries = stack_heads(q2[here, lanes], mask)
        scores = dot_nt(queries, kv[0, :, lanes]) * SCALE
        scores = jnp.where(valid, scores, -1e30)
        top = jnp.maximum(jnp.max(scores, axis=-1, keepdims=True), 0.0)
        powers = jnp.exp(scores - top)
        weight_sum = jnp.sum(powers, axis=-1, keepdims=True) + jnp.exp(-top)
        probs.append((powers / weight_sum).astype(BF))
    for g in range(GROUPS):
        p2[0, g] = probs[g]
        found = dot(probs[g], kv[0, :, width + g * LANES : width + (g + 1) * LANES])
        o2[here, columns(g, LANES)] = merge_heads(found, mask).astype(BF)

    @pl.when(e == examples - 1)
    def _():
        x2[...] = x1[...] + dot(o2[...], weight[3])


def dense_inner(
    where, x2, vec, bias, cotangent, weights, a3, h, slope, near, far, theirs,
    weight, grad, cot, sems,
):
    rows, width = x2.shape
    copies = Copies(sems)
    cot_copy = my_examples(where, cotangent, cot, copies)
    loads = load_weight(where, weight, weights, copies)
    hat, _ = normalise(x2[...])
    a3[...] = (hat * vec[4:5, :] + vec[5:6, :]).astype(BF)
    cot_copy.wait()
    gy = cot[...].reshape(rows, width)
    wait_all(loads)
    flat = grad.shape[0] * grad.shape[1] * grad.shape[2]
    step = flat // grad.shape[0]
    for j in range(4):
        for half in range(2):
            cols = slice(j * width + half * 384, j * width + (half + 1) * 384)
            u = dot(a3[...], weight[j, :, half * 384 : (half + 1) * 384]) + bias[:, cols]
            square = u * u
            t = jnp.tanh(0.7978845608 * u * (1.0 + 0.044715 * square))
            h[:, cols] = (0.5 * u * (1.0 + t)).astype(BF)
            slope[:, cols] = (
                0.5 * (1.0 + t)
                + (0.5 * 0.7978845608) * u * (1.0 - t * t) * (1.0 + (3.0 * 0.044715) * square)
            ).astype(BF)
            part = dot_tn(h[:, cols], gy).astype(BF)
            per = 384 // step
            grad[cols.start // step : cols.start // step + per] = part.reshape(
                (per,) + grad.shape[1:]
            )
    wait_all(store_grad(where, grad, near, far, theirs, Copies(sems), True))


def dense_outer(
    where, x2, vec, a3, h, slope, cotangent, weights, y, du, vecs, bias_grad, near, far, theirs,
    weight, grad, cot, sems,
):
    rows, width = x2.shape
    copies = Copies(sems)
    cot_copy = my_examples(where, cotangent, cot, copies)
    wait_all(load_weight(where, weight, weights, copies, True))
    cot_copy.wait()
    gy = cot[...].reshape(rows, width)
    shards = weight.shape[0]
    step = weight.shape[1] * weight.shape[2]
    whole = weight[...].reshape(shards * step, width)
    for j in range(4):
        cols = columns(j, width)
        low = (dot_nt(gy, whole[cols]) * slope[:, cols].astype(F32)).astype(BF)
        du[:, cols] = low
        bias_grad[:, cols] = jnp.sum(low.astype(F32), axis=0, keepdims=True)
        grad[j] = dot_tn(a3[...], low).astype(BF)
    started = store_grad(where, grad, near, far, theirs, Copies(sems))
    result = x2[...] + dot(h[...], whole) + vec[6:7, :]
    y[...] = result.astype(BF).reshape(y.shape)
    vecs[...] = jnp.sum(gy.astype(F32), axis=0, keepdims=True)
    wait_all(started)


def dense_back(where, x2, vec, du, cotangent, weights, gx2, vecs, weight, cot, sems):
    rows, width = x2.shape
    copies = Copies(sems)
    cot_copy = my_examples(where, cotangent, cot, copies)
    loads = load_weight(where, weight, weights, copies)
    hat, scale = normalise(x2[...])
    cot_copy.wait()
    wait_all(loads)
    da3 = dot_nt(du[:, columns(0, width)], weight[0])
    for j in range(1, 4):
        da3 = da3 + dot_nt(du[:, columns(j, width)], weight[j])
    back, gain_grad, shift_grad = norm_back(da3, vec[4:5, :], hat, scale)
    gx2[...] = cot[...].reshape(rows, width).astype(F32) + back
    vecs[0:1, :] = gain_grad
    vecs[1:2, :] = shift_grad


def cross_backward(
    where, x1, vec, gx2, q2, kv, p2, weights, gx1, vecs, dkv, dq2, out_mem, weight, do2, moved, sems
):
    rows, width = x1.shape
    examples = pl.num_programs(0)
    e = pl.program_id(0)
    length = p2.shape[2] // TOGETHER

    @pl.when(e == 0)
    def _():
        wait_all(load_weight(where, weight, weights, Copies(sems)))
        do2[...] = dot_nt(gx2[...].astype(BF), weight[3]).astype(BF)

    mask = head_mask(length)
    here = rows_of(e * length, length)
    for g in range(GROUPS):
        lanes = columns(g, LANES)
        value_lanes = slice(width + g * LANES, width + (g + 1) * LANES)
        queries = stack_heads(q2[here, lanes], mask)
        grads = stack_heads(do2[here, lanes], mask)
        probs = p2[0, g]
        dp = dot_nt(grads, kv[0, :, value_lanes])
        wide = probs.astype(F32)
        row_sum = jnp.sum(wide * dp, axis=-1, keepdims=True)
        dz = (wide * (dp - row_sum)).astype(BF)
        dkv[0, :, value_lanes] = dot_tn(probs, grads).astype(BF)
        dkv[0, :, lanes] = (dot_tn(dz, queries) * SCALE).astype(BF)
        dq2[here, lanes] = (merge_heads(dot(dz, kv[0, :, lanes]), mask) * SCALE).astype(BF)
    back = dot_nt(dkv[0, :, :width], weight[1]) + dot_nt(dkv[0, :, width:], weight[2])
    moved[...] = back.astype(BF)
    for d, out in enumerate(out_mem):
        slots = out.shape[1]
        out[0] = moved[rows_of((where[3] ^ d) * slots, slots), :]

    @pl.when(e == examples - 1)
    def _():
        hat, scale = normalise(x1[...])
        back, gain_grad, shift_grad = norm_back(
            dot_nt(dq2[...], weight[0]), vec[2:3, :], hat, scale
        )
        gx1[...] = gx2[...] + back
        vecs[0:1, :] = gain_grad
        vecs[1:2, :] = shift_grad


def cross_grads(
    where, gx2, a2, o2, dq2, dkv, all_memory, near, far, theirs, grad, memory, sems
):
    rows, width = gx2.shape
    examples, total, _ = memory.shape
    mem, _, slots, _ = all_memory.shape
    copies = Copies(sems)
    loads = [
        copies.start(all_memory.at[d], memory.at[:, d * slots : (d + 1) * slots, :])
        for d in range(mem)
    ]
    grad[0] = dot_tn(a2[...], dq2[...]).astype(BF)
    grad[3] = dot_tn(o2[...], gx2[...].astype(BF)).astype(BF)
    wait_all(loads)
    flat = memory[...].reshape(examples * total, width)
    for j in range(2):
        part = dkv[:, :, columns(j, width)].reshape(examples * total, width)
        grad[1 + j] = dot_tn(flat, part).astype(BF)
    wait_all(store_grad(where, grad, near, far, theirs, Copies(sems)))


def self_backward(
    group, where, suffix, vec, gx1, a1, qkv, p1, o1, parts, weights, suffix_grad, vecs,
    near, far, theirs, weight, start, grad, dqkv, do1, sems,
):
    rows, width = gx1.shape
    copies = Copies(sems)
    start_copy = my_examples(where, suffix, start, copies)
    loads = load_weight(where, weight, weights, copies)
    gs = gx1[...].astype(BF)
    grad[3] = dot_tn(o1[...], gs).astype(BF)
    wait_all(loads)
    do1[...] = dot_nt(gs, weight[3]).astype(BF)
    mask = head_mask(group)
    for r in range(rows // group):
        here = columns(r, group)
        for g in range(GROUPS):
            lanes = [slice(i * width + g * LANES, i * width + (g + 1) * LANES) for i in range(3)]
            queries = stack_heads(qkv[here, lanes[0]], mask)
            grads = stack_heads(do1[here, lanes[0]], mask)
            probs = p1[r * GROUPS + g]
            dp = dot_nt(grads, qkv[here, lanes[2]])
            wide = probs.astype(F32)
            row_sum = jnp.sum(wide * dp, axis=-1, keepdims=True)
            dz = (wide * (dp - row_sum)).astype(BF)
            dqkv[here, lanes[2]] = dot_tn(probs, grads).astype(BF)
            dqkv[here, lanes[1]] = (dot_tn(dz, queries) * SCALE).astype(BF)
            dq = merge_heads(dot(dz, qkv[here, lanes[1]]), mask) * SCALE
            dqkv[here, lanes[0]] = dq.astype(BF)
    for j in range(3):
        grad[j] = dot_tn(a1[...], dqkv[:, columns(j, width)]).astype(BF)
    start_copy.wait()
    started = store_grad(where, grad, near, far, theirs, Copies(sems))
    da1 = dot_nt(dqkv[:, columns(0, width)], weight[0])
    for j in range(1, 3):
        da1 = da1 + dot_nt(dqkv[:, columns(j, width)], weight[j])
    hat, scale = normalise(start[...].reshape(rows, width).astype(F32))
    back, gain_grad, shift_grad = norm_back(da1, vec[0:1, :], hat, scale)
    suffix_grad[...] = (gx1[...] + back).astype(BF).reshape(suffix_grad.shape)
    found = [gain_grad, shift_grad]
    for ref in parts:
        for r in range(ref.shape[0]):
            found += [ref[r : r + 1, columns(j, width)] for j in range(ref.shape[1] // width)]
    found.append(jnp.zeros((vecs.shape[0] - len(found), width), F32))
    vecs[...] = jnp.concatenate(found, axis=0).astype(BF)
    wait_all(started)


def run(kernel, inputs, outputs, scratch, copies, grid=()):
    def leaf(x):
        return isinstance(x, tuple) and len(x) == 2 and isinstance(x[0], pl.BlockSpec)

    flat_in, tree_in = jax.tree.flatten(inputs, is_leaf=leaf)
    flat_out, tree_out = jax.tree.flatten(outputs, is_leaf=leaf)

    def body(*refs):
        first, second = len(flat_in), len(flat_in) + len(flat_out)
        given = jax.tree.unflatten(tree_in, refs[:first])
        taken = jax.tree.unflatten(tree_out, refs[first:second])
        kernel(*given, *taken, *refs[second:])

    found = pl.pallas_call(
        body,
        grid=grid,
        in_specs=[spec for spec, _ in flat_in],
        out_specs=[spec for spec, _ in flat_out],
        out_shape=[shape for _, shape in flat_out],
        scratch_shapes=scratch + [pltpu.SemaphoreType.DMA((copies,))],
        compiler_params=pltpu.CompilerParams(vmem_limit_bytes=56 * 1024 * 1024),
        cost_estimate=pl.CostEstimate(
            flops=0, bytes_accessed=0, transcendentals=0
        ),
    )(*[x for _, x in flat_in])
    return jax.tree.unflatten(tree_out, found)


def shape_of(dims, dtype):
    return jax.ShapeDtypeStruct(tuple(dims), dtype)


def over_slow(value, slow, fast):
    groups = [[k * fast + b for k in range(slow)] for b in range(fast)]
    return lax.all_to_all(value, "fsdp", 0, 0, axis_index_groups=groups, tiled=True)


class Gather:
    def __init__(self, half, slow, fast):
        self.half, self.slow, self.fast = half, slow, fast

    def send_slow(self, *others):
        half = after(self.half, *others)
        self.came = [half] + [swap(half, "fsdp", k * self.fast) for k in range(1, self.slow)]

    def send_fast(self, *others):
        self.near = jnp.stack([after(piece, *others) for piece in self.came])
        self.near_other = swap(self.near, "mem", 1)
        self.far = [swap(self.near, "fsdp", b) for b in range(1, self.fast)]

    def whole(self):
        mine = [self.near] + self.far
        theirs = [self.near_other] + [swap(piece, "mem", 1) for piece in self.far]
        return mine, theirs

    @staticmethod
    def refs(weights):
        return [[(ANY, x) for x in some] for some in weights]


class Scatter:
    def __init__(self, grads, slow, fast, *others, vectors=None):
        self.near, self.far, theirs = grads
        self.slow, self.fast, self.vectors = slow, fast, vectors
        theirs = [after(part, *others) for part in theirs]
        far = [swap(part, "mem", 1) for part in theirs[1:]]
        far = [jnp.concatenate(far[2 * b : 2 * b + 2]) for b in range(fast - 1)]
        self.sent = [swap(theirs[0], "mem", 1)] + far
        if vectors is not None:
            self.vectors = vectors.astype(F32) + swap(vectors, "mem", 1).astype(F32)

    def add_cores(self):
        self.out = [
            (self.far[b].astype(F32) + self.sent[b + 1].astype(F32)).astype(BF)
            for b in range(self.fast - 1)
        ]
        return self.out

    def send_fast(self):
        self.came = [swap(part, "fsdp", b + 1) for b, part in enumerate(self.out)]
        if self.vectors is not None:
            low = self.vectors.astype(BF)
            self.vectors = [low] + [swap(low, "fsdp", b) for b in range(1, self.fast)]

    def add_fast(self, *others):
        if self.vectors is not None:
            self.vectors, self.came = lax.optimization_barrier((self.vectors, self.came))
            self.vectors = sum(part.astype(F32) for part in self.vectors)
        total = after(self.near, *others).astype(F32) + self.sent[0].astype(F32)
        for part in self.came:
            total = total + part.astype(F32)
        self.total = total.astype(BF).reshape(self.slow, -1, total.shape[-1])
        if self.vectors is not None:
            low = self.vectors.astype(BF)
            low = jnp.broadcast_to(low, (self.slow,) + low.shape)
            self.total = jnp.concatenate([self.total, low], axis=1)
        return self.total

    def send_slow(self):
        self.came = over_slow(self.total, self.slow, self.fast)

    def add_slow(self, *others):
        return jnp.sum(after(self.came, *others).astype(F32), axis=0)


class Replicas:
    def __init__(self, value, rows, across):
        self.rows = rows
        k = 1
        while 2 * k < across:
            low = value.astype(BF)
            value = low.astype(F32) + swap(low, "mem", 2 * k).astype(F32)
            k *= 2
        low = value.astype(BF)
        self.halves = [low, swap(low, "mem", 2 * k)] if across > 1 else [low]

    def swap_cores(self, *others):
        halves, _ = lax.optimization_barrier((self.halves, others))
        self.others = [swap(half[: 2 * self.rows], "mem", 1) for half in halves]

    def combine(self, c):
        rows = self.rows
        other = sum(half.astype(F32) for half in self.others)
        mine = sum(half.astype(F32) for half in self.halves)
        vectors, mine = mine[2 * rows :], mine[: 2 * rows]
        first = jnp.where(c == 0, mine, other)
        second = jnp.where(c == 0, other, mine)
        return [first[:rows], first[rows:], second[:rows], second[rows:]], vectors


def place_rows(where, blocks, outs, scratch, sems):
    copies = Copies(sems)
    loads = []
    for i, (even, odd) in enumerate(blocks):
        for d, piece in enumerate(even):
            loads.append((copies.start(piece, scratch.at[i, 2 * d]), i, 2 * d))
            loads.append((copies.start(odd.at[d], scratch.at[i, 2 * d + 1]), i, 2 * d + 1))
    examples = scratch.shape[2]
    stores = []
    for load, i, d in loads:
        load.wait()
        target = outs[i].at[pl.ds((where[3] ^ d) * examples, examples)]
        stores.append(copies.start(scratch.at[i, d], target))
    wait_all(stores)


def place_memory(where, pieces, out, scratch, sems):
    examples = pieces[0].shape[0]
    copies = Copies(sems)
    loads = [copies.start(piece, scratch.at[d]) for d, piece in enumerate(pieces)]
    stores = []
    for d, load in enumerate(loads):
        load.wait()
        target = out.at[pl.ds((where[3] ^ d) * examples, examples)]
        stores.append(copies.start(scratch.at[d], target))
    wait_all(stores)


def spread_across(value, mem):
    return [value] + [swap(value, "mem", d) for d in range(2, mem, 2)]


def per_device(
    suffix,
    memory,
    counts,
    cotangent,
    self_norm_gain,
    self_norm_bias,
    self_query,
    self_key,
    self_value,
    self_output,
    cross_norm_gain,
    cross_norm_bias,
    cross_query,
    cross_key,
    cross_value,
    cross_output,
    dense_norm_gain,
    dense_norm_bias,
    dense_in,
    dense_in_bias,
    dense_out,
    dense_out_bias,
):
    f = lax.axis_index("fsdp")
    m = lax.axis_index("mem")
    c = m % 2
    fsdp = lax.axis_size("fsdp")
    mem = lax.axis_size("mem")
    across = mem // 2
    slow, fast = fsdp_split(fsdp)
    SHARDS[0] = fsdp
    where = jnp.stack([f // fast, f % fast, c, m]).astype(jnp.int32)
    examples = suffix.shape[0] // mem
    length = suffix.shape[1]
    width = suffix.shape[2]
    slots = memory.shape[1]
    total = mem * slots
    rows = examples * length
    inner = dense_in.shape[1]
    part = width // fsdp
    group = min(128, rows)
    blocks = 4 * fsdp

    def gather(matrices, *others):
        halves = [jnp.concatenate(matrices[:2]), jnp.concatenate(matrices[2:])]
        half = jnp.concatenate([jnp.where(c == 0, *halves), *others])
        return Gather(half, slow, fast)

    cross_gather = gather([cross_query, cross_key, cross_value, cross_output])
    in_gather = gather([dense_in[:, columns(j, width)] for j in range(4)])
    out_gather = gather([dense_out[columns(j, part)] for j in range(4)])
    small = [
        self_norm_gain,
        self_norm_bias,
        cross_norm_gain,
        cross_norm_bias,
        dense_norm_gain,
        dense_norm_bias,
        dense_out_bias,
    ]
    small += [dense_in_bias[columns(j, part)] for j in range(4)]
    small = sum(
        jnp.pad(value[None], ((i, 15 - i), (0, width - part))) for i, value in enumerate(small)
    )
    self_gather = gather([self_query, self_key, self_value, self_output], small)

    def exchange(value):
        blocks = value.reshape((mem, examples) + value.shape[1:])
        return lax.all_to_all(blocks, "mem", 0, 0, tiled=True)

    all_memory = exchange(memory)
    self_gather.send_slow()
    sent = self_gather.came
    self_gather.send_fast(*sent)
    cross_gather.send_slow(*sent)
    sent = [*self_gather.far, *cross_gather.came, all_memory]
    self_gather.far = [after(piece, *sent) for piece in self_gather.far]
    self_weights = self_gather.whole()
    cross_gather.send_fast(*self_gather.far)
    in_gather.send_slow(*self_gather.far)

    half = (2, part, width)
    grads_like = [
        (ANY, shape_of((slow,) + half, BF)),
        (ANY, shape_of((fast - 1, slow) + half, BF)),
        [(ANY, shape_of((slow,) + half, BF))]
        + [(ANY, shape_of((slow // 2,) + half, BF))] * (2 * fast - 2),
    ]

    def flat(dims, dtype):
        return (VMEM, shape_of(dims, dtype))

    def per_example(value):
        dims = value.shape[1:]
        spec = pl.BlockSpec((1,) + dims, lambda e: (e,) + (0,) * len(dims))
        return (spec, value)

    def slots_of_example(value):
        spec = pl.BlockSpec((mem, 1, slots, width), lambda e: (0, e, 0, 0))
        return (spec, value)

    def scratch(*dims):
        return pltpu.VMEM(dims, BF)

    def scatter(grads, *others, vectors=None):
        return Scatter(grads, slow, fast, *others, vectors=vectors)

    wide = (rows, width)
    square = scratch(4, width, width)
    own_rows = scratch(examples, length, width)
    x1, a1, qkv, p1, o1, vec = run(
        functools.partial(self_forward, group),
        [(SMEM, where), (ANY, suffix), Gather.refs(self_weights)],
        [
            flat(wide, F32),
            flat(wide, BF),
            flat((rows, 3 * width), BF),
            flat((rows // group * GROUPS, TOGETHER * group, group), BF),
            flat(wide, BF),
            flat((16, width), F32),
        ],
        [square, own_rows, scratch(fsdp, 16, 128)],
        1 + fsdp + blocks,
    )
    cross_gather.far = [after(piece, x1, *in_gather.came) for piece in cross_gather.far]
    cross_weights = Gather.refs(cross_gather.whole())
    in_gather.send_fast(*cross_gather.far)
    out_gather.send_slow(*cross_gather.far)
    x2, a2, q2, kv, p2, o2 = run(
        cross_forward,
        [(SMEM, where), (SMEM, counts), (VMEM, x1), (VMEM, vec)]
        + [slots_of_example(all_memory), cross_weights],
        [
            flat(wide, F32),
            flat(wide, BF),
            flat(wide, BF),
            per_example(shape_of((examples, total, 2 * width), BF)),
            per_example(shape_of((examples, GROUPS, TOGETHER * length, total), BF)),
            flat(wide, BF),
        ],
        [square],
        blocks,
        (examples,),
    )
    small = [after(piece, x1)[:, 2 * part + 7 : 2 * part + 11, :part] for piece in self_weights[0]]
    order = jnp.arange(fsdp) ^ f
    bias_in = jnp.take(jnp.concatenate(small), order % fast * slow + order // fast, axis=0)
    bias_in = bias_in.astype(F32).reshape(1, inner)
    in_gather.far = [after(piece, x2, *out_gather.came) for piece in in_gather.far]
    in_weights = Gather.refs(in_gather.whole())
    out_gather.send_fast(*in_gather.far)
    a3, h, slope, *grads = run(
        dense_inner,
        [(SMEM, where), (VMEM, x2), (VMEM, vec), (VMEM, bias_in), (ANY, cotangent), in_weights],
        [flat(wide, BF), flat((rows, inner), BF), flat((rows, inner), BF)] + grads_like,
        [square, scratch(fsdp, 4, part, width), own_rows],
        1 + blocks,
    )
    out_gather.far = [after(piece, a3) for piece in out_gather.far]
    out_weights = Gather.refs(out_gather.whole())
    out_scatter = scatter(grads, *out_gather.far)
    out_sum = out_scatter.add_cores()
    out_scatter.send_fast()
    y, du, vecs_y, bias_grad, *grads = run(
        dense_outer,
        [(SMEM, where), (VMEM, after(x2, *out_sum)), (VMEM, vec), (VMEM, a3), (VMEM, h)]
        + [(VMEM, slope), (ANY, cotangent), out_weights],
        [
            flat((examples, length, width), BF),
            flat((rows, inner), BF),
            flat((1, width), F32),
            flat((1, inner), F32),
        ]
        + grads_like,
        [scratch(fsdp, 4, part, width), square, own_rows],
        1 + blocks,
    )
    in_grads = grads
    gx2, vecs_dense = run(
        dense_back,
        [(SMEM, where), (VMEM, x2), (VMEM, vec), (VMEM, du), (ANY, cotangent), in_weights],
        [flat(wide, F32), flat((2, width), F32)],
        [square, own_rows],
        1 + blocks,
    )
    in_scatter = scatter(in_grads, gx2)
    in_sum = in_scatter.add_cores()
    in_scatter.send_fast()
    out_total = out_scatter.add_fast(*in_sum)
    out_scatter.send_slow()
    gx1, vecs_cross, dkv, dq2, grad_memory = run(
        cross_backward,
        [(SMEM, where), (VMEM, x1), (VMEM, vec), (VMEM, after(gx2, out_total, *in_sum)), (VMEM, q2)]
        + [per_example(kv), per_example(p2), cross_weights],
        [
            flat(wide, F32),
            flat((2, width), F32),
            per_example(shape_of((examples, total, 2 * width), BF)),
            flat(wide, BF),
            [per_example(shape_of((examples, slots, width), BF))] * mem,
        ],
        [square, scratch(*wide), scratch(total, width)],
        blocks,
        (examples,),
    )
    out_final = out_scatter.add_slow(gx1)
    mem_pieces = grad_memory[:1] + [swap(grad_memory[d], "mem", d) for d in range(1, mem)]
    grads = run(
        cross_grads,
        [(SMEM, where), (VMEM, after(gx2, out_final)), (VMEM, a2), (VMEM, o2), (VMEM, dq2)]
        + [(VMEM, dkv), (ANY, all_memory)],
        grads_like,
        [square, scratch(examples, total, width)],
        max(mem, blocks),
    )
    in_total = in_scatter.add_fast()
    in_scatter.send_slow()
    cross_scatter = scatter(grads, in_total, *mem_pieces[1:3])
    cross_sum = cross_scatter.add_cores()
    cross_scatter.send_fast()
    in_final = in_scatter.add_slow()
    gx1 = after(gx1, in_final, *cross_sum)
    suffix_part, vecs_self, *grads = run(
        functools.partial(self_backward, group),
        [(SMEM, where), (ANY, suffix), (VMEM, vec), (VMEM, gx1), (VMEM, a1)]
        + [(VMEM, qkv), (VMEM, p1), (VMEM, o1)]
        + [[(VMEM, x) for x in (vecs_cross, vecs_dense, vecs_y, bias_grad)], Gather.refs(self_weights)],
        [flat((examples, length, width), BF), flat((16, width), BF)] + grads_like,
        [square, own_rows, square, scratch(rows, 3 * width), scratch(*wide)],
        1 + blocks,
    )
    self_scatter = scatter(grads, *mem_pieces[3:4], vectors=vecs_self)
    self_sum = self_scatter.add_cores()
    self_scatter.send_fast()
    cross_scatter.add_fast(*self_sum)
    cross_scatter.send_slow()
    dense_sum = after(jnp.concatenate([out_final, in_final]), *self_sum)
    dense_sum = Replicas(dense_sum, 2 * part, across)
    y_rows = spread_across(after(y, *self_sum), mem)
    self_total = self_scatter.add_fast(*dense_sum.halves, *y_rows)
    self_scatter.send_slow()
    cross_sum = Replicas(cross_scatter.add_slow(self_total), part, across)
    suffix_rows = spread_across(after(suffix_part, self_total), mem)
    y_rows = [after(value, self_total) for value in y_rows]
    y_far = swap(jnp.stack(y_rows), "mem", 1)
    dense_sum.swap_cores(self_total)
    mem_pieces = [after(value, self_total) for value in mem_pieces]
    (memory_grad,) = run(
        place_memory,
        [(SMEM, where), [(ANY, value) for value in mem_pieces]],
        [(ANY, shape_of(memory.shape, BF))],
        [scratch(mem, examples, slots, width)],
        2 * mem,
    )
    (out_low, in_low, out_high, in_high), _ = dense_sum.combine(c)
    grad_in = jnp.concatenate([in_low[:part], in_low[part:], in_high[:part], in_high[part:]], axis=1)
    grad_out = jnp.concatenate([out_low, out_high])
    done = [*cross_sum.halves, *suffix_rows, grad_in, grad_out, y_far, memory_grad]
    self_final = Replicas(self_scatter.add_slow(*done), part, across)
    cross_sum.swap_cores(self_final.halves[0])
    suffix_rows = [after(value, self_final.halves[0]) for value in suffix_rows]
    suffix_far = swap(jnp.stack(suffix_rows), "mem", 1)
    blocks = [([(ANY, x) for x in y_rows], (ANY, y_far))]
    blocks += [([(ANY, x) for x in suffix_rows], (ANY, suffix_far))]
    ((block_output, suffix_grad),) = run(
        place_rows,
        [(SMEM, where), blocks],
        [[(ANY, shape_of(suffix.shape, BF))] * 2],
        [scratch(2, mem, examples, length, width)],
        4 * mem,
    )
    grad_cross, _ = cross_sum.combine(c)
    self_final.swap_cores(block_output)
    grad_self, vectors = self_final.combine(c)

    def vector(i):
        return lax.dynamic_slice(vectors, (i, f * part), (1, part)).reshape(part)

    return (
        block_output,
        suffix_grad,
        memory_grad,
        vector(0),
        vector(1),
        *grad_self,
        vector(2),
        vector(3),
        *grad_cross,
        vector(4),
        vector(5),
        grad_in,
        lax.dynamic_slice_in_dim(vectors[7:11].reshape(-1), f * (inner // fsdp), inner // fsdp, 0),
        grad_out,
        vector(6),
    )


def solution(mesh):
    rows = P("fsdp", None, None)
    matrix = P("fsdp", None)
    vector = P("fsdp")
    attention = (vector, vector, matrix, matrix, matrix, matrix)
    params = attention + attention + (vector, vector, matrix, vector, matrix, vector)
    return jax.shard_map(
        per_device,
        mesh=mesh,
        in_specs=(rows, P("fsdp", "mem", None), vector, rows) + params,
        out_specs=(rows, rows, P("fsdp", "mem", None)) + params,
        check_vma=False,
    )
```

```python
import functools

import jax
import jax.numpy as jnp
from jax import lax
from jax.experimental import pallas as pl
from jax.experimental.pallas import tpu as pltpu
from jax.sharding import PartitionSpec as P

HEADS = 12
HEAD = 64
TOGETHER = 4
GROUPS = HEADS // TOGETHER
LANES = TOGETHER * HEAD
SCALE = HEAD ** (-0.5)
BF = jnp.bfloat16
F32 = jnp.float32
ANY = pl.BlockSpec(memory_space=pl.ANY)
SMEM = pl.BlockSpec(memory_space=pltpu.SMEM)
VMEM = pl.BlockSpec(memory_space=pltpu.VMEM)


def swap(value, axis, distance):
    size = lax.axis_size(axis)
    return lax.ppermute(value, axis, [(i, i ^ distance) for i in range(size)])


def after(value, *others):
    return lax.optimization_barrier((value, *others))[0] if others else value


def fsdp_split(size):
    slow = 4 if size % 4 == 0 else 1
    return slow, size // slow


def dot(left, right):
    return jnp.dot(left, right, preferred_element_type=F32)


def dot_nt(left, right):
    return lax.dot_general(left, right, (((1,), (1,)), ((), ())), preferred_element_type=F32)


def dot_tn(left, right):
    return lax.dot_general(left, right, (((0,), (0,)), ((), ())), preferred_element_type=F32)


def rows_of(start, size):
    return pl.ds(pl.multiple_of(start, 16), size)


def block(ref, by_rows, shard, which):
    if by_rows:
        return ref.at[shard, pl.ds(which * 2, 2)]
    rows = ref.shape[1] // SHARDS[0]
    return ref.at[pl.ds(which * 2, 2), rows_of(shard * rows, rows)]


SHARDS = [0]


class Copies:
    def __init__(self, sems):
        self.sems = sems
        self.next = 0

    def start(self, source, target):
        copy = pltpu.make_async_copy(source, target, self.sems.at[self.next])
        self.next += 1
        copy.start()
        return copy


def wait_all(copies):
    for copy in copies:
        copy.wait()


def load_weight(where, whole, weights, copies, by_rows=False):
    z, y, c = where[0], where[1], where[2]
    rows = whole.shape[2] if by_rows else whole.shape[1] // SHARDS[0]
    started = []
    for which, pieces in ((c, weights[0]), (1 - c, weights[1])):
        fast = len(pieces)
        for b, piece in enumerate(pieces):
            for k in range(piece.shape[0]):
                shard = (z ^ k) * fast + (y ^ b)
                for i in range(2):
                    source = piece.at[k, pl.ds(i * rows, rows)]
                    if by_rows:
                        target = whole.at[shard, 2 * which + i]
                    else:
                        target = whole.at[2 * which + i, rows_of(shard * rows, rows)]
                    started.append(copies.start(source, target))
    return started


def store_grad(where, whole, near, far, theirs, copies, by_rows=False):
    y, c = where[1], where[2]
    slow, cut = near.shape[0], near.shape[0] // 2
    fast = (len(theirs) + 1) // 2
    started = []
    for b in range(fast):
        for k in range(slow):
            shard = k * fast + (y ^ b)
            mine = far.at[b - 1, k] if b else near.at[k]
            other = theirs[2 * b - 1 + k // cut].at[k % cut] if b else theirs[0].at[k]
            started.append(copies.start(block(whole, by_rows, shard, 1 - c), other))
            started.append(copies.start(block(whole, by_rows, shard, c), mine))
    return started


def my_examples(where, source, target, copies):
    count = target.shape[0]
    return copies.start(source.at[pl.ds(where[3] * count, count)], target)


def normalise(values):
    centred = values - jnp.mean(values, axis=-1, keepdims=True)
    scale = lax.rsqrt(jnp.mean(centred * centred, axis=-1, keepdims=True) + 1e-06)
    return centred * scale, scale


def norm_back(grad, gain, hat, scale):
    inner = grad * gain
    mean = jnp.mean(inner, axis=-1, keepdims=True)
    along = jnp.mean(inner * hat, axis=-1, keepdims=True)
    return (
        scale * (inner - mean - hat * along),
        jnp.sum(grad * hat, axis=0, keepdims=True),
        jnp.sum(grad, axis=0, keepdims=True),
    )


def head_mask(rows):
    shape = (TOGETHER * rows, LANES)
    row = lax.broadcasted_iota(jnp.int32, shape, 0) // rows
    lane = lax.broadcasted_iota(jnp.int32, shape, 1) // HEAD
    return (row == lane).astype(F32)


def stack_heads(value, mask):
    return (jnp.concatenate([value] * TOGETHER, axis=0).astype(F32) * mask).astype(BF)


def merge_heads(value, mask):
    rows = value.shape[0] // TOGETHER
    value = value * mask
    total = value[:rows]
    for h in range(1, TOGETHER):
        total = total + value[h * rows : (h + 1) * rows]
    return total


def columns(j, width):
    return slice(j * width, (j + 1) * width)


def self_forward(
    group, where, suffix, weights, x1, a1, qkv, p1, o1, vec, weight, start, small, sems
):
    rows, width = x1.shape
    copies = Copies(sems)
    first = my_examples(where, suffix, start, copies)
    fast, slow = len(weights[0]), weights[0][0].shape[0]
    part = width // (fast * slow)
    vectors = []
    for b, piece in enumerate(weights[0]):
        for k in range(slow):
            source = piece.at[k, pl.ds(2 * part, 16), pl.ds(0, 128)]
            vectors.append(copies.start(source, small.at[b * slow + k]))
    loads = load_weight(where, weight, weights, copies)
    wait_all(vectors)
    lane = lax.broadcasted_iota(jnp.int32, (128, width), 0)
    place = lax.broadcasted_iota(jnp.int32, (128, width), 1) - lane
    together = jnp.zeros(vec.shape, F32)
    for i in range(fast * slow):
        shard = (where[0] ^ (i % slow)) * fast + (where[1] ^ (i // slow))
        chosen = ((place == shard * part) & (lane < part)).astype(F32).astype(BF)
        together = together + dot(small[i], chosen)
    vec[...] = together
    first.wait()
    values = start[...].reshape(rows, width).astype(F32)
    hat, _ = normalise(values)
    a1[...] = (hat * vec[0:1, :] + vec[1:2, :]).astype(BF)
    wait_all(loads)
    for j in range(3):
        qkv[:, columns(j, width)] = dot(a1[...], weight[j]).astype(BF)
    mask = head_mask(group)
    length = suffix.shape[1]
    shape = (TOGETHER * group, group)
    row = lax.broadcasted_iota(jnp.int32, shape, 0) % group
    col = lax.broadcasted_iota(jnp.int32, shape, 1)
    seen = (row // length == col // length) & (row >= col)
    for r in range(rows // group):
        here = columns(r, group)
        for g in range(GROUPS):
            lanes = [slice(i * width + g * LANES, i * width + (g + 1) * LANES) for i in range(3)]
            queries = stack_heads(qkv[here, lanes[0]], mask)
            scores = dot_nt(queries, qkv[here, lanes[1]]) * SCALE
            scores = jnp.where(seen, scores, -1e30)
            powers = jnp.exp(scores - jnp.max(scores, axis=-1, keepdims=True))
            probs = (powers / jnp.sum(powers, axis=-1, keepdims=True)).astype(BF)
            p1[r * GROUPS + g] = probs
            found = dot(probs, qkv[here, lanes[2]])
            o1[here, lanes[0]] = merge_heads(found, mask).astype(BF)
    x1[...] = values + dot(o1[...], weight[3])


def cross_forward(
    where, counts, x1, vec, memory, weights, x2, a2, q2, kv, p2, o2, weight, sems
):
    rows, width = x1.shape
    examples = pl.num_programs(0)
    e = pl.program_id(0)
    total = kv.shape[1]
    length = p2.shape[2] // TOGETHER

    @pl.when(e == 0)
    def _():
        loads = load_weight(where, weight, weights, Copies(sems))
        hat, _ = normalise(x1[...])
        a2[...] = (hat * vec[2:3, :] + vec[3:4, :]).astype(BF)
        wait_all(loads)
        q2[...] = dot(a2[...], weight[0]).astype(BF)

    tokens = memory[...].reshape(total, width)
    for j in range(2):
        kv[0, :, columns(j, width)] = dot(tokens, weight[1 + j]).astype(BF)
    mask = head_mask(length)
    position = lax.broadcasted_iota(jnp.int32, (1, total), 1)
    valid = position < counts[where[3] * examples + e]
    here = rows_of(e * length, length)
    probs = []
    for g in range(GROUPS):
        lanes = columns(g, LANES)
        queries = stack_heads(q2[here, lanes], mask)
        scores = dot_nt(queries, kv[0, :, lanes]) * SCALE
        scores = jnp.where(valid, scores, -1e30)
        top = jnp.maximum(jnp.max(scores, axis=-1, keepdims=True), 0.0)
        powers = jnp.exp(scores - top)
        weight_sum = jnp.sum(powers, axis=-1, keepdims=True) + jnp.exp(-top)
        probs.append((powers / weight_sum).astype(BF))
    for g in range(GROUPS):
        p2[0, g] = probs[g]
        found = dot(probs[g], kv[0, :, width + g * LANES : width + (g + 1) * LANES])
        o2[here, columns(g, LANES)] = merge_heads(found, mask).astype(BF)

    @pl.when(e == examples - 1)
    def _():
        x2[...] = x1[...] + dot(o2[...], weight[3])


def dense_inner(
    where, x2, vec, bias, cotangent, weights, a3, h, slope, near, far, theirs,
    weight, grad, cot, sems,
):
    rows, width = x2.shape
    copies = Copies(sems)
    cot_copy = my_examples(where, cotangent, cot, copies)
    loads = load_weight(where, weight, weights, copies)
    hat, _ = normalise(x2[...])
    a3[...] = (hat * vec[4:5, :] + vec[5:6, :]).astype(BF)
    cot_copy.wait()
    gy = cot[...].reshape(rows, width)
    wait_all(loads)
    flat = grad.shape[0] * grad.shape[1] * grad.shape[2]
    step = flat // grad.shape[0]
    for j in range(4):
        for half in range(2):
            cols = slice(j * width + half * 384, j * width + (half + 1) * 384)
            u = dot(a3[...], weight[j, :, half * 384 : (half + 1) * 384]) + bias[:, cols]
            square = u * u
            t = jnp.tanh(0.7978845608 * u * (1.0 + 0.044715 * square))
            h[:, cols] = (0.5 * u * (1.0 + t)).astype(BF)
            slope[:, cols] = (
                0.5 * (1.0 + t)
                + (0.5 * 0.7978845608) * u * (1.0 - t * t) * (1.0 + (3.0 * 0.044715) * square)
            ).astype(BF)
            part = dot_tn(h[:, cols], gy).astype(BF)
            per = 384 // step
            grad[cols.start // step : cols.start // step + per] = part.reshape(
                (per,) + grad.shape[1:]
            )
    wait_all(store_grad(where, grad, near, far, theirs, Copies(sems), True))


def dense_outer(
    where, x2, vec, a3, h, slope, cotangent, weights, y, du, vecs, bias_grad, near, far, theirs,
    weight, grad, cot, sems,
):
    rows, width = x2.shape
    copies = Copies(sems)
    cot_copy = my_examples(where, cotangent, cot, copies)
    wait_all(load_weight(where, weight, weights, copies, True))
    cot_copy.wait()
    gy = cot[...].reshape(rows, width)
    shards = weight.shape[0]
    step = weight.shape[1] * weight.shape[2]
    whole = weight[...].reshape(shards * step, width)
    for j in range(4):
        cols = columns(j, width)
        low = (dot_nt(gy, whole[cols]) * slope[:, cols].astype(F32)).astype(BF)
        du[:, cols] = low
        bias_grad[:, cols] = jnp.sum(low.astype(F32), axis=0, keepdims=True)
        grad[j] = dot_tn(a3[...], low).astype(BF)
    started = store_grad(where, grad, near, far, theirs, Copies(sems))
    result = x2[...] + dot(h[...], whole) + vec[6:7, :]
    y[...] = result.astype(BF).reshape(y.shape)
    vecs[...] = jnp.sum(gy.astype(F32), axis=0, keepdims=True)
    wait_all(started)


def dense_back(where, x2, vec, du, cotangent, weights, gx2, vecs, weight, cot, sems):
    rows, width = x2.shape
    copies = Copies(sems)
    cot_copy = my_examples(where, cotangent, cot, copies)
    loads = load_weight(where, weight, weights, copies)
    hat, scale = normalise(x2[...])
    cot_copy.wait()
    wait_all(loads)
    da3 = dot_nt(du[:, columns(0, width)], weight[0])
    for j in range(1, 4):
        da3 = da3 + dot_nt(du[:, columns(j, width)], weight[j])
    back, gain_grad, shift_grad = norm_back(da3, vec[4:5, :], hat, scale)
    gx2[...] = cot[...].reshape(rows, width).astype(F32) + back
    vecs[0:1, :] = gain_grad
    vecs[1:2, :] = shift_grad


def cross_backward(
    where, x1, vec, gx2, q2, kv, p2, weights, gx1, vecs, dkv, dq2, out_mem, weight, do2, moved, sems
):
    rows, width = x1.shape
    examples = pl.num_programs(0)
    e = pl.program_id(0)
    length = p2.shape[2] // TOGETHER

    @pl.when(e == 0)
    def _():
        wait_all(load_weight(where, weight, weights, Copies(sems)))
        do2[...] = dot_nt(gx2[...].astype(BF), weight[3]).astype(BF)

    mask = head_mask(length)
    here = rows_of(e * length, length)
    for g in range(GROUPS):
        lanes = columns(g, LANES)
        value_lanes = slice(width + g * LANES, width + (g + 1) * LANES)
        queries = stack_heads(q2[here, lanes], mask)
        grads = stack_heads(do2[here, lanes], mask)
        probs = p2[0, g]
        dp = dot_nt(grads, kv[0, :, value_lanes])
        wide = probs.astype(F32)
        row_sum = jnp.sum(wide * dp, axis=-1, keepdims=True)
        dz = (wide * (dp - row_sum)).astype(BF)
        dkv[0, :, value_lanes] = dot_tn(probs, grads).astype(BF)
        dkv[0, :, lanes] = (dot_tn(dz, queries) * SCALE).astype(BF)
        dq2[here, lanes] = (merge_heads(dot(dz, kv[0, :, lanes]), mask) * SCALE).astype(BF)
    back = dot_nt(dkv[0, :, :width], weight[1]) + dot_nt(dkv[0, :, width:], weight[2])
    moved[...] = back.astype(BF)
    for d, out in enumerate(out_mem):
        slots = out.shape[1]
        out[0] = moved[rows_of((where[3] ^ d) * slots, slots), :]

    @pl.when(e == examples - 1)
    def _():
        hat, scale = normalise(x1[...])
        back, gain_grad, shift_grad = norm_back(
            dot_nt(dq2[...], weight[0]), vec[2:3, :], hat, scale
        )
        gx1[...] = gx2[...] + back
        vecs[0:1, :] = gain_grad
        vecs[1:2, :] = shift_grad


def cross_grads(
    where, gx2, a2, o2, dq2, dkv, all_memory, near, far, theirs, grad, memory, sems
):
    rows, width = gx2.shape
    examples, total, _ = memory.shape
    mem, _, slots, _ = all_memory.shape
    copies = Copies(sems)
    loads = [
        copies.start(all_memory.at[d], memory.at[:, d * slots : (d + 1) * slots, :])
        for d in range(mem)
    ]
    grad[0] = dot_tn(a2[...], dq2[...]).astype(BF)
    grad[3] = dot_tn(o2[...], gx2[...].astype(BF)).astype(BF)
    wait_all(loads)
    flat = memory[...].reshape(examples * total, width)
    for j in range(2):
        part = dkv[:, :, columns(j, width)].reshape(examples * total, width)
        grad[1 + j] = dot_tn(flat, part).astype(BF)
    wait_all(store_grad(where, grad, near, far, theirs, Copies(sems)))


def self_backward(
    group, where, suffix, vec, gx1, a1, qkv, p1, o1, parts, weights, suffix_grad, vecs,
    near, far, theirs, weight, start, grad, dqkv, do1, sems,
):
    rows, width = gx1.shape
    copies = Copies(sems)
    start_copy = my_examples(where, suffix, start, copies)
    loads = load_weight(where, weight, weights, copies)
    gs = gx1[...].astype(BF)
    grad[3] = dot_tn(o1[...], gs).astype(BF)
    wait_all(loads)
    do1[...] = dot_nt(gs, weight[3]).astype(BF)
    mask = head_mask(group)
    for r in range(rows // group):
        here = columns(r, group)
        for g in range(GROUPS):
            lanes = [slice(i * width + g * LANES, i * width + (g + 1) * LANES) for i in range(3)]
            queries = stack_heads(qkv[here, lanes[0]], mask)
            grads = stack_heads(do1[here, lanes[0]], mask)
            probs = p1[r * GROUPS + g]
            dp = dot_nt(grads, qkv[here, lanes[2]])
            wide = probs.astype(F32)
            row_sum = jnp.sum(wide * dp, axis=-1, keepdims=True)
            dz = (wide * (dp - row_sum)).astype(BF)
            dqkv[here, lanes[2]] = dot_tn(probs, grads).astype(BF)
            dqkv[here, lanes[1]] = (dot_tn(dz, queries) * SCALE).astype(BF)
            dq = merge_heads(dot(dz, qkv[here, lanes[1]]), mask) * SCALE
            dqkv[here, lanes[0]] = dq.astype(BF)
    for j in range(3):
        grad[j] = dot_tn(a1[...], dqkv[:, columns(j, width)]).astype(BF)
    start_copy.wait()
    started = store_grad(where, grad, near, far, theirs, Copies(sems))
    da1 = dot_nt(dqkv[:, columns(0, width)], weight[0])
    for j in range(1, 3):
        da1 = da1 + dot_nt(dqkv[:, columns(j, width)], weight[j])
    hat, scale = normalise(start[...].reshape(rows, width).astype(F32))
    back, gain_grad, shift_grad = norm_back(da1, vec[0:1, :], hat, scale)
    suffix_grad[...] = (gx1[...] + back).astype(BF).reshape(suffix_grad.shape)
    found = [gain_grad, shift_grad]
    for ref in parts:
        for r in range(ref.shape[0]):
            found += [ref[r : r + 1, columns(j, width)] for j in range(ref.shape[1] // width)]
    found.append(jnp.zeros((vecs.shape[0] - len(found), width), F32))
    vecs[...] = jnp.concatenate(found, axis=0).astype(BF)
    wait_all(started)


def run(kernel, inputs, outputs, scratch, copies, grid=()):
    def leaf(x):
        return isinstance(x, tuple) and len(x) == 2 and isinstance(x[0], pl.BlockSpec)

    flat_in, tree_in = jax.tree.flatten(inputs, is_leaf=leaf)
    flat_out, tree_out = jax.tree.flatten(outputs, is_leaf=leaf)

    def body(*refs):
        first, second = len(flat_in), len(flat_in) + len(flat_out)
        given = jax.tree.unflatten(tree_in, refs[:first])
        taken = jax.tree.unflatten(tree_out, refs[first:second])
        kernel(*given, *taken, *refs[second:])

    found = pl.pallas_call(
        body,
        grid=grid,
        in_specs=[spec for spec, _ in flat_in],
        out_specs=[spec for spec, _ in flat_out],
        out_shape=[shape for _, shape in flat_out],
        scratch_shapes=scratch + [pltpu.SemaphoreType.DMA((copies,))],
        compiler_params=pltpu.CompilerParams(vmem_limit_bytes=56 * 1024 * 1024),
        cost_estimate=pl.CostEstimate(
            flops=0, bytes_accessed=0, transcendentals=0
        ),
    )(*[x for _, x in flat_in])
    return jax.tree.unflatten(tree_out, found)


def shape_of(dims, dtype):
    return jax.ShapeDtypeStruct(tuple(dims), dtype)


def over_slow(value, slow, fast):
    groups = [[k * fast + b for k in range(slow)] for b in range(fast)]
    return lax.all_to_all(value, "fsdp", 0, 0, axis_index_groups=groups, tiled=True)


class Gather:
    def __init__(self, half, slow, fast):
        self.half, self.slow, self.fast = half, slow, fast

    def send_slow(self, *others):
        half = after(self.half, *others)
        self.came = [half] + [swap(half, "fsdp", k * self.fast) for k in range(1, self.slow)]

    def send_fast(self, *others):
        self.near = jnp.stack([after(piece, *others) for piece in self.came])
        self.near_other = swap(self.near, "mem", 1)
        self.far = [swap(self.near, "fsdp", b) for b in range(1, self.fast)]

    def whole(self):
        mine = [self.near] + self.far
        theirs = [self.near_other] + [swap(piece, "mem", 1) for piece in self.far]
        return mine, theirs

    @staticmethod
    def refs(weights):
        return [[(ANY, x) for x in some] for some in weights]


class Scatter:
    def __init__(self, grads, slow, fast, *others, vectors=None):
        self.near, self.far, theirs = grads
        self.slow, self.fast, self.vectors = slow, fast, vectors
        theirs = [after(part, *others) for part in theirs]
        far = [swap(part, "mem", 1) for part in theirs[1:]]
        far = [jnp.concatenate(far[2 * b : 2 * b + 2]) for b in range(fast - 1)]
        self.sent = [swap(theirs[0], "mem", 1)] + far
        if vectors is not None:
            self.vectors = vectors.astype(F32) + swap(vectors, "mem", 1).astype(F32)

    def add_cores(self):
        self.out = [
            (self.far[b].astype(F32) + self.sent[b + 1].astype(F32)).astype(BF)
            for b in range(self.fast - 1)
        ]
        return self.out

    def send_fast(self):
        self.came = [swap(part, "fsdp", b + 1) for b, part in enumerate(self.out)]
        if self.vectors is not None:
            low = self.vectors.astype(BF)
            self.vectors = [low] + [swap(low, "fsdp", b) for b in range(1, self.fast)]

    def add_fast(self, *others):
        if self.vectors is not None:
            self.vectors, self.came = lax.optimization_barrier((self.vectors, self.came))
            self.vectors = sum(part.astype(F32) for part in self.vectors)
        total = after(self.near, *others).astype(F32) + self.sent[0].astype(F32)
        for part in self.came:
            total = total + part.astype(F32)
        self.total = total.astype(BF).reshape(self.slow, -1, total.shape[-1])
        if self.vectors is not None:
            low = self.vectors.astype(BF)
            low = jnp.broadcast_to(low, (self.slow,) + low.shape)
            self.total = jnp.concatenate([self.total, low], axis=1)
        return self.total

    def send_slow(self):
        self.came = over_slow(self.total, self.slow, self.fast)

    def add_slow(self, *others):
        return jnp.sum(after(self.came, *others).astype(F32), axis=0)


class Replicas:
    def __init__(self, value, rows, across):
        self.rows = rows
        k = 1
        while 2 * k < across:
            low = value.astype(BF)
            value = low.astype(F32) + swap(low, "mem", 2 * k).astype(F32)
            k *= 2
        low = value.astype(BF)
        self.halves = [low, swap(low, "mem", 2 * k)] if across > 1 else [low]

    def swap_cores(self, *others):
        halves, _ = lax.optimization_barrier((self.halves, others))
        self.others = [swap(half[: 2 * self.rows], "mem", 1) for half in halves]

    def combine(self, c):
        rows = self.rows
        other = sum(half.astype(F32) for half in self.others)
        mine = sum(half.astype(F32) for half in self.halves)
        vectors, mine = mine[2 * rows :], mine[: 2 * rows]
        first = jnp.where(c == 0, mine, other)
        second = jnp.where(c == 0, other, mine)
        return [first[:rows], first[rows:], second[:rows], second[rows:]], vectors


def place_rows(where, blocks, outs, scratch, sems):
    copies = Copies(sems)
    loads = []
    for i, (even, odd) in enumerate(blocks):
        for d, piece in enumerate(even):
            loads.append((copies.start(piece, scratch.at[i, 2 * d]), i, 2 * d))
            loads.append((copies.start(odd.at[d], scratch.at[i, 2 * d + 1]), i, 2 * d + 1))
    examples = scratch.shape[2]
    stores = []
    for load, i, d in loads:
        load.wait()
        target = outs[i].at[pl.ds((where[3] ^ d) * examples, examples)]
        stores.append(copies.start(scratch.at[i, d], target))
    wait_all(stores)


def place_memory(where, pieces, out, scratch, sems):
    examples = pieces[0].shape[0]
    copies = Copies(sems)
    loads = [copies.start(piece, scratch.at[d]) for d, piece in enumerate(pieces)]
    stores = []
    for d, load in enumerate(loads):
        load.wait()
        target = out.at[pl.ds((where[3] ^ d) * examples, examples)]
        stores.append(copies.start(scratch.at[d], target))
    wait_all(stores)


def spread_across(value, mem):
    return [value] + [swap(value, "mem", d) for d in range(2, mem, 2)]


def per_device(
    suffix,
    memory,
    counts,
    cotangent,
    self_norm_gain,
    self_norm_bias,
    self_query,
    self_key,
    self_value,
    self_output,
    cross_norm_gain,
    cross_norm_bias,
    cross_query,
    cross_key,
    cross_value,
    cross_output,
    dense_norm_gain,
    dense_norm_bias,
    dense_in,
    dense_in_bias,
    dense_out,
    dense_out_bias,
):
    f = lax.axis_index("fsdp")
    m = lax.axis_index("mem")
    c = m % 2
    fsdp = lax.axis_size("fsdp")
    mem = lax.axis_size("mem")
    across = mem // 2
    slow, fast = fsdp_split(fsdp)
    SHARDS[0] = fsdp
    where = jnp.stack([f // fast, f % fast, c, m]).astype(jnp.int32)
    examples = suffix.shape[0] // mem
    length = suffix.shape[1]
    width = suffix.shape[2]
    slots = memory.shape[1]
    total = mem * slots
    rows = examples * length
    inner = dense_in.shape[1]
    part = width // fsdp
    group = min(128, rows)
    blocks = 4 * fsdp

    def gather(matrices, *others):
        halves = [jnp.concatenate(matrices[:2]), jnp.concatenate(matrices[2:])]
        half = jnp.concatenate([jnp.where(c == 0, *halves), *others])
        return Gather(half, slow, fast)

    cross_gather = gather([cross_query, cross_key, cross_value, cross_output])
    in_gather = gather([dense_in[:, columns(j, width)] for j in range(4)])
    out_gather = gather([dense_out[columns(j, part)] for j in range(4)])
    small = [
        self_norm_gain,
        self_norm_bias,
        cross_norm_gain,
        cross_norm_bias,
        dense_norm_gain,
        dense_norm_bias,
        dense_out_bias,
    ]
    small += [dense_in_bias[columns(j, part)] for j in range(4)]
    small = sum(
        jnp.pad(value[None], ((i, 15 - i), (0, width - part))) for i, value in enumerate(small)
    )
    self_gather = gather([self_query, self_key, self_value, self_output], small)

    def exchange(value):
        blocks = value.reshape((mem, examples) + value.shape[1:])
        return lax.all_to_all(blocks, "mem", 0, 0, tiled=True)

    self_gather.send_slow()
    all_memory = exchange(after(memory, self_gather.came[1]))
    sent = self_gather.came
    self_gather.send_fast(*sent)
    cross_gather.send_slow(*sent)
    sent = [*self_gather.far, *cross_gather.came, all_memory]
    self_gather.far = [after(piece, *sent) for piece in self_gather.far]
    self_weights = self_gather.whole()
    cross_gather.send_fast(*self_gather.far)
    in_gather.send_slow(*self_gather.far)

    half = (2, part, width)
    grads_like = [
        (ANY, shape_of((slow,) + half, BF)),
        (ANY, shape_of((fast - 1, slow) + half, BF)),
        [(ANY, shape_of((slow,) + half, BF))]
        + [(ANY, shape_of((slow // 2,) + half, BF))] * (2 * fast - 2),
    ]

    def flat(dims, dtype):
        return (VMEM, shape_of(dims, dtype))

    def per_example(value):
        dims = value.shape[1:]
        spec = pl.BlockSpec((1,) + dims, lambda e: (e,) + (0,) * len(dims))
        return (spec, value)

    def slots_of_example(value):
        spec = pl.BlockSpec((mem, 1, slots, width), lambda e: (0, e, 0, 0))
        return (spec, value)

    def scratch(*dims):
        return pltpu.VMEM(dims, BF)

    def scatter(grads, *others, vectors=None):
        return Scatter(grads, slow, fast, *others, vectors=vectors)

    wide = (rows, width)
    square = scratch(4, width, width)
    own_rows = scratch(examples, length, width)
    x1, a1, qkv, p1, o1, vec = run(
        functools.partial(self_forward, group),
        [(SMEM, where), (ANY, suffix), Gather.refs(self_weights)],
        [
            flat(wide, F32),
            flat(wide, BF),
            flat((rows, 3 * width), BF),
            flat((rows // group * GROUPS, TOGETHER * group, group), BF),
            flat(wide, BF),
            flat((16, width), F32),
        ],
        [square, own_rows, scratch(fsdp, 16, 128)],
        1 + fsdp + blocks,
    )
    cross_gather.far = [after(piece, x1, *in_gather.came) for piece in cross_gather.far]
    cross_weights = Gather.refs(cross_gather.whole())
    in_gather.send_fast(*cross_gather.far)
    out_gather.send_slow(*cross_gather.far)
    x2, a2, q2, kv, p2, o2 = run(
        cross_forward,
        [(SMEM, where), (SMEM, counts), (VMEM, x1), (VMEM, vec)]
        + [slots_of_example(all_memory), cross_weights],
        [
            flat(wide, F32),
            flat(wide, BF),
            flat(wide, BF),
            per_example(shape_of((examples, total, 2 * width), BF)),
            per_example(shape_of((examples, GROUPS, TOGETHER * length, total), BF)),
            flat(wide, BF),
        ],
        [square],
        blocks,
        (examples,),
    )
    small = [after(piece, x1)[:, 2 * part + 7 : 2 * part + 11, :part] for piece in self_weights[0]]
    order = jnp.arange(fsdp) ^ f
    bias_in = jnp.take(jnp.concatenate(small), order % fast * slow + order // fast, axis=0)
    bias_in = bias_in.astype(F32).reshape(1, inner)
    in_gather.far = [after(piece, x2, *out_gather.came) for piece in in_gather.far]
    in_weights = Gather.refs(in_gather.whole())
    out_gather.send_fast(*in_gather.far)
    a3, h, slope, *grads = run(
        dense_inner,
        [(SMEM, where), (VMEM, x2), (VMEM, vec), (VMEM, bias_in), (ANY, cotangent), in_weights],
        [flat(wide, BF), flat((rows, inner), BF), flat((rows, inner), BF)] + grads_like,
        [square, scratch(fsdp, 4, part, width), own_rows],
        1 + blocks,
    )
    out_gather.far = [after(piece, a3) for piece in out_gather.far]
    out_weights = Gather.refs(out_gather.whole())
    out_scatter = scatter(grads, *out_gather.far)
    out_sum = out_scatter.add_cores()
    out_scatter.send_fast()
    y, du, vecs_y, bias_grad, *grads = run(
        dense_outer,
        [(SMEM, where), (VMEM, after(x2, *out_sum)), (VMEM, vec), (VMEM, a3), (VMEM, h)]
        + [(VMEM, slope), (ANY, cotangent), out_weights],
        [
            flat((examples, length, width), BF),
            flat((rows, inner), BF),
            flat((1, width), F32),
            flat((1, inner), F32),
        ]
        + grads_like,
        [scratch(fsdp, 4, part, width), square, own_rows],
        1 + blocks,
    )
    in_grads = grads
    gx2, vecs_dense = run(
        dense_back,
        [(SMEM, where), (VMEM, x2), (VMEM, vec), (VMEM, du), (ANY, cotangent), in_weights],
        [flat(wide, F32), flat((2, width), F32)],
        [square, own_rows],
        1 + blocks,
    )
    in_scatter = scatter(in_grads, gx2)
    in_sum = in_scatter.add_cores()
    in_scatter.send_fast()
    gx1, vecs_cross, dkv, dq2, grad_memory = run(
        cross_backward,
        [(SMEM, where), (VMEM, x1), (VMEM, vec), (VMEM, after(gx2, *in_sum)), (VMEM, q2)]
        + [per_example(kv), per_example(p2), cross_weights],
        [
            flat(wide, F32),
            flat((2, width), F32),
            per_example(shape_of((examples, total, 2 * width), BF)),
            flat(wide, BF),
            [per_example(shape_of((examples, slots, width), BF))] * mem,
        ],
        [square, scratch(*wide), scratch(total, width)],
        blocks,
        (examples,),
    )
    out_total = out_scatter.add_fast(gx1)
    out_scatter.send_slow()
    in_total = in_scatter.add_fast(gx1)
    mem_pieces = grad_memory[:1] + [swap(grad_memory[d], "mem", d) for d in range(1, mem)]
    grads = run(
        cross_grads,
        [(SMEM, where), (VMEM, after(gx2, out_total, in_total)), (VMEM, a2), (VMEM, o2), (VMEM, dq2)]
        + [(VMEM, dkv), (ANY, all_memory)],
        grads_like,
        [square, scratch(examples, total, width)],
        max(mem, blocks),
    )
    out_final = out_scatter.add_slow()
    in_scatter.total = after(in_scatter.total, out_final)
    in_scatter.send_slow()
    cross_scatter = scatter(grads, out_final, *mem_pieces[1:3])
    cross_sum = cross_scatter.add_cores()
    cross_scatter.send_fast()
    gx1 = after(gx1, *cross_sum)
    suffix_part, vecs_self, *grads = run(
        functools.partial(self_backward, group),
        [(SMEM, where), (ANY, suffix), (VMEM, vec), (VMEM, gx1), (VMEM, a1)]
        + [(VMEM, qkv), (VMEM, p1), (VMEM, o1)]
        + [[(VMEM, x) for x in (vecs_cross, vecs_dense, vecs_y, bias_grad)], Gather.refs(self_weights)],
        [flat((examples, length, width), BF), flat((16, width), BF)] + grads_like,
        [square, own_rows, square, scratch(rows, 3 * width), scratch(*wide)],
        1 + blocks,
    )
    self_scatter = scatter(grads, *mem_pieces[3:4], vectors=vecs_self)
    self_sum = self_scatter.add_cores()
    self_scatter.send_fast()
    cross_scatter.add_fast(*self_sum)
    cross_scatter.send_slow()
    in_final = in_scatter.add_slow(*self_sum)
    dense_sum = jnp.concatenate([out_final, in_final])
    dense_sum = Replicas(dense_sum, 2 * part, across)
    y_rows = spread_across(after(y, *self_sum), mem)
    self_total = self_scatter.add_fast(*dense_sum.halves, *y_rows)
    self_scatter.send_slow()
    cross_sum = Replicas(cross_scatter.add_slow(self_total), part, across)
    suffix_rows = spread_across(after(suffix_part, self_total), mem)
    y_rows = [after(value, self_total) for value in y_rows]
    y_far = swap(jnp.stack(y_rows), "mem", 1)
    dense_sum.swap_cores(self_total)
    mem_pieces = [after(value, self_total) for value in mem_pieces]
    (memory_grad,) = run(
        place_memory,
        [(SMEM, where), [(ANY, value) for value in mem_pieces]],
        [(ANY, shape_of(memory.shape, BF))],
        [scratch(mem, examples, slots, width)],
        2 * mem,
    )
    (out_low, in_low, out_high, in_high), _ = dense_sum.combine(c)
    grad_in = jnp.concatenate([in_low[:part], in_low[part:], in_high[:part], in_high[part:]], axis=1)
    grad_out = jnp.concatenate([out_low, out_high])
    done = [*cross_sum.halves, *suffix_rows, grad_in, grad_out, y_far, memory_grad]
    self_final = Replicas(self_scatter.add_slow(*done), part, across)
    cross_sum.swap_cores(self_final.halves[0])
    suffix_rows = [after(value, self_final.halves[0]) for value in suffix_rows]
    suffix_far = swap(jnp.stack(suffix_rows), "mem", 1)
    blocks = [([(ANY, x) for x in y_rows], (ANY, y_far))]
    blocks += [([(ANY, x) for x in suffix_rows], (ANY, suffix_far))]
    ((block_output, suffix_grad),) = run(
        place_rows,
        [(SMEM, where), blocks],
        [[(ANY, shape_of(suffix.shape, BF))] * 2],
        [scratch(2, mem, examples, length, width)],
        4 * mem,
    )
    grad_cross, _ = cross_sum.combine(c)
    self_final.swap_cores(block_output)
    grad_self, vectors = self_final.combine(c)

    def vector(i):
        return lax.dynamic_slice(vectors, (i, f * part), (1, part)).reshape(part)

    return (
        block_output,
        suffix_grad,
        memory_grad,
        vector(0),
        vector(1),
        *grad_self,
        vector(2),
        vector(3),
        *grad_cross,
        vector(4),
        vector(5),
        grad_in,
        lax.dynamic_slice_in_dim(vectors[7:11].reshape(-1), f * (inner // fsdp), inner // fsdp, 0),
        grad_out,
        vector(6),
    )


def solution(mesh):
    rows = P("fsdp", None, None)
    matrix = P("fsdp", None)
    vector = P("fsdp")
    attention = (vector, vector, matrix, matrix, matrix, matrix)
    params = attention + attention + (vector, vector, matrix, vector, matrix, vector)
    return jax.shard_map(
        per_device,
        mesh=mesh,
        in_specs=(rows, P("fsdp", "mem", None), vector, rows) + params,
        out_specs=(rows, rows, P("fsdp", "mem", None)) + params,
        check_vma=False,
    )
```

```python
import functools

import jax
import jax.numpy as jnp
from jax import lax
from jax.experimental import pallas as pl
from jax.experimental.pallas import tpu as pltpu
from jax.sharding import PartitionSpec as P

HEADS = 12
HEAD = 64
TOGETHER = 4
GROUPS = HEADS // TOGETHER
LANES = TOGETHER * HEAD
SCALE = HEAD ** (-0.5)
BF = jnp.bfloat16
F32 = jnp.float32
ANY = pl.BlockSpec(memory_space=pl.ANY)
SMEM = pl.BlockSpec(memory_space=pltpu.SMEM)
VMEM = pl.BlockSpec(memory_space=pltpu.VMEM)


def swap(value, axis, distance):
    size = lax.axis_size(axis)
    return lax.ppermute(value, axis, [(i, i ^ distance) for i in range(size)])


def after(value, *others):
    return lax.optimization_barrier((value, *others))[0] if others else value


def fsdp_split(size):
    slow = 4 if size % 4 == 0 else 1
    return slow, size // slow


def dot(left, right):
    return jnp.dot(left, right, preferred_element_type=F32)


def dot_nt(left, right):
    return lax.dot_general(left, right, (((1,), (1,)), ((), ())), preferred_element_type=F32)


def dot_tn(left, right):
    return lax.dot_general(left, right, (((0,), (0,)), ((), ())), preferred_element_type=F32)


def rows_of(start, size):
    return pl.ds(pl.multiple_of(start, 16), size)


def block(ref, by_rows, shard, which):
    if by_rows:
        return ref.at[shard, pl.ds(which * 2, 2)]
    rows = ref.shape[1] // SHARDS[0]
    return ref.at[pl.ds(which * 2, 2), rows_of(shard * rows, rows)]


SHARDS = [0]


class Copies:
    def __init__(self, sems):
        self.sems = sems
        self.next = 0

    def start(self, source, target):
        copy = pltpu.make_async_copy(source, target, self.sems.at[self.next])
        self.next += 1
        copy.start()
        return copy


def wait_all(copies):
    for copy in copies:
        copy.wait()


def load_weight(where, whole, weights, copies, by_rows=False):
    z, y, c = where[0], where[1], where[2]
    rows = whole.shape[2] if by_rows else whole.shape[1] // SHARDS[0]
    started = []
    for which, pieces in ((c, weights[0]), (1 - c, weights[1])):
        fast = len(pieces)
        for b, piece in enumerate(pieces):
            for k in range(piece.shape[0]):
                shard = (z ^ k) * fast + (y ^ b)
                for i in range(2):
                    source = piece.at[k, pl.ds(i * rows, rows)]
                    if by_rows:
                        target = whole.at[shard, 2 * which + i]
                    else:
                        target = whole.at[2 * which + i, rows_of(shard * rows, rows)]
                    started.append(copies.start(source, target))
    return started


def store_grad(where, whole, near, far, theirs, copies, by_rows=False):
    y, c = where[1], where[2]
    slow, cut = near.shape[0], near.shape[0] // 2
    fast = (len(theirs) + 1) // 2
    started = []
    for b in range(fast):
        for k in range(slow):
            shard = k * fast + (y ^ b)
            mine = far.at[b - 1, k] if b else near.at[k]
            other = theirs[2 * b - 1 + k // cut].at[k % cut] if b else theirs[0].at[k]
            started.append(copies.start(block(whole, by_rows, shard, 1 - c), other))
            started.append(copies.start(block(whole, by_rows, shard, c), mine))
    return started


def my_examples(where, source, target, copies):
    count = target.shape[0]
    return copies.start(source.at[pl.ds(where[3] * count, count)], target)


def normalise(values):
    centred = values - jnp.mean(values, axis=-1, keepdims=True)
    scale = lax.rsqrt(jnp.mean(centred * centred, axis=-1, keepdims=True) + 1e-06)
    return centred * scale, scale


def norm_back(grad, gain, hat, scale):
    inner = grad * gain
    mean = jnp.mean(inner, axis=-1, keepdims=True)
    along = jnp.mean(inner * hat, axis=-1, keepdims=True)
    return (
        scale * (inner - mean - hat * along),
        jnp.sum(grad * hat, axis=0, keepdims=True),
        jnp.sum(grad, axis=0, keepdims=True),
    )


def head_mask(rows):
    shape = (TOGETHER * rows, LANES)
    row = lax.broadcasted_iota(jnp.int32, shape, 0) // rows
    lane = lax.broadcasted_iota(jnp.int32, shape, 1) // HEAD
    return (row == lane).astype(F32)


def stack_heads(value, mask):
    return (jnp.concatenate([value] * TOGETHER, axis=0).astype(F32) * mask).astype(BF)


def merge_heads(value, mask):
    rows = value.shape[0] // TOGETHER
    value = value * mask
    total = value[:rows]
    for h in range(1, TOGETHER):
        total = total + value[h * rows : (h + 1) * rows]
    return total


def columns(j, width):
    return slice(j * width, (j + 1) * width)


def self_forward(
    group, where, suffix, weights, x1, a1, qkv, p1, o1, vec, weight, start, small, sems
):
    rows, width = x1.shape
    copies = Copies(sems)
    first = my_examples(where, suffix, start, copies)
    fast, slow = len(weights[0]), weights[0][0].shape[0]
    part = width // (fast * slow)
    vectors = []
    for b, piece in enumerate(weights[0]):
        for k in range(slow):
            source = piece.at[k, pl.ds(2 * part, 16), pl.ds(0, 128)]
            vectors.append(copies.start(source, small.at[b * slow + k]))
    loads = load_weight(where, weight, weights, copies)
    wait_all(vectors)
    lane = lax.broadcasted_iota(jnp.int32, (128, width), 0)
    place = lax.broadcasted_iota(jnp.int32, (128, width), 1) - lane
    together = jnp.zeros(vec.shape, F32)
    for i in range(fast * slow):
        shard = (where[0] ^ (i % slow)) * fast + (where[1] ^ (i // slow))
        chosen = ((place == shard * part) & (lane < part)).astype(F32).astype(BF)
        together = together + dot(small[i], chosen)
    vec[...] = together
    first.wait()
    values = start[...].reshape(rows, width).astype(F32)
    hat, _ = normalise(values)
    a1[...] = (hat * vec[0:1, :] + vec[1:2, :]).astype(BF)
    wait_all(loads)
    for j in range(3):
        qkv[:, columns(j, width)] = dot(a1[...], weight[j]).astype(BF)
    mask = head_mask(group)
    length = suffix.shape[1]
    shape = (TOGETHER * group, group)
    row = lax.broadcasted_iota(jnp.int32, shape, 0) % group
    col = lax.broadcasted_iota(jnp.int32, shape, 1)
    seen = (row // length == col // length) & (row >= col)
    for r in range(rows // group):
        here = columns(r, group)
        for g in range(GROUPS):
            lanes = [slice(i * width + g * LANES, i * width + (g + 1) * LANES) for i in range(3)]
            queries = stack_heads(qkv[here, lanes[0]], mask)
            scores = dot_nt(queries, qkv[here, lanes[1]]) * SCALE
            scores = jnp.where(seen, scores, -1e30)
            powers = jnp.exp(scores - jnp.max(scores, axis=-1, keepdims=True))
            probs = (powers / jnp.sum(powers, axis=-1, keepdims=True)).astype(BF)
            p1[r * GROUPS + g] = probs
            found = dot(probs, qkv[here, lanes[2]])
            o1[here, lanes[0]] = merge_heads(found, mask).astype(BF)
    x1[...] = values + dot(o1[...], weight[3])


def cross_forward(
    where, counts, x1, vec, memory, weights, x2, a2, q2, kv, p2, o2, weight, sems
):
    rows, width = x1.shape
    per = kv.shape[0]
    step = pl.program_id(0)
    total = kv.shape[1]
    length = p2.shape[2] // TOGETHER

    @pl.when(step == 0)
    def _():
        loads = load_weight(where, weight, weights, Copies(sems))
        hat, _ = normalise(x1[...])
        a2[...] = (hat * vec[2:3, :] + vec[3:4, :]).astype(BF)
        wait_all(loads)
        q2[...] = dot(a2[...], weight[0]).astype(BF)

    for i in range(per):
        tokens = memory[:, i].reshape(total, width)
        for j in range(2):
            kv[i, :, columns(j, width)] = dot(tokens, weight[1 + j]).astype(BF)
    mask = head_mask(length)
    position = lax.broadcasted_iota(jnp.int32, (1, total), 1)
    probs = {}
    for i in range(per):
        e = step * per + i
        valid = position < counts[where[3] * (pl.num_programs(0) * per) + e]
        here = rows_of(e * length, length)
        for g in range(GROUPS):
            lanes = columns(g, LANES)
            queries = stack_heads(q2[here, lanes], mask)
            scores = dot_nt(queries, kv[i, :, lanes]) * SCALE
            scores = jnp.where(valid, scores, -1e30)
            top = jnp.maximum(jnp.max(scores, axis=-1, keepdims=True), 0.0)
            powers = jnp.exp(scores - top)
            weight_sum = jnp.sum(powers, axis=-1, keepdims=True) + jnp.exp(-top)
            probs[i, g] = (powers / weight_sum).astype(BF)
    for i in range(per):
        here = rows_of((step * per + i) * length, length)
        for g in range(GROUPS):
            p2[i, g] = probs[i, g]
            found = dot(probs[i, g], kv[i, :, width + g * LANES : width + (g + 1) * LANES])
            o2[here, columns(g, LANES)] = merge_heads(found, mask).astype(BF)

    @pl.when(step == pl.num_programs(0) - 1)
    def _():
        x2[...] = x1[...] + dot(o2[...], weight[3])


def dense_inner(
    where, x2, vec, bias, cotangent, weights, a3, h, slope, near, far, theirs,
    weight, grad, cot, sems,
):
    rows, width = x2.shape
    copies = Copies(sems)
    cot_copy = my_examples(where, cotangent, cot, copies)
    loads = load_weight(where, weight, weights, copies)
    hat, _ = normalise(x2[...])
    a3[...] = (hat * vec[4:5, :] + vec[5:6, :]).astype(BF)
    cot_copy.wait()
    gy = cot[...].reshape(rows, width)
    wait_all(loads)
    flat = grad.shape[0] * grad.shape[1] * grad.shape[2]
    step = flat // grad.shape[0]
    for j in range(4):
        for half in range(2):
            cols = slice(j * width + half * 384, j * width + (half + 1) * 384)
            u = dot(a3[...], weight[j, :, half * 384 : (half + 1) * 384]) + bias[:, cols]
            square = u * u
            t = jnp.tanh(0.7978845608 * u * (1.0 + 0.044715 * square))
            h[:, cols] = (0.5 * u * (1.0 + t)).astype(BF)
            slope[:, cols] = (
                0.5 * (1.0 + t)
                + (0.5 * 0.7978845608) * u * (1.0 - t * t) * (1.0 + (3.0 * 0.044715) * square)
            ).astype(BF)
            part = dot_tn(h[:, cols], gy).astype(BF)
            per = 384 // step
            grad[cols.start // step : cols.start // step + per] = part.reshape(
                (per,) + grad.shape[1:]
            )
    wait_all(store_grad(where, grad, near, far, theirs, Copies(sems), True))


def dense_outer(
    where, x2, vec, a3, h, slope, cotangent, weights, y, du, vecs, bias_grad, near, far, theirs,
    weight, grad, cot, sems,
):
    rows, width = x2.shape
    copies = Copies(sems)
    cot_copy = my_examples(where, cotangent, cot, copies)
    wait_all(load_weight(where, weight, weights, copies, True))
    cot_copy.wait()
    gy = cot[...].reshape(rows, width)
    shards = weight.shape[0]
    step = weight.shape[1] * weight.shape[2]
    whole = weight[...].reshape(shards * step, width)
    for j in range(4):
        cols = columns(j, width)
        low = (dot_nt(gy, whole[cols]) * slope[:, cols].astype(F32)).astype(BF)
        du[:, cols] = low
        bias_grad[:, cols] = jnp.sum(low.astype(F32), axis=0, keepdims=True)
        grad[j] = dot_tn(a3[...], low).astype(BF)
    started = store_grad(where, grad, near, far, theirs, Copies(sems))
    result = x2[...] + dot(h[...], whole) + vec[6:7, :]
    y[...] = result.astype(BF).reshape(y.shape)
    vecs[...] = jnp.sum(gy.astype(F32), axis=0, keepdims=True)
    wait_all(started)


def dense_back(where, x2, vec, du, cotangent, weights, gx2, vecs, weight, cot, sems):
    rows, width = x2.shape
    copies = Copies(sems)
    cot_copy = my_examples(where, cotangent, cot, copies)
    loads = load_weight(where, weight, weights, copies)
    hat, scale = normalise(x2[...])
    cot_copy.wait()
    wait_all(loads)
    da3 = dot_nt(du[:, columns(0, width)], weight[0])
    for j in range(1, 4):
        da3 = da3 + dot_nt(du[:, columns(j, width)], weight[j])
    back, gain_grad, shift_grad = norm_back(da3, vec[4:5, :], hat, scale)
    gx2[...] = cot[...].reshape(rows, width).astype(F32) + back
    vecs[0:1, :] = gain_grad
    vecs[1:2, :] = shift_grad


def cross_backward(
    where, x1, vec, gx2, q2, kv, p2, weights, gx1, vecs, dkv, dq2, out_mem, weight, do2, moved, sems
):
    rows, width = x1.shape
    per, total = kv.shape[0], kv.shape[1]
    step = pl.program_id(0)
    length = p2.shape[2] // TOGETHER

    @pl.when(step == 0)
    def _():
        wait_all(load_weight(where, weight, weights, Copies(sems)))
        do2[...] = dot_nt(gx2[...].astype(BF), weight[3]).astype(BF)

    mask = head_mask(length)
    pairs = [(i, g) for i in range(per) for g in range(GROUPS)]
    queries, grads, dz = {}, {}, {}
    for i, g in pairs:
        here = rows_of((step * per + i) * length, length)
        lanes = columns(g, LANES)
        queries[i, g] = stack_heads(q2[here, lanes], mask)
        grads[i, g] = stack_heads(do2[here, lanes], mask)
        dp = dot_nt(grads[i, g], kv[i, :, width + g * LANES : width + (g + 1) * LANES])
        wide = p2[i, g].astype(F32)
        row_sum = jnp.sum(wide * dp, axis=-1, keepdims=True)
        dz[i, g] = (wide * (dp - row_sum)).astype(BF)
    for i, g in pairs:
        here = rows_of((step * per + i) * length, length)
        lanes = columns(g, LANES)
        value_lanes = slice(width + g * LANES, width + (g + 1) * LANES)
        dkv[i, :, value_lanes] = dot_tn(p2[i, g], grads[i, g]).astype(BF)
        dkv[i, :, lanes] = (dot_tn(dz[i, g], queries[i, g]) * SCALE).astype(BF)
        dq = merge_heads(dot(dz[i, g], kv[i, :, lanes]), mask) * SCALE
        dq2[here, lanes] = dq.astype(BF)
    for i in range(per):
        back = dot_nt(dkv[i, :, :width], weight[1]) + dot_nt(dkv[i, :, width:], weight[2])
        moved[i] = back.astype(BF)
        for d, out in enumerate(out_mem):
            slots = out.shape[1]
            out[i] = moved[i, rows_of((where[3] ^ d) * slots, slots), :]

    @pl.when(step == pl.num_programs(0) - 1)
    def _():
        hat, scale = normalise(x1[...])
        back, gain_grad, shift_grad = norm_back(
            dot_nt(dq2[...], weight[0]), vec[2:3, :], hat, scale
        )
        gx1[...] = gx2[...] + back
        vecs[0:1, :] = gain_grad
        vecs[1:2, :] = shift_grad


def cross_grads(
    where, gx2, a2, o2, dq2, dkv, all_memory, near, far, theirs, grad, turned, memory, sems
):
    rows, width = gx2.shape
    mem, examples, slots, _ = all_memory.shape
    half = pl.program_id(0)
    tokens = mem * examples * slots

    @pl.when(half == 0)
    def _():
        copies = Copies(sems)
        loads = [
            copies.start(all_memory.at[d], memory.at[:, d * slots : (d + 1) * slots, :])
            for d in range(mem)
        ]
        grad[0] = dot_tn(a2[...], dq2[...]).astype(BF)
        grad[3] = dot_tn(o2[...], gx2[...].astype(BF)).astype(BF)
        wait_all(loads)
        turned[...] = memory[...].reshape(tokens, width).T

    grad[1 + half] = dot(turned[...], dkv[...].reshape(tokens, width)).astype(BF)

    @pl.when(half == 1)
    def _():
        wait_all(store_grad(where, grad, near, far, theirs, Copies(sems)))


def self_backward(
    group, where, suffix, vec, gx1, a1, qkv, p1, o1, parts, weights, suffix_grad, vecs,
    near, far, theirs, weight, start, grad, dqkv, do1, sems,
):
    rows, width = gx1.shape
    copies = Copies(sems)
    start_copy = my_examples(where, suffix, start, copies)
    loads = load_weight(where, weight, weights, copies)
    gs = gx1[...].astype(BF)
    grad[3] = dot_tn(o1[...], gs).astype(BF)
    wait_all(loads)
    do1[...] = dot_nt(gs, weight[3]).astype(BF)
    mask = head_mask(group)
    for r in range(rows // group):
        here = columns(r, group)
        for g in range(GROUPS):
            lanes = [slice(i * width + g * LANES, i * width + (g + 1) * LANES) for i in range(3)]
            queries = stack_heads(qkv[here, lanes[0]], mask)
            grads = stack_heads(do1[here, lanes[0]], mask)
            probs = p1[r * GROUPS + g]
            dp = dot_nt(grads, qkv[here, lanes[2]])
            wide = probs.astype(F32)
            row_sum = jnp.sum(wide * dp, axis=-1, keepdims=True)
            dz = (wide * (dp - row_sum)).astype(BF)
            dqkv[here, lanes[2]] = dot_tn(probs, grads).astype(BF)
            dqkv[here, lanes[1]] = (dot_tn(dz, queries) * SCALE).astype(BF)
            dq = merge_heads(dot(dz, qkv[here, lanes[1]]), mask) * SCALE
            dqkv[here, lanes[0]] = dq.astype(BF)
    for j in range(3):
        grad[j] = dot_tn(a1[...], dqkv[:, columns(j, width)]).astype(BF)
    start_copy.wait()
    started = store_grad(where, grad, near, far, theirs, Copies(sems))
    da1 = dot_nt(dqkv[:, columns(0, width)], weight[0])
    for j in range(1, 3):
        da1 = da1 + dot_nt(dqkv[:, columns(j, width)], weight[j])
    hat, scale = normalise(start[...].reshape(rows, width).astype(F32))
    back, gain_grad, shift_grad = norm_back(da1, vec[0:1, :], hat, scale)
    suffix_grad[...] = (gx1[...] + back).astype(BF).reshape(suffix_grad.shape)
    found = [gain_grad, shift_grad]
    for ref in parts:
        for r in range(ref.shape[0]):
            found += [ref[r : r + 1, columns(j, width)] for j in range(ref.shape[1] // width)]
    found.append(jnp.zeros((vecs.shape[0] - len(found), width), F32))
    vecs[...] = jnp.concatenate(found, axis=0).astype(BF)
    wait_all(started)


def run(kernel, inputs, outputs, scratch, copies, grid=()):
    def leaf(x):
        return isinstance(x, tuple) and len(x) == 2 and isinstance(x[0], pl.BlockSpec)

    flat_in, tree_in = jax.tree.flatten(inputs, is_leaf=leaf)
    flat_out, tree_out = jax.tree.flatten(outputs, is_leaf=leaf)

    def body(*refs):
        first, second = len(flat_in), len(flat_in) + len(flat_out)
        given = jax.tree.unflatten(tree_in, refs[:first])
        taken = jax.tree.unflatten(tree_out, refs[first:second])
        kernel(*given, *taken, *refs[second:])

    found = pl.pallas_call(
        body,
        grid=grid,
        in_specs=[spec for spec, _ in flat_in],
        out_specs=[spec for spec, _ in flat_out],
        out_shape=[shape for _, shape in flat_out],
        scratch_shapes=scratch + [pltpu.SemaphoreType.DMA((copies,))],
        compiler_params=pltpu.CompilerParams(vmem_limit_bytes=56 * 1024 * 1024),
        cost_estimate=pl.CostEstimate(
            flops=0, bytes_accessed=0, transcendentals=0
        ),
    )(*[x for _, x in flat_in])
    return jax.tree.unflatten(tree_out, found)


def shape_of(dims, dtype):
    return jax.ShapeDtypeStruct(tuple(dims), dtype)


def over_slow(value, slow, fast):
    groups = [[k * fast + b for k in range(slow)] for b in range(fast)]
    return lax.all_to_all(value, "fsdp", 0, 0, axis_index_groups=groups, tiled=True)


class Gather:
    def __init__(self, half, slow, fast):
        self.half, self.slow, self.fast = half, slow, fast

    def send_slow(self, *others):
        half = after(self.half, *others)
        self.came = [half] + [swap(half, "fsdp", k * self.fast) for k in range(1, self.slow)]

    def send_fast(self, *others):
        self.near = jnp.stack([after(piece, *others) for piece in self.came])
        self.near_other = swap(self.near, "mem", 1)
        self.far = [swap(self.near, "fsdp", b) for b in range(1, self.fast)]

    def whole(self):
        mine = [self.near] + self.far
        theirs = [self.near_other] + [swap(piece, "mem", 1) for piece in self.far]
        return mine, theirs

    @staticmethod
    def refs(weights):
        return [[(ANY, x) for x in some] for some in weights]


class Scatter:
    def __init__(self, grads, slow, fast, *others, vectors=None):
        self.near, self.far, theirs = grads
        self.slow, self.fast, self.vectors = slow, fast, vectors
        theirs = [after(part, *others) for part in theirs]
        far = [swap(part, "mem", 1) for part in theirs[1:]]
        far = [jnp.concatenate(far[2 * b : 2 * b + 2]) for b in range(fast - 1)]
        self.sent = [swap(theirs[0], "mem", 1)] + far
        if vectors is not None:
            self.vectors = vectors.astype(F32) + swap(vectors, "mem", 1).astype(F32)

    def add_cores(self):
        self.out = [
            (self.far[b].astype(F32) + self.sent[b + 1].astype(F32)).astype(BF)
            for b in range(self.fast - 1)
        ]
        return self.out

    def send_fast(self):
        self.came = [swap(part, "fsdp", b + 1) for b, part in enumerate(self.out)]
        if self.vectors is not None:
            low = self.vectors.astype(BF)
            self.vectors = [low] + [swap(low, "fsdp", b) for b in range(1, self.fast)]

    def add_fast(self, *others):
        if self.vectors is not None:
            self.vectors, self.came = lax.optimization_barrier((self.vectors, self.came))
            self.vectors = sum(part.astype(F32) for part in self.vectors)
        total = after(self.near, *others).astype(F32) + self.sent[0].astype(F32)
        for part in self.came:
            total = total + part.astype(F32)
        self.total = total.astype(BF).reshape(self.slow, -1, total.shape[-1])
        if self.vectors is not None:
            low = self.vectors.astype(BF)
            low = jnp.broadcast_to(low, (self.slow,) + low.shape)
            self.total = jnp.concatenate([self.total, low], axis=1)
        return self.total

    def send_slow(self):
        self.came = over_slow(self.total, self.slow, self.fast)

    def add_slow(self, *others):
        return jnp.sum(after(self.came, *others).astype(F32), axis=0)


class Replicas:
    def __init__(self, value, rows, across):
        self.rows = rows
        k = 1
        while 2 * k < across:
            low = value.astype(BF)
            value = low.astype(F32) + swap(low, "mem", 2 * k).astype(F32)
            k *= 2
        low = value.astype(BF)
        self.halves = [low, swap(low, "mem", 2 * k)] if across > 1 else [low]

    def swap_cores(self, *others):
        halves, _ = lax.optimization_barrier((self.halves, others))
        self.others = [swap(half[: 2 * self.rows], "mem", 1) for half in halves]

    def combine(self, c):
        rows = self.rows
        other = sum(half.astype(F32) for half in self.others)
        mine = sum(half.astype(F32) for half in self.halves)
        vectors, mine = mine[2 * rows :], mine[: 2 * rows]
        first = jnp.where(c == 0, mine, other)
        second = jnp.where(c == 0, other, mine)
        return [first[:rows], first[rows:], second[:rows], second[rows:]], vectors


def place_rows(where, blocks, outs, scratch, sems):
    copies = Copies(sems)
    loads = []
    for i, (even, odd) in enumerate(blocks):
        for d, piece in enumerate(even):
            loads.append((copies.start(piece, scratch.at[i, 2 * d]), i, 2 * d))
            loads.append((copies.start(odd.at[d], scratch.at[i, 2 * d + 1]), i, 2 * d + 1))
    examples = scratch.shape[2]
    stores = []
    for load, i, d in loads:
        load.wait()
        target = outs[i].at[pl.ds((where[3] ^ d) * examples, examples)]
        stores.append(copies.start(scratch.at[i, d], target))
    wait_all(stores)


def place_memory(where, pieces, out, scratch, sems):
    examples = pieces[0].shape[0]
    copies = Copies(sems)
    loads = [copies.start(piece, scratch.at[d]) for d, piece in enumerate(pieces)]
    stores = []
    for d, load in enumerate(loads):
        load.wait()
        target = out.at[pl.ds((where[3] ^ d) * examples, examples)]
        stores.append(copies.start(scratch.at[d], target))
    wait_all(stores)


def spread_across(value, mem):
    return [value] + [swap(value, "mem", d) for d in range(2, mem, 2)]


def per_device(
    suffix,
    memory,
    counts,
    cotangent,
    self_norm_gain,
    self_norm_bias,
    self_query,
    self_key,
    self_value,
    self_output,
    cross_norm_gain,
    cross_norm_bias,
    cross_query,
    cross_key,
    cross_value,
    cross_output,
    dense_norm_gain,
    dense_norm_bias,
    dense_in,
    dense_in_bias,
    dense_out,
    dense_out_bias,
):
    f = lax.axis_index("fsdp")
    m = lax.axis_index("mem")
    c = m % 2
    fsdp = lax.axis_size("fsdp")
    mem = lax.axis_size("mem")
    across = mem // 2
    slow, fast = fsdp_split(fsdp)
    SHARDS[0] = fsdp
    where = jnp.stack([f // fast, f % fast, c, m]).astype(jnp.int32)
    examples = suffix.shape[0] // mem
    length = suffix.shape[1]
    width = suffix.shape[2]
    slots = memory.shape[1]
    total = mem * slots
    rows = examples * length
    inner = dense_in.shape[1]
    part = width // fsdp
    group = min(128, rows)
    blocks = 4 * fsdp

    def gather(matrices, *others):
        halves = [jnp.concatenate(matrices[:2]), jnp.concatenate(matrices[2:])]
        half = jnp.concatenate([jnp.where(c == 0, *halves), *others])
        return Gather(half, slow, fast)

    cross_gather = gather([cross_query, cross_key, cross_value, cross_output])
    in_gather = gather([dense_in[:, columns(j, width)] for j in range(4)])
    out_gather = gather([dense_out[columns(j, part)] for j in range(4)])
    small = [
        self_norm_gain,
        self_norm_bias,
        cross_norm_gain,
        cross_norm_bias,
        dense_norm_gain,
        dense_norm_bias,
        dense_out_bias,
    ]
    small += [dense_in_bias[columns(j, part)] for j in range(4)]
    small = sum(
        jnp.pad(value[None], ((i, 15 - i), (0, width - part))) for i, value in enumerate(small)
    )
    self_gather = gather([self_query, self_key, self_value, self_output], small)

    def exchange(value):
        blocks = value.reshape((mem, examples) + value.shape[1:])
        return lax.all_to_all(blocks, "mem", 0, 0, tiled=True)

    all_memory = exchange(memory)
    self_gather.send_slow()
    sent = self_gather.came
    self_gather.send_fast(*sent)
    cross_gather.send_slow(*sent)
    sent = [*self_gather.far, *cross_gather.came, all_memory]
    self_gather.far = [after(piece, *sent) for piece in self_gather.far]
    self_weights = self_gather.whole()
    cross_gather.send_fast(*self_gather.far)
    in_gather.send_slow(*self_gather.far)

    half = (2, part, width)
    grads_like = [
        (ANY, shape_of((slow,) + half, BF)),
        (ANY, shape_of((fast - 1, slow) + half, BF)),
        [(ANY, shape_of((slow,) + half, BF))]
        + [(ANY, shape_of((slow // 2,) + half, BF))] * (2 * fast - 2),
    ]

    def flat(dims, dtype):
        return (VMEM, shape_of(dims, dtype))

    per = 2 if examples % 2 == 0 else 1

    def per_example(value):
        dims = value.shape[1:]
        spec = pl.BlockSpec((per,) + dims, lambda e: (e,) + (0,) * len(dims))
        return (spec, value)

    def slots_of_example(value):
        spec = pl.BlockSpec((mem, per, slots, width), lambda e: (0, e, 0, 0))
        return (spec, value)

    def scratch(*dims):
        return pltpu.VMEM(dims, BF)

    def scatter(grads, *others, vectors=None):
        return Scatter(grads, slow, fast, *others, vectors=vectors)

    wide = (rows, width)
    square = scratch(4, width, width)
    own_rows = scratch(examples, length, width)
    x1, a1, qkv, p1, o1, vec = run(
        functools.partial(self_forward, group),
        [(SMEM, where), (ANY, suffix), Gather.refs(self_weights)],
        [
            flat(wide, F32),
            flat(wide, BF),
            flat((rows, 3 * width), BF),
            flat((rows // group * GROUPS, TOGETHER * group, group), BF),
            flat(wide, BF),
            flat((16, width), F32),
        ],
        [square, own_rows, scratch(fsdp, 16, 128)],
        1 + fsdp + blocks,
    )
    cross_gather.far = [after(piece, x1, *in_gather.came) for piece in cross_gather.far]
    cross_weights = Gather.refs(cross_gather.whole())
    in_gather.send_fast(*cross_gather.far)
    out_gather.send_slow(*cross_gather.far)
    x2, a2, q2, kv, p2, o2 = run(
        cross_forward,
        [(SMEM, where), (SMEM, counts), (VMEM, x1), (VMEM, vec)]
        + [slots_of_example(all_memory), cross_weights],
        [
            flat(wide, F32),
            flat(wide, BF),
            flat(wide, BF),
            per_example(shape_of((examples, total, 2 * width), BF)),
            per_example(shape_of((examples, GROUPS, TOGETHER * length, total), BF)),
            flat(wide, BF),
        ],
        [square],
        blocks,
        (examples // per,),
    )
    small = [after(piece, x1)[:, 2 * part + 7 : 2 * part + 11, :part] for piece in self_weights[0]]
    order = jnp.arange(fsdp) ^ f
    bias_in = jnp.take(jnp.concatenate(small), order % fast * slow + order // fast, axis=0)
    bias_in = bias_in.astype(F32).reshape(1, inner)
    in_gather.far = [after(piece, x2, *out_gather.came) for piece in in_gather.far]
    in_weights = Gather.refs(in_gather.whole())
    out_gather.send_fast(*in_gather.far)
    a3, h, slope, *grads = run(
        dense_inner,
        [(SMEM, where), (VMEM, x2), (VMEM, vec), (VMEM, bias_in), (ANY, cotangent), in_weights],
        [flat(wide, BF), flat((rows, inner), BF), flat((rows, inner), BF)] + grads_like,
        [square, scratch(fsdp, 4, part, width), own_rows],
        1 + blocks,
    )
    out_gather.far = [after(piece, a3) for piece in out_gather.far]
    out_weights = Gather.refs(out_gather.whole())
    out_scatter = scatter(grads, *out_gather.far)
    out_sum = out_scatter.add_cores()
    out_scatter.send_fast()
    y, du, vecs_y, bias_grad, *grads = run(
        dense_outer,
        [(SMEM, where), (VMEM, after(x2, *out_sum)), (VMEM, vec), (VMEM, a3), (VMEM, h)]
        + [(VMEM, slope), (ANY, cotangent), out_weights],
        [
            flat((examples, length, width), BF),
            flat((rows, inner), BF),
            flat((1, width), F32),
            flat((1, inner), F32),
        ]
        + grads_like,
        [scratch(fsdp, 4, part, width), square, own_rows],
        1 + blocks,
    )
    in_grads = grads
    gx2, vecs_dense = run(
        dense_back,
        [(SMEM, where), (VMEM, x2), (VMEM, vec), (VMEM, du), (ANY, cotangent), in_weights],
        [flat(wide, F32), flat((2, width), F32)],
        [square, own_rows],
        1 + blocks,
    )
    in_scatter = scatter(in_grads, gx2)
    in_sum = in_scatter.add_cores()
    in_scatter.send_fast()
    gx1, vecs_cross, dkv, dq2, grad_memory = run(
        cross_backward,
        [(SMEM, where), (VMEM, x1), (VMEM, vec), (VMEM, after(gx2, *in_sum, *out_scatter.came)), (VMEM, q2)]
        + [per_example(kv), per_example(p2), cross_weights],
        [
            flat(wide, F32),
            flat((2, width), F32),
            per_example(shape_of((examples, total, 2 * width), BF)),
            flat(wide, BF),
            [per_example(shape_of((examples, slots, width), BF))] * mem,
        ],
        [square, scratch(*wide), scratch(per, total, width)],
        blocks,
        (examples // per,),
    )
    in_scatter.came, _ = lax.optimization_barrier((in_scatter.came, gx1))
    out_total = out_scatter.add_fast(gx1)
    out_scatter.send_slow()
    mem_pieces = grad_memory[:1] + [swap(grad_memory[d], "mem", d) for d in range(1, mem)]
    grads = run(
        cross_grads,
        [(SMEM, where), (VMEM, after(gx2, out_total, *in_scatter.came)), (VMEM, a2), (VMEM, o2), (VMEM, dq2)]
        + [(pl.BlockSpec((examples, total, width), lambda j: (0, 0, j)), dkv), (ANY, all_memory)],
        grads_like,
        [square, scratch(width, examples * total), scratch(examples, total, width)],
        max(mem, blocks),
        (2,),
    )
    out_final = out_scatter.add_slow()
    in_scatter.add_fast(out_final)
    in_scatter.send_slow()
    cross_scatter = scatter(grads, out_final)
    cross_sum = cross_scatter.add_cores()
    cross_scatter.send_fast()
    gx1 = after(gx1, *cross_sum)
    suffix_part, vecs_self, *grads = run(
        functools.partial(self_backward, group),
        [(SMEM, where), (ANY, suffix), (VMEM, vec), (VMEM, gx1), (VMEM, a1)]
        + [(VMEM, qkv), (VMEM, p1), (VMEM, o1)]
        + [[(VMEM, x) for x in (vecs_cross, vecs_dense, vecs_y, bias_grad)], Gather.refs(self_weights)],
        [flat((examples, length, width), BF), flat((16, width), BF)] + grads_like,
        [square, own_rows, square, scratch(rows, 3 * width), scratch(*wide)],
        1 + blocks,
    )
    self_scatter = scatter(grads, *mem_pieces[1:3], vectors=vecs_self)
    self_sum = self_scatter.add_cores()
    self_scatter.send_fast()
    cross_scatter.add_fast(*self_sum)
    cross_scatter.send_slow()
    in_final = in_scatter.add_slow(*self_sum)
    dense_sum = jnp.concatenate([out_final, in_final])
    dense_sum = Replicas(dense_sum, 2 * part, across)
    self_total = self_scatter.add_fast(*dense_sum.halves, *mem_pieces[3:])
    self_scatter.send_slow()
    cross_sum = Replicas(cross_scatter.add_slow(self_total), part, across)
    suffix_rows = spread_across(after(suffix_part, self_total), mem)
    y_rows = spread_across(after(y, self_total), mem)
    dense_sum.swap_cores(self_total)
    mem_pieces = [after(value, self_total) for value in mem_pieces]
    (memory_grad,) = run(
        place_memory,
        [(SMEM, where), [(ANY, value) for value in mem_pieces]],
        [(ANY, shape_of(memory.shape, BF))],
        [scratch(mem, examples, slots, width)],
        2 * mem,
    )
    (out_low, in_low, out_high, in_high), _ = dense_sum.combine(c)
    grad_in = jnp.concatenate([in_low[:part], in_low[part:], in_high[:part], in_high[part:]], axis=1)
    grad_out = jnp.concatenate([out_low, out_high])
    done = [*cross_sum.halves, *suffix_rows, *y_rows, grad_in, grad_out, memory_grad]
    self_final = Replicas(self_scatter.add_slow(*done), part, across)
    cross_sum.swap_cores(self_final.halves[0])
    y_rows = [after(value, self_final.halves[0]) for value in y_rows]
    y_far = swap(jnp.stack(y_rows), "mem", 1)
    suffix_rows = [after(value, self_final.halves[0]) for value in suffix_rows]
    suffix_far = swap(jnp.stack(suffix_rows), "mem", 1)
    blocks = [([(ANY, x) for x in y_rows], (ANY, y_far))]
    blocks += [([(ANY, x) for x in suffix_rows], (ANY, suffix_far))]
    ((block_output, suffix_grad),) = run(
        place_rows,
        [(SMEM, where), blocks],
        [[(ANY, shape_of(suffix.shape, BF))] * 2],
        [scratch(2, mem, examples, length, width)],
        4 * mem,
    )
    grad_cross, _ = cross_sum.combine(c)
    self_final.swap_cores(block_output)
    grad_self, vectors = self_final.combine(c)

    def vector(i):
        return lax.dynamic_slice(vectors, (i, f * part), (1, part)).reshape(part)

    return (
        block_output,
        suffix_grad,
        memory_grad,
        vector(0),
        vector(1),
        *grad_self,
        vector(2),
        vector(3),
        *grad_cross,
        vector(4),
        vector(5),
        grad_in,
        lax.dynamic_slice_in_dim(vectors[7:11].reshape(-1), f * (inner // fsdp), inner // fsdp, 0),
        grad_out,
        vector(6),
    )


def solution(mesh):
    rows = P("fsdp", None, None)
    matrix = P("fsdp", None)
    vector = P("fsdp")
    attention = (vector, vector, matrix, matrix, matrix, matrix)
    params = attention + attention + (vector, vector, matrix, vector, matrix, vector)
    return jax.shard_map(
        per_device,
        mesh=mesh,
        in_specs=(rows, P("fsdp", "mem", None), vector, rows) + params,
        out_specs=(rows, rows, P("fsdp", "mem", None)) + params,
        check_vma=False,
    )
```

```python
import functools

import jax
import jax.numpy as jnp
from jax import lax
from jax.experimental import pallas as pl
from jax.experimental.pallas import tpu as pltpu
from jax.sharding import PartitionSpec as P

HEADS = 12
HEAD = 64
TOGETHER = 4
GROUPS = HEADS // TOGETHER
LANES = TOGETHER * HEAD
SCALE = HEAD ** (-0.5)
BF = jnp.bfloat16
F32 = jnp.float32
ANY = pl.BlockSpec(memory_space=pl.ANY)
SMEM = pl.BlockSpec(memory_space=pltpu.SMEM)
VMEM = pl.BlockSpec(memory_space=pltpu.VMEM)


def swap(value, axis, distance):
    size = lax.axis_size(axis)
    return lax.ppermute(value, axis, [(i, i ^ distance) for i in range(size)])


def after(value, *others):
    return lax.optimization_barrier((value, *others))[0] if others else value


def fsdp_split(size):
    slow = 4 if size % 4 == 0 else 1
    return slow, size // slow


def dot(left, right):
    return jnp.dot(left, right, preferred_element_type=F32)


def dot_nt(left, right):
    return lax.dot_general(left, right, (((1,), (1,)), ((), ())), preferred_element_type=F32)


def dot_tn(left, right):
    return lax.dot_general(left, right, (((0,), (0,)), ((), ())), preferred_element_type=F32)


def rows_of(start, size):
    return pl.ds(pl.multiple_of(start, 16), size)


def block(ref, by_rows, shard, which):
    if by_rows:
        return ref.at[shard, pl.ds(which * 2, 2)]
    rows = ref.shape[1] // SHARDS[0]
    return ref.at[pl.ds(which * 2, 2), rows_of(shard * rows, rows)]


SHARDS = [0]


class Copies:
    def __init__(self, sems):
        self.sems = sems
        self.next = 0

    def start(self, source, target):
        copy = pltpu.make_async_copy(source, target, self.sems.at[self.next])
        self.next += 1
        copy.start()
        return copy


def wait_all(copies):
    for copy in copies:
        copy.wait()


def load_weight(where, whole, weights, copies, by_rows=False):
    z, y, c = where[0], where[1], where[2]
    rows = whole.shape[2] if by_rows else whole.shape[1] // SHARDS[0]
    started = []
    for which, pieces in ((c, weights[0]), (1 - c, weights[1])):
        fast = len(pieces)
        for b, piece in enumerate(pieces):
            for k in range(piece.shape[0]):
                shard = (z ^ k) * fast + (y ^ b)
                for i in range(2):
                    source = piece.at[k, pl.ds(i * rows, rows)]
                    if by_rows:
                        target = whole.at[shard, 2 * which + i]
                    else:
                        target = whole.at[2 * which + i, rows_of(shard * rows, rows)]
                    started.append(copies.start(source, target))
    return started


def store_grad(where, whole, near, far, theirs, copies, by_rows=False):
    y, c = where[1], where[2]
    slow, cut = near.shape[0], near.shape[0] // 2
    fast = (len(theirs) + 1) // 2
    started = []
    for b in range(fast):
        for k in range(slow):
            shard = k * fast + (y ^ b)
            mine = far.at[b - 1, k] if b else near.at[k]
            other = theirs[2 * b - 1 + k // cut].at[k % cut] if b else theirs[0].at[k]
            started.append(copies.start(block(whole, by_rows, shard, 1 - c), other))
            started.append(copies.start(block(whole, by_rows, shard, c), mine))
    return started


def my_examples(where, source, target, copies):
    count = target.shape[0]
    return copies.start(source.at[pl.ds(where[3] * count, count)], target)


def normalise(values):
    centred = values - jnp.mean(values, axis=-1, keepdims=True)
    scale = lax.rsqrt(jnp.mean(centred * centred, axis=-1, keepdims=True) + 1e-06)
    return centred * scale, scale


def norm_back(grad, gain, hat, scale):
    inner = grad * gain
    mean = jnp.mean(inner, axis=-1, keepdims=True)
    along = jnp.mean(inner * hat, axis=-1, keepdims=True)
    return (
        scale * (inner - mean - hat * along),
        jnp.sum(grad * hat, axis=0, keepdims=True),
        jnp.sum(grad, axis=0, keepdims=True),
    )


def head_mask(rows):
    shape = (TOGETHER * rows, LANES)
    row = lax.broadcasted_iota(jnp.int32, shape, 0) // rows
    lane = lax.broadcasted_iota(jnp.int32, shape, 1) // HEAD
    return (row == lane).astype(F32)


def stack_heads(value, mask):
    return (jnp.concatenate([value] * TOGETHER, axis=0).astype(F32) * mask).astype(BF)


def merge_heads(value, mask):
    rows = value.shape[0] // TOGETHER
    value = value * mask
    total = value[:rows]
    for h in range(1, TOGETHER):
        total = total + value[h * rows : (h + 1) * rows]
    return total


def columns(j, width):
    return slice(j * width, (j + 1) * width)


def self_forward(
    group, where, suffix, weights, x1, a1, qkv, p1, o1, vec, weight, start, small, sems
):
    rows, width = x1.shape
    copies = Copies(sems)
    first = my_examples(where, suffix, start, copies)
    fast, slow = len(weights[0]), weights[0][0].shape[0]
    part = width // (fast * slow)
    vectors = []
    for b, piece in enumerate(weights[0]):
        for k in range(slow):
            source = piece.at[k, pl.ds(2 * part, 16), pl.ds(0, 128)]
            vectors.append(copies.start(source, small.at[b * slow + k]))
    loads = load_weight(where, weight, weights, copies)
    wait_all(vectors)
    lane = lax.broadcasted_iota(jnp.int32, (128, width), 0)
    place = lax.broadcasted_iota(jnp.int32, (128, width), 1) - lane
    together = jnp.zeros(vec.shape, F32)
    for i in range(fast * slow):
        shard = (where[0] ^ (i % slow)) * fast + (where[1] ^ (i // slow))
        chosen = ((place == shard * part) & (lane < part)).astype(F32).astype(BF)
        together = together + dot(small[i], chosen)
    vec[...] = together
    first.wait()
    values = start[...].reshape(rows, width).astype(F32)
    hat, _ = normalise(values)
    a1[...] = (hat * vec[0:1, :] + vec[1:2, :]).astype(BF)
    wait_all(loads)
    for j in range(3):
        qkv[:, columns(j, width)] = dot(a1[...], weight[j]).astype(BF)
    mask = head_mask(group)
    length = suffix.shape[1]
    shape = (TOGETHER * group, group)
    row = lax.broadcasted_iota(jnp.int32, shape, 0) % group
    col = lax.broadcasted_iota(jnp.int32, shape, 1)
    seen = (row // length == col // length) & (row >= col)
    for r in range(rows // group):
        here = columns(r, group)
        for g in range(GROUPS):
            lanes = [slice(i * width + g * LANES, i * width + (g + 1) * LANES) for i in range(3)]
            queries = stack_heads(qkv[here, lanes[0]], mask)
            scores = dot_nt(queries, qkv[here, lanes[1]]) * SCALE
            scores = jnp.where(seen, scores, -1e30)
            powers = jnp.exp(scores - jnp.max(scores, axis=-1, keepdims=True))
            probs = (powers / jnp.sum(powers, axis=-1, keepdims=True)).astype(BF)
            p1[r * GROUPS + g] = probs
            found = dot(probs, qkv[here, lanes[2]])
            o1[here, lanes[0]] = merge_heads(found, mask).astype(BF)
    x1[...] = values + dot(o1[...], weight[3])


def cross_forward(
    where, counts, x1, vec, memory, weights, x2, a2, q2, kv, p2, o2, weight, sems
):
    rows, width = x1.shape
    per = kv.shape[0]
    step = pl.program_id(0)
    total = kv.shape[1]
    length = p2.shape[2] // TOGETHER

    @pl.when(step == 0)
    def _():
        loads = load_weight(where, weight, weights, Copies(sems))
        hat, _ = normalise(x1[...])
        a2[...] = (hat * vec[2:3, :] + vec[3:4, :]).astype(BF)
        wait_all(loads)
        q2[...] = dot(a2[...], weight[0]).astype(BF)

    for i in range(per):
        tokens = memory[:, i].reshape(total, width)
        for j in range(2):
            kv[i, :, columns(j, width)] = dot(tokens, weight[1 + j]).astype(BF)
    mask = head_mask(length)
    position = lax.broadcasted_iota(jnp.int32, (1, total), 1)
    probs = {}
    for i in range(per):
        e = step * per + i
        valid = position < counts[where[3] * (pl.num_programs(0) * per) + e]
        here = rows_of(e * length, length)
        for g in range(GROUPS):
            lanes = columns(g, LANES)
            queries = stack_heads(q2[here, lanes], mask)
            scores = dot_nt(queries, kv[i, :, lanes]) * SCALE
            scores = jnp.where(valid, scores, -1e30)
            top = jnp.maximum(jnp.max(scores, axis=-1, keepdims=True), 0.0)
            powers = jnp.exp(scores - top)
            weight_sum = jnp.sum(powers, axis=-1, keepdims=True) + jnp.exp(-top)
            probs[i, g] = (powers / weight_sum).astype(BF)
    for i in range(per):
        here = rows_of((step * per + i) * length, length)
        for g in range(GROUPS):
            p2[i, g] = probs[i, g]
            found = dot(probs[i, g], kv[i, :, width + g * LANES : width + (g + 1) * LANES])
            o2[here, columns(g, LANES)] = merge_heads(found, mask).astype(BF)

    @pl.when(step == pl.num_programs(0) - 1)
    def _():
        x2[...] = x1[...] + dot(o2[...], weight[3])


def dense_inner(
    where, x2, vec, bias, cotangent, weights, a3, h, slope, near, far, theirs,
    weight, grad, cot, sems,
):
    rows, width = x2.shape
    copies = Copies(sems)
    cot_copy = my_examples(where, cotangent, cot, copies)
    loads = load_weight(where, weight, weights, copies)
    hat, _ = normalise(x2[...])
    a3[...] = (hat * vec[4:5, :] + vec[5:6, :]).astype(BF)
    cot_copy.wait()
    gy = cot[...].reshape(rows, width)
    wait_all(loads)
    flat = grad.shape[0] * grad.shape[1] * grad.shape[2]
    step = flat // grad.shape[0]
    for j in range(4):
        for half in range(2):
            cols = slice(j * width + half * 384, j * width + (half + 1) * 384)
            u = dot(a3[...], weight[j, :, half * 384 : (half + 1) * 384]) + bias[:, cols]
            square = u * u
            t = jnp.tanh(0.7978845608 * u * (1.0 + 0.044715 * square))
            h[:, cols] = (0.5 * u * (1.0 + t)).astype(BF)
            slope[:, cols] = (
                0.5 * (1.0 + t)
                + (0.5 * 0.7978845608) * u * (1.0 - t * t) * (1.0 + (3.0 * 0.044715) * square)
            ).astype(BF)
            part = dot_tn(h[:, cols], gy).astype(BF)
            per = 384 // step
            grad[cols.start // step : cols.start // step + per] = part.reshape(
                (per,) + grad.shape[1:]
            )
    wait_all(store_grad(where, grad, near, far, theirs, Copies(sems), True))


def dense_outer(
    where, x2, vec, a3, h, slope, cotangent, weights, y, du, vecs, bias_grad, near, far, theirs,
    weight, grad, cot, sems,
):
    rows, width = x2.shape
    copies = Copies(sems)
    cot_copy = my_examples(where, cotangent, cot, copies)
    wait_all(load_weight(where, weight, weights, copies, True))
    cot_copy.wait()
    gy = cot[...].reshape(rows, width)
    shards = weight.shape[0]
    step = weight.shape[1] * weight.shape[2]
    whole = weight[...].reshape(shards * step, width)
    for j in range(4):
        cols = columns(j, width)
        low = (dot_nt(gy, whole[cols]) * slope[:, cols].astype(F32)).astype(BF)
        du[:, cols] = low
        bias_grad[:, cols] = jnp.sum(low.astype(F32), axis=0, keepdims=True)
        grad[j] = dot_tn(a3[...], low).astype(BF)
    started = store_grad(where, grad, near, far, theirs, Copies(sems))
    result = x2[...] + dot(h[...], whole) + vec[6:7, :]
    y[...] = result.astype(BF).reshape(y.shape)
    vecs[...] = jnp.sum(gy.astype(F32), axis=0, keepdims=True)
    wait_all(started)


def dense_back(where, x2, vec, du, cotangent, weights, gx2, vecs, weight, cot, sems):
    rows, width = x2.shape
    copies = Copies(sems)
    cot_copy = my_examples(where, cotangent, cot, copies)
    loads = load_weight(where, weight, weights, copies)
    hat, scale = normalise(x2[...])
    cot_copy.wait()
    wait_all(loads)
    da3 = dot_nt(du[:, columns(0, width)], weight[0])
    for j in range(1, 4):
        da3 = da3 + dot_nt(du[:, columns(j, width)], weight[j])
    back, gain_grad, shift_grad = norm_back(da3, vec[4:5, :], hat, scale)
    gx2[...] = cot[...].reshape(rows, width).astype(F32) + back
    vecs[0:1, :] = gain_grad
    vecs[1:2, :] = shift_grad


def cross_backward(
    where, x1, vec, gx2, q2, kv, p2, weights, gx1, vecs, dkv, dq2, out_mem, weight, do2, moved, sems
):
    rows, width = x1.shape
    per, total = kv.shape[0], kv.shape[1]
    step = pl.program_id(0)
    length = p2.shape[2] // TOGETHER

    @pl.when(step == 0)
    def _():
        wait_all(load_weight(where, weight, weights, Copies(sems)))
        do2[...] = dot_nt(gx2[...].astype(BF), weight[3]).astype(BF)

    mask = head_mask(length)
    pairs = [(i, g) for i in range(per) for g in range(GROUPS)]
    queries, grads, dz = {}, {}, {}
    for i, g in pairs:
        here = rows_of((step * per + i) * length, length)
        lanes = columns(g, LANES)
        queries[i, g] = stack_heads(q2[here, lanes], mask)
        grads[i, g] = stack_heads(do2[here, lanes], mask)
        dp = dot_nt(grads[i, g], kv[i, :, width + g * LANES : width + (g + 1) * LANES])
        wide = p2[i, g].astype(F32)
        row_sum = jnp.sum(wide * dp, axis=-1, keepdims=True)
        dz[i, g] = (wide * (dp - row_sum)).astype(BF)
    for i, g in pairs:
        here = rows_of((step * per + i) * length, length)
        lanes = columns(g, LANES)
        value_lanes = slice(width + g * LANES, width + (g + 1) * LANES)
        dkv[i, :, value_lanes] = dot_tn(p2[i, g], grads[i, g]).astype(BF)
        dkv[i, :, lanes] = (dot_tn(dz[i, g], queries[i, g]) * SCALE).astype(BF)
        dq = merge_heads(dot(dz[i, g], kv[i, :, lanes]), mask) * SCALE
        dq2[here, lanes] = dq.astype(BF)
    for i in range(per):
        back = dot_nt(dkv[i, :, :width], weight[1]) + dot_nt(dkv[i, :, width:], weight[2])
        moved[i] = back.astype(BF)
        for d, out in enumerate(out_mem):
            slots = out.shape[1]
            out[i] = moved[i, rows_of((where[3] ^ d) * slots, slots), :]

    @pl.when(step == pl.num_programs(0) - 1)
    def _():
        hat, scale = normalise(x1[...])
        back, gain_grad, shift_grad = norm_back(
            dot_nt(dq2[...], weight[0]), vec[2:3, :], hat, scale
        )
        gx1[...] = gx2[...] + back
        vecs[0:1, :] = gain_grad
        vecs[1:2, :] = shift_grad


def cross_grads(
    where, gx2, a2, o2, dq2, dkv, all_memory, near, far, theirs, grad, turned, memory, sems
):
    rows, width = gx2.shape
    mem, examples, slots, _ = all_memory.shape
    half = pl.program_id(0)
    tokens = mem * examples * slots

    @pl.when(half == 0)
    def _():
        copies = Copies(sems)
        loads = [
            copies.start(all_memory.at[d], memory.at[:, d * slots : (d + 1) * slots, :])
            for d in range(mem)
        ]
        grad[0] = dot_tn(a2[...], dq2[...]).astype(BF)
        grad[3] = dot_tn(o2[...], gx2[...].astype(BF)).astype(BF)
        wait_all(loads)
        turned[...] = memory[...].reshape(tokens, width).T

    grad[1 + half] = dot(turned[...], dkv[...].reshape(tokens, width)).astype(BF)

    @pl.when(half == 1)
    def _():
        wait_all(store_grad(where, grad, near, far, theirs, Copies(sems)))


def self_backward(
    group, where, suffix, vec, gx1, a1, qkv, p1, o1, parts, weights, suffix_grad, vecs,
    near, far, theirs, weight, start, grad, dqkv, do1, sems,
):
    rows, width = gx1.shape
    copies = Copies(sems)
    start_copy = my_examples(where, suffix, start, copies)
    loads = load_weight(where, weight, weights, copies)
    gs = gx1[...].astype(BF)
    grad[3] = dot_tn(o1[...], gs).astype(BF)
    wait_all(loads)
    do1[...] = dot_nt(gs, weight[3]).astype(BF)
    mask = head_mask(group)
    for r in range(rows // group):
        here = columns(r, group)
        for g in range(GROUPS):
            lanes = [slice(i * width + g * LANES, i * width + (g + 1) * LANES) for i in range(3)]
            queries = stack_heads(qkv[here, lanes[0]], mask)
            grads = stack_heads(do1[here, lanes[0]], mask)
            probs = p1[r * GROUPS + g]
            dp = dot_nt(grads, qkv[here, lanes[2]])
            wide = probs.astype(F32)
            row_sum = jnp.sum(wide * dp, axis=-1, keepdims=True)
            dz = (wide * (dp - row_sum)).astype(BF)
            dqkv[here, lanes[2]] = dot_tn(probs, grads).astype(BF)
            dqkv[here, lanes[1]] = (dot_tn(dz, queries) * SCALE).astype(BF)
            dq = merge_heads(dot(dz, qkv[here, lanes[1]]), mask) * SCALE
            dqkv[here, lanes[0]] = dq.astype(BF)
    for j in range(3):
        grad[j] = dot_tn(a1[...], dqkv[:, columns(j, width)]).astype(BF)
    start_copy.wait()
    started = store_grad(where, grad, near, far, theirs, Copies(sems))
    da1 = dot_nt(dqkv[:, columns(0, width)], weight[0])
    for j in range(1, 3):
        da1 = da1 + dot_nt(dqkv[:, columns(j, width)], weight[j])
    hat, scale = normalise(start[...].reshape(rows, width).astype(F32))
    back, gain_grad, shift_grad = norm_back(da1, vec[0:1, :], hat, scale)
    suffix_grad[...] = (gx1[...] + back).astype(BF).reshape(suffix_grad.shape)
    found = [gain_grad, shift_grad]
    for ref in parts:
        for r in range(ref.shape[0]):
            found += [ref[r : r + 1, columns(j, width)] for j in range(ref.shape[1] // width)]
    found.append(jnp.zeros((vecs.shape[0] - len(found), width), F32))
    vecs[...] = jnp.concatenate(found, axis=0).astype(BF)
    wait_all(started)


def run(kernel, inputs, outputs, scratch, copies, grid=(), moved=0):
    def leaf(x):
        return isinstance(x, tuple) and len(x) == 2 and isinstance(x[0], pl.BlockSpec)

    flat_in, tree_in = jax.tree.flatten(inputs, is_leaf=leaf)
    flat_out, tree_out = jax.tree.flatten(outputs, is_leaf=leaf)

    def body(*refs):
        first, second = len(flat_in), len(flat_in) + len(flat_out)
        given = jax.tree.unflatten(tree_in, refs[:first])
        taken = jax.tree.unflatten(tree_out, refs[first:second])
        kernel(*given, *taken, *refs[second:])

    found = pl.pallas_call(
        body,
        grid=grid,
        in_specs=[spec for spec, _ in flat_in],
        out_specs=[spec for spec, _ in flat_out],
        out_shape=[shape for _, shape in flat_out],
        scratch_shapes=scratch + [pltpu.SemaphoreType.DMA((copies,))],
        compiler_params=pltpu.CompilerParams(vmem_limit_bytes=56 * 1024 * 1024),
        cost_estimate=pl.CostEstimate(
            flops=0, bytes_accessed=moved, transcendentals=0
        ),
    )(*[x for _, x in flat_in])
    return jax.tree.unflatten(tree_out, found)


def shape_of(dims, dtype):
    return jax.ShapeDtypeStruct(tuple(dims), dtype)


def over_slow(value, slow, fast):
    groups = [[k * fast + b for k in range(slow)] for b in range(fast)]
    return lax.all_to_all(value, "fsdp", 0, 0, axis_index_groups=groups, tiled=True)


class Gather:
    def __init__(self, half, slow, fast):
        self.half, self.slow, self.fast = half, slow, fast

    def send_slow(self, *others):
        half = after(self.half, *others)
        self.came = [half] + [swap(half, "fsdp", k * self.fast) for k in range(1, self.slow)]

    def send_fast(self, *others):
        self.near = jnp.stack([after(piece, *others) for piece in self.came])
        self.near_other = swap(self.near, "mem", 1)
        self.far = [swap(self.near, "fsdp", b) for b in range(1, self.fast)]

    def whole(self):
        mine = [self.near] + self.far
        theirs = [self.near_other] + [swap(piece, "mem", 1) for piece in self.far]
        return mine, theirs

    @staticmethod
    def refs(weights):
        return [[(ANY, x) for x in some] for some in weights]


class Scatter:
    def __init__(self, grads, slow, fast, *others, vectors=None):
        self.near, self.far, theirs = grads
        self.slow, self.fast, self.vectors = slow, fast, vectors
        theirs = [after(part, *others) for part in theirs]
        far = [swap(part, "mem", 1) for part in theirs[1:]]
        far = [jnp.concatenate(far[2 * b : 2 * b + 2]) for b in range(fast - 1)]
        self.sent = [swap(theirs[0], "mem", 1)] + far
        if vectors is not None:
            self.vectors = vectors.astype(F32) + swap(vectors, "mem", 1).astype(F32)

    def add_cores(self, *others):
        far = after(self.far, *others)
        self.out = [
            (far[b].astype(F32) + self.sent[b + 1].astype(F32)).astype(BF)
            for b in range(self.fast - 1)
        ]
        return self.out

    def send_fast(self):
        self.came = [swap(part, "fsdp", b + 1) for b, part in enumerate(self.out)]
        if self.vectors is not None:
            low = self.vectors.astype(BF)
            self.vectors = [low] + [swap(low, "fsdp", b) for b in range(1, self.fast)]

    def add_fast(self, *others):
        if self.vectors is not None:
            self.vectors, self.came = lax.optimization_barrier((self.vectors, self.came))
            self.vectors = sum(part.astype(F32) for part in self.vectors)
        total = after(self.near, *others).astype(F32) + self.sent[0].astype(F32)
        for part in self.came:
            total = total + part.astype(F32)
        self.total = total.astype(BF).reshape(self.slow, -1, total.shape[-1])
        if self.vectors is not None:
            low = self.vectors.astype(BF)
            low = jnp.broadcast_to(low, (self.slow,) + low.shape)
            self.total = jnp.concatenate([self.total, low], axis=1)
        return self.total

    def send_slow(self):
        self.came = over_slow(self.total, self.slow, self.fast)

    def add_slow(self, *others):
        return jnp.sum(after(self.came, *others).astype(F32), axis=0)


class Replicas:
    def __init__(self, value, rows, across):
        self.rows = rows
        k = 1
        while 2 * k < across:
            low = value.astype(BF)
            value = low.astype(F32) + swap(low, "mem", 2 * k).astype(F32)
            k *= 2
        low = value.astype(BF)
        self.halves = [low, swap(low, "mem", 2 * k)] if across > 1 else [low]

    def swap_cores(self, *others):
        halves, _ = lax.optimization_barrier((self.halves, others))
        self.others = [swap(half[: 2 * self.rows], "mem", 1) for half in halves]

    def combine(self, c):
        rows = self.rows
        other = sum(half.astype(F32) for half in self.others)
        mine = sum(half.astype(F32) for half in self.halves)
        vectors, mine = mine[2 * rows :], mine[: 2 * rows]
        first = jnp.where(c == 0, mine, other)
        second = jnp.where(c == 0, other, mine)
        return [first[:rows], first[rows:], second[:rows], second[rows:]], vectors


def place_rows(where, blocks, outs, scratch, sems):
    copies = Copies(sems)
    loads = []
    for i, (even, odd) in enumerate(blocks):
        for d, piece in enumerate(even):
            loads.append((copies.start(piece, scratch.at[i, 2 * d]), i, 2 * d))
            loads.append((copies.start(odd.at[d], scratch.at[i, 2 * d + 1]), i, 2 * d + 1))
    examples = scratch.shape[2]
    stores = []
    for load, i, d in loads:
        load.wait()
        target = outs[i].at[pl.ds((where[3] ^ d) * examples, examples)]
        stores.append(copies.start(scratch.at[i, d], target))
    wait_all(stores)


def place_memory(where, pieces, out, scratch, sems):
    examples = pieces[0].shape[0]
    copies = Copies(sems)
    loads = [copies.start(piece, scratch.at[d]) for d, piece in enumerate(pieces)]
    stores = []
    for d, load in enumerate(loads):
        load.wait()
        target = out.at[pl.ds((where[3] ^ d) * examples, examples)]
        stores.append(copies.start(scratch.at[d], target))
    wait_all(stores)


def spread_across(value, mem):
    return [value] + [swap(value, "mem", d) for d in range(2, mem, 2)]


def per_device(
    suffix,
    memory,
    counts,
    cotangent,
    self_norm_gain,
    self_norm_bias,
    self_query,
    self_key,
    self_value,
    self_output,
    cross_norm_gain,
    cross_norm_bias,
    cross_query,
    cross_key,
    cross_value,
    cross_output,
    dense_norm_gain,
    dense_norm_bias,
    dense_in,
    dense_in_bias,
    dense_out,
    dense_out_bias,
):
    f = lax.axis_index("fsdp")
    m = lax.axis_index("mem")
    c = m % 2
    fsdp = lax.axis_size("fsdp")
    mem = lax.axis_size("mem")
    across = mem // 2
    slow, fast = fsdp_split(fsdp)
    SHARDS[0] = fsdp
    where = jnp.stack([f // fast, f % fast, c, m]).astype(jnp.int32)
    examples = suffix.shape[0] // mem
    length = suffix.shape[1]
    width = suffix.shape[2]
    slots = memory.shape[1]
    total = mem * slots
    rows = examples * length
    inner = dense_in.shape[1]
    part = width // fsdp
    group = min(128, rows)
    blocks = 4 * fsdp

    def gather(matrices, *others):
        halves = [jnp.concatenate(matrices[:2]), jnp.concatenate(matrices[2:])]
        half = jnp.concatenate([jnp.where(c == 0, *halves), *others])
        return Gather(half, slow, fast)

    cross_gather = gather([cross_query, cross_key, cross_value, cross_output])
    in_gather = gather([dense_in[:, columns(j, width)] for j in range(4)])
    out_gather = gather([dense_out[columns(j, part)] for j in range(4)])
    small = [
        self_norm_gain,
        self_norm_bias,
        cross_norm_gain,
        cross_norm_bias,
        dense_norm_gain,
        dense_norm_bias,
        dense_out_bias,
    ]
    small += [dense_in_bias[columns(j, part)] for j in range(4)]
    small = sum(
        jnp.pad(value[None], ((i, 15 - i), (0, width - part))) for i, value in enumerate(small)
    )
    self_gather = gather([self_query, self_key, self_value, self_output], small)

    def exchange(value):
        blocks = value.reshape((mem, examples) + value.shape[1:])
        return lax.all_to_all(blocks, "mem", 0, 0, tiled=True)

    all_memory = exchange(memory)
    self_gather.send_slow()
    sent = self_gather.came
    self_gather.send_fast(*sent)
    cross_gather.send_slow(*sent)
    sent = [*self_gather.far, *cross_gather.came, all_memory]
    self_gather.far = [after(piece, *sent) for piece in self_gather.far]
    self_weights = self_gather.whole()
    cross_gather.send_fast(*self_gather.far)
    in_gather.send_slow(*self_gather.far)

    half = (2, part, width)
    grads_like = [
        (ANY, shape_of((slow,) + half, BF)),
        (ANY, shape_of((fast - 1, slow) + half, BF)),
        [(ANY, shape_of((slow,) + half, BF))]
        + [(ANY, shape_of((slow // 2,) + half, BF))] * (2 * fast - 2),
    ]

    def flat(dims, dtype):
        return (VMEM, shape_of(dims, dtype))

    per = 2 if examples % 2 == 0 else 1

    def per_example(value):
        dims = value.shape[1:]
        spec = pl.BlockSpec((per,) + dims, lambda e: (e,) + (0,) * len(dims))
        return (spec, value)

    def slots_of_example(value):
        spec = pl.BlockSpec((mem, per, slots, width), lambda e: (0, e, 0, 0))
        return (spec, value)

    def scratch(*dims):
        return pltpu.VMEM(dims, BF)

    def scatter(grads, *others, vectors=None):
        return Scatter(grads, slow, fast, *others, vectors=vectors)

    wide = (rows, width)
    square = scratch(4, width, width)
    own_rows = scratch(examples, length, width)
    x1, a1, qkv, p1, o1, vec = run(
        functools.partial(self_forward, group),
        [(SMEM, where), (ANY, suffix), Gather.refs(self_weights)],
        [
            flat(wide, F32),
            flat(wide, BF),
            flat((rows, 3 * width), BF),
            flat((rows // group * GROUPS, TOGETHER * group, group), BF),
            flat(wide, BF),
            flat((16, width), F32),
        ],
        [square, own_rows, scratch(fsdp, 16, 128)],
        1 + fsdp + blocks,
    )
    cross_gather.far = [after(piece, x1, *in_gather.came) for piece in cross_gather.far]
    cross_weights = Gather.refs(cross_gather.whole())
    in_gather.send_fast(*cross_gather.far)
    out_gather.send_slow(*cross_gather.far)
    x2, a2, q2, kv, p2, o2 = run(
        cross_forward,
        [(SMEM, where), (SMEM, counts), (VMEM, x1), (VMEM, vec)]
        + [slots_of_example(all_memory), cross_weights],
        [
            flat(wide, F32),
            flat(wide, BF),
            flat(wide, BF),
            per_example(shape_of((examples, total, 2 * width), BF)),
            per_example(shape_of((examples, GROUPS, TOGETHER * length, total), BF)),
            flat(wide, BF),
        ],
        [square],
        blocks,
        (examples // per,),
    )
    small = [after(piece, x1)[:, 2 * part + 7 : 2 * part + 11, :part] for piece in self_weights[0]]
    order = jnp.arange(fsdp) ^ f
    bias_in = jnp.take(jnp.concatenate(small), order % fast * slow + order // fast, axis=0)
    bias_in = bias_in.astype(F32).reshape(1, inner)
    in_gather.far = [after(piece, x2, *out_gather.came) for piece in in_gather.far]
    in_weights = Gather.refs(in_gather.whole())
    out_gather.send_fast(*in_gather.far)
    a3, h, slope, *grads = run(
        dense_inner,
        [(SMEM, where), (VMEM, x2), (VMEM, vec), (VMEM, bias_in), (ANY, cotangent), in_weights],
        [flat(wide, BF), flat((rows, inner), BF), flat((rows, inner), BF)] + grads_like,
        [square, scratch(fsdp, 4, part, width), own_rows],
        1 + blocks,
    )
    out_gather.far = [after(piece, a3) for piece in out_gather.far]
    out_weights = Gather.refs(out_gather.whole())
    out_scatter = scatter(grads, *out_gather.far)
    out_sum = out_scatter.add_cores()
    out_scatter.send_fast()
    y, du, vecs_y, bias_grad, *grads = run(
        dense_outer,
        [(SMEM, where), (VMEM, after(x2, *out_sum)), (VMEM, vec), (VMEM, a3), (VMEM, h)]
        + [(VMEM, slope), (ANY, cotangent), out_weights],
        [
            flat((examples, length, width), BF),
            flat((rows, inner), BF),
            flat((1, width), F32),
            flat((1, inner), F32),
        ]
        + grads_like,
        [scratch(fsdp, 4, part, width), square, own_rows],
        1 + blocks,
    )
    in_grads = grads
    gx2, vecs_dense = run(
        dense_back,
        [(SMEM, where), (VMEM, x2), (VMEM, vec), (VMEM, du), (ANY, cotangent), in_weights],
        [flat(wide, F32), flat((2, width), F32)],
        [square, own_rows],
        1 + blocks,
    )
    in_scatter = scatter(in_grads, gx2)
    in_sum = in_scatter.add_cores(*out_scatter.came)
    in_scatter.send_fast()
    gx1, vecs_cross, dkv, dq2, grad_memory = run(
        cross_backward,
        [(SMEM, where), (VMEM, x1), (VMEM, vec), (VMEM, after(gx2, *in_sum)), (VMEM, q2)]
        + [per_example(kv), per_example(p2), cross_weights],
        [
            flat(wide, F32),
            flat((2, width), F32),
            per_example(shape_of((examples, total, 2 * width), BF)),
            flat(wide, BF),
            [per_example(shape_of((examples, slots, width), BF))] * mem,
        ],
        [square, scratch(*wide), scratch(per, total, width)],
        blocks,
        (examples // per,),
        60_000_000,
    )
    in_scatter.came, _ = lax.optimization_barrier((in_scatter.came, gx1))
    out_total = out_scatter.add_fast(*in_scatter.came)
    out_scatter.send_slow()
    mem_pieces = grad_memory[:1] + [swap(grad_memory[d], "mem", d) for d in range(1, mem)]
    grads = run(
        cross_grads,
        [(SMEM, where), (VMEM, after(gx2, out_total, *in_scatter.came)), (VMEM, a2), (VMEM, o2), (VMEM, dq2)]
        + [(pl.BlockSpec((examples, total, width), lambda j: (0, 0, j)), dkv), (ANY, all_memory)],
        grads_like,
        [square, scratch(width, examples * total), scratch(examples, total, width)],
        max(mem, blocks),
        (2,),
        45_000_000,
    )
    out_final = out_scatter.add_slow()
    in_scatter.add_fast(out_final)
    in_scatter.send_slow()
    cross_scatter = scatter(grads, out_final, *mem_pieces[1:3])
    cross_sum = cross_scatter.add_cores()
    cross_scatter.send_fast()
    gx1 = after(gx1, *cross_sum)
    suffix_part, vecs_self, *grads = run(
        functools.partial(self_backward, group),
        [(SMEM, where), (ANY, suffix), (VMEM, vec), (VMEM, gx1), (VMEM, a1)]
        + [(VMEM, qkv), (VMEM, p1), (VMEM, o1)]
        + [[(VMEM, x) for x in (vecs_cross, vecs_dense, vecs_y, bias_grad)], Gather.refs(self_weights)],
        [flat((examples, length, width), BF), flat((16, width), BF)] + grads_like,
        [square, own_rows, square, scratch(rows, 3 * width), scratch(*wide)],
        1 + blocks,
        moved=40_000_000,
    )
    self_scatter = scatter(grads, *mem_pieces[3:4], vectors=vecs_self)
    self_sum = self_scatter.add_cores()
    self_scatter.send_fast()
    cross_scatter.add_fast(*self_sum)
    cross_scatter.send_slow()
    in_final = in_scatter.add_slow(*self_sum)
    dense_sum = jnp.concatenate([out_final, in_final])
    dense_sum = Replicas(dense_sum, 2 * part, across)
    self_total = self_scatter.add_fast(*dense_sum.halves)
    self_scatter.send_slow()
    cross_sum = Replicas(cross_scatter.add_slow(self_total), part, across)
    suffix_rows = spread_across(after(suffix_part, self_total), mem)
    y_rows = spread_across(after(y, self_total), mem)
    dense_sum.swap_cores(self_total)
    mem_pieces = [after(value, self_total) for value in mem_pieces]
    (memory_grad,) = run(
        place_memory,
        [(SMEM, where), [(ANY, value) for value in mem_pieces]],
        [(ANY, shape_of(memory.shape, BF))],
        [scratch(mem, examples, slots, width)],
        2 * mem,
    )
    (out_low, in_low, out_high, in_high), _ = dense_sum.combine(c)
    grad_in = jnp.concatenate([in_low[:part], in_low[part:], in_high[:part], in_high[part:]], axis=1)
    grad_out = jnp.concatenate([out_low, out_high])
    done = [*cross_sum.halves, *suffix_rows, *y_rows, grad_in, grad_out, memory_grad]
    self_final = Replicas(self_scatter.add_slow(*done), part, across)
    cross_sum.swap_cores(self_final.halves[0])
    y_rows = [after(value, self_final.halves[0]) for value in y_rows]
    y_far = swap(jnp.stack(y_rows), "mem", 1)
    suffix_rows = [after(value, self_final.halves[0]) for value in suffix_rows]
    suffix_far = swap(jnp.stack(suffix_rows), "mem", 1)
    blocks = [([(ANY, x) for x in y_rows], (ANY, y_far))]
    blocks += [([(ANY, x) for x in suffix_rows], (ANY, suffix_far))]
    ((block_output, suffix_grad),) = run(
        place_rows,
        [(SMEM, where), blocks],
        [[(ANY, shape_of(suffix.shape, BF))] * 2],
        [scratch(2, mem, examples, length, width)],
        4 * mem,
    )
    grad_cross, _ = cross_sum.combine(c)
    self_final.swap_cores(block_output)
    grad_self, vectors = self_final.combine(c)

    def vector(i):
        return lax.dynamic_slice(vectors, (i, f * part), (1, part)).reshape(part)

    return (
        block_output,
        suffix_grad,
        memory_grad,
        vector(0),
        vector(1),
        *grad_self,
        vector(2),
        vector(3),
        *grad_cross,
        vector(4),
        vector(5),
        grad_in,
        lax.dynamic_slice_in_dim(vectors[7:11].reshape(-1), f * (inner // fsdp), inner // fsdp, 0),
        grad_out,
        vector(6),
    )


def solution(mesh):
    rows = P("fsdp", None, None)
    matrix = P("fsdp", None)
    vector = P("fsdp")
    attention = (vector, vector, matrix, matrix, matrix, matrix)
    params = attention + attention + (vector, vector, matrix, vector, matrix, vector)
    return jax.shard_map(
        per_device,
        mesh=mesh,
        in_specs=(rows, P("fsdp", "mem", None), vector, rows) + params,
        out_specs=(rows, rows, P("fsdp", "mem", None)) + params,
        check_vma=False,
    )
```

```python
import functools

import jax
import jax.numpy as jnp
from jax import lax
from jax.experimental import pallas as pl
from jax.experimental.pallas import tpu as pltpu
from jax.sharding import PartitionSpec as P

HEADS = 12
HEAD = 64
TOGETHER = 4
GROUPS = HEADS // TOGETHER
LANES = TOGETHER * HEAD
SCALE = HEAD ** (-0.5)
BF = jnp.bfloat16
F32 = jnp.float32
ANY = pl.BlockSpec(memory_space=pl.ANY)
SMEM = pl.BlockSpec(memory_space=pltpu.SMEM)
VMEM = pl.BlockSpec(memory_space=pltpu.VMEM)


def swap(value, axis, distance):
    size = lax.axis_size(axis)
    return lax.ppermute(value, axis, [(i, i ^ distance) for i in range(size)])


def after(value, *others):
    return lax.optimization_barrier((value, *others))[0] if others else value


def fsdp_split(size):
    slow = 4 if size % 4 == 0 else 1
    return slow, size // slow


def dot(left, right):
    return jnp.dot(left, right, preferred_element_type=F32)


def dot_nt(left, right):
    return lax.dot_general(left, right, (((1,), (1,)), ((), ())), preferred_element_type=F32)


def dot_tn(left, right):
    return lax.dot_general(left, right, (((0,), (0,)), ((), ())), preferred_element_type=F32)


def rows_of(start, size):
    return pl.ds(pl.multiple_of(start, 16), size)


def block(ref, by_rows, shard, which):
    if by_rows:
        return ref.at[shard, pl.ds(which * 2, 2)]
    rows = ref.shape[1] // SHARDS[0]
    return ref.at[pl.ds(which * 2, 2), rows_of(shard * rows, rows)]


SHARDS = [0]


class Copies:
    def __init__(self, sems):
        self.sems = sems
        self.next = 0

    def start(self, source, target):
        copy = pltpu.make_async_copy(source, target, self.sems.at[self.next])
        self.next += 1
        copy.start()
        return copy


def wait_all(copies):
    for copy in copies:
        copy.wait()


def load_weight(where, whole, weights, copies, by_rows=False):
    z, y, c = where[0], where[1], where[2]
    rows = whole.shape[2] if by_rows else whole.shape[1] // SHARDS[0]
    started = []
    for which, pieces in ((c, weights[0]), (1 - c, weights[1])):
        fast = len(pieces)
        for b, piece in enumerate(pieces):
            for k in range(piece.shape[0]):
                shard = (z ^ k) * fast + (y ^ b)
                for i in range(2):
                    source = piece.at[k, pl.ds(i * rows, rows)]
                    if by_rows:
                        target = whole.at[shard, 2 * which + i]
                    else:
                        target = whole.at[2 * which + i, rows_of(shard * rows, rows)]
                    started.append(copies.start(source, target))
    return started


def store_grad(where, whole, near, far, theirs, copies, by_rows=False):
    y, c = where[1], where[2]
    slow, cut = near.shape[0], near.shape[0] // 2
    fast = (len(theirs) + 1) // 2
    started = []
    for b in range(fast):
        for k in range(slow):
            shard = k * fast + (y ^ b)
            mine = far.at[b - 1, k] if b else near.at[k]
            other = theirs[2 * b - 1 + k // cut].at[k % cut] if b else theirs[0].at[k]
            started.append(copies.start(block(whole, by_rows, shard, 1 - c), other))
            started.append(copies.start(block(whole, by_rows, shard, c), mine))
    return started


def my_examples(where, source, target, copies):
    count = target.shape[0]
    return copies.start(source.at[pl.ds(where[3] * count, count)], target)


def normalise(values):
    centred = values - jnp.mean(values, axis=-1, keepdims=True)
    scale = lax.rsqrt(jnp.mean(centred * centred, axis=-1, keepdims=True) + 1e-06)
    return centred * scale, scale


def norm_back(grad, gain, hat, scale):
    inner = grad * gain
    mean = jnp.mean(inner, axis=-1, keepdims=True)
    along = jnp.mean(inner * hat, axis=-1, keepdims=True)
    return (
        scale * (inner - mean - hat * along),
        jnp.sum(grad * hat, axis=0, keepdims=True),
        jnp.sum(grad, axis=0, keepdims=True),
    )


def head_mask(rows):
    shape = (TOGETHER * rows, LANES)
    row = lax.broadcasted_iota(jnp.int32, shape, 0) // rows
    lane = lax.broadcasted_iota(jnp.int32, shape, 1) // HEAD
    return (row == lane).astype(F32)


def stack_heads(value, mask):
    return (jnp.concatenate([value] * TOGETHER, axis=0).astype(F32) * mask).astype(BF)


def merge_heads(value, mask):
    rows = value.shape[0] // TOGETHER
    value = value * mask
    total = value[:rows]
    for h in range(1, TOGETHER):
        total = total + value[h * rows : (h + 1) * rows]
    return total


def columns(j, width):
    return slice(j * width, (j + 1) * width)


def self_forward(
    group, where, suffix, weights, x1, a1, qkv, p1, o1, vec, weight, start, small, sems
):
    rows, width = x1.shape
    copies = Copies(sems)
    first = my_examples(where, suffix, start, copies)
    fast, slow = len(weights[0]), weights[0][0].shape[0]
    part = width // (fast * slow)
    vectors = []
    for b, piece in enumerate(weights[0]):
        for k in range(slow):
            source = piece.at[k, pl.ds(2 * part, 16), pl.ds(0, 128)]
            vectors.append(copies.start(source, small.at[b * slow + k]))
    loads = load_weight(where, weight, weights, copies)
    wait_all(vectors)
    lane = lax.broadcasted_iota(jnp.int32, (128, width), 0)
    place = lax.broadcasted_iota(jnp.int32, (128, width), 1) - lane
    together = jnp.zeros(vec.shape, F32)
    for i in range(fast * slow):
        shard = (where[0] ^ (i % slow)) * fast + (where[1] ^ (i // slow))
        chosen = ((place == shard * part) & (lane < part)).astype(F32).astype(BF)
        together = together + dot(small[i], chosen)
    vec[...] = together
    first.wait()
    values = start[...].reshape(rows, width).astype(F32)
    hat, _ = normalise(values)
    a1[...] = (hat * vec[0:1, :] + vec[1:2, :]).astype(BF)
    wait_all(loads)
    for j in range(3):
        qkv[:, columns(j, width)] = dot(a1[...], weight[j]).astype(BF)
    mask = head_mask(group)
    length = suffix.shape[1]
    shape = (TOGETHER * group, group)
    row = lax.broadcasted_iota(jnp.int32, shape, 0) % group
    col = lax.broadcasted_iota(jnp.int32, shape, 1)
    seen = (row // length == col // length) & (row >= col)
    for r in range(rows // group):
        here = columns(r, group)
        for g in range(GROUPS):
            lanes = [slice(i * width + g * LANES, i * width + (g + 1) * LANES) for i in range(3)]
            queries = stack_heads(qkv[here, lanes[0]], mask)
            scores = dot_nt(queries, qkv[here, lanes[1]]) * SCALE
            scores = jnp.where(seen, scores, -1e30)
            powers = jnp.exp(scores - jnp.max(scores, axis=-1, keepdims=True))
            probs = (powers / jnp.sum(powers, axis=-1, keepdims=True)).astype(BF)
            p1[r * GROUPS + g] = probs
            found = dot(probs, qkv[here, lanes[2]])
            o1[here, lanes[0]] = merge_heads(found, mask).astype(BF)
    x1[...] = values + dot(o1[...], weight[3])


def cross_forward(
    where, counts, x1, vec, memory, weights, x2, a2, q2, kv, p2, o2, weight, sems
):
    rows, width = x1.shape
    per = kv.shape[0]
    step = pl.program_id(0)
    total = kv.shape[1]
    length = p2.shape[2] // TOGETHER

    @pl.when(step == 0)
    def _():
        loads = load_weight(where, weight, weights, Copies(sems))
        hat, _ = normalise(x1[...])
        a2[...] = (hat * vec[2:3, :] + vec[3:4, :]).astype(BF)
        wait_all(loads)
        q2[...] = dot(a2[...], weight[0]).astype(BF)

    for i in range(per):
        tokens = memory[:, i].reshape(total, width)
        for j in range(2):
            kv[i, :, columns(j, width)] = dot(tokens, weight[1 + j]).astype(BF)
    mask = head_mask(length)
    position = lax.broadcasted_iota(jnp.int32, (1, total), 1)
    probs = {}
    for i in range(per):
        e = step * per + i
        valid = position < counts[where[3] * (pl.num_programs(0) * per) + e]
        here = rows_of(e * length, length)
        for g in range(GROUPS):
            lanes = columns(g, LANES)
            queries = stack_heads(q2[here, lanes], mask)
            scores = dot_nt(queries, kv[i, :, lanes]) * SCALE
            scores = jnp.where(valid, scores, -1e30)
            top = jnp.maximum(jnp.max(scores, axis=-1, keepdims=True), 0.0)
            powers = jnp.exp(scores - top)
            weight_sum = jnp.sum(powers, axis=-1, keepdims=True) + jnp.exp(-top)
            probs[i, g] = (powers / weight_sum).astype(BF)
    for i in range(per):
        here = rows_of((step * per + i) * length, length)
        for g in range(GROUPS):
            p2[i, g] = probs[i, g]
            found = dot(probs[i, g], kv[i, :, width + g * LANES : width + (g + 1) * LANES])
            o2[here, columns(g, LANES)] = merge_heads(found, mask).astype(BF)

    @pl.when(step == pl.num_programs(0) - 1)
    def _():
        x2[...] = x1[...] + dot(o2[...], weight[3])


def dense_inner(
    where, x2, vec, bias, cotangent, weights, a3, h, slope, near, far, theirs,
    weight, grad, cot, sems,
):
    rows, width = x2.shape
    copies = Copies(sems)
    cot_copy = my_examples(where, cotangent, cot, copies)
    loads = load_weight(where, weight, weights, copies)
    hat, _ = normalise(x2[...])
    a3[...] = (hat * vec[4:5, :] + vec[5:6, :]).astype(BF)
    cot_copy.wait()
    gy = cot[...].reshape(rows, width)
    wait_all(loads)
    flat = grad.shape[0] * grad.shape[1] * grad.shape[2]
    step = flat // grad.shape[0]
    for j in range(4):
        for half in range(2):
            cols = slice(j * width + half * 384, j * width + (half + 1) * 384)
            u = dot(a3[...], weight[j, :, half * 384 : (half + 1) * 384]) + bias[:, cols]
            square = u * u
            t = jnp.tanh(0.7978845608 * u * (1.0 + 0.044715 * square))
            h[:, cols] = (0.5 * u * (1.0 + t)).astype(BF)
            slope[:, cols] = (
                0.5 * (1.0 + t)
                + (0.5 * 0.7978845608) * u * (1.0 - t * t) * (1.0 + (3.0 * 0.044715) * square)
            ).astype(BF)
            part = dot_tn(h[:, cols], gy).astype(BF)
            per = 384 // step
            grad[cols.start // step : cols.start // step + per] = part.reshape(
                (per,) + grad.shape[1:]
            )
    wait_all(store_grad(where, grad, near, far, theirs, Copies(sems), True))


def dense_outer(
    where, x2, vec, a3, h, slope, cotangent, weights, y, du, vecs, bias_grad, near, far, theirs,
    weight, grad, cot, sems,
):
    rows, width = x2.shape
    copies = Copies(sems)
    cot_copy = my_examples(where, cotangent, cot, copies)
    wait_all(load_weight(where, weight, weights, copies, True))
    cot_copy.wait()
    gy = cot[...].reshape(rows, width)
    shards = weight.shape[0]
    step = weight.shape[1] * weight.shape[2]
    whole = weight[...].reshape(shards * step, width)
    for j in range(4):
        cols = columns(j, width)
        low = (dot_nt(gy, whole[cols]) * slope[:, cols].astype(F32)).astype(BF)
        du[:, cols] = low
        bias_grad[:, cols] = jnp.sum(low.astype(F32), axis=0, keepdims=True)
        grad[j] = dot_tn(a3[...], low).astype(BF)
    started = store_grad(where, grad, near, far, theirs, Copies(sems))
    result = x2[...] + dot(h[...], whole) + vec[6:7, :]
    y[...] = result.astype(BF).reshape(y.shape)
    vecs[...] = jnp.sum(gy.astype(F32), axis=0, keepdims=True)
    wait_all(started)


def dense_back(where, x2, vec, du, cotangent, weights, gx2, vecs, weight, cot, sems):
    rows, width = x2.shape
    copies = Copies(sems)
    cot_copy = my_examples(where, cotangent, cot, copies)
    loads = load_weight(where, weight, weights, copies)
    hat, scale = normalise(x2[...])
    cot_copy.wait()
    wait_all(loads)
    da3 = dot_nt(du[:, columns(0, width)], weight[0])
    for j in range(1, 4):
        da3 = da3 + dot_nt(du[:, columns(j, width)], weight[j])
    back, gain_grad, shift_grad = norm_back(da3, vec[4:5, :], hat, scale)
    gx2[...] = cot[...].reshape(rows, width).astype(F32) + back
    vecs[0:1, :] = gain_grad
    vecs[1:2, :] = shift_grad


def cross_backward(
    where, x1, vec, gx2, q2, kv, p2, weights, gx1, vecs, dkv, dq2, out_mem, weight, do2, moved, sems
):
    rows, width = x1.shape
    per, total = kv.shape[0], kv.shape[1]
    step = pl.program_id(0)
    length = p2.shape[2] // TOGETHER

    @pl.when(step == 0)
    def _():
        wait_all(load_weight(where, weight, weights, Copies(sems)))
        do2[...] = dot_nt(gx2[...].astype(BF), weight[3]).astype(BF)

    mask = head_mask(length)
    pairs = [(i, g) for i in range(per) for g in range(GROUPS)]
    queries, grads, dz = {}, {}, {}
    for i, g in pairs:
        here = rows_of((step * per + i) * length, length)
        lanes = columns(g, LANES)
        queries[i, g] = stack_heads(q2[here, lanes], mask)
        grads[i, g] = stack_heads(do2[here, lanes], mask)
        dp = dot_nt(grads[i, g], kv[i, :, width + g * LANES : width + (g + 1) * LANES])
        wide = p2[i, g].astype(F32)
        row_sum = jnp.sum(wide * dp, axis=-1, keepdims=True)
        dz[i, g] = (wide * (dp - row_sum)).astype(BF)
    for i, g in pairs:
        here = rows_of((step * per + i) * length, length)
        lanes = columns(g, LANES)
        value_lanes = slice(width + g * LANES, width + (g + 1) * LANES)
        dkv[i, :, value_lanes] = dot_tn(p2[i, g], grads[i, g]).astype(BF)
        dkv[i, :, lanes] = (dot_tn(dz[i, g], queries[i, g]) * SCALE).astype(BF)
        dq = merge_heads(dot(dz[i, g], kv[i, :, lanes]), mask) * SCALE
        dq2[here, lanes] = dq.astype(BF)
    for i in range(per):
        back = dot_nt(dkv[i, :, :width], weight[1]) + dot_nt(dkv[i, :, width:], weight[2])
        moved[i] = back.astype(BF)
        for d, out in enumerate(out_mem):
            slots = out.shape[1]
            out[i] = moved[i, rows_of((where[3] ^ d) * slots, slots), :]

    @pl.when(step == pl.num_programs(0) - 1)
    def _():
        hat, scale = normalise(x1[...])
        back, gain_grad, shift_grad = norm_back(
            dot_nt(dq2[...], weight[0]), vec[2:3, :], hat, scale
        )
        gx1[...] = gx2[...] + back
        vecs[0:1, :] = gain_grad
        vecs[1:2, :] = shift_grad


def cross_grads(
    where, gx2, a2, o2, dq2, dkv, all_memory, near, far, theirs, grad, turned, memory, sems
):
    rows, width = gx2.shape
    mem, examples, slots, _ = all_memory.shape
    half = pl.program_id(0)
    tokens = mem * examples * slots

    @pl.when(half == 0)
    def _():
        copies = Copies(sems)
        loads = [
            copies.start(all_memory.at[d], memory.at[:, d * slots : (d + 1) * slots, :])
            for d in range(mem)
        ]
        grad[0] = dot_tn(a2[...], dq2[...]).astype(BF)
        grad[3] = dot_tn(o2[...], gx2[...].astype(BF)).astype(BF)
        wait_all(loads)
        turned[...] = memory[...].reshape(tokens, width).T

    grad[1 + half] = dot(turned[...], dkv[...].reshape(tokens, width)).astype(BF)

    @pl.when(half == 1)
    def _():
        wait_all(store_grad(where, grad, near, far, theirs, Copies(sems)))


def self_backward(
    group, where, suffix, vec, gx1, a1, qkv, p1, o1, parts, weights, suffix_grad, vecs,
    near, far, theirs, weight, start, grad, dqkv, do1, sems,
):
    rows, width = gx1.shape
    copies = Copies(sems)
    start_copy = my_examples(where, suffix, start, copies)
    loads = load_weight(where, weight, weights, copies)
    gs = gx1[...].astype(BF)
    grad[3] = dot_tn(o1[...], gs).astype(BF)
    wait_all(loads)
    do1[...] = dot_nt(gs, weight[3]).astype(BF)
    mask = head_mask(group)
    for r in range(rows // group):
        here = columns(r, group)
        for g in range(GROUPS):
            lanes = [slice(i * width + g * LANES, i * width + (g + 1) * LANES) for i in range(3)]
            queries = stack_heads(qkv[here, lanes[0]], mask)
            grads = stack_heads(do1[here, lanes[0]], mask)
            probs = p1[r * GROUPS + g]
            dp = dot_nt(grads, qkv[here, lanes[2]])
            wide = probs.astype(F32)
            row_sum = jnp.sum(wide * dp, axis=-1, keepdims=True)
            dz = (wide * (dp - row_sum)).astype(BF)
            dqkv[here, lanes[2]] = dot_tn(probs, grads).astype(BF)
            dqkv[here, lanes[1]] = (dot_tn(dz, queries) * SCALE).astype(BF)
            dq = merge_heads(dot(dz, qkv[here, lanes[1]]), mask) * SCALE
            dqkv[here, lanes[0]] = dq.astype(BF)
    for j in range(3):
        grad[j] = dot_tn(a1[...], dqkv[:, columns(j, width)]).astype(BF)
    start_copy.wait()
    started = store_grad(where, grad, near, far, theirs, Copies(sems))
    da1 = dot_nt(dqkv[:, columns(0, width)], weight[0])
    for j in range(1, 3):
        da1 = da1 + dot_nt(dqkv[:, columns(j, width)], weight[j])
    hat, scale = normalise(start[...].reshape(rows, width).astype(F32))
    back, gain_grad, shift_grad = norm_back(da1, vec[0:1, :], hat, scale)
    suffix_grad[...] = (gx1[...] + back).astype(BF).reshape(suffix_grad.shape)
    found = [gain_grad, shift_grad]
    for ref in parts:
        for r in range(ref.shape[0]):
            found += [ref[r : r + 1, columns(j, width)] for j in range(ref.shape[1] // width)]
    found.append(jnp.zeros((vecs.shape[0] - len(found), width), F32))
    vecs[...] = jnp.concatenate(found, axis=0).astype(BF)
    wait_all(started)


def run(kernel, inputs, outputs, scratch, copies, grid=(), moved=0):
    def leaf(x):
        return isinstance(x, tuple) and len(x) == 2 and isinstance(x[0], pl.BlockSpec)

    flat_in, tree_in = jax.tree.flatten(inputs, is_leaf=leaf)
    flat_out, tree_out = jax.tree.flatten(outputs, is_leaf=leaf)

    def body(*refs):
        first, second = len(flat_in), len(flat_in) + len(flat_out)
        given = jax.tree.unflatten(tree_in, refs[:first])
        taken = jax.tree.unflatten(tree_out, refs[first:second])
        kernel(*given, *taken, *refs[second:])

    found = pl.pallas_call(
        body,
        grid=grid,
        in_specs=[spec for spec, _ in flat_in],
        out_specs=[spec for spec, _ in flat_out],
        out_shape=[shape for _, shape in flat_out],
        scratch_shapes=scratch + [pltpu.SemaphoreType.DMA((copies,))],
        compiler_params=pltpu.CompilerParams(vmem_limit_bytes=56 * 1024 * 1024),
        cost_estimate=pl.CostEstimate(
            flops=0, bytes_accessed=moved, transcendentals=0
        ),
    )(*[x for _, x in flat_in])
    return jax.tree.unflatten(tree_out, found)


def shape_of(dims, dtype):
    return jax.ShapeDtypeStruct(tuple(dims), dtype)


def over_slow(value, slow, fast):
    groups = [[k * fast + b for k in range(slow)] for b in range(fast)]
    return lax.all_to_all(value, "fsdp", 0, 0, axis_index_groups=groups, tiled=True)


class Gather:
    def __init__(self, half, slow, fast):
        self.half, self.slow, self.fast = half, slow, fast

    def send_slow(self, *others):
        half = after(self.half, *others)
        self.came = [half] + [swap(half, "fsdp", k * self.fast) for k in range(1, self.slow)]

    def send_fast(self, *others):
        self.near = jnp.stack([after(piece, *others) for piece in self.came])
        self.near_other = swap(self.near, "mem", 1)
        self.far = [swap(self.near, "fsdp", b) for b in range(1, self.fast)]

    def whole(self):
        mine = [self.near] + self.far
        theirs = [self.near_other] + [swap(piece, "mem", 1) for piece in self.far]
        return mine, theirs

    @staticmethod
    def refs(weights):
        return [[(ANY, x) for x in some] for some in weights]


class Scatter:
    def __init__(self, grads, slow, fast, *others, vectors=None):
        self.near, self.far, theirs = grads
        self.slow, self.fast, self.vectors = slow, fast, vectors
        theirs = [after(part, *others) for part in theirs]
        far = [swap(part, "mem", 1) for part in theirs[1:]]
        far = [jnp.concatenate(far[2 * b : 2 * b + 2]) for b in range(fast - 1)]
        self.sent = [swap(theirs[0], "mem", 1)] + far
        if vectors is not None:
            self.vectors = vectors.astype(F32) + swap(vectors, "mem", 1).astype(F32)

    def add_cores(self, *others):
        far = after(self.far, *others)
        self.out = [
            (far[b].astype(F32) + self.sent[b + 1].astype(F32)).astype(BF)
            for b in range(self.fast - 1)
        ]
        return self.out

    def send_fast(self):
        self.came = [swap(part, "fsdp", b + 1) for b, part in enumerate(self.out)]
        if self.vectors is not None:
            low = self.vectors.astype(BF)
            self.vectors = [low] + [swap(low, "fsdp", b) for b in range(1, self.fast)]

    def add_fast(self, *others):
        if self.vectors is not None:
            self.vectors, self.came = lax.optimization_barrier((self.vectors, self.came))
            self.vectors = sum(part.astype(F32) for part in self.vectors)
        total = after(self.near, *others).astype(F32) + self.sent[0].astype(F32)
        for part in self.came:
            total = total + part.astype(F32)
        self.total = total.astype(BF).reshape(self.slow, -1, total.shape[-1])
        if self.vectors is not None:
            low = self.vectors.astype(BF)
            low = jnp.broadcast_to(low, (self.slow,) + low.shape)
            self.total = jnp.concatenate([self.total, low], axis=1)
        return self.total

    def send_slow(self):
        self.came = over_slow(self.total, self.slow, self.fast)

    def add_slow(self, *others):
        return jnp.sum(after(self.came, *others).astype(F32), axis=0)


class Replicas:
    def __init__(self, value, rows, across):
        self.rows = rows
        k = 1
        while 2 * k < across:
            low = value.astype(BF)
            value = low.astype(F32) + swap(low, "mem", 2 * k).astype(F32)
            k *= 2
        low = value.astype(BF)
        self.halves = [low, swap(low, "mem", 2 * k)] if across > 1 else [low]

    def swap_cores(self, *others):
        halves, _ = lax.optimization_barrier((self.halves, others))
        self.others = [swap(half[: 2 * self.rows], "mem", 1) for half in halves]

    def combine(self, c):
        rows = self.rows
        other = sum(half.astype(F32) for half in self.others)
        mine = sum(half.astype(F32) for half in self.halves)
        vectors, mine = mine[2 * rows :], mine[: 2 * rows]
        first = jnp.where(c == 0, mine, other)
        second = jnp.where(c == 0, other, mine)
        return [first[:rows], first[rows:], second[:rows], second[rows:]], vectors


def place_rows(where, blocks, outs, scratch, sems):
    copies = Copies(sems)
    loads = []
    for i, (even, odd) in enumerate(blocks):
        for d, piece in enumerate(even):
            loads.append((copies.start(piece, scratch.at[i, 2 * d]), i, 2 * d))
            loads.append((copies.start(odd.at[d], scratch.at[i, 2 * d + 1]), i, 2 * d + 1))
    examples = scratch.shape[2]
    stores = []
    for load, i, d in loads:
        load.wait()
        target = outs[i].at[pl.ds((where[3] ^ d) * examples, examples)]
        stores.append(copies.start(scratch.at[i, d], target))
    wait_all(stores)


def place_memory(where, pieces, out, scratch, sems):
    examples = pieces[0].shape[0]
    copies = Copies(sems)
    loads = [copies.start(piece, scratch.at[d]) for d, piece in enumerate(pieces)]
    stores = []
    for d, load in enumerate(loads):
        load.wait()
        target = out.at[pl.ds((where[3] ^ d) * examples, examples)]
        stores.append(copies.start(scratch.at[d], target))
    wait_all(stores)


def spread_across(value, mem):
    return [value] + [swap(value, "mem", d) for d in range(2, mem, 2)]


def per_device(
    suffix,
    memory,
    counts,
    cotangent,
    self_norm_gain,
    self_norm_bias,
    self_query,
    self_key,
    self_value,
    self_output,
    cross_norm_gain,
    cross_norm_bias,
    cross_query,
    cross_key,
    cross_value,
    cross_output,
    dense_norm_gain,
    dense_norm_bias,
    dense_in,
    dense_in_bias,
    dense_out,
    dense_out_bias,
):
    f = lax.axis_index("fsdp")
    m = lax.axis_index("mem")
    c = m % 2
    fsdp = lax.axis_size("fsdp")
    mem = lax.axis_size("mem")
    across = mem // 2
    slow, fast = fsdp_split(fsdp)
    SHARDS[0] = fsdp
    where = jnp.stack([f // fast, f % fast, c, m]).astype(jnp.int32)
    examples = suffix.shape[0] // mem
    length = suffix.shape[1]
    width = suffix.shape[2]
    slots = memory.shape[1]
    total = mem * slots
    rows = examples * length
    inner = dense_in.shape[1]
    part = width // fsdp
    group = min(128, rows)
    blocks = 4 * fsdp

    def gather(matrices, *others):
        halves = [jnp.concatenate(matrices[:2]), jnp.concatenate(matrices[2:])]
        half = jnp.concatenate([jnp.where(c == 0, *halves), *others])
        return Gather(half, slow, fast)

    cross_gather = gather([cross_query, cross_key, cross_value, cross_output])
    in_gather = gather([dense_in[:, columns(j, width)] for j in range(4)])
    out_gather = gather([dense_out[columns(j, part)] for j in range(4)])
    small = [
        self_norm_gain,
        self_norm_bias,
        cross_norm_gain,
        cross_norm_bias,
        dense_norm_gain,
        dense_norm_bias,
        dense_out_bias,
    ]
    small += [dense_in_bias[columns(j, part)] for j in range(4)]
    small = sum(
        jnp.pad(value[None], ((i, 15 - i), (0, width - part))) for i, value in enumerate(small)
    )
    self_gather = gather([self_query, self_key, self_value, self_output], small)

    def exchange(value):
        blocks = value.reshape((mem, examples) + value.shape[1:])
        return lax.all_to_all(blocks, "mem", 0, 0, tiled=True)

    all_memory = exchange(memory)
    self_gather.send_slow()
    sent = self_gather.came
    self_gather.send_fast(*sent)
    cross_gather.send_slow(*sent)
    sent = [*self_gather.far, *cross_gather.came, all_memory]
    self_gather.far = [after(piece, *sent) for piece in self_gather.far]
    self_weights = self_gather.whole()
    cross_gather.send_fast(*self_gather.far)
    in_gather.send_slow(*self_gather.far)

    half = (2, part, width)
    grads_like = [
        (ANY, shape_of((slow,) + half, BF)),
        (ANY, shape_of((fast - 1, slow) + half, BF)),
        [(ANY, shape_of((slow,) + half, BF))]
        + [(ANY, shape_of((slow // 2,) + half, BF))] * (2 * fast - 2),
    ]

    def flat(dims, dtype):
        return (VMEM, shape_of(dims, dtype))

    per = 2 if examples % 2 == 0 else 1

    def per_example(value):
        dims = value.shape[1:]
        spec = pl.BlockSpec((per,) + dims, lambda e: (e,) + (0,) * len(dims))
        return (spec, value)

    def slots_of_example(value):
        spec = pl.BlockSpec((mem, per, slots, width), lambda e: (0, e, 0, 0))
        return (spec, value)

    def scratch(*dims):
        return pltpu.VMEM(dims, BF)

    def scatter(grads, *others, vectors=None):
        return Scatter(grads, slow, fast, *others, vectors=vectors)

    wide = (rows, width)
    square = scratch(4, width, width)
    own_rows = scratch(examples, length, width)
    x1, a1, qkv, p1, o1, vec = run(
        functools.partial(self_forward, group),
        [(SMEM, where), (ANY, suffix), Gather.refs(self_weights)],
        [
            flat(wide, F32),
            flat(wide, BF),
            flat((rows, 3 * width), BF),
            flat((rows // group * GROUPS, TOGETHER * group, group), BF),
            flat(wide, BF),
            flat((16, width), F32),
        ],
        [square, own_rows, scratch(fsdp, 16, 128)],
        1 + fsdp + blocks,
    )
    cross_gather.far = [after(piece, x1, *in_gather.came) for piece in cross_gather.far]
    cross_weights = Gather.refs(cross_gather.whole())
    in_gather.send_fast(*cross_gather.far)
    out_gather.send_slow(*cross_gather.far)
    x2, a2, q2, kv, p2, o2 = run(
        cross_forward,
        [(SMEM, where), (SMEM, counts), (VMEM, x1), (VMEM, vec)]
        + [slots_of_example(all_memory), cross_weights],
        [
            flat(wide, F32),
            flat(wide, BF),
            flat(wide, BF),
            per_example(shape_of((examples, total, 2 * width), BF)),
            per_example(shape_of((examples, GROUPS, TOGETHER * length, total), BF)),
            flat(wide, BF),
        ],
        [square],
        blocks,
        (examples // per,),
    )
    small = [after(piece, x1)[:, 2 * part + 7 : 2 * part + 11, :part] for piece in self_weights[0]]
    order = jnp.arange(fsdp) ^ f
    bias_in = jnp.take(jnp.concatenate(small), order % fast * slow + order // fast, axis=0)
    bias_in = bias_in.astype(F32).reshape(1, inner)
    in_gather.far = [after(piece, x2, *out_gather.came) for piece in in_gather.far]
    in_weights = Gather.refs(in_gather.whole())
    out_gather.send_fast(*in_gather.far)
    a3, h, slope, *grads = run(
        dense_inner,
        [(SMEM, where), (VMEM, x2), (VMEM, vec), (VMEM, bias_in), (ANY, cotangent), in_weights],
        [flat(wide, BF), flat((rows, inner), BF), flat((rows, inner), BF)] + grads_like,
        [square, scratch(fsdp, 4, part, width), own_rows],
        1 + blocks,
    )
    out_gather.far = [after(piece, a3) for piece in out_gather.far]
    out_weights = Gather.refs(out_gather.whole())
    out_scatter = scatter(grads, *out_gather.far)
    out_sum = out_scatter.add_cores()
    out_scatter.send_fast()
    y, du, vecs_y, bias_grad, *grads = run(
        dense_outer,
        [(SMEM, where), (VMEM, after(x2, *out_sum)), (VMEM, vec), (VMEM, a3), (VMEM, h)]
        + [(VMEM, slope), (ANY, cotangent), out_weights],
        [
            flat((examples, length, width), BF),
            flat((rows, inner), BF),
            flat((1, width), F32),
            flat((1, inner), F32),
        ]
        + grads_like,
        [scratch(fsdp, 4, part, width), square, own_rows],
        1 + blocks,
    )
    in_grads = grads
    gx2, vecs_dense = run(
        dense_back,
        [(SMEM, where), (VMEM, x2), (VMEM, vec), (VMEM, du), (ANY, cotangent), in_weights],
        [flat(wide, F32), flat((2, width), F32)],
        [square, own_rows],
        1 + blocks,
    )
    in_scatter = scatter(in_grads, gx2)
    in_sum = in_scatter.add_cores(*out_scatter.came)
    in_scatter.send_fast()
    gx1, vecs_cross, dkv, dq2, grad_memory = run(
        cross_backward,
        [(SMEM, where), (VMEM, x1), (VMEM, vec), (VMEM, after(gx2, *in_sum)), (VMEM, q2)]
        + [per_example(kv), per_example(p2), cross_weights],
        [
            flat(wide, F32),
            flat((2, width), F32),
            per_example(shape_of((examples, total, 2 * width), BF)),
            flat(wide, BF),
            [per_example(shape_of((examples, slots, width), BF))] * mem,
        ],
        [square, scratch(*wide), scratch(per, total, width)],
        blocks,
        (examples // per,),
        60_000_000,
    )
    in_scatter.came, _ = lax.optimization_barrier((in_scatter.came, gx1))
    dense_total = [one.add_fast(*in_scatter.came) for one in (out_scatter, in_scatter)]
    dense_total = jnp.concatenate(dense_total, axis=1)
    dense_came = over_slow(dense_total, slow, fast)
    mem_pieces = grad_memory[:1] + [swap(grad_memory[d], "mem", d) for d in range(1, mem)]
    grads = run(
        cross_grads,
        [(SMEM, where), (VMEM, after(gx2, dense_total)), (VMEM, a2), (VMEM, o2), (VMEM, dq2)]
        + [(pl.BlockSpec((examples, total, width), lambda j: (0, 0, j)), dkv), (ANY, all_memory)],
        grads_like,
        [square, scratch(width, examples * total), scratch(examples, total, width)],
        max(mem, blocks),
        (2,),
    )
    cross_scatter = scatter(grads, *mem_pieces[1:3])
    cross_sum = cross_scatter.add_cores()
    cross_scatter.send_fast()
    gx1 = after(gx1, *cross_sum)
    suffix_part, vecs_self, *grads = run(
        functools.partial(self_backward, group),
        [(SMEM, where), (ANY, suffix), (VMEM, vec), (VMEM, gx1), (VMEM, a1)]
        + [(VMEM, qkv), (VMEM, p1), (VMEM, o1)]
        + [[(VMEM, x) for x in (vecs_cross, vecs_dense, vecs_y, bias_grad)], Gather.refs(self_weights)],
        [flat((examples, length, width), BF), flat((16, width), BF)] + grads_like,
        [square, own_rows, square, scratch(rows, 3 * width), scratch(*wide)],
        1 + blocks,
    )
    self_scatter = scatter(grads, *mem_pieces[3:4], vectors=vecs_self)
    self_sum = self_scatter.add_cores()
    self_scatter.send_fast()
    cross_scatter.add_fast(*self_sum)
    cross_scatter.send_slow()
    dense_sum = jnp.sum(after(dense_came, *self_sum).astype(F32), axis=0)
    dense_sum = Replicas(dense_sum, 2 * part, across)
    self_total = self_scatter.add_fast(*dense_sum.halves)
    self_scatter.send_slow()
    cross_sum = Replicas(cross_scatter.add_slow(self_total), part, across)
    suffix_rows = spread_across(after(suffix_part, self_total), mem)
    y_rows = spread_across(after(y, self_total), mem)
    dense_sum.swap_cores(self_total)
    mem_pieces = [after(value, self_total) for value in mem_pieces]
    (memory_grad,) = run(
        place_memory,
        [(SMEM, where), [(ANY, value) for value in mem_pieces]],
        [(ANY, shape_of(memory.shape, BF))],
        [scratch(mem, examples, slots, width)],
        2 * mem,
    )
    (out_low, in_low, out_high, in_high), _ = dense_sum.combine(c)
    grad_in = jnp.concatenate([in_low[:part], in_low[part:], in_high[:part], in_high[part:]], axis=1)
    grad_out = jnp.concatenate([out_low, out_high])
    done = [*cross_sum.halves, *suffix_rows, *y_rows, grad_in, grad_out, memory_grad]
    self_final = Replicas(self_scatter.add_slow(*done), part, across)
    cross_sum.swap_cores(self_final.halves[0])
    y_rows = [after(value, self_final.halves[0]) for value in y_rows]
    y_far = swap(jnp.stack(y_rows), "mem", 1)
    suffix_rows = [after(value, self_final.halves[0]) for value in suffix_rows]
    suffix_far = swap(jnp.stack(suffix_rows), "mem", 1)
    blocks = [([(ANY, x) for x in y_rows], (ANY, y_far))]
    blocks += [([(ANY, x) for x in suffix_rows], (ANY, suffix_far))]
    ((block_output, suffix_grad),) = run(
        place_rows,
        [(SMEM, where), blocks],
        [[(ANY, shape_of(suffix.shape, BF))] * 2],
        [scratch(2, mem, examples, length, width)],
        4 * mem,
    )
    grad_cross, _ = cross_sum.combine(c)
    self_final.swap_cores(block_output)
    grad_self, vectors = self_final.combine(c)

    def vector(i):
        return lax.dynamic_slice(vectors, (i, f * part), (1, part)).reshape(part)

    return (
        block_output,
        suffix_grad,
        memory_grad,
        vector(0),
        vector(1),
        *grad_self,
        vector(2),
        vector(3),
        *grad_cross,
        vector(4),
        vector(5),
        grad_in,
        lax.dynamic_slice_in_dim(vectors[7:11].reshape(-1), f * (inner // fsdp), inner // fsdp, 0),
        grad_out,
        vector(6),
    )


def solution(mesh):
    rows = P("fsdp", None, None)
    matrix = P("fsdp", None)
    vector = P("fsdp")
    attention = (vector, vector, matrix, matrix, matrix, matrix)
    params = attention + attention + (vector, vector, matrix, vector, matrix, vector)
    return jax.shard_map(
        per_device,
        mesh=mesh,
        in_specs=(rows, P("fsdp", "mem", None), vector, rows) + params,
        out_specs=(rows, rows, P("fsdp", "mem", None)) + params,
        check_vma=False,
    )
```

```python
import functools

import jax
import jax.numpy as jnp
from jax import lax
from jax.experimental import pallas as pl
from jax.experimental.pallas import tpu as pltpu
from jax.sharding import PartitionSpec as P

HEADS = 12
HEAD = 64
TOGETHER = 4
GROUPS = HEADS // TOGETHER
LANES = TOGETHER * HEAD
SCALE = HEAD ** (-0.5)
BF = jnp.bfloat16
F32 = jnp.float32
ANY = pl.BlockSpec(memory_space=pl.ANY)
SMEM = pl.BlockSpec(memory_space=pltpu.SMEM)
VMEM = pl.BlockSpec(memory_space=pltpu.VMEM)


def swap(value, axis, distance):
    size = lax.axis_size(axis)
    return lax.ppermute(value, axis, [(i, i ^ distance) for i in range(size)])


def after(value, *others):
    return lax.optimization_barrier((value, *others))[0] if others else value


def fsdp_split(size):
    slow = 4 if size % 4 == 0 else 1
    return slow, size // slow


def dot(left, right):
    return jnp.dot(left, right, preferred_element_type=F32)


def dot_nt(left, right):
    return lax.dot_general(left, right, (((1,), (1,)), ((), ())), preferred_element_type=F32)


def dot_tn(left, right):
    return lax.dot_general(left, right, (((0,), (0,)), ((), ())), preferred_element_type=F32)


def rows_of(start, size):
    return pl.ds(pl.multiple_of(start, 16), size)


def block(ref, by_rows, shard, which):
    if by_rows:
        return ref.at[shard, pl.ds(which * 2, 2)]
    rows = ref.shape[1] // SHARDS[0]
    return ref.at[pl.ds(which * 2, 2), rows_of(shard * rows, rows)]


SHARDS = [0]


class Copies:
    def __init__(self, sems):
        self.sems = sems
        self.next = 0

    def start(self, source, target):
        copy = pltpu.make_async_copy(source, target, self.sems.at[self.next])
        self.next += 1
        copy.start()
        return copy


def wait_all(copies):
    for copy in copies:
        copy.wait()


def load_weight(where, whole, weights, copies, by_rows=False):
    z, y, c = where[0], where[1], where[2]
    rows = whole.shape[2] if by_rows else whole.shape[1] // SHARDS[0]
    started = []
    for which, pieces in ((c, weights[0]), (1 - c, weights[1])):
        slow = 4 if SHARDS[0] % 4 == 0 else 1
        fast = SHARDS[0] // slow
        for b, k in [(b, k) for b in range(fast) for k in range(slow)]:
            shard = (z ^ k) * fast + (y ^ b)
            first = slow - pieces[b].shape[0]
            piece = pieces[b].at[k - first] if k >= first else pieces[fast + b]
            for i in range(2):
                source = piece.at[pl.ds(i * rows, rows)]
                if by_rows:
                    target = whole.at[shard, 2 * which + i]
                else:
                    target = whole.at[2 * which + i, rows_of(shard * rows, rows)]
                started.append(copies.start(source, target))
    return started


def store_grad(where, whole, near, far, theirs, copies, by_rows=False):
    y, c = where[1], where[2]
    slow, cut = near.shape[0], near.shape[0] // 2
    fast = (len(theirs) + 1) // 2
    started = []
    for b in range(fast):
        for k in range(slow):
            shard = k * fast + (y ^ b)
            mine = far.at[b - 1, k] if b else near.at[k]
            other = theirs[2 * b - 1 + k // cut].at[k % cut] if b else theirs[0].at[k]
            started.append(copies.start(block(whole, by_rows, shard, 1 - c), other))
            started.append(copies.start(block(whole, by_rows, shard, c), mine))
    return started


def my_examples(where, source, target, copies):
    count = target.shape[0]
    return copies.start(source.at[pl.ds(where[3] * count, count)], target)


def normalise(values):
    centred = values - jnp.mean(values, axis=-1, keepdims=True)
    scale = lax.rsqrt(jnp.mean(centred * centred, axis=-1, keepdims=True) + 1e-06)
    return centred * scale, scale


def norm_back(grad, gain, hat, scale):
    inner = grad * gain
    mean = jnp.mean(inner, axis=-1, keepdims=True)
    along = jnp.mean(inner * hat, axis=-1, keepdims=True)
    return (
        scale * (inner - mean - hat * along),
        jnp.sum(grad * hat, axis=0, keepdims=True),
        jnp.sum(grad, axis=0, keepdims=True),
    )


def head_mask(rows):
    shape = (TOGETHER * rows, LANES)
    row = lax.broadcasted_iota(jnp.int32, shape, 0) // rows
    lane = lax.broadcasted_iota(jnp.int32, shape, 1) // HEAD
    return (row == lane).astype(F32)


def stack_heads(value, mask):
    return (jnp.concatenate([value] * TOGETHER, axis=0).astype(F32) * mask).astype(BF)


def merge_heads(value, mask):
    rows = value.shape[0] // TOGETHER
    value = value * mask
    total = value[:rows]
    for h in range(1, TOGETHER):
        total = total + value[h * rows : (h + 1) * rows]
    return total


def columns(j, width):
    return slice(j * width, (j + 1) * width)


def self_forward(
    group, where, suffix, weights, x1, a1, qkv, p1, o1, vec, weight, start, small, sems
):
    rows, width = x1.shape
    copies = Copies(sems)
    first = my_examples(where, suffix, start, copies)
    fast, slow = len(weights[0]), weights[0][0].shape[0]
    part = width // (fast * slow)
    vectors = []
    for b, piece in enumerate(weights[0]):
        for k in range(slow):
            source = piece.at[k, pl.ds(2 * part, 16), pl.ds(0, 128)]
            vectors.append(copies.start(source, small.at[b * slow + k]))
    loads = load_weight(where, weight, weights, copies)
    wait_all(vectors)
    lane = lax.broadcasted_iota(jnp.int32, (128, width), 0)
    place = lax.broadcasted_iota(jnp.int32, (128, width), 1) - lane
    together = jnp.zeros(vec.shape, F32)
    for i in range(fast * slow):
        shard = (where[0] ^ (i % slow)) * fast + (where[1] ^ (i // slow))
        chosen = ((place == shard * part) & (lane < part)).astype(F32).astype(BF)
        together = together + dot(small[i], chosen)
    vec[...] = together
    first.wait()
    values = start[...].reshape(rows, width).astype(F32)
    hat, _ = normalise(values)
    a1[...] = (hat * vec[0:1, :] + vec[1:2, :]).astype(BF)
    wait_all(loads)
    for j in range(3):
        qkv[:, columns(j, width)] = dot(a1[...], weight[j]).astype(BF)
    mask = head_mask(group)
    length = suffix.shape[1]
    shape = (TOGETHER * group, group)
    row = lax.broadcasted_iota(jnp.int32, shape, 0) % group
    col = lax.broadcasted_iota(jnp.int32, shape, 1)
    seen = (row // length == col // length) & (row >= col)
    for r in range(rows // group):
        here = columns(r, group)
        for g in range(GROUPS):
            lanes = [slice(i * width + g * LANES, i * width + (g + 1) * LANES) for i in range(3)]
            queries = stack_heads(qkv[here, lanes[0]], mask)
            scores = dot_nt(queries, qkv[here, lanes[1]]) * SCALE
            scores = jnp.where(seen, scores, -1e30)
            powers = jnp.exp(scores - jnp.max(scores, axis=-1, keepdims=True))
            probs = (powers / jnp.sum(powers, axis=-1, keepdims=True)).astype(BF)
            p1[r * GROUPS + g] = probs
            found = dot(probs, qkv[here, lanes[2]])
            o1[here, lanes[0]] = merge_heads(found, mask).astype(BF)
    x1[...] = values + dot(o1[...], weight[3])


def cross_forward(
    where, counts, x1, vec, memory, weights, x2, a2, q2, kv, p2, o2, turned, weight, sems
):
    rows, width = x1.shape
    per = kv.shape[0]
    step = pl.program_id(0)
    total = kv.shape[1]
    length = p2.shape[2] // TOGETHER

    @pl.when(step == 0)
    def _():
        loads = load_weight(where, weight, weights, Copies(sems))
        hat, _ = normalise(x1[...])
        a2[...] = (hat * vec[2:3, :] + vec[3:4, :]).astype(BF)
        wait_all(loads)
        q2[...] = dot(a2[...], weight[0]).astype(BF)

    for i in range(per):
        tokens = memory[:, i].reshape(total, width)
        for j in range(2):
            kv[i, :, columns(j, width)] = dot(tokens, weight[1 + j]).astype(BF)
        turned[:, columns(i, total)] = tokens.T
    mask = head_mask(length)
    position = lax.broadcasted_iota(jnp.int32, (1, total), 1)
    probs = {}
    for i in range(per):
        e = step * per + i
        valid = position < counts[where[3] * (pl.num_programs(0) * per) + e]
        here = rows_of(e * length, length)
        for g in range(GROUPS):
            lanes = columns(g, LANES)
            queries = stack_heads(q2[here, lanes], mask)
            scores = dot_nt(queries, kv[i, :, lanes]) * SCALE
            scores = jnp.where(valid, scores, -1e30)
            top = jnp.maximum(jnp.max(scores, axis=-1, keepdims=True), 0.0)
            powers = jnp.exp(scores - top)
            weight_sum = jnp.sum(powers, axis=-1, keepdims=True) + jnp.exp(-top)
            probs[i, g] = (powers / weight_sum).astype(BF)
    for i in range(per):
        here = rows_of((step * per + i) * length, length)
        for g in range(GROUPS):
            p2[i, g] = probs[i, g]
            found = dot(probs[i, g], kv[i, :, width + g * LANES : width + (g + 1) * LANES])
            o2[here, columns(g, LANES)] = merge_heads(found, mask).astype(BF)

    @pl.when(step == pl.num_programs(0) - 1)
    def _():
        x2[...] = x1[...] + dot(o2[...], weight[3])


def dense_inner(
    where, x2, vec, bias, cotangent, weights, a3, h, slope, near, far, theirs,
    weight, grad, cot, sems,
):
    rows, width = x2.shape
    copies = Copies(sems)
    cot_copy = my_examples(where, cotangent, cot, copies)
    loads = load_weight(where, weight, weights, copies)
    hat, _ = normalise(x2[...])
    a3[...] = (hat * vec[4:5, :] + vec[5:6, :]).astype(BF)
    cot_copy.wait()
    gy = cot[...].reshape(rows, width)
    wait_all(loads)
    flat = grad.shape[0] * grad.shape[1] * grad.shape[2]
    step = flat // grad.shape[0]
    for j in range(4):
        for half in range(2):
            cols = slice(j * width + half * 384, j * width + (half + 1) * 384)
            u = dot(a3[...], weight[j, :, half * 384 : (half + 1) * 384]) + bias[:, cols]
            square = u * u
            t = jnp.tanh(0.7978845608 * u * (1.0 + 0.044715 * square))
            h[:, cols] = (0.5 * u * (1.0 + t)).astype(BF)
            slope[:, cols] = (
                0.5 * (1.0 + t)
                + (0.5 * 0.7978845608) * u * (1.0 - t * t) * (1.0 + (3.0 * 0.044715) * square)
            ).astype(BF)
            part = dot_tn(h[:, cols], gy).astype(BF)
            per = 384 // step
            grad[cols.start // step : cols.start // step + per] = part.reshape(
                (per,) + grad.shape[1:]
            )
    wait_all(store_grad(where, grad, near, far, theirs, Copies(sems), True))


def dense_outer(
    where, x2, vec, a3, h, slope, cotangent, weights, y, du, vecs, bias_grad, near, far, theirs,
    weight, grad, cot, sems,
):
    rows, width = x2.shape
    copies = Copies(sems)
    cot_copy = my_examples(where, cotangent, cot, copies)
    wait_all(load_weight(where, weight, weights, copies, True))
    cot_copy.wait()
    gy = cot[...].reshape(rows, width)
    shards = weight.shape[0]
    step = weight.shape[1] * weight.shape[2]
    whole = weight[...].reshape(shards * step, width)
    for j in range(4):
        cols = columns(j, width)
        low = (dot_nt(gy, whole[cols]) * slope[:, cols].astype(F32)).astype(BF)
        du[:, cols] = low
        bias_grad[:, cols] = jnp.sum(low.astype(F32), axis=0, keepdims=True)
        grad[j] = dot_tn(a3[...], low).astype(BF)
    started = store_grad(where, grad, near, far, theirs, Copies(sems))
    result = x2[...] + dot(h[...], whole) + vec[6:7, :]
    y[...] = result.astype(BF).reshape(y.shape)
    vecs[...] = jnp.sum(gy.astype(F32), axis=0, keepdims=True)
    wait_all(started)


def dense_back(where, x2, vec, du, cotangent, weights, gx2, vecs, weight, cot, sems):
    rows, width = x2.shape
    copies = Copies(sems)
    cot_copy = my_examples(where, cotangent, cot, copies)
    loads = load_weight(where, weight, weights, copies)
    hat, scale = normalise(x2[...])
    cot_copy.wait()
    wait_all(loads)
    da3 = dot_nt(du[:, columns(0, width)], weight[0])
    for j in range(1, 4):
        da3 = da3 + dot_nt(du[:, columns(j, width)], weight[j])
    back, gain_grad, shift_grad = norm_back(da3, vec[4:5, :], hat, scale)
    gx2[...] = cot[...].reshape(rows, width).astype(F32) + back
    vecs[0:1, :] = gain_grad
    vecs[1:2, :] = shift_grad


def cross_backward(
    where, x1, vec, gx2, q2, kv, p2, weights, gx1, vecs, dkv, dq2, out_mem, weight, do2, moved, sems
):
    rows, width = x1.shape
    per, total = kv.shape[0], kv.shape[1]
    step = pl.program_id(0)
    length = p2.shape[2] // TOGETHER

    @pl.when(step == 0)
    def _():
        wait_all(load_weight(where, weight, weights, Copies(sems)))
        do2[...] = dot_nt(gx2[...].astype(BF), weight[3]).astype(BF)

    mask = head_mask(length)
    pairs = [(i, g) for i in range(per) for g in range(GROUPS)]
    queries, grads, dz = {}, {}, {}
    for i, g in pairs:
        here = rows_of((step * per + i) * length, length)
        lanes = columns(g, LANES)
        queries[i, g] = stack_heads(q2[here, lanes], mask)
        grads[i, g] = stack_heads(do2[here, lanes], mask)
        dp = dot_nt(grads[i, g], kv[i, :, width + g * LANES : width + (g + 1) * LANES])
        wide = p2[i, g].astype(F32)
        row_sum = jnp.sum(wide * dp, axis=-1, keepdims=True)
        dz[i, g] = (wide * (dp - row_sum)).astype(BF)
    for i, g in pairs:
        here = rows_of((step * per + i) * length, length)
        lanes = columns(g, LANES)
        value_lanes = slice(width + g * LANES, width + (g + 1) * LANES)
        dkv[i, :, value_lanes] = dot_tn(p2[i, g], grads[i, g]).astype(BF)
        dkv[i, :, lanes] = (dot_tn(dz[i, g], queries[i, g]) * SCALE).astype(BF)
        dq = merge_heads(dot(dz[i, g], kv[i, :, lanes]), mask) * SCALE
        dq2[here, lanes] = dq.astype(BF)
    for i in range(per):
        back = dot_nt(dkv[i, :, :width], weight[1]) + dot_nt(dkv[i, :, width:], weight[2])
        moved[i] = back.astype(BF)
        for d, out in enumerate(out_mem):
            slots = out.shape[1]
            out[i] = moved[i, rows_of((where[3] ^ d) * slots, slots), :]

    @pl.when(step == pl.num_programs(0) - 1)
    def _():
        hat, scale = normalise(x1[...])
        back, gain_grad, shift_grad = norm_back(
            dot_nt(dq2[...], weight[0]), vec[2:3, :], hat, scale
        )
        gx1[...] = gx2[...] + back
        vecs[0:1, :] = gain_grad
        vecs[1:2, :] = shift_grad


def cross_grads(where, gx2, a2, o2, dq2, dkv, turned, near, far, theirs, grad, memory, sems):
    width = gx2.shape[1]
    half = pl.program_id(0)

    @pl.when(half == 0)
    def _():
        load = Copies(sems).start(turned, memory)
        grad[0] = dot_tn(a2[...], dq2[...]).astype(BF)
        grad[3] = dot_tn(o2[...], gx2[...].astype(BF)).astype(BF)
        load.wait()

    part = dkv[...].reshape(memory.shape[1], width)
    grad[1 + half] = dot(memory[...], part).astype(BF)

    @pl.when(half == 1)
    def _():
        wait_all(store_grad(where, grad, near, far, theirs, Copies(sems)))


def self_backward(
    group, where, suffix, vec, gx1, a1, qkv, p1, o1, parts, weights, suffix_grad, vecs,
    near, far, theirs, weight, start, grad, dqkv, do1, sems,
):
    rows, width = gx1.shape
    copies = Copies(sems)
    start_copy = my_examples(where, suffix, start, copies)
    loads = load_weight(where, weight, weights, copies)
    gs = gx1[...].astype(BF)
    grad[3] = dot_tn(o1[...], gs).astype(BF)
    wait_all(loads)
    do1[...] = dot_nt(gs, weight[3]).astype(BF)
    mask = head_mask(group)
    for r in range(rows // group):
        here = columns(r, group)
        for g in range(GROUPS):
            lanes = [slice(i * width + g * LANES, i * width + (g + 1) * LANES) for i in range(3)]
            queries = stack_heads(qkv[here, lanes[0]], mask)
            grads = stack_heads(do1[here, lanes[0]], mask)
            probs = p1[r * GROUPS + g]
            dp = dot_nt(grads, qkv[here, lanes[2]])
            wide = probs.astype(F32)
            row_sum = jnp.sum(wide * dp, axis=-1, keepdims=True)
            dz = (wide * (dp - row_sum)).astype(BF)
            dqkv[here, lanes[2]] = dot_tn(probs, grads).astype(BF)
            dqkv[here, lanes[1]] = (dot_tn(dz, queries) * SCALE).astype(BF)
            dq = merge_heads(dot(dz, qkv[here, lanes[1]]), mask) * SCALE
            dqkv[here, lanes[0]] = dq.astype(BF)
    for j in range(3):
        grad[j] = dot_tn(a1[...], dqkv[:, columns(j, width)]).astype(BF)
    start_copy.wait()
    started = store_grad(where, grad, near, far, theirs, Copies(sems))
    da1 = dot_nt(dqkv[:, columns(0, width)], weight[0])
    for j in range(1, 3):
        da1 = da1 + dot_nt(dqkv[:, columns(j, width)], weight[j])
    hat, scale = normalise(start[...].reshape(rows, width).astype(F32))
    back, gain_grad, shift_grad = norm_back(da1, vec[0:1, :], hat, scale)
    suffix_grad[...] = (gx1[...] + back).astype(BF).reshape(suffix_grad.shape)
    found = [gain_grad, shift_grad]
    for ref in parts:
        for r in range(ref.shape[0]):
            found += [ref[r : r + 1, columns(j, width)] for j in range(ref.shape[1] // width)]
    found.append(jnp.zeros((vecs.shape[0] - len(found), width), F32))
    vecs[...] = jnp.concatenate(found, axis=0).astype(BF)
    wait_all(started)


def run(kernel, inputs, outputs, scratch, copies, grid=(), moved=0):
    def leaf(x):
        return isinstance(x, tuple) and len(x) == 2 and isinstance(x[0], pl.BlockSpec)

    flat_in, tree_in = jax.tree.flatten(inputs, is_leaf=leaf)
    flat_out, tree_out = jax.tree.flatten(outputs, is_leaf=leaf)

    def body(*refs):
        first, second = len(flat_in), len(flat_in) + len(flat_out)
        given = jax.tree.unflatten(tree_in, refs[:first])
        taken = jax.tree.unflatten(tree_out, refs[first:second])
        kernel(*given, *taken, *refs[second:])

    found = pl.pallas_call(
        body,
        grid=grid,
        in_specs=[spec for spec, _ in flat_in],
        out_specs=[spec for spec, _ in flat_out],
        out_shape=[shape for _, shape in flat_out],
        scratch_shapes=scratch + [pltpu.SemaphoreType.DMA((copies,))],
        compiler_params=pltpu.CompilerParams(vmem_limit_bytes=56 * 1024 * 1024),
        cost_estimate=pl.CostEstimate(
            flops=0, bytes_accessed=moved, transcendentals=0
        ),
    )(*[x for _, x in flat_in])
    return jax.tree.unflatten(tree_out, found)


def shape_of(dims, dtype):
    return jax.ShapeDtypeStruct(tuple(dims), dtype)


def over_slow(value, slow, fast):
    groups = [[k * fast + b for k in range(slow)] for b in range(fast)]
    return lax.all_to_all(value, "fsdp", 0, 0, axis_index_groups=groups, tiled=True)


class Gather:
    def __init__(self, half, slow, fast):
        self.half, self.slow, self.fast = half, slow, fast
        self.own, self.own_other = [], []

    def send_slow(self, *others):
        half = after(self.half, *others)
        self.came = [half] + [swap(half, "fsdp", k * self.fast) for k in range(1, self.slow)]

    def send_own(self):
        self.own = [self.half] + [swap(self.half, "fsdp", b) for b in range(1, self.fast)]

    def send_own_cores(self, *others):
        self.own_other = [swap(after(piece, *others), "mem", 1) for piece in self.own]

    def send_fast(self, *others):
        came = [after(piece, *others) for piece in self.came[1 if self.own else 0 :]]
        self.near = jnp.stack(came)
        self.near_other = swap(self.near, "mem", 1)
        self.far = [swap(self.near, "fsdp", b) for b in range(1, self.fast)]

    def whole(self):
        mine = [self.near] + self.far
        theirs = [self.near_other] + [swap(piece, "mem", 1) for piece in self.far]
        return mine + self.own, theirs + self.own_other

    @staticmethod
    def refs(weights):
        return [[(ANY, x) for x in some] for some in weights]


class Scatter:
    def __init__(self, grads, slow, fast, *others, vectors=None):
        self.near, self.far, theirs = grads
        self.slow, self.fast, self.vectors = slow, fast, vectors
        theirs = [after(part, *others) for part in theirs]
        far = [swap(part, "mem", 1) for part in theirs[1:]]
        far = [jnp.concatenate(far[2 * b : 2 * b + 2]) for b in range(fast - 1)]
        self.sent = [swap(theirs[0], "mem", 1)] + far
        if vectors is not None:
            self.vectors = vectors.astype(F32) + swap(vectors, "mem", 1).astype(F32)

    def add_cores(self, *others):
        far = after(self.far, *others)
        self.out = [
            (far[b].astype(F32) + self.sent[b + 1].astype(F32)).astype(BF)
            for b in range(self.fast - 1)
        ]
        return self.out

    def send_fast(self):
        self.came = [swap(part, "fsdp", b + 1) for b, part in enumerate(self.out)]
        if self.vectors is not None:
            low = self.vectors.astype(BF)
            self.vectors = [low] + [swap(low, "fsdp", b) for b in range(1, self.fast)]

    def add_fast(self, *others):
        if self.vectors is not None:
            self.vectors, self.came = lax.optimization_barrier((self.vectors, self.came))
            self.vectors = sum(part.astype(F32) for part in self.vectors)
        total = after(self.near, *others).astype(F32) + self.sent[0].astype(F32)
        for part in self.came:
            total = total + part.astype(F32)
        self.total = total.astype(BF).reshape(self.slow, -1, total.shape[-1])
        if self.vectors is not None:
            low = self.vectors.astype(BF)
            low = jnp.broadcast_to(low, (self.slow,) + low.shape)
            self.total = jnp.concatenate([self.total, low], axis=1)
        return self.total

    def send_slow(self):
        self.came = over_slow(self.total, self.slow, self.fast)

    def add_slow(self, *others):
        return jnp.sum(after(self.came, *others).astype(F32), axis=0)


class Replicas:
    def __init__(self, value, rows, across):
        self.rows = rows
        k = 1
        while 2 * k < across:
            low = value.astype(BF)
            value = low.astype(F32) + swap(low, "mem", 2 * k).astype(F32)
            k *= 2
        low = value.astype(BF)
        self.halves = [low, swap(low, "mem", 2 * k)] if across > 1 else [low]

    def swap_cores(self, *others):
        halves, _ = lax.optimization_barrier((self.halves, others))
        self.others = [swap(half[: 2 * self.rows], "mem", 1) for half in halves]

    def combine(self, c):
        rows = self.rows
        other = sum(half.astype(F32) for half in self.others)
        mine = sum(half.astype(F32) for half in self.halves)
        vectors, mine = mine[2 * rows :], mine[: 2 * rows]
        first = jnp.where(c == 0, mine, other)
        second = jnp.where(c == 0, other, mine)
        return [first[:rows], first[rows:], second[:rows], second[rows:]], vectors


def place_rows(where, blocks, outs, scratch, sems):
    copies = Copies(sems)
    loads = []
    for i, (even, odd) in enumerate(blocks):
        for d, piece in enumerate(even):
            loads.append((copies.start(piece, scratch.at[i, 2 * d]), i, 2 * d))
            loads.append((copies.start(odd.at[d], scratch.at[i, 2 * d + 1]), i, 2 * d + 1))
    examples = scratch.shape[2]
    stores = []
    for load, i, d in loads:
        load.wait()
        target = outs[i].at[pl.ds((where[3] ^ d) * examples, examples)]
        stores.append(copies.start(scratch.at[i, d], target))
    wait_all(stores)


def place_memory(where, pieces, out, scratch, sems):
    examples = pieces[0].shape[0]
    copies = Copies(sems)
    loads = [copies.start(piece, scratch.at[d]) for d, piece in enumerate(pieces)]
    stores = []
    for d, load in enumerate(loads):
        load.wait()
        target = out.at[pl.ds((where[3] ^ d) * examples, examples)]
        stores.append(copies.start(scratch.at[d], target))
    wait_all(stores)


def spread_across(value, mem):
    return [value] + [swap(value, "mem", d) for d in range(2, mem, 2)]


def per_device(
    suffix,
    memory,
    counts,
    cotangent,
    self_norm_gain,
    self_norm_bias,
    self_query,
    self_key,
    self_value,
    self_output,
    cross_norm_gain,
    cross_norm_bias,
    cross_query,
    cross_key,
    cross_value,
    cross_output,
    dense_norm_gain,
    dense_norm_bias,
    dense_in,
    dense_in_bias,
    dense_out,
    dense_out_bias,
):
    f = lax.axis_index("fsdp")
    m = lax.axis_index("mem")
    c = m % 2
    fsdp = lax.axis_size("fsdp")
    mem = lax.axis_size("mem")
    across = mem // 2
    slow, fast = fsdp_split(fsdp)
    SHARDS[0] = fsdp
    where = jnp.stack([f // fast, f % fast, c, m]).astype(jnp.int32)
    examples = suffix.shape[0] // mem
    length = suffix.shape[1]
    width = suffix.shape[2]
    slots = memory.shape[1]
    total = mem * slots
    rows = examples * length
    inner = dense_in.shape[1]
    part = width // fsdp
    group = min(128, rows)
    blocks = 4 * fsdp

    def gather(matrices, *others):
        halves = [jnp.concatenate(matrices[:2]), jnp.concatenate(matrices[2:])]
        half = jnp.concatenate([jnp.where(c == 0, *halves), *others])
        return Gather(half, slow, fast)

    cross_gather = gather([cross_query, cross_key, cross_value, cross_output])
    in_gather = gather([dense_in[:, columns(j, width)] for j in range(4)])
    out_gather = gather([dense_out[columns(j, part)] for j in range(4)])
    small = [
        self_norm_gain,
        self_norm_bias,
        cross_norm_gain,
        cross_norm_bias,
        dense_norm_gain,
        dense_norm_bias,
        dense_out_bias,
    ]
    small += [dense_in_bias[columns(j, part)] for j in range(4)]
    small = sum(
        jnp.pad(value[None], ((i, 15 - i), (0, width - part))) for i, value in enumerate(small)
    )
    self_gather = gather([self_query, self_key, self_value, self_output], small)

    def exchange(value):
        blocks = value.reshape((mem, examples) + value.shape[1:])
        return lax.all_to_all(blocks, "mem", 0, 0, tiled=True)

    all_memory = exchange(after(memory, self_gather.half))
    self_gather.send_slow()
    out_gather.send_own()
    sent = [*self_gather.came, *out_gather.own[1:]]
    self_gather.send_fast(*sent)
    cross_gather.send_slow(*sent)
    sent = [*self_gather.far, *cross_gather.came, all_memory]
    self_gather.far = [after(piece, *sent) for piece in self_gather.far]
    self_weights = self_gather.whole()
    cross_gather.send_fast(*self_gather.far)
    in_gather.send_slow(*self_gather.far)

    half = (2, part, width)
    grads_like = [
        (ANY, shape_of((slow,) + half, BF)),
        (ANY, shape_of((fast - 1, slow) + half, BF)),
        [(ANY, shape_of((slow,) + half, BF))]
        + [(ANY, shape_of((slow // 2,) + half, BF))] * (2 * fast - 2),
    ]

    def flat(dims, dtype):
        return (VMEM, shape_of(dims, dtype))

    per = 2 if examples % 2 == 0 else 1

    def per_example(value):
        dims = value.shape[1:]
        spec = pl.BlockSpec((per,) + dims, lambda e: (e,) + (0,) * len(dims))
        return (spec, value)

    def slots_of_example(value):
        spec = pl.BlockSpec((mem, per, slots, width), lambda e: (0, e, 0, 0))
        return (spec, value)

    def scratch(*dims):
        return pltpu.VMEM(dims, BF)

    def scatter(grads, *others, vectors=None):
        return Scatter(grads, slow, fast, *others, vectors=vectors)

    wide = (rows, width)
    square = scratch(4, width, width)
    own_rows = scratch(examples, length, width)
    x1, a1, qkv, p1, o1, vec = run(
        functools.partial(self_forward, group),
        [(SMEM, where), (ANY, suffix), Gather.refs(self_weights)],
        [
            flat(wide, F32),
            flat(wide, BF),
            flat((rows, 3 * width), BF),
            flat((rows // group * GROUPS, TOGETHER * group, group), BF),
            flat(wide, BF),
            flat((16, width), F32),
        ],
        [square, own_rows, scratch(fsdp, 16, 128)],
        1 + fsdp + blocks,
    )
    cross_gather.far = [after(piece, x1, *in_gather.came) for piece in cross_gather.far]
    cross_weights = Gather.refs(cross_gather.whole())
    in_gather.send_fast(*cross_gather.far)
    out_gather.send_slow(*cross_gather.far)
    out_gather.send_own_cores(*cross_gather.far)
    tokens = examples * total
    turned_spec = pl.BlockSpec((width, per * total), lambda e: (0, e))
    x2, a2, q2, kv, p2, o2, turned = run(
        cross_forward,
        [(SMEM, where), (SMEM, counts), (VMEM, x1), (VMEM, vec)]
        + [slots_of_example(all_memory), cross_weights],
        [
            flat(wide, F32),
            flat(wide, BF),
            flat(wide, BF),
            per_example(shape_of((examples, total, 2 * width), BF)),
            per_example(shape_of((examples, GROUPS, TOGETHER * length, total), BF)),
            flat(wide, BF),
            (turned_spec, shape_of((width, tokens), BF)),
        ],
        [square],
        blocks,
        (examples // per,),
    )
    small = [after(piece, x1)[:, 2 * part + 7 : 2 * part + 11, :part] for piece in self_weights[0]]
    order = jnp.arange(fsdp) ^ f
    bias_in = jnp.take(jnp.concatenate(small), order % fast * slow + order // fast, axis=0)
    bias_in = bias_in.astype(F32).reshape(1, inner)
    in_gather.far = [after(piece, x2, *out_gather.came) for piece in in_gather.far]
    in_weights = Gather.refs(in_gather.whole())
    out_gather.send_fast(*in_gather.far)
    ready = after(x2, out_gather.near_other, *out_gather.own_other)
    a3, h, slope, *grads = run(
        dense_inner,
        [(SMEM, where), (VMEM, ready), (VMEM, vec), (VMEM, bias_in), (ANY, cotangent), in_weights],
        [flat(wide, BF), flat((rows, inner), BF), flat((rows, inner), BF)] + grads_like,
        [square, scratch(fsdp, 4, part, width), own_rows],
        1 + blocks,
    )
    out_gather.far = [after(piece, a3) for piece in out_gather.far]
    out_weights = Gather.refs(out_gather.whole())
    out_scatter = scatter(grads, *out_gather.far)
    out_sum = out_scatter.add_cores()
    out_scatter.send_fast()
    y, du, vecs_y, bias_grad, *grads = run(
        dense_outer,
        [(SMEM, where), (VMEM, after(x2, *out_sum)), (VMEM, vec), (VMEM, a3), (VMEM, h)]
        + [(VMEM, slope), (ANY, cotangent), out_weights],
        [
            flat((examples, length, width), BF),
            flat((rows, inner), BF),
            flat((1, width), F32),
            flat((1, inner), F32),
        ]
        + grads_like,
        [scratch(fsdp, 4, part, width), square, own_rows],
        1 + blocks,
    )
    in_grads = grads
    gx2, vecs_dense = run(
        dense_back,
        [(SMEM, where), (VMEM, x2), (VMEM, vec), (VMEM, du), (ANY, cotangent), in_weights],
        [flat(wide, F32), flat((2, width), F32)],
        [square, own_rows],
        1 + blocks,
    )
    in_scatter = scatter(in_grads, gx2)
    in_sum = in_scatter.add_cores(*out_scatter.came)
    in_scatter.send_fast()
    gx1, vecs_cross, dkv, dq2, grad_memory = run(
        cross_backward,
        [(SMEM, where), (VMEM, x1), (VMEM, vec), (VMEM, after(gx2, *in_sum)), (VMEM, q2)]
        + [per_example(kv), per_example(p2), cross_weights],
        [
            flat(wide, F32),
            flat((2, width), F32),
            per_example(shape_of((examples, total, 2 * width), BF)),
            flat(wide, BF),
            [per_example(shape_of((examples, slots, width), BF))] * mem,
        ],
        [square, scratch(*wide), scratch(per, total, width)],
        blocks,
        (examples // per,),
        60_000_000,
    )
    in_scatter.came, _ = lax.optimization_barrier((in_scatter.came, gx1))
    dense_total = [one.add_fast(*in_scatter.came) for one in (out_scatter, in_scatter)]
    dense_total = jnp.concatenate(dense_total, axis=1)
    dense_came = over_slow(dense_total, slow, fast)
    mem_pieces = grad_memory[:1] + [swap(grad_memory[d], "mem", d) for d in range(1, mem)]
    grads = run(
        cross_grads,
        [(SMEM, where), (VMEM, after(gx2, dense_total)), (VMEM, a2), (VMEM, o2), (VMEM, dq2)]
        + [(pl.BlockSpec((examples, total, width), lambda j: (0, 0, j)), dkv), (ANY, turned)],
        grads_like,
        [square, scratch(width, tokens)],
        blocks,
        (2,),
    )
    cross_scatter = scatter(grads, *mem_pieces[1:3])
    cross_sum = cross_scatter.add_cores()
    cross_scatter.send_fast()
    gx1 = after(gx1, *cross_sum)
    suffix_part, vecs_self, *grads = run(
        functools.partial(self_backward, group),
        [(SMEM, where), (ANY, suffix), (VMEM, vec), (VMEM, gx1), (VMEM, a1)]
        + [(VMEM, qkv), (VMEM, p1), (VMEM, o1)]
        + [[(VMEM, x) for x in (vecs_cross, vecs_dense, vecs_y, bias_grad)], Gather.refs(self_weights)],
        [flat((examples, length, width), BF), flat((16, width), BF)] + grads_like,
        [square, own_rows, square, scratch(rows, 3 * width), scratch(*wide)],
        1 + blocks,
    )
    self_scatter = scatter(grads, *mem_pieces[3:4], vectors=vecs_self)
    self_sum = self_scatter.add_cores()
    self_scatter.send_fast()
    cross_scatter.add_fast(*self_sum)
    cross_scatter.send_slow()
    dense_sum = jnp.sum(after(dense_came, *self_sum).astype(F32), axis=0)
    dense_sum = Replicas(dense_sum, 2 * part, across)
    self_total = self_scatter.add_fast(*dense_sum.halves)
    self_scatter.send_slow()
    cross_sum = Replicas(cross_scatter.add_slow(self_total), part, across)
    suffix_rows = spread_across(after(suffix_part, self_total), mem)
    y_rows = spread_across(after(y, self_total), mem)
    dense_sum.swap_cores(self_total)
    mem_pieces = [after(value, self_total) for value in mem_pieces]
    (memory_grad,) = run(
        place_memory,
        [(SMEM, where), [(ANY, value) for value in mem_pieces]],
        [(ANY, shape_of(memory.shape, BF))],
        [scratch(mem, examples, slots, width)],
        2 * mem,
    )
    (out_low, in_low, out_high, in_high), _ = dense_sum.combine(c)
    grad_in = jnp.concatenate([in_low[:part], in_low[part:], in_high[:part], in_high[part:]], axis=1)
    grad_out = jnp.concatenate([out_low, out_high])
    y_all, suffix_all = jnp.stack(y_rows), jnp.stack(suffix_rows)
    done = [*cross_sum.halves, y_all, suffix_all, grad_in, grad_out, memory_grad]
    self_final = Replicas(self_scatter.add_slow(*done), part, across)
    cross_sum.swap_cores(self_final.halves[0])
    y_far = swap(after(y_all, self_final.halves[0]), "mem", 1)
    suffix_far = swap(after(suffix_all, self_final.halves[0]), "mem", 1)
    blocks = [([(ANY, x) for x in y_rows], (ANY, y_far))]
    blocks += [([(ANY, x) for x in suffix_rows], (ANY, suffix_far))]
    ((block_output, suffix_grad),) = run(
        place_rows,
        [(SMEM, where), blocks],
        [[(ANY, shape_of(suffix.shape, BF))] * 2],
        [scratch(2, mem, examples, length, width)],
        4 * mem,
    )
    grad_cross, _ = cross_sum.combine(c)
    self_final.swap_cores(block_output)
    grad_self, vectors = self_final.combine(c)

    def vector(i):
        return lax.dynamic_slice(vectors, (i, f * part), (1, part)).reshape(part)

    return (
        block_output,
        suffix_grad,
        memory_grad,
        vector(0),
        vector(1),
        *grad_self,
        vector(2),
        vector(3),
        *grad_cross,
        vector(4),
        vector(5),
        grad_in,
        lax.dynamic_slice_in_dim(vectors[7:11].reshape(-1), f * (inner // fsdp), inner // fsdp, 0),
        grad_out,
        vector(6),
    )


def solution(mesh):
    rows = P("fsdp", None, None)
    matrix = P("fsdp", None)
    vector = P("fsdp")
    attention = (vector, vector, matrix, matrix, matrix, matrix)
    params = attention + attention + (vector, vector, matrix, vector, matrix, vector)
    return jax.shard_map(
        per_device,
        mesh=mesh,
        in_specs=(rows, P("fsdp", "mem", None), vector, rows) + params,
        out_specs=(rows, rows, P("fsdp", "mem", None)) + params,
        check_vma=False,
    )
```

```python
import functools

import jax
import jax.numpy as jnp
from jax import lax
from jax.experimental import pallas as pl
from jax.experimental.pallas import tpu as pltpu
from jax.sharding import PartitionSpec as P

HEADS = 12
HEAD = 64
TOGETHER = 4
GROUPS = HEADS // TOGETHER
LANES = TOGETHER * HEAD
SCALE = HEAD ** (-0.5)
BF = jnp.bfloat16
F32 = jnp.float32
ANY = pl.BlockSpec(memory_space=pl.ANY)
SMEM = pl.BlockSpec(memory_space=pltpu.SMEM)
VMEM = pl.BlockSpec(memory_space=pltpu.VMEM)


def swap(value, axis, distance):
    size = lax.axis_size(axis)
    return lax.ppermute(value, axis, [(i, i ^ distance) for i in range(size)])


def after(value, *others):
    return lax.optimization_barrier((value, *others))[0] if others else value


def fsdp_split(size):
    slow = 4 if size % 4 == 0 else 1
    return slow, size // slow


def dot(left, right):
    return jnp.dot(left, right, preferred_element_type=F32)


def dot_nt(left, right):
    return lax.dot_general(left, right, (((1,), (1,)), ((), ())), preferred_element_type=F32)


def dot_tn(left, right):
    return lax.dot_general(left, right, (((0,), (0,)), ((), ())), preferred_element_type=F32)


def rows_of(start, size):
    return pl.ds(pl.multiple_of(start, 16), size)


def block(ref, by_rows, shard, which):
    if by_rows:
        return ref.at[shard, pl.ds(which * 2, 2)]
    rows = ref.shape[1] // SHARDS[0]
    return ref.at[pl.ds(which * 2, 2), rows_of(shard * rows, rows)]


SHARDS = [0]


class Copies:
    def __init__(self, sems):
        self.sems = sems
        self.next = 0

    def start(self, source, target):
        copy = pltpu.make_async_copy(source, target, self.sems.at[self.next])
        self.next += 1
        copy.start()
        return copy


def wait_all(copies):
    for copy in copies:
        copy.wait()


def load_weight(where, whole, weights, copies, by_rows=False):
    z, y, c = where[0], where[1], where[2]
    rows = whole.shape[2] if by_rows else whole.shape[1] // SHARDS[0]
    started = []
    for which, pieces in ((c, weights[0]), (1 - c, weights[1])):
        slow = 4 if SHARDS[0] % 4 == 0 else 1
        fast = SHARDS[0] // slow
        for b, k in [(b, k) for b in range(fast) for k in range(slow)]:
            shard = (z ^ k) * fast + (y ^ b)
            first = slow - pieces[b].shape[0]
            piece = pieces[b].at[k - first] if k >= first else pieces[fast + b]
            for i in range(2):
                source = piece.at[pl.ds(i * rows, rows)]
                if by_rows:
                    target = whole.at[shard, 2 * which + i]
                else:
                    target = whole.at[2 * which + i, rows_of(shard * rows, rows)]
                started.append(copies.start(source, target))
    return started


def store_grad(where, whole, near, far, theirs, copies, by_rows=False):
    y, c = where[1], where[2]
    slow, cut = near.shape[0], near.shape[0] // 2
    fast = (len(theirs) + 1) // 2
    started = []
    for b in range(fast):
        for k in range(slow):
            shard = k * fast + (y ^ b)
            mine = far.at[b - 1, k] if b else near.at[k]
            other = theirs[2 * b - 1 + k // cut].at[k % cut] if b else theirs[0].at[k]
            started.append(copies.start(block(whole, by_rows, shard, 1 - c), other))
            started.append(copies.start(block(whole, by_rows, shard, c), mine))
    return started


def my_examples(where, source, target, copies):
    count = target.shape[0]
    return copies.start(source.at[pl.ds(where[3] * count, count)], target)


def normalise(values):
    centred = values - jnp.mean(values, axis=-1, keepdims=True)
    scale = lax.rsqrt(jnp.mean(centred * centred, axis=-1, keepdims=True) + 1e-06)
    return centred * scale, scale


def norm_back(grad, gain, hat, scale):
    inner = grad * gain
    mean = jnp.mean(inner, axis=-1, keepdims=True)
    along = jnp.mean(inner * hat, axis=-1, keepdims=True)
    return (
        scale * (inner - mean - hat * along),
        jnp.sum(grad * hat, axis=0, keepdims=True),
        jnp.sum(grad, axis=0, keepdims=True),
    )


def head_mask(rows):
    shape = (TOGETHER * rows, LANES)
    row = lax.broadcasted_iota(jnp.int32, shape, 0) // rows
    lane = lax.broadcasted_iota(jnp.int32, shape, 1) // HEAD
    return (row == lane).astype(F32)


def stack_heads(value, mask):
    return (jnp.concatenate([value] * TOGETHER, axis=0).astype(F32) * mask).astype(BF)


def merge_heads(value, mask):
    rows = value.shape[0] // TOGETHER
    value = value * mask
    total = value[:rows]
    for h in range(1, TOGETHER):
        total = total + value[h * rows : (h + 1) * rows]
    return total


def columns(j, width):
    return slice(j * width, (j + 1) * width)


def self_forward(
    group, where, suffix, weights, x1, a1, qkv, p1, o1, vec, weight, start, small, sems
):
    rows, width = x1.shape
    copies = Copies(sems)
    first = my_examples(where, suffix, start, copies)
    fast, slow = len(weights[0]), weights[0][0].shape[0]
    part = width // (fast * slow)
    vectors = []
    for b, piece in enumerate(weights[0]):
        for k in range(slow):
            source = piece.at[k, pl.ds(2 * part, 16), pl.ds(0, 128)]
            vectors.append(copies.start(source, small.at[b * slow + k]))
    loads = load_weight(where, weight, weights, copies)
    wait_all(vectors)
    lane = lax.broadcasted_iota(jnp.int32, (128, width), 0)
    place = lax.broadcasted_iota(jnp.int32, (128, width), 1) - lane
    together = jnp.zeros(vec.shape, F32)
    for i in range(fast * slow):
        shard = (where[0] ^ (i % slow)) * fast + (where[1] ^ (i // slow))
        chosen = ((place == shard * part) & (lane < part)).astype(F32).astype(BF)
        together = together + dot(small[i], chosen)
    vec[...] = together
    first.wait()
    values = start[...].reshape(rows, width).astype(F32)
    hat, _ = normalise(values)
    a1[...] = (hat * vec[0:1, :] + vec[1:2, :]).astype(BF)
    wait_all(loads)
    for j in range(3):
        qkv[:, columns(j, width)] = dot(a1[...], weight[j]).astype(BF)
    mask = head_mask(group)
    length = suffix.shape[1]
    shape = (TOGETHER * group, group)
    row = lax.broadcasted_iota(jnp.int32, shape, 0) % group
    col = lax.broadcasted_iota(jnp.int32, shape, 1)
    seen = (row // length == col // length) & (row >= col)
    for r in range(rows // group):
        here = columns(r, group)
        for g in range(GROUPS):
            lanes = [slice(i * width + g * LANES, i * width + (g + 1) * LANES) for i in range(3)]
            queries = stack_heads(qkv[here, lanes[0]], mask)
            scores = dot_nt(queries, qkv[here, lanes[1]]) * SCALE
            scores = jnp.where(seen, scores, -1e30)
            powers = jnp.exp(scores - jnp.max(scores, axis=-1, keepdims=True))
            probs = (powers / jnp.sum(powers, axis=-1, keepdims=True)).astype(BF)
            p1[r * GROUPS + g] = probs
            found = dot(probs, qkv[here, lanes[2]])
            o1[here, lanes[0]] = merge_heads(found, mask).astype(BF)
    x1[...] = values + dot(o1[...], weight[3])


def cross_forward(
    where, counts, x1, vec, memory, weights, x2, a2, q2, kv, p2, o2, turned, weight, sems
):
    rows, width = x1.shape
    per = kv.shape[0]
    step = pl.program_id(0)
    total = kv.shape[1]
    length = p2.shape[2] // TOGETHER

    @pl.when(step == 0)
    def _():
        loads = load_weight(where, weight, weights, Copies(sems))
        hat, _ = normalise(x1[...])
        a2[...] = (hat * vec[2:3, :] + vec[3:4, :]).astype(BF)
        wait_all(loads)
        q2[...] = dot(a2[...], weight[0]).astype(BF)

    for i in range(per):
        tokens = memory[:, i].reshape(total, width)
        for j in range(2):
            kv[i, :, columns(j, width)] = dot(tokens, weight[1 + j]).astype(BF)
        turned[:, columns(i, total)] = tokens.T
    mask = head_mask(length)
    position = lax.broadcasted_iota(jnp.int32, (1, total), 1)
    probs = {}
    for i in range(per):
        e = step * per + i
        valid = position < counts[where[3] * (pl.num_programs(0) * per) + e]
        here = rows_of(e * length, length)
        for g in range(GROUPS):
            lanes = columns(g, LANES)
            queries = stack_heads(q2[here, lanes], mask)
            scores = dot_nt(queries, kv[i, :, lanes]) * SCALE
            scores = jnp.where(valid, scores, -1e30)
            top = jnp.maximum(jnp.max(scores, axis=-1, keepdims=True), 0.0)
            powers = jnp.exp(scores - top)
            weight_sum = jnp.sum(powers, axis=-1, keepdims=True) + jnp.exp(-top)
            probs[i, g] = (powers / weight_sum).astype(BF)
    for i in range(per):
        here = rows_of((step * per + i) * length, length)
        for g in range(GROUPS):
            p2[i, g] = probs[i, g]
            found = dot(probs[i, g], kv[i, :, width + g * LANES : width + (g + 1) * LANES])
            o2[here, columns(g, LANES)] = merge_heads(found, mask).astype(BF)

    @pl.when(step == pl.num_programs(0) - 1)
    def _():
        x2[...] = x1[...] + dot(o2[...], weight[3])


def dense_inner(
    where, x2, vec, bias, cotangent, weights, a3, h, slope, near, far, theirs,
    weight, grad, cot, sems,
):
    rows, width = x2.shape
    copies = Copies(sems)
    cot_copy = my_examples(where, cotangent, cot, copies)
    loads = load_weight(where, weight, weights, copies)
    hat, _ = normalise(x2[...])
    a3[...] = (hat * vec[4:5, :] + vec[5:6, :]).astype(BF)
    cot_copy.wait()
    gy = cot[...].reshape(rows, width)
    wait_all(loads)
    flat = grad.shape[0] * grad.shape[1] * grad.shape[2]
    step = flat // grad.shape[0]
    for j in range(4):
        for half in range(2):
            cols = slice(j * width + half * 384, j * width + (half + 1) * 384)
            u = dot(a3[...], weight[j, :, half * 384 : (half + 1) * 384]) + bias[:, cols]
            square = u * u
            t = jnp.tanh(0.7978845608 * u * (1.0 + 0.044715 * square))
            h[:, cols] = (0.5 * u * (1.0 + t)).astype(BF)
            slope[:, cols] = (
                0.5 * (1.0 + t)
                + (0.5 * 0.7978845608) * u * (1.0 - t * t) * (1.0 + (3.0 * 0.044715) * square)
            ).astype(BF)
            part = dot_tn(h[:, cols], gy).astype(BF)
            per = 384 // step
            grad[cols.start // step : cols.start // step + per] = part.reshape(
                (per,) + grad.shape[1:]
            )
    wait_all(store_grad(where, grad, near, far, theirs, Copies(sems), True))


def dense_outer(
    where, x2, vec, a3, h, slope, cotangent, weights, y, du, vecs, bias_grad, near, far, theirs,
    weight, grad, cot, sems,
):
    rows, width = x2.shape
    copies = Copies(sems)
    cot_copy = my_examples(where, cotangent, cot, copies)
    wait_all(load_weight(where, weight, weights, copies, True))
    cot_copy.wait()
    gy = cot[...].reshape(rows, width)
    shards = weight.shape[0]
    step = weight.shape[1] * weight.shape[2]
    whole = weight[...].reshape(shards * step, width)
    for j in range(4):
        cols = columns(j, width)
        low = (dot_nt(gy, whole[cols]) * slope[:, cols].astype(F32)).astype(BF)
        du[:, cols] = low
        bias_grad[:, cols] = jnp.sum(low.astype(F32), axis=0, keepdims=True)
        grad[j] = dot_tn(a3[...], low).astype(BF)
    started = store_grad(where, grad, near, far, theirs, Copies(sems))
    result = x2[...] + dot(h[...], whole) + vec[6:7, :]
    y[...] = result.astype(BF).reshape(y.shape)
    vecs[...] = jnp.sum(gy.astype(F32), axis=0, keepdims=True)
    wait_all(started)


def dense_back(where, x2, vec, du, cotangent, weights, gx2, vecs, weight, cot, sems):
    rows, width = x2.shape
    copies = Copies(sems)
    cot_copy = my_examples(where, cotangent, cot, copies)
    loads = load_weight(where, weight, weights, copies)
    hat, scale = normalise(x2[...])
    cot_copy.wait()
    wait_all(loads)
    da3 = dot_nt(du[:, columns(0, width)], weight[0])
    for j in range(1, 4):
        da3 = da3 + dot_nt(du[:, columns(j, width)], weight[j])
    back, gain_grad, shift_grad = norm_back(da3, vec[4:5, :], hat, scale)
    gx2[...] = cot[...].reshape(rows, width).astype(F32) + back
    vecs[0:1, :] = gain_grad
    vecs[1:2, :] = shift_grad


def cross_backward(
    where, x1, vec, gx2, q2, kv, p2, weights, gx1, vecs, dkv, dq2, out_mem, weight, do2, moved, sems
):
    rows, width = x1.shape
    per, total = kv.shape[0], kv.shape[1]
    step = pl.program_id(0)
    length = p2.shape[2] // TOGETHER

    @pl.when(step == 0)
    def _():
        wait_all(load_weight(where, weight, weights, Copies(sems)))
        do2[...] = dot_nt(gx2[...].astype(BF), weight[3]).astype(BF)

    mask = head_mask(length)
    pairs = [(i, g) for i in range(per) for g in range(GROUPS)]
    queries, grads, dz = {}, {}, {}
    for i, g in pairs:
        here = rows_of((step * per + i) * length, length)
        lanes = columns(g, LANES)
        queries[i, g] = stack_heads(q2[here, lanes], mask)
        grads[i, g] = stack_heads(do2[here, lanes], mask)
        dp = dot_nt(grads[i, g], kv[i, :, width + g * LANES : width + (g + 1) * LANES])
        wide = p2[i, g].astype(F32)
        row_sum = jnp.sum(wide * dp, axis=-1, keepdims=True)
        dz[i, g] = (wide * (dp - row_sum)).astype(BF)
    for i, g in pairs:
        here = rows_of((step * per + i) * length, length)
        lanes = columns(g, LANES)
        value_lanes = slice(width + g * LANES, width + (g + 1) * LANES)
        dkv[i, :, value_lanes] = dot_tn(p2[i, g], grads[i, g]).astype(BF)
        dkv[i, :, lanes] = (dot_tn(dz[i, g], queries[i, g]) * SCALE).astype(BF)
        dq = merge_heads(dot(dz[i, g], kv[i, :, lanes]), mask) * SCALE
        dq2[here, lanes] = dq.astype(BF)
    for i in range(per):
        back = dot_nt(dkv[i, :, :width], weight[1]) + dot_nt(dkv[i, :, width:], weight[2])
        moved[i] = back.astype(BF)
        for d, out in enumerate(out_mem):
            slots = out.shape[1]
            out[i] = moved[i, rows_of((where[3] ^ d) * slots, slots), :]

    @pl.when(step == pl.num_programs(0) - 1)
    def _():
        hat, scale = normalise(x1[...])
        back, gain_grad, shift_grad = norm_back(
            dot_nt(dq2[...], weight[0]), vec[2:3, :], hat, scale
        )
        gx1[...] = gx2[...] + back
        vecs[0:1, :] = gain_grad
        vecs[1:2, :] = shift_grad


def cross_grads(where, gx2, a2, o2, dq2, dkv, turned, near, far, theirs, grad, memory, sems):
    width = gx2.shape[1]
    half = pl.program_id(0)

    @pl.when(half == 0)
    def _():
        load = Copies(sems).start(turned, memory)
        grad[0] = dot_tn(a2[...], dq2[...]).astype(BF)
        grad[3] = dot_tn(o2[...], gx2[...].astype(BF)).astype(BF)
        load.wait()

    part = dkv[...].reshape(memory.shape[1], width)
    grad[1 + half] = dot(memory[...], part).astype(BF)

    @pl.when(half == 1)
    def _():
        wait_all(store_grad(where, grad, near, far, theirs, Copies(sems)))


def self_backward(
    group, where, suffix, vec, gx1, a1, qkv, p1, o1, parts, weights, suffix_grad, vecs,
    near, far, theirs, weight, start, grad, dqkv, do1, sems,
):
    rows, width = gx1.shape
    copies = Copies(sems)
    start_copy = my_examples(where, suffix, start, copies)
    loads = load_weight(where, weight, weights, copies)
    gs = gx1[...].astype(BF)
    grad[3] = dot_tn(o1[...], gs).astype(BF)
    wait_all(loads)
    do1[...] = dot_nt(gs, weight[3]).astype(BF)
    mask = head_mask(group)
    for r in range(rows // group):
        here = columns(r, group)
        for g in range(GROUPS):
            lanes = [slice(i * width + g * LANES, i * width + (g + 1) * LANES) for i in range(3)]
            queries = stack_heads(qkv[here, lanes[0]], mask)
            grads = stack_heads(do1[here, lanes[0]], mask)
            probs = p1[r * GROUPS + g]
            dp = dot_nt(grads, qkv[here, lanes[2]])
            wide = probs.astype(F32)
            row_sum = jnp.sum(wide * dp, axis=-1, keepdims=True)
            dz = (wide * (dp - row_sum)).astype(BF)
            dqkv[here, lanes[2]] = dot_tn(probs, grads).astype(BF)
            dqkv[here, lanes[1]] = (dot_tn(dz, queries) * SCALE).astype(BF)
            dq = merge_heads(dot(dz, qkv[here, lanes[1]]), mask) * SCALE
            dqkv[here, lanes[0]] = dq.astype(BF)
    for j in range(3):
        grad[j] = dot_tn(a1[...], dqkv[:, columns(j, width)]).astype(BF)
    start_copy.wait()
    started = store_grad(where, grad, near, far, theirs, Copies(sems))
    da1 = dot_nt(dqkv[:, columns(0, width)], weight[0])
    for j in range(1, 3):
        da1 = da1 + dot_nt(dqkv[:, columns(j, width)], weight[j])
    hat, scale = normalise(start[...].reshape(rows, width).astype(F32))
    back, gain_grad, shift_grad = norm_back(da1, vec[0:1, :], hat, scale)
    suffix_grad[...] = (gx1[...] + back).astype(BF).reshape(suffix_grad.shape)
    found = [gain_grad, shift_grad]
    for ref in parts:
        for r in range(ref.shape[0]):
            found += [ref[r : r + 1, columns(j, width)] for j in range(ref.shape[1] // width)]
    found.append(jnp.zeros((vecs.shape[0] - len(found), width), F32))
    vecs[...] = jnp.concatenate(found, axis=0).astype(BF)
    wait_all(started)


def run(kernel, inputs, outputs, scratch, copies, grid=(), moved=0):
    def leaf(x):
        return isinstance(x, tuple) and len(x) == 2 and isinstance(x[0], pl.BlockSpec)

    flat_in, tree_in = jax.tree.flatten(inputs, is_leaf=leaf)
    flat_out, tree_out = jax.tree.flatten(outputs, is_leaf=leaf)

    def body(*refs):
        first, second = len(flat_in), len(flat_in) + len(flat_out)
        given = jax.tree.unflatten(tree_in, refs[:first])
        taken = jax.tree.unflatten(tree_out, refs[first:second])
        kernel(*given, *taken, *refs[second:])

    found = pl.pallas_call(
        body,
        grid=grid,
        in_specs=[spec for spec, _ in flat_in],
        out_specs=[spec for spec, _ in flat_out],
        out_shape=[shape for _, shape in flat_out],
        scratch_shapes=scratch + [pltpu.SemaphoreType.DMA((copies,))],
        compiler_params=pltpu.CompilerParams(vmem_limit_bytes=56 * 1024 * 1024),
        cost_estimate=pl.CostEstimate(
            flops=0, bytes_accessed=moved, transcendentals=0
        ),
    )(*[x for _, x in flat_in])
    return jax.tree.unflatten(tree_out, found)


def shape_of(dims, dtype):
    return jax.ShapeDtypeStruct(tuple(dims), dtype)


def over_slow(value, slow, fast):
    groups = [[k * fast + b for k in range(slow)] for b in range(fast)]
    return lax.all_to_all(value, "fsdp", 0, 0, axis_index_groups=groups, tiled=True)


class Gather:
    def __init__(self, half, slow, fast):
        self.half, self.slow, self.fast = half, slow, fast
        self.own, self.own_other = [], []

    def send_slow(self, *others):
        half = after(self.half, *others)
        self.came = [half] + [swap(half, "fsdp", k * self.fast) for k in range(1, self.slow)]

    def send_own(self):
        self.own = [self.half] + [swap(self.half, "fsdp", b) for b in range(1, self.fast)]

    def send_own_cores(self, *others):
        self.own_other = [swap(after(piece, *others), "mem", 1) for piece in self.own]

    def send_fast(self, *others):
        came = [after(piece, *others) for piece in self.came[1 if self.own else 0 :]]
        self.near = jnp.stack(came)
        self.near_other = swap(self.near, "mem", 1)
        self.far = [swap(self.near, "fsdp", b) for b in range(1, self.fast)]

    def whole(self):
        mine = [self.near] + self.far
        theirs = [self.near_other] + [swap(piece, "mem", 1) for piece in self.far]
        return mine + self.own, theirs + self.own_other

    @staticmethod
    def refs(weights):
        return [[(ANY, x) for x in some] for some in weights]


class Scatter:
    def __init__(self, grads, slow, fast, *others, vectors=None):
        self.near, self.far, theirs = grads
        self.slow, self.fast, self.vectors = slow, fast, vectors
        theirs = [after(part, *others) for part in theirs]
        far = [swap(part, "mem", 1) for part in theirs[1:]]
        far = [jnp.concatenate(far[2 * b : 2 * b + 2]) for b in range(fast - 1)]
        self.sent = [swap(theirs[0], "mem", 1)] + far
        if vectors is not None:
            self.vectors = vectors.astype(F32) + swap(vectors, "mem", 1).astype(F32)

    def add_cores(self, *others):
        far = after(self.far, *others)
        self.out = [
            (far[b].astype(F32) + self.sent[b + 1].astype(F32)).astype(BF)
            for b in range(self.fast - 1)
        ]
        return self.out

    def send_fast(self):
        self.came = [swap(part, "fsdp", b + 1) for b, part in enumerate(self.out)]
        if self.vectors is not None:
            low = self.vectors.astype(BF)
            self.vectors = [low] + [swap(low, "fsdp", b) for b in range(1, self.fast)]

    def add_fast(self, *others):
        if self.vectors is not None:
            self.vectors, self.came = lax.optimization_barrier((self.vectors, self.came))
            self.vectors = sum(part.astype(F32) for part in self.vectors)
        total = after(self.near, *others).astype(F32) + self.sent[0].astype(F32)
        for part in self.came:
            total = total + part.astype(F32)
        self.total = total.astype(BF).reshape(self.slow, -1, total.shape[-1])
        if self.vectors is not None:
            low = self.vectors.astype(BF)
            low = jnp.broadcast_to(low, (self.slow,) + low.shape)
            self.total = jnp.concatenate([self.total, low], axis=1)
        return self.total

    def send_slow(self):
        self.came = over_slow(self.total, self.slow, self.fast)

    def add_slow(self, *others):
        return jnp.sum(after(self.came, *others).astype(F32), axis=0)


class Replicas:
    def __init__(self, value, rows, across):
        self.rows = rows
        k = 1
        while 2 * k < across:
            low = value.astype(BF)
            value = low.astype(F32) + swap(low, "mem", 2 * k).astype(F32)
            k *= 2
        low = value.astype(BF)
        self.halves = [low, swap(low, "mem", 2 * k)] if across > 1 else [low]

    def swap_cores(self, *others):
        halves, _ = lax.optimization_barrier((self.halves, others))
        self.others = [swap(half[: 2 * self.rows], "mem", 1) for half in halves]

    def combine(self, c):
        rows = self.rows
        other = sum(half.astype(F32) for half in self.others)
        mine = sum(half.astype(F32) for half in self.halves)
        vectors, mine = mine[2 * rows :], mine[: 2 * rows]
        first = jnp.where(c == 0, mine, other)
        second = jnp.where(c == 0, other, mine)
        return [first[:rows], first[rows:], second[:rows], second[rows:]], vectors


def place_rows(where, blocks, outs, scratch, sems):
    copies = Copies(sems)
    loads = []
    for i, (even, odd) in enumerate(blocks):
        for d, piece in enumerate(even):
            loads.append((copies.start(piece, scratch.at[i, 2 * d]), i, 2 * d))
            loads.append((copies.start(odd.at[d], scratch.at[i, 2 * d + 1]), i, 2 * d + 1))
    examples = scratch.shape[2]
    stores = []
    for load, i, d in loads:
        load.wait()
        target = outs[i].at[pl.ds((where[3] ^ d) * examples, examples)]
        stores.append(copies.start(scratch.at[i, d], target))
    wait_all(stores)


def place_memory(where, pieces, out, scratch, sems):
    examples = scratch.shape[1]
    copies = Copies(sems)
    loads = []
    for d, parts in enumerate(pieces):
        start = 0
        for part in parts:
            held = scratch.at[d, pl.ds(start, part.shape[0])]
            loads.append((copies.start(part, held), held, (where[3] ^ d) * examples + start))
            start += part.shape[0]
    stores = []
    for load, held, place in loads:
        load.wait()
        stores.append(copies.start(held, out.at[pl.ds(place, held.shape[0])]))
    wait_all(stores)


def spread_across(value, mem):
    return [value] + [swap(value, "mem", d) for d in range(2, mem, 2)]


def per_device(
    suffix,
    memory,
    counts,
    cotangent,
    self_norm_gain,
    self_norm_bias,
    self_query,
    self_key,
    self_value,
    self_output,
    cross_norm_gain,
    cross_norm_bias,
    cross_query,
    cross_key,
    cross_value,
    cross_output,
    dense_norm_gain,
    dense_norm_bias,
    dense_in,
    dense_in_bias,
    dense_out,
    dense_out_bias,
):
    f = lax.axis_index("fsdp")
    m = lax.axis_index("mem")
    c = m % 2
    fsdp = lax.axis_size("fsdp")
    mem = lax.axis_size("mem")
    across = mem // 2
    slow, fast = fsdp_split(fsdp)
    SHARDS[0] = fsdp
    where = jnp.stack([f // fast, f % fast, c, m]).astype(jnp.int32)
    examples = suffix.shape[0] // mem
    length = suffix.shape[1]
    width = suffix.shape[2]
    slots = memory.shape[1]
    total = mem * slots
    rows = examples * length
    inner = dense_in.shape[1]
    part = width // fsdp
    group = min(128, rows)
    blocks = 4 * fsdp

    def gather(matrices, *others):
        halves = [jnp.concatenate(matrices[:2]), jnp.concatenate(matrices[2:])]
        half = jnp.concatenate([jnp.where(c == 0, *halves), *others])
        return Gather(half, slow, fast)

    cross_gather = gather([cross_query, cross_key, cross_value, cross_output])
    in_gather = gather([dense_in[:, columns(j, width)] for j in range(4)])
    out_gather = gather([dense_out[columns(j, part)] for j in range(4)])
    small = [
        self_norm_gain,
        self_norm_bias,
        cross_norm_gain,
        cross_norm_bias,
        dense_norm_gain,
        dense_norm_bias,
        dense_out_bias,
    ]
    small += [dense_in_bias[columns(j, part)] for j in range(4)]
    small = sum(
        jnp.pad(value[None], ((i, 15 - i), (0, width - part))) for i, value in enumerate(small)
    )
    self_gather = gather([self_query, self_key, self_value, self_output], small)

    def exchange(value):
        blocks = value.reshape((mem, examples) + value.shape[1:])
        return lax.all_to_all(blocks, "mem", 0, 0, tiled=True)

    all_memory = exchange(after(memory, self_gather.half))
    self_gather.send_slow()
    out_gather.send_own()
    sent = [*self_gather.came, *out_gather.own[1:]]
    self_gather.send_fast(*sent)
    cross_gather.send_slow(*sent)
    sent = [*self_gather.far, *cross_gather.came, all_memory]
    self_gather.far = [after(piece, *sent) for piece in self_gather.far]
    self_weights = self_gather.whole()
    cross_gather.send_fast(*self_gather.far)
    in_gather.send_slow(*self_gather.far)

    half = (2, part, width)
    grads_like = [
        (ANY, shape_of((slow,) + half, BF)),
        (ANY, shape_of((fast - 1, slow) + half, BF)),
        [(ANY, shape_of((slow,) + half, BF))]
        + [(ANY, shape_of((slow // 2,) + half, BF))] * (2 * fast - 2),
    ]

    def flat(dims, dtype):
        return (VMEM, shape_of(dims, dtype))

    per = 2 if examples % 2 == 0 else 1

    def per_example(value):
        dims = value.shape[1:]
        spec = pl.BlockSpec((per,) + dims, lambda e: (e,) + (0,) * len(dims))
        return (spec, value)

    def slots_of_example(value):
        spec = pl.BlockSpec((mem, per, slots, width), lambda e: (0, e, 0, 0))
        return (spec, value)

    def scratch(*dims):
        return pltpu.VMEM(dims, BF)

    def scatter(grads, *others, vectors=None):
        return Scatter(grads, slow, fast, *others, vectors=vectors)

    wide = (rows, width)
    square = scratch(4, width, width)
    own_rows = scratch(examples, length, width)
    x1, a1, qkv, p1, o1, vec = run(
        functools.partial(self_forward, group),
        [(SMEM, where), (ANY, suffix), Gather.refs(self_weights)],
        [
            flat(wide, F32),
            flat(wide, BF),
            flat((rows, 3 * width), BF),
            flat((rows // group * GROUPS, TOGETHER * group, group), BF),
            flat(wide, BF),
            flat((16, width), F32),
        ],
        [square, own_rows, scratch(fsdp, 16, 128)],
        1 + fsdp + blocks,
    )
    small = [after(piece, x1)[:, 2 * part + 7 : 2 * part + 11, :part] for piece in self_weights[0]]
    order = jnp.arange(fsdp) ^ f
    bias_in = jnp.take(jnp.concatenate(small), order % fast * slow + order // fast, axis=0)
    bias_in = bias_in.astype(F32).reshape(1, inner)
    cross_gather.far = [after(piece, x1, *in_gather.came) for piece in cross_gather.far]
    cross_weights = Gather.refs(cross_gather.whole())
    in_gather.send_fast(*cross_gather.far)
    out_gather.send_slow(*cross_gather.far)
    out_gather.send_own_cores(*cross_gather.far)
    tokens = examples * total
    turned_spec = pl.BlockSpec((width, per * total), lambda e: (0, e))
    x2, a2, q2, kv, p2, o2, turned = run(
        cross_forward,
        [(SMEM, where), (SMEM, counts), (VMEM, after(x1, bias_in)), (VMEM, vec)]
        + [slots_of_example(all_memory), cross_weights],
        [
            flat(wide, F32),
            flat(wide, BF),
            flat(wide, BF),
            per_example(shape_of((examples, total, 2 * width), BF)),
            per_example(shape_of((examples, GROUPS, TOGETHER * length, total), BF)),
            flat(wide, BF),
            (turned_spec, shape_of((width, tokens), BF)),
        ],
        [square],
        blocks,
        (examples // per,),
    )
    in_gather.far = [after(piece, x2, *out_gather.came) for piece in in_gather.far]
    in_weights = Gather.refs(in_gather.whole())
    out_gather.send_fast(*in_gather.far)
    ready = after(x2, out_gather.near_other, *out_gather.own_other)
    a3, h, slope, *grads = run(
        dense_inner,
        [(SMEM, where), (VMEM, ready), (VMEM, vec), (VMEM, bias_in), (ANY, cotangent), in_weights],
        [flat(wide, BF), flat((rows, inner), BF), flat((rows, inner), BF)] + grads_like,
        [square, scratch(fsdp, 4, part, width), own_rows],
        1 + blocks,
    )
    out_gather.far = [after(piece, a3) for piece in out_gather.far]
    out_weights = Gather.refs(out_gather.whole())
    out_scatter = scatter(grads, *out_gather.far)
    out_sum = out_scatter.add_cores()
    out_scatter.send_fast()
    y, du, vecs_y, bias_grad, *grads = run(
        dense_outer,
        [(SMEM, where), (VMEM, after(x2, *out_sum)), (VMEM, vec), (VMEM, a3), (VMEM, h)]
        + [(VMEM, slope), (ANY, cotangent), out_weights],
        [
            flat((examples, length, width), BF),
            flat((rows, inner), BF),
            flat((1, width), F32),
            flat((1, inner), F32),
        ]
        + grads_like,
        [scratch(fsdp, 4, part, width), square, own_rows],
        1 + blocks,
    )
    in_grads = grads
    gx2, vecs_dense = run(
        dense_back,
        [(SMEM, where), (VMEM, x2), (VMEM, vec), (VMEM, du), (ANY, cotangent), in_weights],
        [flat(wide, F32), flat((2, width), F32)],
        [square, own_rows],
        1 + blocks,
    )
    in_scatter = scatter(in_grads, gx2)
    in_sum = in_scatter.add_cores(*out_scatter.came)
    in_scatter.send_fast()
    gx1, vecs_cross, dkv, dq2, grad_memory = run(
        cross_backward,
        [(SMEM, where), (VMEM, x1), (VMEM, vec), (VMEM, after(gx2, *in_sum)), (VMEM, q2)]
        + [per_example(kv), per_example(p2), cross_weights],
        [
            flat(wide, F32),
            flat((2, width), F32),
            per_example(shape_of((examples, total, 2 * width), BF)),
            flat(wide, BF),
            [per_example(shape_of((examples, slots, width), BF))] * mem,
        ],
        [square, scratch(*wide), scratch(per, total, width)],
        blocks,
        (examples // per,),
        60_000_000,
    )
    in_scatter.came, _ = lax.optimization_barrier((in_scatter.came, gx1))
    dense_total = [one.add_fast(*in_scatter.came) for one in (out_scatter, in_scatter)]
    dense_total = jnp.concatenate(dense_total, axis=1)
    dense_came = over_slow(dense_total, slow, fast)
    cut = examples // 2
    mem_pieces = [grad_memory[:1]]
    for d in range(1, mem):
        parts = [grad_memory[d][:cut], grad_memory[d][cut:]] if d == 2 else [grad_memory[d]]
        mem_pieces.append([swap(part, "mem", d) for part in parts])
    grads = run(
        cross_grads,
        [(SMEM, where), (VMEM, after(gx2, dense_total)), (VMEM, a2), (VMEM, o2), (VMEM, dq2)]
        + [(pl.BlockSpec((examples, total, width), lambda j: (0, 0, j)), dkv), (ANY, turned)],
        grads_like,
        [square, scratch(width, tokens)],
        blocks,
        (2,),
    )
    cross_scatter = scatter(grads, *mem_pieces[1], *mem_pieces[2][:1])
    cross_sum = cross_scatter.add_cores()
    cross_scatter.send_fast()
    gx1 = after(gx1, *cross_sum)
    suffix_part, vecs_self, *grads = run(
        functools.partial(self_backward, group),
        [(SMEM, where), (ANY, suffix), (VMEM, vec), (VMEM, gx1), (VMEM, a1)]
        + [(VMEM, qkv), (VMEM, p1), (VMEM, o1)]
        + [[(VMEM, x) for x in (vecs_cross, vecs_dense, vecs_y, bias_grad)], Gather.refs(self_weights)],
        [flat((examples, length, width), BF), flat((16, width), BF)] + grads_like,
        [square, own_rows, square, scratch(rows, 3 * width), scratch(*wide)],
        1 + blocks,
    )
    self_scatter = scatter(grads, *mem_pieces[3], vectors=vecs_self)
    self_sum = self_scatter.add_cores()
    self_scatter.send_fast()
    cross_scatter.add_fast(*self_sum)
    cross_scatter.send_slow()
    dense_sum = jnp.sum(after(dense_came, *self_sum).astype(F32), axis=0)
    dense_sum = Replicas(dense_sum, 2 * part, across)
    self_total = self_scatter.add_fast(*dense_sum.halves)
    self_scatter.send_slow()
    cross_sum = Replicas(cross_scatter.add_slow(self_total), part, across)
    suffix_rows = spread_across(after(suffix_part, self_total), mem)
    y_rows = spread_across(after(y, self_total), mem)
    dense_sum.swap_cores(self_total)
    mem_pieces = [[after(part, self_total) for part in parts] for parts in mem_pieces]
    (memory_grad,) = run(
        place_memory,
        [(SMEM, where), [[(ANY, part) for part in parts] for parts in mem_pieces]],
        [(ANY, shape_of(memory.shape, BF))],
        [scratch(mem, examples, slots, width)],
        2 * mem + 2,
    )
    (out_low, in_low, out_high, in_high), _ = dense_sum.combine(c)
    grad_in = jnp.concatenate([in_low[:part], in_low[part:], in_high[:part], in_high[part:]], axis=1)
    grad_out = jnp.concatenate([out_low, out_high])
    y_all, suffix_all = jnp.stack(y_rows), jnp.stack(suffix_rows)
    done = [*cross_sum.halves, y_all, suffix_all, grad_in, grad_out, memory_grad]
    self_final = Replicas(self_scatter.add_slow(*done), part, across)
    cross_sum.swap_cores(self_final.halves[0])
    y_far = swap(after(y_all, self_final.halves[0]), "mem", 1)
    suffix_far = swap(after(suffix_all, self_final.halves[0]), "mem", 1)
    blocks = [([(ANY, x) for x in y_rows], (ANY, y_far))]
    blocks += [([(ANY, x) for x in suffix_rows], (ANY, suffix_far))]
    ((block_output, suffix_grad),) = run(
        place_rows,
        [(SMEM, where), blocks],
        [[(ANY, shape_of(suffix.shape, BF))] * 2],
        [scratch(2, mem, examples, length, width)],
        4 * mem,
    )
    grad_cross, _ = cross_sum.combine(c)
    self_final.swap_cores(block_output)
    grad_self, vectors = self_final.combine(c)

    def vector(i):
        return lax.dynamic_slice(vectors, (i, f * part), (1, part)).reshape(part)

    return (
        block_output,
        suffix_grad,
        memory_grad,
        vector(0),
        vector(1),
        *grad_self,
        vector(2),
        vector(3),
        *grad_cross,
        vector(4),
        vector(5),
        grad_in,
        lax.dynamic_slice_in_dim(vectors[7:11].reshape(-1), f * (inner // fsdp), inner // fsdp, 0),
        grad_out,
        vector(6),
    )


def solution(mesh):
    rows = P("fsdp", None, None)
    matrix = P("fsdp", None)
    vector = P("fsdp")
    attention = (vector, vector, matrix, matrix, matrix, matrix)
    params = attention + attention + (vector, vector, matrix, vector, matrix, vector)
    return jax.shard_map(
        per_device,
        mesh=mesh,
        in_specs=(rows, P("fsdp", "mem", None), vector, rows) + params,
        out_specs=(rows, rows, P("fsdp", "mem", None)) + params,
        check_vma=False,
    )
```

```python
import functools

import jax
import jax.numpy as jnp
from jax import lax
from jax.experimental import pallas as pl
from jax.experimental.pallas import tpu as pltpu
from jax.sharding import PartitionSpec as P

HEADS = 12
HEAD = 64
TOGETHER = 4
GROUPS = HEADS // TOGETHER
LANES = TOGETHER * HEAD
SCALE = HEAD ** (-0.5)
BF = jnp.bfloat16
F32 = jnp.float32
ANY = pl.BlockSpec(memory_space=pl.ANY)
SMEM = pl.BlockSpec(memory_space=pltpu.SMEM)
VMEM = pl.BlockSpec(memory_space=pltpu.VMEM)


def swap(value, axis, distance):
    size = lax.axis_size(axis)
    return lax.ppermute(value, axis, [(i, i ^ distance) for i in range(size)])


def after(value, *others):
    return lax.optimization_barrier((value, *others))[0] if others else value


def fsdp_split(size):
    slow = 4 if size % 4 == 0 else 1
    return slow, size // slow


def dot(left, right):
    return jnp.dot(left, right, preferred_element_type=F32)


def dot_nt(left, right):
    return lax.dot_general(left, right, (((1,), (1,)), ((), ())), preferred_element_type=F32)


def dot_tn(left, right):
    return lax.dot_general(left, right, (((0,), (0,)), ((), ())), preferred_element_type=F32)


def rows_of(start, size):
    return pl.ds(pl.multiple_of(start, 16), size)


def block(ref, by_rows, shard, which):
    if by_rows:
        return ref.at[shard, pl.ds(which * 2, 2)]
    rows = ref.shape[1] // SHARDS[0]
    return ref.at[pl.ds(which * 2, 2), rows_of(shard * rows, rows)]


SHARDS = [0]


class Copies:
    def __init__(self, sems):
        self.sems = sems
        self.next = 0

    def start(self, source, target):
        copy = pltpu.make_async_copy(source, target, self.sems.at[self.next])
        self.next += 1
        copy.start()
        return copy


def wait_all(copies):
    for copy in copies:
        copy.wait()


def load_weight(where, whole, weights, copies, by_rows=False):
    z, y, c = where[0], where[1], where[2]
    rows = whole.shape[2] if by_rows else whole.shape[1] // SHARDS[0]
    started = []
    for which, pieces in ((c, weights[0]), (1 - c, weights[1])):
        slow = 4 if SHARDS[0] % 4 == 0 else 1
        fast = SHARDS[0] // slow
        for b, k in [(b, k) for b in range(fast) for k in range(slow)]:
            shard = (z ^ k) * fast + (y ^ b)
            first = slow - pieces[b].shape[0]
            piece = pieces[b].at[k - first] if k >= first else pieces[fast + b]
            for i in range(2):
                source = piece.at[pl.ds(i * rows, rows)]
                if by_rows:
                    target = whole.at[shard, 2 * which + i]
                else:
                    target = whole.at[2 * which + i, rows_of(shard * rows, rows)]
                started.append(copies.start(source, target))
    return started


def store_grad(where, whole, near, far, theirs, copies, by_rows=False):
    y, c = where[1], where[2]
    slow, cut = near.shape[0], near.shape[0] // 2
    fast = (len(theirs) + 1) // 2
    started = []
    for b in range(fast):
        for k in range(slow):
            shard = k * fast + (y ^ b)
            mine = far.at[b - 1, k] if b else near.at[k]
            other = theirs[2 * b - 1 + k // cut].at[k % cut] if b else theirs[0].at[k]
            started.append(copies.start(block(whole, by_rows, shard, 1 - c), other))
            started.append(copies.start(block(whole, by_rows, shard, c), mine))
    return started


def my_examples(where, source, target, copies):
    count = target.shape[0]
    return copies.start(source.at[pl.ds(where[3] * count, count)], target)


def normalise(values):
    centred = values - jnp.mean(values, axis=-1, keepdims=True)
    scale = lax.rsqrt(jnp.mean(centred * centred, axis=-1, keepdims=True) + 1e-06)
    return centred * scale, scale


def norm_back(grad, gain, hat, scale):
    inner = grad * gain
    mean = jnp.mean(inner, axis=-1, keepdims=True)
    along = jnp.mean(inner * hat, axis=-1, keepdims=True)
    return (
        scale * (inner - mean - hat * along),
        jnp.sum(grad * hat, axis=0, keepdims=True),
        jnp.sum(grad, axis=0, keepdims=True),
    )


def head_mask(rows):
    shape = (TOGETHER * rows, LANES)
    row = lax.broadcasted_iota(jnp.int32, shape, 0) // rows
    lane = lax.broadcasted_iota(jnp.int32, shape, 1) // HEAD
    return (row == lane).astype(F32)


def stack_heads(value, mask):
    return (jnp.concatenate([value] * TOGETHER, axis=0).astype(F32) * mask).astype(BF)


def merge_heads(value, mask):
    rows = value.shape[0] // TOGETHER
    value = value * mask
    total = value[:rows]
    for h in range(1, TOGETHER):
        total = total + value[h * rows : (h + 1) * rows]
    return total


def columns(j, width):
    return slice(j * width, (j + 1) * width)


def self_forward(
    group, where, suffix, weights, x1, a1, qkv, p1, o1, vec, weight, start, small, sems
):
    rows, width = x1.shape
    copies = Copies(sems)
    first = my_examples(where, suffix, start, copies)
    fast, slow = len(weights[0]), weights[0][0].shape[0]
    part = width // (fast * slow)
    vectors = []
    for b, piece in enumerate(weights[0]):
        for k in range(slow):
            source = piece.at[k, pl.ds(2 * part, 16), pl.ds(0, 128)]
            vectors.append(copies.start(source, small.at[b * slow + k]))
    loads = load_weight(where, weight, weights, copies)
    wait_all(vectors)
    lane = lax.broadcasted_iota(jnp.int32, (128, width), 0)
    place = lax.broadcasted_iota(jnp.int32, (128, width), 1) - lane
    together = jnp.zeros(vec.shape, F32)
    for i in range(fast * slow):
        shard = (where[0] ^ (i % slow)) * fast + (where[1] ^ (i // slow))
        chosen = ((place == shard * part) & (lane < part)).astype(F32).astype(BF)
        together = together + dot(small[i], chosen)
    vec[...] = together
    first.wait()
    values = start[...].reshape(rows, width).astype(F32)
    hat, _ = normalise(values)
    a1[...] = (hat * vec[0:1, :] + vec[1:2, :]).astype(BF)
    wait_all(loads)
    for j in range(3):
        qkv[:, columns(j, width)] = dot(a1[...], weight[j]).astype(BF)
    mask = head_mask(group)
    length = suffix.shape[1]
    shape = (TOGETHER * group, group)
    row = lax.broadcasted_iota(jnp.int32, shape, 0) % group
    col = lax.broadcasted_iota(jnp.int32, shape, 1)
    seen = (row // length == col // length) & (row >= col)
    for r in range(rows // group):
        here = columns(r, group)
        for g in range(GROUPS):
            lanes = [slice(i * width + g * LANES, i * width + (g + 1) * LANES) for i in range(3)]
            queries = stack_heads(qkv[here, lanes[0]], mask)
            scores = dot_nt(queries, qkv[here, lanes[1]]) * SCALE
            scores = jnp.where(seen, scores, -1e30)
            powers = jnp.exp(scores - jnp.max(scores, axis=-1, keepdims=True))
            probs = (powers / jnp.sum(powers, axis=-1, keepdims=True)).astype(BF)
            p1[r * GROUPS + g] = probs
            found = dot(probs, qkv[here, lanes[2]])
            o1[here, lanes[0]] = merge_heads(found, mask).astype(BF)
    x1[...] = values + dot(o1[...], weight[3])


def cross_forward(
    where, counts, x1, vec, memory, weights, x2, a2, q2, kv, p2, o2, turned, weight, sems
):
    rows, width = x1.shape
    per = kv.shape[0]
    step = pl.program_id(0)
    total = kv.shape[1]
    length = p2.shape[2] // TOGETHER

    @pl.when(step == 0)
    def _():
        loads = load_weight(where, weight, weights, Copies(sems))
        hat, _ = normalise(x1[...])
        a2[...] = (hat * vec[2:3, :] + vec[3:4, :]).astype(BF)
        wait_all(loads)
        q2[...] = dot(a2[...], weight[0]).astype(BF)

    for i in range(per):
        tokens = memory[:, i].reshape(total, width)
        for j in range(2):
            kv[i, :, columns(j, width)] = dot(tokens, weight[1 + j]).astype(BF)
        turned[:, columns(i, total)] = tokens.T
    mask = head_mask(length)
    position = lax.broadcasted_iota(jnp.int32, (1, total), 1)
    probs = {}
    for i in range(per):
        e = step * per + i
        valid = position < counts[where[3] * (pl.num_programs(0) * per) + e]
        here = rows_of(e * length, length)
        for g in range(GROUPS):
            lanes = columns(g, LANES)
            queries = stack_heads(q2[here, lanes], mask)
            scores = dot_nt(queries, kv[i, :, lanes]) * SCALE
            scores = jnp.where(valid, scores, -1e30)
            top = jnp.maximum(jnp.max(scores, axis=-1, keepdims=True), 0.0)
            powers = jnp.exp(scores - top)
            weight_sum = jnp.sum(powers, axis=-1, keepdims=True) + jnp.exp(-top)
            probs[i, g] = (powers / weight_sum).astype(BF)
    for i in range(per):
        here = rows_of((step * per + i) * length, length)
        for g in range(GROUPS):
            p2[i, g] = probs[i, g]
            found = dot(probs[i, g], kv[i, :, width + g * LANES : width + (g + 1) * LANES])
            o2[here, columns(g, LANES)] = merge_heads(found, mask).astype(BF)

    @pl.when(step == pl.num_programs(0) - 1)
    def _():
        x2[...] = x1[...] + dot(o2[...], weight[3])


def dense_inner(
    where, x2, vec, bias, cotangent, weights, a3, h, slope, near, far, theirs,
    weight, grad, cot, sems,
):
    rows, width = x2.shape
    copies = Copies(sems)
    cot_copy = my_examples(where, cotangent, cot, copies)
    loads = load_weight(where, weight, weights, copies)
    hat, _ = normalise(x2[...])
    a3[...] = (hat * vec[4:5, :] + vec[5:6, :]).astype(BF)
    cot_copy.wait()
    gy = cot[...].reshape(rows, width)
    wait_all(loads)
    flat = grad.shape[0] * grad.shape[1] * grad.shape[2]
    step = flat // grad.shape[0]
    for j in range(4):
        for half in range(2):
            cols = slice(j * width + half * 384, j * width + (half + 1) * 384)
            u = dot(a3[...], weight[j, :, half * 384 : (half + 1) * 384]) + bias[:, cols]
            square = u * u
            t = jnp.tanh(0.7978845608 * u * (1.0 + 0.044715 * square))
            h[:, cols] = (0.5 * u * (1.0 + t)).astype(BF)
            slope[:, cols] = (
                0.5 * (1.0 + t)
                + (0.5 * 0.7978845608) * u * (1.0 - t * t) * (1.0 + (3.0 * 0.044715) * square)
            ).astype(BF)
            part = dot_tn(h[:, cols], gy).astype(BF)
            per = 384 // step
            grad[cols.start // step : cols.start // step + per] = part.reshape(
                (per,) + grad.shape[1:]
            )
    wait_all(store_grad(where, grad, near, far, theirs, Copies(sems), True))


def dense_outer(
    where, x2, vec, a3, h, slope, cotangent, weights, y, du, vecs, bias_grad, near, far, theirs,
    weight, grad, cot, sems,
):
    rows, width = x2.shape
    copies = Copies(sems)
    cot_copy = my_examples(where, cotangent, cot, copies)
    wait_all(load_weight(where, weight, weights, copies, True))
    cot_copy.wait()
    gy = cot[...].reshape(rows, width)
    shards = weight.shape[0]
    step = weight.shape[1] * weight.shape[2]
    whole = weight[...].reshape(shards * step, width)
    for j in range(4):
        cols = columns(j, width)
        low = (dot_nt(gy, whole[cols]) * slope[:, cols].astype(F32)).astype(BF)
        du[:, cols] = low
        bias_grad[:, cols] = jnp.sum(low.astype(F32), axis=0, keepdims=True)
        grad[j] = dot_tn(a3[...], low).astype(BF)
    started = store_grad(where, grad, near, far, theirs, Copies(sems))
    result = x2[...] + dot(h[...], whole) + vec[6:7, :]
    y[...] = result.astype(BF).reshape(y.shape)
    vecs[...] = jnp.sum(gy.astype(F32), axis=0, keepdims=True)
    wait_all(started)


def dense_back(where, x2, vec, du, cotangent, weights, gx2, vecs, weight, cot, sems):
    rows, width = x2.shape
    copies = Copies(sems)
    cot_copy = my_examples(where, cotangent, cot, copies)
    loads = load_weight(where, weight, weights, copies)
    hat, scale = normalise(x2[...])
    cot_copy.wait()
    wait_all(loads)
    da3 = dot_nt(du[:, columns(0, width)], weight[0])
    for j in range(1, 4):
        da3 = da3 + dot_nt(du[:, columns(j, width)], weight[j])
    back, gain_grad, shift_grad = norm_back(da3, vec[4:5, :], hat, scale)
    gx2[...] = cot[...].reshape(rows, width).astype(F32) + back
    vecs[0:1, :] = gain_grad
    vecs[1:2, :] = shift_grad


def cross_backward(
    where, x1, vec, gx2, q2, kv, p2, weights, gx1, vecs, dkv, dq2, out_mem, weight, do2, moved, sems
):
    rows, width = x1.shape
    per, total = kv.shape[0], kv.shape[1]
    step = pl.program_id(0)
    length = p2.shape[2] // TOGETHER

    @pl.when(step == 0)
    def _():
        wait_all(load_weight(where, weight, weights, Copies(sems)))
        do2[...] = dot_nt(gx2[...].astype(BF), weight[3]).astype(BF)

    mask = head_mask(length)
    pairs = [(i, g) for i in range(per) for g in range(GROUPS)]
    queries, grads, dz = {}, {}, {}
    for i, g in pairs:
        here = rows_of((step * per + i) * length, length)
        lanes = columns(g, LANES)
        queries[i, g] = stack_heads(q2[here, lanes], mask)
        grads[i, g] = stack_heads(do2[here, lanes], mask)
        dp = dot_nt(grads[i, g], kv[i, :, width + g * LANES : width + (g + 1) * LANES])
        wide = p2[i, g].astype(F32)
        row_sum = jnp.sum(wide * dp, axis=-1, keepdims=True)
        dz[i, g] = (wide * (dp - row_sum)).astype(BF)
    for i, g in pairs:
        here = rows_of((step * per + i) * length, length)
        lanes = columns(g, LANES)
        value_lanes = slice(width + g * LANES, width + (g + 1) * LANES)
        dkv[i, :, value_lanes] = dot_tn(p2[i, g], grads[i, g]).astype(BF)
        dkv[i, :, lanes] = (dot_tn(dz[i, g], queries[i, g]) * SCALE).astype(BF)
        dq = merge_heads(dot(dz[i, g], kv[i, :, lanes]), mask) * SCALE
        dq2[here, lanes] = dq.astype(BF)
    for i in range(per):
        back = dot_nt(dkv[i, :, :width], weight[1]) + dot_nt(dkv[i, :, width:], weight[2])
        moved[i] = back.astype(BF)
        for d, out in enumerate(out_mem):
            slots = out.shape[1]
            out[i] = moved[i, rows_of((where[3] ^ d) * slots, slots), :]

    @pl.when(step == pl.num_programs(0) - 1)
    def _():
        hat, scale = normalise(x1[...])
        back, gain_grad, shift_grad = norm_back(
            dot_nt(dq2[...], weight[0]), vec[2:3, :], hat, scale
        )
        gx1[...] = gx2[...] + back
        vecs[0:1, :] = gain_grad
        vecs[1:2, :] = shift_grad


def cross_grads(where, gx2, a2, o2, dq2, dkv, turned, near, far, theirs, grad, memory, sems):
    width = gx2.shape[1]
    half = pl.program_id(0)

    @pl.when(half == 0)
    def _():
        load = Copies(sems).start(turned, memory)
        grad[0] = dot_tn(a2[...], dq2[...]).astype(BF)
        grad[3] = dot_tn(o2[...], gx2[...].astype(BF)).astype(BF)
        load.wait()

    part = dkv[...].reshape(memory.shape[1], width)
    grad[1 + half] = dot(memory[...], part).astype(BF)

    @pl.when(half == 1)
    def _():
        wait_all(store_grad(where, grad, near, far, theirs, Copies(sems)))


def self_backward(
    group, where, suffix, vec, gx1, a1, qkv, p1, o1, parts, weights, suffix_grad, vecs,
    near, far, theirs, weight, start, grad, dqkv, do1, sems,
):
    rows, width = gx1.shape
    copies = Copies(sems)
    start_copy = my_examples(where, suffix, start, copies)
    loads = load_weight(where, weight, weights, copies)
    gs = gx1[...].astype(BF)
    grad[3] = dot_tn(o1[...], gs).astype(BF)
    wait_all(loads)
    do1[...] = dot_nt(gs, weight[3]).astype(BF)
    mask = head_mask(group)
    for r in range(rows // group):
        here = columns(r, group)
        for g in range(GROUPS):
            lanes = [slice(i * width + g * LANES, i * width + (g + 1) * LANES) for i in range(3)]
            queries = stack_heads(qkv[here, lanes[0]], mask)
            grads = stack_heads(do1[here, lanes[0]], mask)
            probs = p1[r * GROUPS + g]
            dp = dot_nt(grads, qkv[here, lanes[2]])
            wide = probs.astype(F32)
            row_sum = jnp.sum(wide * dp, axis=-1, keepdims=True)
            dz = (wide * (dp - row_sum)).astype(BF)
            dqkv[here, lanes[2]] = dot_tn(probs, grads).astype(BF)
            dqkv[here, lanes[1]] = (dot_tn(dz, queries) * SCALE).astype(BF)
            dq = merge_heads(dot(dz, qkv[here, lanes[1]]), mask) * SCALE
            dqkv[here, lanes[0]] = dq.astype(BF)
    for j in range(3):
        grad[j] = dot_tn(a1[...], dqkv[:, columns(j, width)]).astype(BF)
    start_copy.wait()
    started = store_grad(where, grad, near, far, theirs, Copies(sems))
    da1 = dot_nt(dqkv[:, columns(0, width)], weight[0])
    for j in range(1, 3):
        da1 = da1 + dot_nt(dqkv[:, columns(j, width)], weight[j])
    hat, scale = normalise(start[...].reshape(rows, width).astype(F32))
    back, gain_grad, shift_grad = norm_back(da1, vec[0:1, :], hat, scale)
    suffix_grad[...] = (gx1[...] + back).astype(BF).reshape(suffix_grad.shape)
    found = [gain_grad, shift_grad]
    for ref in parts:
        for r in range(ref.shape[0]):
            found += [ref[r : r + 1, columns(j, width)] for j in range(ref.shape[1] // width)]
    found.append(jnp.zeros((vecs.shape[0] - len(found), width), F32))
    vecs[...] = jnp.concatenate(found, axis=0).astype(BF)
    wait_all(started)


def run(kernel, inputs, outputs, scratch, copies, grid=(), moved=0):
    def leaf(x):
        return isinstance(x, tuple) and len(x) == 2 and isinstance(x[0], pl.BlockSpec)

    flat_in, tree_in = jax.tree.flatten(inputs, is_leaf=leaf)
    flat_out, tree_out = jax.tree.flatten(outputs, is_leaf=leaf)

    def body(*refs):
        first, second = len(flat_in), len(flat_in) + len(flat_out)
        given = jax.tree.unflatten(tree_in, refs[:first])
        taken = jax.tree.unflatten(tree_out, refs[first:second])
        kernel(*given, *taken, *refs[second:])

    found = pl.pallas_call(
        body,
        grid=grid,
        in_specs=[spec for spec, _ in flat_in],
        out_specs=[spec for spec, _ in flat_out],
        out_shape=[shape for _, shape in flat_out],
        scratch_shapes=scratch + [pltpu.SemaphoreType.DMA((copies,))],
        compiler_params=pltpu.CompilerParams(vmem_limit_bytes=56 * 1024 * 1024),
        cost_estimate=pl.CostEstimate(
            flops=0, bytes_accessed=moved, transcendentals=0
        ),
    )(*[x for _, x in flat_in])
    return jax.tree.unflatten(tree_out, found)


def shape_of(dims, dtype):
    return jax.ShapeDtypeStruct(tuple(dims), dtype)


def over_slow(value, slow, fast):
    groups = [[k * fast + b for k in range(slow)] for b in range(fast)]
    return lax.all_to_all(value, "fsdp", 0, 0, axis_index_groups=groups, tiled=True)


class Gather:
    def __init__(self, half, slow, fast):
        self.half, self.slow, self.fast = half, slow, fast
        self.own, self.own_other = [], []

    def send_slow(self, *others):
        half = after(self.half, *others)
        self.came = [half] + [swap(half, "fsdp", k * self.fast) for k in range(1, self.slow)]

    def send_own(self):
        self.own = [self.half] + [swap(self.half, "fsdp", b) for b in range(1, self.fast)]

    def send_own_cores(self, *others):
        self.own_other = [swap(after(piece, *others), "mem", 1) for piece in self.own]

    def send_fast(self, *others):
        came = [after(piece, *others) for piece in self.came[1 if self.own else 0 :]]
        self.near = jnp.stack(came)
        self.near_other = swap(self.near, "mem", 1)
        self.far = [swap(self.near, "fsdp", b) for b in range(1, self.fast)]

    def whole(self):
        mine = [self.near] + self.far
        theirs = [self.near_other] + [swap(piece, "mem", 1) for piece in self.far]
        return mine + self.own, theirs + self.own_other

    @staticmethod
    def refs(weights):
        return [[(ANY, x) for x in some] for some in weights]


class Scatter:
    def __init__(self, grads, slow, fast, *others, vectors=None):
        self.near, self.far, theirs = grads
        self.slow, self.fast, self.vectors = slow, fast, vectors
        theirs = [after(part, *others) for part in theirs]
        far = [swap(part, "mem", 1) for part in theirs[1:]]
        far = [jnp.concatenate(far[2 * b : 2 * b + 2]) for b in range(fast - 1)]
        self.sent = [swap(theirs[0], "mem", 1)] + far
        if vectors is not None:
            self.vectors = vectors.astype(F32) + swap(vectors, "mem", 1).astype(F32)

    def add_cores(self, *others):
        far = after(self.far, *others)
        self.out = [
            (far[b].astype(F32) + self.sent[b + 1].astype(F32)).astype(BF)
            for b in range(self.fast - 1)
        ]
        return self.out

    def send_fast(self):
        self.came = [swap(part, "fsdp", b + 1) for b, part in enumerate(self.out)]
        if self.vectors is not None:
            low = self.vectors.astype(BF)
            self.vectors = [low] + [swap(low, "fsdp", b) for b in range(1, self.fast)]

    def add_fast(self, *others):
        if self.vectors is not None:
            self.vectors, self.came = lax.optimization_barrier((self.vectors, self.came))
            self.vectors = sum(part.astype(F32) for part in self.vectors)
        total = after(self.near, *others).astype(F32) + self.sent[0].astype(F32)
        for part in self.came:
            total = total + part.astype(F32)
        self.total = total.astype(BF).reshape(self.slow, -1, total.shape[-1])
        if self.vectors is not None:
            low = self.vectors.astype(BF)
            low = jnp.broadcast_to(low, (self.slow,) + low.shape)
            self.total = jnp.concatenate([self.total, low], axis=1)
        return self.total

    def send_slow(self):
        self.came = over_slow(self.total, self.slow, self.fast)

    def add_slow(self, *others):
        return jnp.sum(after(self.came, *others).astype(F32), axis=0)


class Replicas:
    def __init__(self, value, rows, across):
        self.rows = rows
        k = 1
        while 2 * k < across:
            low = value.astype(BF)
            value = low.astype(F32) + swap(low, "mem", 2 * k).astype(F32)
            k *= 2
        low = value.astype(BF)
        self.halves = [low, swap(low, "mem", 2 * k)] if across > 1 else [low]

    def swap_cores(self, *others):
        halves, _ = lax.optimization_barrier((self.halves, others))
        self.others = [swap(half[: 2 * self.rows], "mem", 1) for half in halves]

    def combine(self, c):
        rows = self.rows
        other = sum(half.astype(F32) for half in self.others)
        mine = sum(half.astype(F32) for half in self.halves)
        vectors, mine = mine[2 * rows :], mine[: 2 * rows]
        first = jnp.where(c == 0, mine, other)
        second = jnp.where(c == 0, other, mine)
        return [first[:rows], first[rows:], second[:rows], second[rows:]], vectors


def place_rows(where, blocks, outs, scratch, sems):
    copies = Copies(sems)
    loads = []
    for i, (even, odd) in enumerate(blocks):
        for d, piece in enumerate(even):
            loads.append((copies.start(piece, scratch.at[i, 2 * d]), i, 2 * d))
            loads.append((copies.start(odd.at[d], scratch.at[i, 2 * d + 1]), i, 2 * d + 1))
    examples = scratch.shape[2]
    stores = []
    for load, i, d in loads:
        load.wait()
        target = outs[i].at[pl.ds((where[3] ^ d) * examples, examples)]
        stores.append(copies.start(scratch.at[i, d], target))
    wait_all(stores)


def place_memory(where, pieces, out, scratch, sems):
    examples = scratch.shape[1]
    copies = Copies(sems)
    loads = []
    for d, parts in enumerate(pieces):
        start = 0
        for part in parts:
            held = scratch.at[d, pl.ds(start, part.shape[0])]
            loads.append((copies.start(part, held), held, (where[3] ^ d) * examples + start))
            start += part.shape[0]
    stores = []
    for load, held, place in loads:
        load.wait()
        stores.append(copies.start(held, out.at[pl.ds(place, held.shape[0])]))
    wait_all(stores)


def spread_across(value, mem):
    return [value] + [swap(value, "mem", d) for d in range(2, mem, 2)]


def per_device(
    suffix,
    memory,
    counts,
    cotangent,
    self_norm_gain,
    self_norm_bias,
    self_query,
    self_key,
    self_value,
    self_output,
    cross_norm_gain,
    cross_norm_bias,
    cross_query,
    cross_key,
    cross_value,
    cross_output,
    dense_norm_gain,
    dense_norm_bias,
    dense_in,
    dense_in_bias,
    dense_out,
    dense_out_bias,
):
    f = lax.axis_index("fsdp")
    m = lax.axis_index("mem")
    c = m % 2
    fsdp = lax.axis_size("fsdp")
    mem = lax.axis_size("mem")
    across = mem // 2
    slow, fast = fsdp_split(fsdp)
    SHARDS[0] = fsdp
    where = jnp.stack([f // fast, f % fast, c, m]).astype(jnp.int32)
    examples = suffix.shape[0] // mem
    length = suffix.shape[1]
    width = suffix.shape[2]
    slots = memory.shape[1]
    total = mem * slots
    rows = examples * length
    inner = dense_in.shape[1]
    part = width // fsdp
    group = min(128, rows)
    blocks = 4 * fsdp

    def gather(matrices, *others):
        halves = [jnp.concatenate(matrices[:2]), jnp.concatenate(matrices[2:])]
        half = jnp.concatenate([jnp.where(c == 0, *halves), *others])
        return Gather(half, slow, fast)

    cross_gather = gather([cross_query, cross_key, cross_value, cross_output])
    in_gather = gather([dense_in[:, columns(j, width)] for j in range(4)])
    out_gather = gather([dense_out[columns(j, part)] for j in range(4)])
    small = [
        self_norm_gain,
        self_norm_bias,
        cross_norm_gain,
        cross_norm_bias,
        dense_norm_gain,
        dense_norm_bias,
        dense_out_bias,
    ]
    small += [dense_in_bias[columns(j, part)] for j in range(4)]
    small = sum(
        jnp.pad(value[None], ((i, 15 - i), (0, width - part))) for i, value in enumerate(small)
    )
    self_gather = gather([self_query, self_key, self_value, self_output], small)

    def exchange(value):
        blocks = value.reshape((mem, examples) + value.shape[1:])
        return lax.all_to_all(blocks, "mem", 0, 0, tiled=True)

    all_memory = exchange(after(memory, self_gather.half))
    self_gather.send_slow()
    out_gather.send_own()
    sent = [*self_gather.came, *out_gather.own[1:]]
    self_gather.send_fast(*sent)
    cross_gather.send_slow(*sent)
    sent = [*self_gather.far, *cross_gather.came, all_memory]
    self_gather.far = [after(piece, *sent) for piece in self_gather.far]
    self_weights = self_gather.whole()
    cross_gather.send_fast(*self_gather.far)
    in_gather.send_slow(*self_gather.far)

    half = (2, part, width)
    grads_like = [
        (ANY, shape_of((slow,) + half, BF)),
        (ANY, shape_of((fast - 1, slow) + half, BF)),
        [(ANY, shape_of((slow,) + half, BF))]
        + [(ANY, shape_of((slow // 2,) + half, BF))] * (2 * fast - 2),
    ]

    def flat(dims, dtype):
        return (VMEM, shape_of(dims, dtype))

    per = 2 if examples % 2 == 0 else 1

    def per_example(value):
        dims = value.shape[1:]
        spec = pl.BlockSpec((per,) + dims, lambda e: (e,) + (0,) * len(dims))
        return (spec, value)

    def slots_of_example(value):
        spec = pl.BlockSpec((mem, per, slots, width), lambda e: (0, e, 0, 0))
        return (spec, value)

    def scratch(*dims):
        return pltpu.VMEM(dims, BF)

    def scatter(grads, *others, vectors=None):
        return Scatter(grads, slow, fast, *others, vectors=vectors)

    wide = (rows, width)
    square = scratch(4, width, width)
    own_rows = scratch(examples, length, width)
    x1, a1, qkv, p1, o1, vec = run(
        functools.partial(self_forward, group),
        [(SMEM, where), (ANY, suffix), Gather.refs(self_weights)],
        [
            flat(wide, F32),
            flat(wide, BF),
            flat((rows, 3 * width), BF),
            flat((rows // group * GROUPS, TOGETHER * group, group), BF),
            flat(wide, BF),
            flat((16, width), F32),
        ],
        [square, own_rows, scratch(fsdp, 16, 128)],
        1 + fsdp + blocks,
    )
    small = [after(piece, x1)[:, 2 * part + 7 : 2 * part + 11, :part] for piece in self_weights[0]]
    order = jnp.arange(fsdp) ^ f
    bias_in = jnp.take(jnp.concatenate(small), order % fast * slow + order // fast, axis=0)
    bias_in = bias_in.astype(F32).reshape(1, inner)
    cross_gather.far = [after(piece, x1, *in_gather.came) for piece in cross_gather.far]
    cross_weights = Gather.refs(cross_gather.whole())
    in_gather.send_fast(*cross_gather.far)
    out_gather.send_slow(*cross_gather.far)
    out_gather.send_own_cores(*cross_gather.far)
    tokens = examples * total
    turned_spec = pl.BlockSpec((width, per * total), lambda e: (0, e))
    x2, a2, q2, kv, p2, o2, turned = run(
        cross_forward,
        [(SMEM, where), (SMEM, counts), (VMEM, after(x1, bias_in)), (VMEM, vec)]
        + [slots_of_example(all_memory), cross_weights],
        [
            flat(wide, F32),
            flat(wide, BF),
            flat(wide, BF),
            per_example(shape_of((examples, total, 2 * width), BF)),
            per_example(shape_of((examples, GROUPS, TOGETHER * length, total), BF)),
            flat(wide, BF),
            (turned_spec, shape_of((width, tokens), BF)),
        ],
        [square],
        blocks,
        (examples // per,),
    )
    in_gather.far = [after(piece, x2, *out_gather.came) for piece in in_gather.far]
    in_weights = Gather.refs(in_gather.whole())
    out_gather.send_fast(*in_gather.far)
    ready = after(x2, out_gather.near_other, *out_gather.own_other)
    a3, h, slope, *grads = run(
        dense_inner,
        [(SMEM, where), (VMEM, ready), (VMEM, vec), (VMEM, bias_in), (ANY, cotangent), in_weights],
        [flat(wide, BF), flat((rows, inner), BF), flat((rows, inner), BF)] + grads_like,
        [square, scratch(fsdp, 4, part, width), own_rows],
        1 + blocks,
    )
    out_gather.far = [after(piece, a3) for piece in out_gather.far]
    out_weights = Gather.refs(out_gather.whole())
    out_scatter = scatter(grads, *out_gather.far)
    out_sum = out_scatter.add_cores()
    out_scatter.send_fast()
    y, du, vecs_y, bias_grad, *grads = run(
        dense_outer,
        [(SMEM, where), (VMEM, after(x2, *out_sum)), (VMEM, vec), (VMEM, a3), (VMEM, h)]
        + [(VMEM, slope), (ANY, cotangent), out_weights],
        [
            flat((examples, length, width), BF),
            flat((rows, inner), BF),
            flat((1, width), F32),
            flat((1, inner), F32),
        ]
        + grads_like,
        [scratch(fsdp, 4, part, width), square, own_rows],
        1 + blocks,
    )
    in_grads = grads
    gx2, vecs_dense = run(
        dense_back,
        [(SMEM, where), (VMEM, x2), (VMEM, vec), (VMEM, du), (ANY, cotangent), in_weights],
        [flat(wide, F32), flat((2, width), F32)],
        [square, own_rows],
        1 + blocks,
    )
    in_scatter = scatter(in_grads, gx2)
    in_sum = in_scatter.add_cores(*out_scatter.came)
    in_scatter.send_fast()
    out_total = out_scatter.add_fast(*in_sum)
    out_scatter.send_slow()
    gx1, vecs_cross, dkv, dq2, grad_memory = run(
        cross_backward,
        [(SMEM, where), (VMEM, x1), (VMEM, vec), (VMEM, after(gx2, out_total, *in_sum)), (VMEM, q2)]
        + [per_example(kv), per_example(p2), cross_weights],
        [
            flat(wide, F32),
            flat((2, width), F32),
            per_example(shape_of((examples, total, 2 * width), BF)),
            flat(wide, BF),
            [per_example(shape_of((examples, slots, width), BF))] * mem,
        ],
        [square, scratch(*wide), scratch(per, total, width)],
        blocks,
        (examples // per,),
        60_000_000,
    )
    in_scatter.came, _ = lax.optimization_barrier((in_scatter.came, gx1))
    out_final = out_scatter.add_slow(*in_scatter.came)
    in_total = in_scatter.add_fast(out_final)
    in_scatter.send_slow()
    cut = examples // 2
    mem_pieces = [grad_memory[:1]]
    for d in range(1, mem):
        parts = [grad_memory[d][:cut], grad_memory[d][cut:]] if d == 2 else [grad_memory[d]]
        mem_pieces.append([swap(part, "mem", d) for part in parts])
    grads = run(
        cross_grads,
        [(SMEM, where), (VMEM, after(gx2, in_total)), (VMEM, a2), (VMEM, o2), (VMEM, dq2)]
        + [(pl.BlockSpec((examples, total, width), lambda j: (0, 0, j)), dkv), (ANY, turned)],
        grads_like,
        [square, scratch(width, tokens)],
        blocks,
        (2,),
    )
    cross_scatter = scatter(grads, *mem_pieces[1], *mem_pieces[2][:1])
    cross_sum = cross_scatter.add_cores()
    cross_scatter.send_fast()
    gx1 = after(gx1, *cross_sum)
    suffix_part, vecs_self, *grads = run(
        functools.partial(self_backward, group),
        [(SMEM, where), (ANY, suffix), (VMEM, vec), (VMEM, gx1), (VMEM, a1)]
        + [(VMEM, qkv), (VMEM, p1), (VMEM, o1)]
        + [[(VMEM, x) for x in (vecs_cross, vecs_dense, vecs_y, bias_grad)], Gather.refs(self_weights)],
        [flat((examples, length, width), BF), flat((16, width), BF)] + grads_like,
        [square, own_rows, square, scratch(rows, 3 * width), scratch(*wide)],
        1 + blocks,
    )
    in_final = in_scatter.add_slow(suffix_part)
    self_scatter = scatter(grads, in_final, *mem_pieces[3], vectors=vecs_self)
    self_sum = self_scatter.add_cores()
    self_scatter.send_fast()
    cross_scatter.add_fast(*self_sum)
    cross_scatter.send_slow()
    dense_sum = jnp.concatenate([out_final, after(in_final, *self_sum)])
    dense_sum = Replicas(dense_sum, 2 * part, across)
    self_total = self_scatter.add_fast(*dense_sum.halves)
    self_scatter.send_slow()
    cross_sum = Replicas(cross_scatter.add_slow(self_total), part, across)
    suffix_rows = spread_across(after(suffix_part, self_total), mem)
    y_rows = spread_across(after(y, self_total), mem)
    dense_sum.swap_cores(self_total)
    mem_pieces = [[after(part, self_total) for part in parts] for parts in mem_pieces]
    (memory_grad,) = run(
        place_memory,
        [(SMEM, where), [[(ANY, part) for part in parts] for parts in mem_pieces]],
        [(ANY, shape_of(memory.shape, BF))],
        [scratch(mem, examples, slots, width)],
        2 * mem + 2,
    )
    (out_low, in_low, out_high, in_high), _ = dense_sum.combine(c)
    grad_in = jnp.concatenate([in_low[:part], in_low[part:], in_high[:part], in_high[part:]], axis=1)
    grad_out = jnp.concatenate([out_low, out_high])
    y_all, suffix_all = jnp.stack(y_rows), jnp.stack(suffix_rows)
    done = [*cross_sum.halves, y_all, suffix_all, grad_in, grad_out, memory_grad]
    self_final = Replicas(self_scatter.add_slow(*done), part, across)
    cross_sum.swap_cores(self_final.halves[0])
    y_far = swap(after(y_all, self_final.halves[0]), "mem", 1)
    suffix_far = swap(after(suffix_all, self_final.halves[0]), "mem", 1)
    blocks = [([(ANY, x) for x in y_rows], (ANY, y_far))]
    blocks += [([(ANY, x) for x in suffix_rows], (ANY, suffix_far))]
    ((block_output, suffix_grad),) = run(
        place_rows,
        [(SMEM, where), blocks],
        [[(ANY, shape_of(suffix.shape, BF))] * 2],
        [scratch(2, mem, examples, length, width)],
        4 * mem,
    )
    grad_cross, _ = cross_sum.combine(c)
    self_final.swap_cores(block_output)
    grad_self, vectors = self_final.combine(c)

    def vector(i):
        return lax.dynamic_slice(vectors, (i, f * part), (1, part)).reshape(part)

    return (
        block_output,
        suffix_grad,
        memory_grad,
        vector(0),
        vector(1),
        *grad_self,
        vector(2),
        vector(3),
        *grad_cross,
        vector(4),
        vector(5),
        grad_in,
        lax.dynamic_slice_in_dim(vectors[7:11].reshape(-1), f * (inner // fsdp), inner // fsdp, 0),
        grad_out,
        vector(6),
    )


def solution(mesh):
    rows = P("fsdp", None, None)
    matrix = P("fsdp", None)
    vector = P("fsdp")
    attention = (vector, vector, matrix, matrix, matrix, matrix)
    params = attention + attention + (vector, vector, matrix, vector, matrix, vector)
    return jax.shard_map(
        per_device,
        mesh=mesh,
        in_specs=(rows, P("fsdp", "mem", None), vector, rows) + params,
        out_specs=(rows, rows, P("fsdp", "mem", None)) + params,
        check_vma=False,
    )
```
